32 devices in a mesh: dp: 8 (over y, x, core), head: 4 (over z).
Axes of the slice: x: 2, y: 2, z: 4, core: 2. Of those that a mesh axis runs over, the one named last changes fastest.
Arguments:
- layer_input: bfloat16 [8192, 1024], P('dp'), may hold values from -6 to 6
- w_query: bfloat16 [1024, 1024], P(None, 'head'), may hold values from -0.1875 to 0.1875
- w_key: bfloat16 [1024, 1024], P(None, 'head'), may hold values from -0.1875 to 0.1875
- w_value: bfloat16 [1024, 1024], P(None, 'head'), may hold values from -0.1875 to 0.1875
- w_gate: bfloat16 [1024, 1024], replicated, may hold values from -0.1875 to 0.1875
- w_out: bfloat16 [1024, 1024], replicated, may hold values from -0.1875 to 0.1875
- w_first: bfloat16 [1024, 2816], P(None, 'head'), may hold values from -0.1875 to 0.1875
- w_second: bfloat16 [1024, 2816], P(None, 'head'), may hold values from -0.1875 to 0.1875
- w_third: bfloat16 [2816, 1024], P('head'), may hold values from -0.109375 to 0.109375
- decay_rates: float32 [8], P('head'), may hold values from 0.00048828125 to 0.04
- seq_lengths: int32 [8], P('dp'), may hold values from 769 to 1024, as said below
- cotangent: bfloat16 [8192, 1024], P(('dp', 'head')), may hold values from -6 to 6
Outputs:
- output: bfloat16 [8192, 1024], P(('dp', 'head'))
- input_grad: bfloat16 [8192, 1024], P(('dp', 'head'))
- grad_query: float32 [1024, 1024], P('dp', 'head')
- grad_key: float32 [1024, 1024], P('dp', 'head')
- grad_value: float32 [1024, 1024], P('dp', 'head')
- grad_gate: float32 [1024, 1024], P(('dp', 'head'))
- grad_out: float32 [1024, 1024], P(('dp', 'head'))
- grad_first: float32 [1024, 2816], P('dp', 'head')
- grad_second: float32 [1024, 2816], P('dp', 'head')
- grad_third: float32 [2816, 1024], P('head', 'dp')
The draws below stay inside these ranges and needn't reach their ends.
Inputs may be any that keep to these rules, and one draw needn't show every extreme that they name: `seq_lengths`: one bucket in every draw holds a sequence of all 1024 slots.
All inputs are finite; a program needn't handle non-finite values.
Results may differ from the reference program's by a relative error of at most 0.018.
Values may be sent and summed in bfloat16 or wider, within the bound.
A program may use at most 128 MiB of HBM per device.

```python
import math
import jax
import jax.numpy as jnp
from jax import lax

D = 1024
HEADS = 8
HDIM = 128
FF = 2816
SPAN = 512
GROUP_TOK = 1024
TOKENS = 8192
N_DP = 8


def draw_seq_lengths(key, part):
    key = jax.random.fold_in(key, 11)
    first_key, second_key, third_key = jax.random.split(key, 3)
    quarter = GROUP_TOK // 4
    short_one = jax.random.randint(first_key, (N_DP,), 0, quarter)
    short_two = jax.random.randint(second_key, (N_DP,), 0, quarter)
    lengths = GROUP_TOK - jnp.minimum(short_one, short_two)
    chosen = jax.random.randint(third_key, (), 0, N_DP)
    return jnp.where(jnp.arange(N_DP) == chosen, GROUP_TOK, lengths).astype(jnp.int32)


def block_scale(own_key, shape, cuts, low, high):
    def one(dim, blocks):
        draws = jax.random.uniform(jax.random.fold_in(jax.random.fold_in(own_key, 6), dim), (blocks,), jnp.float32, low / len(cuts), high / len(cuts))
        return jnp.repeat(jnp.exp(draws), shape[dim] // blocks).reshape((-1,) + (1,) * (len(shape) - dim - 1))

    level = one(*cuts[0])
    for cut in cuts[1:]:
        level = level * one(*cut)
    return level


def noise(own_key, dims, deviation, limit, cuts=(), dtype=jnp.bfloat16):
    values = deviation * jax.random.normal(own_key, dims, jnp.float32)
    if cuts:
        values = values * block_scale(own_key, dims, cuts, -0.22, 0.18)
    return jnp.clip(values, -limit, limit).astype(dtype)


def setup_inputs(seed: int = 0) -> dict:
    key_list = jax.random.split(jax.random.key(seed), 13)
    return {
        "layer_input": noise(key_list[0], (TOKENS, D), 1.0, 6.0, ((0, 8),)),
        "w_query": noise(key_list[1], (D, D), D ** -0.5, 0.1875, ((1, 4),)),
        "w_key": noise(key_list[2], (D, D), D ** -0.5, 0.1875, ((1, 4),)),
        "w_value": noise(key_list[3], (D, D), D ** -0.5, 0.1875, ((1, 4),)),
        "w_gate": noise(key_list[4], (D, D), D ** -0.5, 0.1875),
        "w_out": noise(key_list[5], (D, D), D ** -0.5, 0.1875),
        "w_first": noise(key_list[6], (D, FF), D ** -0.5, 0.1875, ((1, 4),)),
        "w_second": noise(key_list[7], (D, FF), D ** -0.5, 0.1875, ((1, 4),)),
        "w_third": noise(key_list[8], (FF, D), FF ** -0.5, 0.109375, ((0, 4),)),
        "decay_rates": jnp.clip(jnp.exp(math.log(0.04) - 4.405743 * jax.random.uniform(key_list[9], (HEADS,), jnp.float32) ** block_scale(key_list[9], (HEADS,), ((0, 4),), -0.2, 0.2)), 0.00048828125, 0.04),
        "seq_lengths": draw_seq_lengths(jax.random.fold_in(key_list[12], 71), 0),
        "cotangent": noise(key_list[11], (TOKENS, D), 1.0, 6.0, ((0, 32),)),
    }


epsilon = 1e-06

@jax.custom_vjp
def low(v):
    return lax.optimization_barrier(v.astype(jnp.bfloat16)).astype(jnp.float32)

@jax.custom_vjp
def low_back(v):
    return v

def low_keep(v):
    return (low(v), None)

def low_pass(kept, grad):
    return (grad,)

def back_keep(v):
    return (v, None)

def back_low(kept, grad):
    return (low(grad),)
low.defvjp(low_keep, low_pass)
low_back.defvjp(back_keep, back_low)

def normalize(values):
    return values * lax.rsqrt(lax.optimization_barrier(jnp.mean(values * values, axis=-1, keepdims=True)) + epsilon)

def matmul_high(left, right):
    return jnp.dot(left, right, precision=lax.Precision.HIGHEST)

def head_attention(queries, all_keys, values, rate_value):
    span_count = queries.shape[0] // SPAN
    positions = jnp.arange(SPAN).astype(jnp.float32)
    offset = positions[:, None] - positions[None, :]
    causal = offset >= 0
    decay_inner = jnp.where(causal, jnp.exp(-rate_value * jnp.where(causal, offset, 0.0)), 0.0)
    query_decay = jnp.exp(-rate_value * (positions + 1.0))[:, None]
    key_decay = jnp.exp(-rate_value * (SPAN - 1.0 - positions))[:, None]
    block_decay = jnp.exp(-rate_value * SPAN)

    def span_step(state, span_data):
        query_blk, key_blk, value_blk = span_data
        scores = low_back(matmul_high(query_blk, key_blk.T))
        weights = low(scores * decay_inner)
        result = matmul_high(weights, value_blk) + matmul_high(query_blk * query_decay, state)
        state = block_decay * state + matmul_high((key_blk * key_decay).T, value_blk)
        return (state, result)
    initial = jnp.zeros((HDIM, HDIM), jnp.float32)
    shaped = (queries.reshape(span_count, SPAN, HDIM), all_keys.reshape(span_count, SPAN, HDIM), values.reshape(span_count, SPAN, HDIM))
    final_state, results = lax.scan(jax.checkpoint(span_step), initial, shaped)
    return results.reshape(span_count * SPAN, HDIM)

def layer_forward(inputs, w_query, w_key, w_value, w_gate, w_out, w_first, w_second, w_third, key_mask, rates):
    token_count = inputs.shape[0]
    normed = low(normalize(inputs))
    queries = low(jax.nn.silu(low_back(matmul_high(normed, w_query))))
    all_keys = low(key_mask * jax.nn.silu(low_back(matmul_high(normed, w_key))))
    values = low(key_mask * low_back(matmul_high(normed, w_value)))
    mixed_out = jax.vmap(head_attention, in_axes=(1, 1, 1, 0), out_axes=1)(queries.reshape(token_count, HEADS, HDIM), all_keys.reshape(token_count, HEADS, HDIM), values.reshape(token_count, HEADS, HDIM), rates)
    attention = low_back(low(mixed_out.reshape(token_count, D)))
    gated = low(normalize(attention) * low_back(matmul_high(normed, w_gate)))
    hidden = inputs + key_mask * low_back(matmul_high(gated, w_out))
    hidden_low = low(normalize(hidden))
    product = low(low_back(matmul_high(hidden_low, w_first)) * low_back(matmul_high(hidden_low, w_second)))
    return hidden + key_mask * low_back(matmul_high(product, w_third))

def reference(layer_input, w_query, w_key, w_value, w_gate, w_out, w_first, w_second, w_third, decay_rates, seq_lengths, cotangent):
    params = tuple((weight_arg.astype(jnp.float32) for weight_arg in (w_query, w_key, w_value, w_gate, w_out, w_first, w_second, w_third)))
    inputs = layer_input.astype(jnp.float32).reshape(N_DP, GROUP_TOK, D)
    upstream = cotangent.astype(jnp.float32).reshape(N_DP, GROUP_TOK, D)
    positions = jnp.arange(GROUP_TOK).astype(jnp.int32)
    rates = decay_rates.astype(jnp.float32)

    def group_step(running, group_data):
        group_input, group_upstream, seq_length = group_data
        key_mask = (positions < seq_length).astype(jnp.float32)[:, None]

        def forward(inner_input, *weight_list):
            return layer_forward(inner_input, *weight_list, key_mask, rates)
        result, pullback = jax.vjp(forward, group_input, *params)
        grad_list = pullback(group_upstream)
        running = tuple((entry + grad_entry for entry, grad_entry in zip(running, grad_list[1:])))
        return (running, (result.astype(jnp.bfloat16), grad_list[0].astype(jnp.bfloat16)))
    initial = tuple((jnp.zeros_like(weight_arg) for weight_arg in params))
    running, (outputs, input_grads) = lax.scan(group_step, initial, (inputs, upstream, seq_lengths))
    return (outputs.reshape(TOKENS, D), input_grads.reshape(TOKENS, D), running[0], running[1], running[2], running[3], running[4], running[5], running[6], running[7])
```

```python
import functools

import jax
import jax.numpy as jnp
from jax import lax
from jax.experimental import pallas as pl
from jax.experimental.pallas import tpu as pltpu
from jax.sharding import PartitionSpec as P

SPAN = 512
HDIM = 128

epsilon = 1e-06
bf16 = jnp.bfloat16
f32 = jnp.float32
VMEM_LIMIT = 48 * 2**20


def inverse_rms(values):
    return lax.rsqrt(jnp.mean(values * values, axis=-1, keepdims=True) + epsilon)


def normalize(values):
    return values * inverse_rms(values)


def norm_back(values, incoming):
    inverse = inverse_rms(values)
    unit_rows = values * inverse
    return inverse * (incoming - unit_rows * jnp.mean(incoming * unit_rows, axis=-1, keepdims=True))


def dot_plain(left, right):
    return jnp.dot(left, right, preferred_element_type=f32)


def dot_right_t(left, right):
    return lax.dot_general(left, right, (((1,), (1,)), ((), ())), preferred_element_type=f32)


def dot_left_t(left, right):
    return lax.dot_general(left, right, (((0,), (0,)), ((), ())), preferred_element_type=f32)


def column(length):
    return lax.broadcasted_iota(jnp.int32, (length, 1), 0)


def inner_decay(rate):
    rows = lax.broadcasted_iota(jnp.int32, (SPAN, SPAN), 0)
    cols = lax.broadcasted_iota(jnp.int32, (SPAN, SPAN), 1)
    offset = rows - cols
    return jnp.where(offset >= 0, jnp.exp(-rate * jnp.maximum(offset, 0).astype(f32)), 0.0)


def attend_kernel(
    meta, rates, x, w_own_q, w_own_k, w_own_v, w_other,
    normed, attention, queries, keys, values, query_slope, key_slope, states,
):
    pair, length = meta[0], meta[1]
    start = pl.multiple_of(pair * SPAN, SPAN)
    rows = x.shape[0]
    head_width = w_own_q.shape[1]

    def norm_step(i, carry):
        place = pl.ds(pl.multiple_of(i * 128, 128), 128)
        normed[place, :] = normalize(x[place, :].astype(f32)).astype(bf16)
        return carry

    lax.fori_loop(0, rows // 128, norm_step, 0)
    block = normed[pl.ds(start, SPAN), :]
    mask = (start + column(SPAN) < length).astype(f32)
    early_mask = (column(SPAN) < length).astype(f32) * pair.astype(f32)
    early = normed[0:SPAN, :]
    places = column(SPAN).astype(f32)
    for part in range(2):
        if part == 0:
            wq, wk, wv = w_own_q[...], w_own_k[...], w_own_v[...]
        else:
            wq, wk, wv = (w_other[:, i * head_width : (i + 1) * head_width] for i in range(3))
        pre_query = dot_plain(block, wq)
        pre_key = dot_plain(block, wk)
        pre_value = dot_plain(block, wv)
        sigmoid_query = jax.nn.sigmoid(pre_query)
        sigmoid_key = jax.nn.sigmoid(pre_key)
        query = (pre_query * sigmoid_query).astype(bf16)
        key = (mask * (pre_key * sigmoid_key)).astype(bf16)
        value = (mask * pre_value).astype(bf16)
        wide = slice(part * head_width, (part + 1) * head_width)
        query_slope[:, wide] = (sigmoid_query * (1.0 + pre_query * (1.0 - sigmoid_query))).astype(bf16)
        key_slope[:, wide] = (mask * (sigmoid_key * (1.0 + pre_key * (1.0 - sigmoid_key)))).astype(bf16)
        queries[:, wide] = query
        keys[:, wide] = key
        values[:, wide] = value
        early_key = dot_plain(early, wk)
        early_key = early_mask * (early_key * jax.nn.sigmoid(early_key)).astype(bf16).astype(f32)
        early_value = (early_mask * dot_plain(early, wv)).astype(bf16)
        for head in range(head_width // HDIM):
            index = part * (head_width // HDIM) + head
            rate = rates[index]
            cols = slice(head * HDIM, (head + 1) * HDIM)
            q, k, v = query[:, cols], key[:, cols], value[:, cols]
            scores = dot_right_t(q, k)
            weights = (scores * inner_decay(rate)).astype(bf16)
            keyed = (early_key[:, cols] * jnp.exp(-rate * (SPAN - 1.0 - places))).astype(bf16)
            state = dot_left_t(keyed, early_value[:, cols])
            states[index] = state
            decayed = (q.astype(f32) * jnp.exp(-rate * (places + 1.0))).astype(bf16)
            out = dot_plain(weights, v) + dot_plain(decayed, state.astype(bf16))
            attention[:, index * HDIM : (index + 1) * HDIM] = out.astype(bf16)


def state_kernel(rates, queries, upstream, state_grad):
    places = column(SPAN).astype(f32)
    for index in range(state_grad.shape[0]):
        cols = slice(index * HDIM, (index + 1) * HDIM)
        decayed = (queries[:, cols].astype(f32) * jnp.exp(-rates[index] * (places + 1.0))).astype(bf16)
        state_grad[index] = dot_left_t(decayed, upstream[:, cols])


def attend_back_kernel(
    meta, rates, queries, keys, values, upstream, query_slope, key_slope, states, state_grad, pre_grads
):
    pair, length = meta[0], meta[1]
    mask = (pair * SPAN + column(SPAN) < length).astype(f32)
    places = column(SPAN).astype(f32)
    heads = states.shape[0]
    half = heads // 2
    for index in range(heads):
        rate = rates[index]
        cols = slice(index * HDIM, (index + 1) * HDIM)
        q, k, v, g = queries[:, cols], keys[:, cols], values[:, cols], upstream[:, cols]
        decay = inner_decay(rate)
        query_decay = jnp.exp(-rate * (places + 1.0))
        key_decay = jnp.exp(-rate * (SPAN - 1.0 - places))
        state = states[index].astype(bf16)
        carried = state_grad[index].astype(bf16)
        weights = (dot_right_t(q, k) * decay).astype(bf16)
        score_grad = (dot_right_t(g, v) * decay).astype(bf16)
        dq = dot_plain(score_grad, k) + query_decay * dot_right_t(g, state)
        dk = dot_left_t(score_grad, q) + key_decay * dot_right_t(v, carried)
        dv = dot_left_t(weights, g) + key_decay * dot_plain(k, carried)
        base = (index // half) * (3 * half * HDIM) + (index % half) * HDIM
        pre_grads[:, base : base + HDIM] = (dq * query_slope[:, cols].astype(f32)).astype(bf16)
        base += half * HDIM
        pre_grads[:, base : base + HDIM] = (dk * key_slope[:, cols].astype(f32)).astype(bf16)
        base += half * HDIM
        pre_grads[:, base : base + HDIM] = (dv * mask).astype(bf16)


def vmem():
    return pl.BlockSpec(memory_space=pltpu.VMEM)


def smem():
    return pl.BlockSpec(memory_space=pltpu.SMEM)


def local_call(body, name, out_shapes, args, scalars, flops):
    size = sum(int(a.size) * a.dtype.itemsize for a in list(args) + list(out_shapes))
    return pl.pallas_call(
        body,
        out_shape=out_shapes,
        in_specs=[smem()] * scalars + [vmem()] * (len(args) - scalars),
        out_specs=[vmem()] * len(out_shapes),
        compiler_params=pltpu.CompilerParams(vmem_limit_bytes=VMEM_LIMIT),
        cost_estimate=pl.CostEstimate(flops=flops, bytes_accessed=size, transcendentals=0),
        name=name,
    )(*args)


def shards(
    n_dp, n_head,
    layer_input, w_query, w_key, w_value, w_gate, w_out, w_first, w_second, w_third,
    decay_rates, seq_lengths, cotangent,
):
    group_rows, width = layer_input.shape
    row_count = cotangent.shape[0]
    heads = decay_rates.shape[0]
    head_width = w_query.shape[1]
    place = lax.axis_index("dp")
    own = lax.axis_index("head")
    member, pair = own % 2, own // 2
    bits = n_dp.bit_length() - 1
    length = seq_lengths[0]

    def to_mate(array, bit):
        return lax.ppermute(array, "head", [(i, i ^ bit) for i in range(n_head)])

    def across(array, bit):
        return lax.ppermute(array, "dp", [(i, i ^ (1 << bit)) for i in range(n_dp)])

    def gathered(weight, axis):
        size = weight.shape[axis] // n_dp
        share = lax.dynamic_slice_in_dim(weight, place * size, size, axis)
        return lax.all_gather(to_mate(share, 2), "dp", axis=axis, tiled=True)

    w_heads = jnp.concatenate([w_query, w_key, w_value], axis=1)
    w_heads_other = gathered(w_heads, 0)
    w_first_other = gathered(w_first, 0)
    w_second_other = gathered(w_second, 0)
    w_third_other = gathered(w_third, 1)
    rates = jnp.concatenate([decay_rates, to_mate(decay_rates, 2)])

    block_start = pair * SPAN
    row_start = own * row_count
    positions = jnp.arange(row_count, dtype=jnp.int32)[:, None]
    row_mask = (row_start + positions < length).astype(f32)
    upstream = cotangent.astype(f32)
    last_own = (row_mask * upstream).astype(bf16)
    last_mate = to_mate(last_own, 1)

    meta = jnp.stack([pair, length]).astype(jnp.int32)
    both = 2 * head_width
    shape = jax.ShapeDtypeStruct
    block_shape = shape((SPAN, both), bf16)
    normed, attention_block, queries, keys, values, query_slope, key_slope, states = local_call(
        attend_kernel, "attend",
        [shape(layer_input.shape, bf16)] + [block_shape] * 6 + [shape((2 * heads, HDIM, HDIM), f32)],
        [meta, rates, layer_input, w_query, w_key, w_value, w_heads_other], 2, 6 * 10**9,
    )

    def rows_of(array, index):
        return lax.dynamic_slice_in_dim(array, index * row_count, row_count, 0)

    def ordered(mine, other):
        even, odd = jnp.where(member == 0, mine, other), jnp.where(member == 0, other, mine)
        flip = lambda a: jnp.where(pair == 0, a, jnp.concatenate([a[:, head_width:], a[:, :head_width]], axis=1))
        even, odd = flip(even), flip(odd)
        return jnp.concatenate(
            [even[:, :head_width], odd[:, :head_width], even[:, head_width:], odd[:, head_width:]], axis=1
        )

    def pieces(array):
        cut = [array[:, i * head_width : (i + 1) * head_width] for i in range(4)]
        even, odd = jnp.concatenate([cut[0], cut[2]], axis=1), jnp.concatenate([cut[1], cut[3]], axis=1)
        flip = lambda a: jnp.where(pair == 0, a, jnp.concatenate([a[:, head_width:], a[:, :head_width]], axis=1))
        even, odd = flip(even), flip(odd)
        return jnp.where(member == 0, even, odd), jnp.where(member == 0, odd, even)

    received = to_mate(rows_of(attention_block, 1 - member), 1)
    attention = ordered(rows_of(attention_block, member), received).astype(f32)
    attention_norm = normalize(attention)
    rows_low = rows_of(normed, own)
    input_rows = rows_of(layer_input, own).astype(f32)
    gate_pre = dot_plain(rows_low, w_gate)
    gated = (attention_norm * gate_pre).astype(bf16)
    hidden = input_rows + row_mask * dot_plain(gated, w_out)
    hidden_low = normalize(hidden).astype(bf16)
    hidden_mate = to_mate(hidden_low, 1)

    w_first_all = jnp.concatenate([w_first, w_first_other], axis=1)
    w_second_all = jnp.concatenate([w_second, w_second_other], axis=1)
    w_third_all = jnp.concatenate([w_third, w_third_other], axis=0)

    def forward_rows(rows_in):
        first, second = dot_plain(rows_in, w_first_all), dot_plain(rows_in, w_second_all)
        return first.astype(bf16), second.astype(bf16), (first * second).astype(bf16)

    def backward_rows(last, first, second):
        product_grad = dot_right_t(last, w_third_all)
        first_grad = (product_grad * second.astype(f32)).astype(bf16)
        second_grad = (product_grad * first.astype(f32)).astype(bf16)
        return first_grad, second_grad, dot_right_t(first_grad, w_first_all) + dot_right_t(second_grad, w_second_all)

    first_mate, second_mate, product_mate = forward_rows(hidden_mate)
    first_grad_mate, second_grad_mate, norm_grad_mate = backward_rows(last_mate, first_mate, second_mate)
    norm_grad_in = to_mate(norm_grad_mate.astype(bf16), 1)
    mix_in = to_mate(dot_plain(product_mate, w_third_all).astype(bf16), 1)
    first_own, second_own, product_own = forward_rows(hidden_low)
    first_grad_own, second_grad_own, norm_grad_own = backward_rows(last_own, first_own, second_own)
    hidden_grad = upstream + norm_back(hidden, norm_grad_own + norm_grad_in.astype(f32))
    mixed = dot_plain(product_own, w_third_all) + mix_in.astype(f32)
    output = (hidden + row_mask * mixed).astype(bf16)

    branch_grad = (row_mask * hidden_grad).astype(bf16)
    gated_grad = dot_right_t(branch_grad, w_out)
    gate_grad = (gated_grad * attention_norm).astype(bf16)
    attention_grad = norm_back(attention, gated_grad * gate_pre).astype(bf16)
    mine, for_mate = pieces(attention_grad)
    from_mate = to_mate(for_mate, 1)
    grad_block = jnp.concatenate(
        [jnp.where(member == 0, mine, from_mate), jnp.where(member == 0, from_mate, mine)], axis=0
    )
    state_shape = shape((2 * heads, HDIM, HDIM), f32)
    (state_grad,) = local_call(
        state_kernel, "state_grad", [state_shape], [rates, queries, grad_block], 1, 10**8
    )
    swapped = jnp.concatenate([state_grad[heads:], state_grad[:heads]], axis=0)
    carried = lax.ppermute(swapped, "head", [(i, i - 2) for i in range(2, n_head)])
    (pre_grads,) = local_call(
        attend_back_kernel, "attend_back", [shape((SPAN, 3 * both), bf16)],
        [meta, rates, queries, keys, values, grad_block, query_slope, key_slope, states, carried], 2, 2 * 10**9,
    )
    head_terms = dot_right_t(pre_grads[:, : 3 * head_width], w_heads) + dot_right_t(
        pre_grads[:, 3 * head_width :], w_heads_other
    )
    head_terms = head_terms.astype(bf16)
    terms_in = to_mate(rows_of(head_terms, 1 - member), 1)
    input_norm_grad = (
        rows_of(head_terms, member).astype(f32) + terms_in.astype(f32) + dot_right_t(gate_grad, w_gate)
    )
    input_grad = (hidden_grad + norm_back(input_rows, input_norm_grad)).astype(bf16)

    def summed(left, right, order):
        left = left.reshape((left.shape[0],) + (2,) * bits + (width // n_dp,))

        def pick(array, axis, bit, which):
            side = (place // (1 << bit)) % 2
            return lax.dynamic_index_in_dim(array, side if which else 1 - side, axis, keepdims=False)

        left_axis = lambda bit, done: 1 + (bits - 1 - bit) - sum(1 for b in done if b > bit)
        first_bit = order[0]
        make = lambda which: dot_left_t(
            pick(left, left_axis(first_bit, []), first_bit, which).reshape(left.shape[0], width // 2), right
        ).astype(bf16)
        arrived = across(make(False), first_bit)
        total = (make(True).astype(f32) + arrived.astype(f32)).astype(bf16)
        total = total.reshape((2,) * (bits - 1) + (width // n_dp, right.shape[1]))
        done = [first_bit]
        for bit in order[1:]:
            axis = left_axis(bit, done) - 1
            arrived = across(pick(total, axis, bit, False), bit)
            total = (pick(total, axis, bit, True).astype(f32) + arrived.astype(f32)).astype(bf16)
            done.append(bit)
        return total

    def with_mate(total):
        size = total.shape[1] // 2
        return total[:, :size].astype(f32) + to_mate(total[:, size:], 2).astype(f32)

    def over_heads(total):
        for bit in (1, 2):
            cut = total.reshape((2, -1) + total.shape[1:]) if bit == 2 else total.reshape((2, 2, -1) + total.shape[1:])
            side = (own // bit) % 2
            axis = 0 if bit == 2 else 1
            arrived = to_mate(lax.dynamic_index_in_dim(cut, 1 - side, axis, keepdims=False), bit)
            total = lax.dynamic_index_in_dim(cut, side, axis, keepdims=False).astype(f32) + arrived.astype(f32)
            if bit == 1:
                total = total.astype(bf16).reshape((-1,) + total.shape[2:])
        return total

    up = list(range(bits))
    down = [0] + up[:0:-1]
    stack = lambda a, b: jnp.concatenate([a, b], axis=0)
    hidden_all = stack(hidden_low, hidden_mate)
    last_all = stack(last_own, last_mate)
    grad_third_t = with_mate(summed(last_all, stack(product_own, product_mate), up))
    grad_first = with_mate(summed(hidden_all, stack(first_grad_own, first_grad_mate), up))
    grad_second = with_mate(summed(hidden_all, stack(second_grad_own, second_grad_mate), down))
    grad_out = over_heads(summed(gated, branch_grad, down))
    grad_gate = over_heads(summed(rows_low, gate_grad, up))
    normed_block = lax.dynamic_slice_in_dim(normed, block_start, SPAN, 0)
    grad_heads = with_mate(summed(normed_block, pre_grads, down))
    return (
        output,
        input_grad,
        grad_heads[:, :head_width],
        grad_heads[:, head_width : 2 * head_width],
        grad_heads[:, 2 * head_width :],
        grad_gate,
        grad_out,
        grad_first,
        grad_second,
        grad_third_t.T,
    )


def solution(mesh):
    placed = (
        P("dp", None),
        P(None, "head"),
        P(None, "head"),
        P(None, "head"),
        P(),
        P(),
        P(None, "head"),
        P(None, "head"),
        P("head", None),
        P("head"),
        P("dp"),
        P(("dp", "head"), None),
    )
    return jax.shard_map(
        functools.partial(shards, mesh.shape["dp"], mesh.shape["head"]),
        mesh=mesh,
        in_specs=placed,
        out_specs=(
            P(("dp", "head"), None),
            P(("dp", "head"), None),
            P("dp", "head"),
            P("dp", "head"),
            P("dp", "head"),
            P(("dp", "head"), None),
            P(("dp", "head"), None),
            P("dp", "head"),
            P("dp", "head"),
            P("head", "dp"),
        ),
        check_vma=False,
    )
```

```python
import functools

import jax
import jax.numpy as jnp
from jax import lax
from jax.experimental import pallas as pl
from jax.experimental.pallas import tpu as pltpu
from jax.sharding import PartitionSpec as P

SPAN = 512
HDIM = 128

epsilon = 1e-06
bf16 = jnp.bfloat16
f32 = jnp.float32
VMEM_LIMIT = 48 * 2**20


def inverse_rms(values):
    return lax.rsqrt(jnp.mean(values * values, axis=-1, keepdims=True) + epsilon)


def normalize(values):
    return values * inverse_rms(values)


def norm_back(values, incoming):
    inverse = inverse_rms(values)
    unit_rows = values * inverse
    return inverse * (incoming - unit_rows * jnp.mean(incoming * unit_rows, axis=-1, keepdims=True))


def dot_plain(left, right):
    return jnp.dot(left, right, preferred_element_type=f32)


def dot_right_t(left, right):
    return lax.dot_general(left, right, (((1,), (1,)), ((), ())), preferred_element_type=f32)


def dot_left_t(left, right):
    return lax.dot_general(left, right, (((0,), (0,)), ((), ())), preferred_element_type=f32)


def column(length):
    return lax.broadcasted_iota(jnp.int32, (length, 1), 0)


def inner_decay(rate):
    rows = lax.broadcasted_iota(jnp.int32, (SPAN, SPAN), 0)
    cols = lax.broadcasted_iota(jnp.int32, (SPAN, SPAN), 1)
    offset = rows - cols
    return jnp.where(offset >= 0, jnp.exp(-rate * jnp.maximum(offset, 0).astype(f32)), 0.0)


def attend_kernel(
    meta, rates, x, w_own_q, w_own_k, w_own_v, w_other,
    normed, attention, queries, keys, values, query_slope, key_slope, states,
):
    pair, length = meta[0], meta[1]
    start = pl.multiple_of(pair * SPAN, SPAN)
    rows = x.shape[0]
    head_width = w_own_q.shape[1]

    def norm_step(i, carry):
        place = pl.ds(pl.multiple_of(i * 128, 128), 128)
        normed[place, :] = normalize(x[place, :].astype(f32)).astype(bf16)
        return carry

    lax.fori_loop(0, rows // 128, norm_step, 0)
    block = normed[pl.ds(start, SPAN), :]
    mask = (start + column(SPAN) < length).astype(f32)
    early_mask = (column(SPAN) < length).astype(f32) * pair.astype(f32)
    early = normed[0:SPAN, :]
    places = column(SPAN).astype(f32)
    for part in range(2):
        if part == 0:
            wq, wk, wv = w_own_q[...], w_own_k[...], w_own_v[...]
        else:
            wq, wk, wv = (w_other[:, i * head_width : (i + 1) * head_width] for i in range(3))
        pre_query = dot_plain(block, wq)
        pre_key = dot_plain(block, wk)
        pre_value = dot_plain(block, wv)
        sigmoid_query = jax.nn.sigmoid(pre_query)
        sigmoid_key = jax.nn.sigmoid(pre_key)
        query = (pre_query * sigmoid_query).astype(bf16)
        key = (mask * (pre_key * sigmoid_key)).astype(bf16)
        value = (mask * pre_value).astype(bf16)
        wide = slice(part * head_width, (part + 1) * head_width)
        query_slope[:, wide] = (sigmoid_query * (1.0 + pre_query * (1.0 - sigmoid_query))).astype(bf16)
        key_slope[:, wide] = (mask * (sigmoid_key * (1.0 + pre_key * (1.0 - sigmoid_key)))).astype(bf16)
        queries[:, wide] = query
        keys[:, wide] = key
        values[:, wide] = value
        early_key = dot_plain(early, wk)
        early_key = early_mask * (early_key * jax.nn.sigmoid(early_key)).astype(bf16).astype(f32)
        early_value = (early_mask * dot_plain(early, wv)).astype(bf16)
        for head in range(head_width // HDIM):
            index = part * (head_width // HDIM) + head
            rate = rates[index]
            cols = slice(head * HDIM, (head + 1) * HDIM)
            q, k, v = query[:, cols], key[:, cols], value[:, cols]
            scores = dot_right_t(q, k)
            weights = (scores * inner_decay(rate)).astype(bf16)
            keyed = (early_key[:, cols] * jnp.exp(-rate * (SPAN - 1.0 - places))).astype(bf16)
            state = dot_left_t(keyed, early_value[:, cols])
            states[index] = state
            decayed = (q.astype(f32) * jnp.exp(-rate * (places + 1.0))).astype(bf16)
            out = dot_plain(weights, v) + dot_plain(decayed, state.astype(bf16))
            attention[:, index * HDIM : (index + 1) * HDIM] = out.astype(bf16)


def state_kernel(rates, queries, upstream, state_grad):
    places = column(SPAN).astype(f32)
    for index in range(state_grad.shape[0]):
        cols = slice(index * HDIM, (index + 1) * HDIM)
        decayed = (queries[:, cols].astype(f32) * jnp.exp(-rates[index] * (places + 1.0))).astype(bf16)
        state_grad[index] = dot_left_t(decayed, upstream[:, cols])


def attend_back_kernel(
    meta, rates, queries, keys, values, upstream, query_slope, key_slope, states, state_grad, pre_grads
):
    pair, length = meta[0], meta[1]
    mask = (pair * SPAN + column(SPAN) < length).astype(f32)
    places = column(SPAN).astype(f32)
    heads = states.shape[0]
    half = heads // 2
    for index in range(heads):
        rate = rates[index]
        cols = slice(index * HDIM, (index + 1) * HDIM)
        q, k, v, g = queries[:, cols], keys[:, cols], values[:, cols], upstream[:, cols]
        decay = inner_decay(rate)
        query_decay = jnp.exp(-rate * (places + 1.0))
        key_decay = jnp.exp(-rate * (SPAN - 1.0 - places))
        state = states[index].astype(bf16)
        carried = state_grad[index].astype(bf16)
        weights = (dot_right_t(q, k) * decay).astype(bf16)
        score_grad = (dot_right_t(g, v) * decay).astype(bf16)
        dq = dot_plain(score_grad, k) + query_decay * dot_right_t(g, state)
        dk = dot_left_t(score_grad, q) + key_decay * dot_right_t(v, carried)
        dv = dot_left_t(weights, g) + key_decay * dot_plain(k, carried)
        base = (index // half) * (3 * half * HDIM) + (index % half) * HDIM
        pre_grads[:, base : base + HDIM] = (dq * query_slope[:, cols].astype(f32)).astype(bf16)
        base += half * HDIM
        pre_grads[:, base : base + HDIM] = (dk * key_slope[:, cols].astype(f32)).astype(bf16)
        base += half * HDIM
        pre_grads[:, base : base + HDIM] = (dv * mask).astype(bf16)


MESH = pl.DeviceIdType.MESH


class Links:
    def __init__(self, send_sems, recv_sems):
        self.send_sems, self.recv_sems, self.started = send_sems, recv_sems, []

    def send(self, source, target, device):
        index = len(self.started)
        copy = pltpu.make_async_remote_copy(
            src_ref=source,
            dst_ref=target,
            send_sem=self.send_sems.at[index],
            recv_sem=self.recv_sems.at[index],
            device_id=device,
            device_id_type=MESH,
        )
        copy.start()
        self.started.append(copy)
        return copy

    def finish(self):
        for copy in self.started:
            copy.wait_send()


def partners():
    place, own = lax.axis_index("dp"), lax.axis_index("head")

    def flip(index, bit):
        return index + (1 << bit) * (1 - 2 * ((index // (1 << bit)) % 2))

    return {
        "core": (flip(place, 0), own),
        "x": (flip(place, 1), own),
        "y": (flip(place, 2), own),
        "mate": (place, flip(own, 0)),
        "far": (place, flip(own, 1)),
    }


def enter(others):
    barrier = pltpu.get_barrier_semaphore()
    for device in others.values():
        pl.semaphore_signal(barrier, inc=1, device_id=device, device_id_type=MESH)
    pl.semaphore_wait(barrier, len(others))


class Gather:
    def __init__(self, links, others, place, share, first, second):
        self.links, self.others, self.share = links, others, share
        flip = lambda index, bit: index + (1 << bit) * (1 - 2 * ((index // (1 << bit)) % 2))
        bits = {"x": 1, "y": 2}
        self.first, self.second = first, second
        self.mine = place
        self.near = flip(place, bits[first])
        self.next = flip(place, bits[second])
        self.cross = flip(self.near, bits[second])
        self.waits = []

    def step(self, sends, device):
        for copy in self.waits:
            copy.wait_recv()
        self.waits = [self.links.send(self.share(i), self.share(i), self.others[device]) for i in sends]

    def fetch(self, sources):
        self.waits = [self.links.send(a, b, self.others["far"]) for a, b in sources]

    def one(self):
        self.step([self.mine], self.first)

    def two(self):
        self.step([self.mine, self.near], self.second)

    def three(self):
        self.step([self.mine, self.near, self.next, self.cross], "core")

    def done(self):
        for copy in self.waits:
            copy.wait_recv()
        self.waits = []


def front_kernel(
    scalars, rates_own, x_in, w_query, w_key, w_value, w_first, w_second, w_third,
    normed, attention, queries, keys, values, query_slope, key_slope, states, attention_in,
    heads_other, first_other, second_other, third_other,
    x, heads_own, rates_other, local_sems, send_sems, recv_sems,
):
    place, own = lax.axis_index("dp"), lax.axis_index("head")
    pair, member = own // 2, own % 2
    length = scalars[0]
    start = pl.multiple_of(pair * SPAN, SPAN)
    rows, width = x.shape
    head_width = w_query.shape[1]
    others = partners()
    loads = [pltpu.make_async_copy(x_in, x, local_sems.at[0])]
    for i, weight in enumerate((w_query, w_key, w_value)):
        loads.append(pltpu.make_async_copy(
            weight, heads_own.at[:, i * head_width : (i + 1) * head_width], local_sems.at[1 + i]
        ))
    for load in loads:
        load.start()
    enter(others)
    links = Links(send_sems, recv_sems)
    rows_share = width // 8
    by_rows = lambda ref: lambda i: ref.at[pl.ds(pl.multiple_of(i * rows_share, rows_share), rows_share), :]
    by_cols = lambda ref: lambda i: ref.at[:, pl.ds(pl.multiple_of(i * rows_share, rows_share), rows_share)]
    rates_copy = links.send(rates_own, rates_other, others["far"])
    heads = Gather(links, others, place, by_rows(heads_other), "x", "y")
    first = Gather(links, others, place, by_rows(first_other), "y", "x")
    second = Gather(links, others, place, by_rows(second_other), "x", "y")
    third = Gather(links, others, place, by_cols(third_other), "y", "x")
    heads.fetch([
        (by_rows(weight)(place), by_rows(heads_other)(place).at[:, i * head_width : (i + 1) * head_width])
        for i, weight in enumerate((w_query, w_key, w_value))
    ])
    first.fetch([(by_rows(w_first)(place), by_rows(first_other)(place))])
    second.fetch([(by_rows(w_second)(place), by_rows(second_other)(place))])
    third.fetch([(by_cols(w_third)(place), by_cols(third_other)(place))])

    loads[0].wait()

    def norm_step(i, carry):
        where = pl.ds(pl.multiple_of(i * 128, 128), 128)
        normed[where, :] = normalize(x[where, :].astype(f32)).astype(bf16)
        return carry

    lax.fori_loop(0, rows // 128, norm_step, 0)
    for load in loads[1:]:
        load.wait()
    mask = (start + column(SPAN) < length).astype(f32)
    early_mask = (column(SPAN) < length).astype(f32) * pair.astype(f32)
    places = column(SPAN).astype(f32)
    half_rows = SPAN // 2

    def project(weights, part):
        block = normed[pl.ds(start, SPAN), :]
        early = normed[0:SPAN, :]
        wide = slice(part * head_width, (part + 1) * head_width)
        pre_query = dot_plain(block, weights[:, :head_width])
        sigmoid = jax.nn.sigmoid(pre_query)
        queries[:, wide] = (pre_query * sigmoid).astype(bf16)
        query_slope[:, wide] = (sigmoid * (1.0 + pre_query * (1.0 - sigmoid))).astype(bf16)
        pre_key = dot_plain(block, weights[:, head_width : 2 * head_width])
        sigmoid = jax.nn.sigmoid(pre_key)
        keys[:, wide] = (mask * (pre_key * sigmoid)).astype(bf16)
        key_slope[:, wide] = (mask * (sigmoid * (1.0 + pre_key * (1.0 - sigmoid)))).astype(bf16)
        values[:, wide] = (mask * dot_plain(block, weights[:, 2 * head_width :])).astype(bf16)
        early_key = dot_plain(early, weights[:, head_width : 2 * head_width])
        early_key = early_mask * (early_key * jax.nn.sigmoid(early_key)).astype(bf16).astype(f32)
        early_value = (early_mask * dot_plain(early, weights[:, 2 * head_width :])).astype(bf16)
        return early_key, early_value

    def attend(part, early_key, early_value, rates):
        for head in range(head_width // HDIM):
            index = part * (head_width // HDIM) + head
            rate = rates[head : head + 1, 0:1]
            cols = slice(index * HDIM, (index + 1) * HDIM)
            early = slice(head * HDIM, (head + 1) * HDIM)
            q, k, v = queries[:, cols], keys[:, cols], values[:, cols]
            weights = (dot_right_t(q, k) * inner_decay(rate)).astype(bf16)
            keyed = (early_key[:, early] * jnp.exp(-rate * (SPAN - 1.0 - places))).astype(bf16)
            state = dot_left_t(keyed, early_value[:, early])
            states[index] = state
            decayed = (q.astype(f32) * jnp.exp(-rate * (places + 1.0))).astype(bf16)
            out = dot_plain(weights, v) + dot_plain(decayed, state.astype(bf16))
            attention[:, cols] = out.astype(bf16)
        wide = slice(part * head_width, (part + 1) * head_width)
        mate_rows = pl.ds(pl.multiple_of((1 - member) * half_rows, half_rows), half_rows)
        return links.send(attention.at[mate_rows, wide], attention_in.at[:, wide], others["mate"])

    early_key, early_value = project(heads_own, 0)
    heads.one()
    attention_own = attend(0, early_key, early_value, rates_own)
    heads.two()
    first.one()
    heads.three()
    second.one()
    first.two()
    heads.done()
    early_key, early_value = project(heads_other, 1)
    second.two()
    third.one()
    first.three()
    rates_copy.wait_recv()
    attention_far = attend(1, early_key, early_value, rates_other)
    third.two()
    second.three()
    third.three()
    attention_own.wait_recv()
    attention_far.wait_recv()
    for gather in (first, second, third):
        gather.done()
    links.finish()


def vmem():
    return pl.BlockSpec(memory_space=pltpu.VMEM)


def smem():
    return pl.BlockSpec(memory_space=pltpu.SMEM)


def local_call(body, name, out_shapes, args, scalars, flops):
    size = sum(int(a.size) * a.dtype.itemsize for a in list(args) + list(out_shapes))
    return pl.pallas_call(
        body,
        out_shape=out_shapes,
        in_specs=[smem()] * scalars + [vmem()] * (len(args) - scalars),
        out_specs=[vmem()] * len(out_shapes),
        compiler_params=pltpu.CompilerParams(vmem_limit_bytes=VMEM_LIMIT),
        cost_estimate=pl.CostEstimate(flops=flops, bytes_accessed=size, transcendentals=0),
        name=name,
    )(*args)


def shards(
    n_dp, n_head,
    layer_input, w_query, w_key, w_value, w_gate, w_out, w_first, w_second, w_third,
    decay_rates, seq_lengths, cotangent,
):
    group_rows, width = layer_input.shape
    row_count = cotangent.shape[0]
    heads = decay_rates.shape[0]
    head_width = w_query.shape[1]
    place = lax.axis_index("dp")
    own = lax.axis_index("head")
    member, pair = own % 2, own // 2
    bits = n_dp.bit_length() - 1
    length = seq_lengths[0]

    def to_mate(array, bit):
        return lax.ppermute(array, "head", [(i, i ^ bit) for i in range(n_head)])

    def across(array, bit):
        return lax.ppermute(array, "dp", [(i, i ^ (1 << bit)) for i in range(n_dp)])

    def gathered(weight, axis):
        size = weight.shape[axis] // n_dp
        share = lax.dynamic_slice_in_dim(weight, place * size, size, axis)
        return lax.all_gather(to_mate(share, 2), "dp", axis=axis, tiled=True)

    kernel_path = n_dp == 8
    w_heads = jnp.concatenate([w_query, w_key, w_value], axis=1)
    rates = jnp.concatenate([decay_rates, to_mate(decay_rates, 2)])
    if not kernel_path:
        w_heads_other = gathered(w_heads, 0)
        w_first_other = gathered(w_first, 0)
        w_second_other = gathered(w_second, 0)
        w_third_other = gathered(w_third, 1)

    block_start = pair * SPAN
    row_start = own * row_count
    positions = jnp.arange(row_count, dtype=jnp.int32)[:, None]
    row_mask = (row_start + positions < length).astype(f32)
    upstream = cotangent.astype(f32)
    last_own = (row_mask * upstream).astype(bf16)
    last_mate = to_mate(last_own, 1)

    meta = jnp.stack([pair, length]).astype(jnp.int32)
    both = 2 * head_width
    shape = jax.ShapeDtypeStruct
    block_shape = shape((SPAN, both), bf16)
    outs = [shape(layer_input.shape, bf16)] + [block_shape] * 6 + [shape((2 * heads, HDIM, HDIM), f32)]
    if kernel_path:
        rates_own = jnp.broadcast_to(jnp.pad(decay_rates, (0, 8 - heads))[:, None], (8, 128))
        outs += [
            shape((row_count, both), bf16), shape((width, 3 * head_width), bf16),
            shape(w_first.shape, bf16), shape(w_second.shape, bf16), shape(w_third.shape, bf16),
        ]
        (
            normed, attention_block, queries, keys, values, query_slope, key_slope, states,
            attention_in, w_heads_other, w_first_other, w_second_other, w_third_other,
        ) = pl.pallas_call(
            front_kernel,
            out_shape=outs,
            in_specs=[smem(), vmem()] + [pl.BlockSpec(memory_space=pl.ANY)] * 7,
            out_specs=[vmem()] * len(outs),
            scratch_shapes=[
                pltpu.VMEM(layer_input.shape, bf16),
                pltpu.VMEM((width, 3 * head_width), bf16),
                pltpu.VMEM((8, 128), f32),
                pltpu.SemaphoreType.DMA((4,)),
                pltpu.SemaphoreType.DMA((40,)),
                pltpu.SemaphoreType.DMA((40,)),
            ],
            compiler_params=pltpu.CompilerParams(
                collective_id=0, has_side_effects=True, vmem_limit_bytes=VMEM_LIMIT
            ),
            name="front",
        )(seq_lengths, rates_own, layer_input, w_query, w_key, w_value, w_first, w_second, w_third)
    else:
        normed, attention_block, queries, keys, values, query_slope, key_slope, states = local_call(
            attend_kernel, "attend", outs,
            [meta, rates, layer_input, w_query, w_key, w_value, w_heads_other], 2, 6 * 10**9,
        )

    def rows_of(array, index):
        return lax.dynamic_slice_in_dim(array, index * row_count, row_count, 0)

    def ordered(mine, other):
        even, odd = jnp.where(member == 0, mine, other), jnp.where(member == 0, other, mine)
        flip = lambda a: jnp.where(pair == 0, a, jnp.concatenate([a[:, head_width:], a[:, :head_width]], axis=1))
        even, odd = flip(even), flip(odd)
        return jnp.concatenate(
            [even[:, :head_width], odd[:, :head_width], even[:, head_width:], odd[:, head_width:]], axis=1
        )

    def pieces(array):
        cut = [array[:, i * head_width : (i + 1) * head_width] for i in range(4)]
        even, odd = jnp.concatenate([cut[0], cut[2]], axis=1), jnp.concatenate([cut[1], cut[3]], axis=1)
        flip = lambda a: jnp.where(pair == 0, a, jnp.concatenate([a[:, head_width:], a[:, :head_width]], axis=1))
        even, odd = flip(even), flip(odd)
        return jnp.where(member == 0, even, odd), jnp.where(member == 0, odd, even)

    received = attention_in if kernel_path else to_mate(rows_of(attention_block, 1 - member), 1)
    attention = ordered(rows_of(attention_block, member), received).astype(f32)
    attention_norm = normalize(attention)
    rows_low = rows_of(normed, own)
    input_rows = rows_of(layer_input, own).astype(f32)
    gate_pre = dot_plain(rows_low, w_gate)
    gated = (attention_norm * gate_pre).astype(bf16)
    hidden = input_rows + row_mask * dot_plain(gated, w_out)
    hidden_low = normalize(hidden).astype(bf16)
    hidden_mate = to_mate(hidden_low, 1)

    w_first_all = jnp.concatenate([w_first, w_first_other], axis=1)
    w_second_all = jnp.concatenate([w_second, w_second_other], axis=1)
    w_third_all = jnp.concatenate([w_third, w_third_other], axis=0)

    def forward_rows(rows_in):
        first, second = dot_plain(rows_in, w_first_all), dot_plain(rows_in, w_second_all)
        return first.astype(bf16), second.astype(bf16), (first * second).astype(bf16)

    def backward_rows(last, first, second):
        product_grad = dot_right_t(last, w_third_all)
        first_grad = (product_grad * second.astype(f32)).astype(bf16)
        second_grad = (product_grad * first.astype(f32)).astype(bf16)
        return first_grad, second_grad, dot_right_t(first_grad, w_first_all) + dot_right_t(second_grad, w_second_all)

    first_mate, second_mate, product_mate = forward_rows(hidden_mate)
    first_grad_mate, second_grad_mate, norm_grad_mate = backward_rows(last_mate, first_mate, second_mate)
    norm_grad_in = to_mate(norm_grad_mate.astype(bf16), 1)
    mix_in = to_mate(dot_plain(product_mate, w_third_all).astype(bf16), 1)
    first_own, second_own, product_own = forward_rows(hidden_low)
    first_grad_own, second_grad_own, norm_grad_own = backward_rows(last_own, first_own, second_own)
    hidden_grad = upstream + norm_back(hidden, norm_grad_own + norm_grad_in.astype(f32))
    mixed = dot_plain(product_own, w_third_all) + mix_in.astype(f32)
    output = (hidden + row_mask * mixed).astype(bf16)

    branch_grad = (row_mask * hidden_grad).astype(bf16)
    gated_grad = dot_right_t(branch_grad, w_out)
    gate_grad = (gated_grad * attention_norm).astype(bf16)
    attention_grad = norm_back(attention, gated_grad * gate_pre).astype(bf16)
    mine, for_mate = pieces(attention_grad)
    from_mate = to_mate(for_mate, 1)
    grad_block = jnp.concatenate(
        [jnp.where(member == 0, mine, from_mate), jnp.where(member == 0, from_mate, mine)], axis=0
    )
    state_shape = shape((2 * heads, HDIM, HDIM), f32)
    (state_grad,) = local_call(
        state_kernel, "state_grad", [state_shape], [rates, queries, grad_block], 1, 10**8
    )
    swapped = jnp.concatenate([state_grad[heads:], state_grad[:heads]], axis=0)
    carried = lax.ppermute(swapped, "head", [(i, i - 2) for i in range(2, n_head)])
    (pre_grads,) = local_call(
        attend_back_kernel, "attend_back", [shape((SPAN, 3 * both), bf16)],
        [meta, rates, queries, keys, values, grad_block, query_slope, key_slope, states, carried], 2, 2 * 10**9,
    )
    head_terms = dot_right_t(pre_grads[:, : 3 * head_width], w_heads) + dot_right_t(
        pre_grads[:, 3 * head_width :], w_heads_other
    )
    head_terms = head_terms.astype(bf16)
    terms_in = to_mate(rows_of(head_terms, 1 - member), 1)
    input_norm_grad = (
        rows_of(head_terms, member).astype(f32) + terms_in.astype(f32) + dot_right_t(gate_grad, w_gate)
    )
    input_grad = (hidden_grad + norm_back(input_rows, input_norm_grad)).astype(bf16)

    def summed(left, right, order):
        left = left.reshape((left.shape[0],) + (2,) * bits + (width // n_dp,))

        def pick(array, axis, bit, which):
            side = (place // (1 << bit)) % 2
            return lax.dynamic_index_in_dim(array, side if which else 1 - side, axis, keepdims=False)

        left_axis = lambda bit, done: 1 + (bits - 1 - bit) - sum(1 for b in done if b > bit)
        first_bit = order[0]
        make = lambda which: dot_left_t(
            pick(left, left_axis(first_bit, []), first_bit, which).reshape(left.shape[0], width // 2), right
        ).astype(bf16)
        arrived = across(make(False), first_bit)
        total = (make(True).astype(f32) + arrived.astype(f32)).astype(bf16)
        total = total.reshape((2,) * (bits - 1) + (width // n_dp, right.shape[1]))
        done = [first_bit]
        for bit in order[1:]:
            axis = left_axis(bit, done) - 1
            arrived = across(pick(total, axis, bit, False), bit)
            total = (pick(total, axis, bit, True).astype(f32) + arrived.astype(f32)).astype(bf16)
            done.append(bit)
        return total

    def with_mate(total):
        size = total.shape[1] // 2
        return total[:, :size].astype(f32) + to_mate(total[:, size:], 2).astype(f32)

    def over_heads(total):
        for bit in (1, 2):
            cut = total.reshape((2, -1) + total.shape[1:]) if bit == 2 else total.reshape((2, 2, -1) + total.shape[1:])
            side = (own // bit) % 2
            axis = 0 if bit == 2 else 1
            arrived = to_mate(lax.dynamic_index_in_dim(cut, 1 - side, axis, keepdims=False), bit)
            total = lax.dynamic_index_in_dim(cut, side, axis, keepdims=False).astype(f32) + arrived.astype(f32)
            if bit == 1:
                total = total.astype(bf16).reshape((-1,) + total.shape[2:])
        return total

    up = list(range(bits))
    down = [0] + up[:0:-1]
    stack = lambda a, b: jnp.concatenate([a, b], axis=0)
    hidden_all = stack(hidden_low, hidden_mate)
    last_all = stack(last_own, last_mate)
    grad_third_t = with_mate(summed(last_all, stack(product_own, product_mate), up))
    grad_first = with_mate(summed(hidden_all, stack(first_grad_own, first_grad_mate), up))
    grad_second = with_mate(summed(hidden_all, stack(second_grad_own, second_grad_mate), down))
    grad_out = over_heads(summed(gated, branch_grad, down))
    grad_gate = over_heads(summed(rows_low, gate_grad, up))
    normed_block = lax.dynamic_slice_in_dim(normed, block_start, SPAN, 0)
    grad_heads = with_mate(summed(normed_block, pre_grads, down))
    return (
        output,
        input_grad,
        grad_heads[:, :head_width],
        grad_heads[:, head_width : 2 * head_width],
        grad_heads[:, 2 * head_width :],
        grad_gate,
        grad_out,
        grad_first,
        grad_second,
        grad_third_t.T,
    )


def solution(mesh):
    placed = (
        P("dp", None),
        P(None, "head"),
        P(None, "head"),
        P(None, "head"),
        P(),
        P(),
        P(None, "head"),
        P(None, "head"),
        P("head", None),
        P("head"),
        P("dp"),
        P(("dp", "head"), None),
    )
    return jax.shard_map(
        functools.partial(shards, mesh.shape["dp"], mesh.shape["head"]),
        mesh=mesh,
        in_specs=placed,
        out_specs=(
            P(("dp", "head"), None),
            P(("dp", "head"), None),
            P("dp", "head"),
            P("dp", "head"),
            P("dp", "head"),
            P(("dp", "head"), None),
            P(("dp", "head"), None),
            P("dp", "head"),
            P("dp", "head"),
            P("head", "dp"),
        ),
        check_vma=False,
    )
```

```python
import functools
import types

import jax
import jax.numpy as jnp
from jax import lax
from jax.experimental import pallas as pl
from jax.experimental.pallas import tpu as pltpu
from jax.sharding import PartitionSpec as P

SPAN = 512
HDIM = 128

epsilon = 1e-06
bf16 = jnp.bfloat16
f32 = jnp.float32
VMEM_LIMIT = 48 * 2**20
VMEM_ALL = 63 * 2**20


def inverse_rms(values):
    return lax.rsqrt(jnp.mean(values * values, axis=-1, keepdims=True) + epsilon)


def normalize(values):
    return values * inverse_rms(values)


def norm_back(values, incoming):
    inverse = inverse_rms(values)
    unit_rows = values * inverse
    return inverse * (incoming - unit_rows * jnp.mean(incoming * unit_rows, axis=-1, keepdims=True))


def dot_plain(left, right):
    return jnp.dot(left, right, preferred_element_type=f32)


def dot_right_t(left, right):
    return lax.dot_general(left, right, (((1,), (1,)), ((), ())), preferred_element_type=f32)


def dot_left_t(left, right):
    return lax.dot_general(left, right, (((0,), (0,)), ((), ())), preferred_element_type=f32)


def transposed(values):
    return values.T


def column(length):
    return lax.broadcasted_iota(jnp.int32, (length, 1), 0)


def inner_decay(rate):
    rows = lax.broadcasted_iota(jnp.int32, (SPAN, SPAN), 0)
    cols = lax.broadcasted_iota(jnp.int32, (SPAN, SPAN), 1)
    offset = rows - cols
    return jnp.where(offset >= 0, jnp.exp(-rate * jnp.maximum(offset, 0).astype(f32)), 0.0)


def attend_kernel(
    meta, rates, x, w_own_q, w_own_k, w_own_v, w_other,
    normed, attention, queries, keys, values, query_slope, key_slope, states,
):
    pair, length = meta[0], meta[1]
    start = pl.multiple_of(pair * SPAN, SPAN)
    rows = x.shape[0]
    head_width = w_own_q.shape[1]

    def norm_step(i, carry):
        place = pl.ds(pl.multiple_of(i * 128, 128), 128)
        normed[place, :] = normalize(x[place, :].astype(f32)).astype(bf16)
        return carry

    lax.fori_loop(0, rows // 128, norm_step, 0)
    block = normed[pl.ds(start, SPAN), :]
    mask = (start + column(SPAN) < length).astype(f32)
    early_mask = (column(SPAN) < length).astype(f32) * pair.astype(f32)
    early = normed[0:SPAN, :]
    places = column(SPAN).astype(f32)
    for part in range(2):
        if part == 0:
            wq, wk, wv = w_own_q[...], w_own_k[...], w_own_v[...]
        else:
            wq, wk, wv = (w_other[:, i * head_width : (i + 1) * head_width] for i in range(3))
        pre_query = dot_plain(block, wq)
        pre_key = dot_plain(block, wk)
        pre_value = dot_plain(block, wv)
        sigmoid_query = jax.nn.sigmoid(pre_query)
        sigmoid_key = jax.nn.sigmoid(pre_key)
        query = (pre_query * sigmoid_query).astype(bf16)
        key = (mask * (pre_key * sigmoid_key)).astype(bf16)
        value = (mask * pre_value).astype(bf16)
        wide = slice(part * head_width, (part + 1) * head_width)
        query_slope[:, wide] = (sigmoid_query * (1.0 + pre_query * (1.0 - sigmoid_query))).astype(bf16)
        key_slope[:, wide] = (mask * (sigmoid_key * (1.0 + pre_key * (1.0 - sigmoid_key)))).astype(bf16)
        queries[:, wide] = query
        keys[:, wide] = key
        values[:, wide] = value
        early_key = dot_plain(early, wk)
        early_key = early_mask * (early_key * jax.nn.sigmoid(early_key)).astype(bf16).astype(f32)
        early_value = (early_mask * dot_plain(early, wv)).astype(bf16)
        for head in range(head_width // HDIM):
            index = part * (head_width // HDIM) + head
            rate = rates[index]
            cols = slice(head * HDIM, (head + 1) * HDIM)
            q, k, v = query[:, cols], key[:, cols], value[:, cols]
            scores = dot_right_t(q, k)
            weights = (scores * inner_decay(rate)).astype(bf16)
            keyed = (early_key[:, cols] * jnp.exp(-rate * (SPAN - 1.0 - places))).astype(bf16)
            state = dot_left_t(keyed, early_value[:, cols])
            states[index] = state
            decayed = (q.astype(f32) * jnp.exp(-rate * (places + 1.0))).astype(bf16)
            out = dot_plain(weights, v) + dot_plain(decayed, state.astype(bf16))
            attention[:, index * HDIM : (index + 1) * HDIM] = out.astype(bf16)


def state_kernel(rates, queries, upstream, state_grad):
    places = column(SPAN).astype(f32)
    for index in range(state_grad.shape[0]):
        cols = slice(index * HDIM, (index + 1) * HDIM)
        decayed = (queries[:, cols].astype(f32) * jnp.exp(-rates[index] * (places + 1.0))).astype(bf16)
        state_grad[index] = dot_left_t(decayed, upstream[:, cols])


def attend_back_kernel(
    meta, rates, queries, keys, values, upstream, query_slope, key_slope, states, state_grad, pre_grads
):
    pair, length = meta[0], meta[1]
    mask = (pair * SPAN + column(SPAN) < length).astype(f32)
    places = column(SPAN).astype(f32)
    heads = states.shape[0]
    half = heads // 2
    for index in range(heads):
        rate = rates[index]
        cols = slice(index * HDIM, (index + 1) * HDIM)
        q, k, v, g = queries[:, cols], keys[:, cols], values[:, cols], upstream[:, cols]
        decay = inner_decay(rate)
        query_decay = jnp.exp(-rate * (places + 1.0))
        key_decay = jnp.exp(-rate * (SPAN - 1.0 - places))
        state = states[index].astype(bf16)
        carried = state_grad[index].astype(bf16)
        weights = (dot_right_t(q, k) * decay).astype(bf16)
        score_grad = (dot_right_t(g, v) * decay).astype(bf16)
        dq = dot_plain(score_grad, k) + query_decay * dot_right_t(g, state)
        dk = dot_left_t(score_grad, q) + key_decay * dot_right_t(v, carried)
        dv = dot_left_t(weights, g) + key_decay * dot_plain(k, carried)
        base = (index // half) * (3 * half * HDIM) + (index % half) * HDIM
        pre_grads[:, base : base + HDIM] = (dq * query_slope[:, cols].astype(f32)).astype(bf16)
        base += half * HDIM
        pre_grads[:, base : base + HDIM] = (dk * key_slope[:, cols].astype(f32)).astype(bf16)
        base += half * HDIM
        pre_grads[:, base : base + HDIM] = (dv * mask).astype(bf16)


def vmem():
    return pl.BlockSpec(memory_space=pltpu.VMEM)


def smem():
    return pl.BlockSpec(memory_space=pltpu.SMEM)


def local_call(body, name, out_shapes, args, scalars, flops):
    size = sum(int(a.size) * a.dtype.itemsize for a in list(args) + list(out_shapes))
    return pl.pallas_call(
        body,
        out_shape=out_shapes,
        in_specs=[smem()] * scalars + [vmem()] * (len(args) - scalars),
        out_specs=[vmem()] * len(out_shapes),
        compiler_params=pltpu.CompilerParams(vmem_limit_bytes=VMEM_LIMIT),
        cost_estimate=pl.CostEstimate(flops=flops, bytes_accessed=size, transcendentals=0),
        name=name,
    )(*args)


def shards(
    n_dp, n_head,
    layer_input, w_query, w_key, w_value, w_gate, w_out, w_first, w_second, w_third,
    decay_rates, seq_lengths, cotangent,
):
    group_rows, width = layer_input.shape
    row_count = cotangent.shape[0]
    heads = decay_rates.shape[0]
    head_width = w_query.shape[1]
    place = lax.axis_index("dp")
    own = lax.axis_index("head")
    member, pair = own % 2, own // 2
    bits = n_dp.bit_length() - 1
    length = seq_lengths[0]

    def to_mate(array, bit):
        return lax.ppermute(array, "head", [(i, i ^ bit) for i in range(n_head)])

    def across(array, bit):
        return lax.ppermute(array, "dp", [(i, i ^ (1 << bit)) for i in range(n_dp)])

    def gathered(weight, axis):
        size = weight.shape[axis] // n_dp
        share = lax.dynamic_slice_in_dim(weight, place * size, size, axis)
        return lax.all_gather(to_mate(share, 2), "dp", axis=axis, tiled=True)

    w_heads = jnp.concatenate([w_query, w_key, w_value], axis=1)
    w_heads_other = gathered(w_heads, 0)
    w_first_other = gathered(w_first, 0)
    w_second_other = gathered(w_second, 0)
    w_third_other = gathered(w_third, 1)
    rates = jnp.concatenate([decay_rates, to_mate(decay_rates, 2)])

    block_start = pair * SPAN
    row_start = own * row_count
    positions = jnp.arange(row_count, dtype=jnp.int32)[:, None]
    row_mask = (row_start + positions < length).astype(f32)
    upstream = cotangent.astype(f32)
    last_own = (row_mask * upstream).astype(bf16)
    last_mate = to_mate(last_own, 1)

    meta = jnp.stack([pair, length]).astype(jnp.int32)
    both = 2 * head_width
    shape = jax.ShapeDtypeStruct
    block_shape = shape((SPAN, both), bf16)
    normed, attention_block, queries, keys, values, query_slope, key_slope, states = local_call(
        attend_kernel, "attend",
        [shape(layer_input.shape, bf16)] + [block_shape] * 6 + [shape((2 * heads, HDIM, HDIM), f32)],
        [meta, rates, layer_input, w_query, w_key, w_value, w_heads_other], 2, 6 * 10**9,
    )

    def rows_of(array, index):
        return lax.dynamic_slice_in_dim(array, index * row_count, row_count, 0)

    def ordered(mine, other):
        even, odd = jnp.where(member == 0, mine, other), jnp.where(member == 0, other, mine)
        flip = lambda a: jnp.where(pair == 0, a, jnp.concatenate([a[:, head_width:], a[:, :head_width]], axis=1))
        even, odd = flip(even), flip(odd)
        return jnp.concatenate(
            [even[:, :head_width], odd[:, :head_width], even[:, head_width:], odd[:, head_width:]], axis=1
        )

    def pieces(array):
        cut = [array[:, i * head_width : (i + 1) * head_width] for i in range(4)]
        even, odd = jnp.concatenate([cut[0], cut[2]], axis=1), jnp.concatenate([cut[1], cut[3]], axis=1)
        flip = lambda a: jnp.where(pair == 0, a, jnp.concatenate([a[:, head_width:], a[:, :head_width]], axis=1))
        even, odd = flip(even), flip(odd)
        return jnp.where(member == 0, even, odd), jnp.where(member == 0, odd, even)

    received = to_mate(rows_of(attention_block, 1 - member), 1)
    attention = ordered(rows_of(attention_block, member), received).astype(f32)
    attention_norm = normalize(attention)
    rows_low = rows_of(normed, own)
    input_rows = rows_of(layer_input, own).astype(f32)
    gate_pre = dot_plain(rows_low, w_gate)
    gated = (attention_norm * gate_pre).astype(bf16)
    hidden = input_rows + row_mask * dot_plain(gated, w_out)
    hidden_low = normalize(hidden).astype(bf16)
    hidden_mate = to_mate(hidden_low, 1)

    w_first_all = jnp.concatenate([w_first, w_first_other], axis=1)
    w_second_all = jnp.concatenate([w_second, w_second_other], axis=1)
    w_third_all = jnp.concatenate([w_third, w_third_other], axis=0)

    def forward_rows(rows_in):
        first, second = dot_plain(rows_in, w_first_all), dot_plain(rows_in, w_second_all)
        return first.astype(bf16), second.astype(bf16), (first * second).astype(bf16)

    def backward_rows(last, first, second):
        product_grad = dot_right_t(last, w_third_all)
        first_grad = (product_grad * second.astype(f32)).astype(bf16)
        second_grad = (product_grad * first.astype(f32)).astype(bf16)
        return first_grad, second_grad, dot_right_t(first_grad, w_first_all) + dot_right_t(second_grad, w_second_all)

    first_mate, second_mate, product_mate = forward_rows(hidden_mate)
    first_grad_mate, second_grad_mate, norm_grad_mate = backward_rows(last_mate, first_mate, second_mate)
    norm_grad_in = to_mate(norm_grad_mate.astype(bf16), 1)
    mix_in = to_mate(dot_plain(product_mate, w_third_all).astype(bf16), 1)
    first_own, second_own, product_own = forward_rows(hidden_low)
    first_grad_own, second_grad_own, norm_grad_own = backward_rows(last_own, first_own, second_own)
    hidden_grad = upstream + norm_back(hidden, norm_grad_own + norm_grad_in.astype(f32))
    mixed = dot_plain(product_own, w_third_all) + mix_in.astype(f32)
    output = (hidden + row_mask * mixed).astype(bf16)

    branch_grad = (row_mask * hidden_grad).astype(bf16)
    gated_grad = dot_right_t(branch_grad, w_out)
    gate_grad = (gated_grad * attention_norm).astype(bf16)
    attention_grad = norm_back(attention, gated_grad * gate_pre).astype(bf16)
    mine, for_mate = pieces(attention_grad)
    from_mate = to_mate(for_mate, 1)
    grad_block = jnp.concatenate(
        [jnp.where(member == 0, mine, from_mate), jnp.where(member == 0, from_mate, mine)], axis=0
    )
    state_shape = shape((2 * heads, HDIM, HDIM), f32)
    (state_grad,) = local_call(
        state_kernel, "state_grad", [state_shape], [rates, queries, grad_block], 1, 10**8
    )
    swapped = jnp.concatenate([state_grad[heads:], state_grad[:heads]], axis=0)
    carried = lax.ppermute(swapped, "head", [(i, i - 2) for i in range(2, n_head)])
    (pre_grads,) = local_call(
        attend_back_kernel, "attend_back", [shape((SPAN, 3 * both), bf16)],
        [meta, rates, queries, keys, values, grad_block, query_slope, key_slope, states, carried], 2, 2 * 10**9,
    )
    head_terms = dot_right_t(pre_grads[:, : 3 * head_width], w_heads) + dot_right_t(
        pre_grads[:, 3 * head_width :], w_heads_other
    )
    head_terms = head_terms.astype(bf16)
    terms_in = to_mate(rows_of(head_terms, 1 - member), 1)
    input_norm_grad = (
        rows_of(head_terms, member).astype(f32) + terms_in.astype(f32) + dot_right_t(gate_grad, w_gate)
    )
    input_grad = (hidden_grad + norm_back(input_rows, input_norm_grad)).astype(bf16)

    def summed(left, right, order):
        left = left.reshape((left.shape[0],) + (2,) * bits + (width // n_dp,))

        def pick(array, axis, bit, which):
            side = (place // (1 << bit)) % 2
            return lax.dynamic_index_in_dim(array, side if which else 1 - side, axis, keepdims=False)

        left_axis = lambda bit, done: 1 + (bits - 1 - bit) - sum(1 for b in done if b > bit)
        first_bit = order[0]
        make = lambda which: dot_left_t(
            pick(left, left_axis(first_bit, []), first_bit, which).reshape(left.shape[0], width // 2), right
        ).astype(bf16)
        arrived = across(make(False), first_bit)
        total = (make(True).astype(f32) + arrived.astype(f32)).astype(bf16)
        total = total.reshape((2,) * (bits - 1) + (width // n_dp, right.shape[1]))
        done = [first_bit]
        for bit in order[1:]:
            axis = left_axis(bit, done) - 1
            arrived = across(pick(total, axis, bit, False), bit)
            total = (pick(total, axis, bit, True).astype(f32) + arrived.astype(f32)).astype(bf16)
            done.append(bit)
        return total

    def with_mate(total):
        size = total.shape[1] // 2
        return total[:, :size].astype(f32) + to_mate(total[:, size:], 2).astype(f32)

    def over_heads(total):
        for bit in (1, 2):
            cut = total.reshape((2, -1) + total.shape[1:]) if bit == 2 else total.reshape((2, 2, -1) + total.shape[1:])
            side = (own // bit) % 2
            axis = 0 if bit == 2 else 1
            arrived = to_mate(lax.dynamic_index_in_dim(cut, 1 - side, axis, keepdims=False), bit)
            total = lax.dynamic_index_in_dim(cut, side, axis, keepdims=False).astype(f32) + arrived.astype(f32)
            if bit == 1:
                total = total.astype(bf16).reshape((-1,) + total.shape[2:])
        return total

    up = list(range(bits))
    down = [0] + up[:0:-1]
    stack = lambda a, b: jnp.concatenate([a, b], axis=0)
    hidden_all = stack(hidden_low, hidden_mate)
    last_all = stack(last_own, last_mate)
    grad_third_t = with_mate(summed(last_all, stack(product_own, product_mate), up))
    grad_first = with_mate(summed(hidden_all, stack(first_grad_own, first_grad_mate), up))
    grad_second = with_mate(summed(hidden_all, stack(second_grad_own, second_grad_mate), down))
    grad_out = over_heads(summed(gated, branch_grad, down))
    grad_gate = over_heads(summed(rows_low, gate_grad, up))
    normed_block = lax.dynamic_slice_in_dim(normed, block_start, SPAN, 0)
    grad_heads = with_mate(summed(normed_block, pre_grads, down))
    return (
        output,
        input_grad,
        grad_heads[:, :head_width],
        grad_heads[:, head_width : 2 * head_width],
        grad_heads[:, 2 * head_width :],
        grad_gate,
        grad_out,
        grad_first,
        grad_second,
        grad_third_t.T,
    )


MESH = pl.DeviceIdType.MESH


def flipped(index, bit):
    return index + (1 << bit) * (1 - 2 * ((index // (1 << bit)) % 2))


def part(index, size):
    return pl.ds(pl.multiple_of(index * size, size), size)


class Links:
    def __init__(self, others, send_sems, recv_sems):
        self.others, self.send_sems, self.recv_sems, self.started = others, send_sems, recv_sems, []

    def send(self, source, target, device):
        index = len(self.started)
        copy = pltpu.make_async_remote_copy(
            src_ref=source,
            dst_ref=target,
            send_sem=self.send_sems.at[index],
            recv_sem=self.recv_sems.at[index],
            device_id=self.others[device],
            device_id_type=MESH,
        )
        copy.start()
        self.started.append(copy)
        copy.sent = False
        return copy

    def left(self, copies):
        for copy in copies:
            if not copy.sent:
                copy.wait_send()
                copy.sent = True

    def finish(self):
        self.left(self.started)


def arrived(copies):
    for copy in copies:
        copy.wait_recv()


class Gather:
    def __init__(self, links, place, share, halves):
        self.links, self.share, self.halves = links, share, halves
        self.places = [place, flipped(place, 1), flipped(place, 2), flipped(flipped(place, 1), 2)]

    def pass_on(self, which, device):
        ref = self.share(self.places[which])
        return self.links.send(ref, ref, device)

    def fetch(self, sources):
        self.waits = [self.links.send(a, b, "far") for a, b in sources]

    def spread(self):
        arrived(self.waits)
        self.from_x, self.from_y = self.pass_on(0, "x"), self.pass_on(0, "y")
        self.waits = [self.pass_on(0, "core")]

    def cross(self):
        arrived([self.from_x])
        first, second = self.halves
        ref = self.share(self.places[1])
        crossing = [self.links.send(first(ref), first(ref), "y")]
        arrived([self.from_y])
        ref = self.share(self.places[2])
        crossing.append(self.links.send(second(ref), second(ref), "x"))
        self.waits += [self.pass_on(1, "core"), self.pass_on(2, "core")]
        self.crossing = crossing

    def last(self):
        arrived(self.crossing)
        self.waits.append(self.pass_on(3, "core"))

    def done(self):
        arrived(self.waits)


class Chain:
    def __init__(self, links, place, total, halves_in, quarter_in, order):
        self.links, self.total, self.halves_in, self.quarter_in, self.order = links, total, halves_in, quarter_in, order
        self.x, self.y = (place // 2) % 2, (place // 4) % 2
        self.rows = quarter_in.shape[0]

    def chunk(self, y, x):
        return self.total.at[part(2 * y + x, self.rows), :]

    def start(self):
        links, rows = self.links, self.rows
        if self.order == "xy":
            self.waits = [
                links.send(self.chunk(y, 1 - self.x), self.halves_in.at[y * rows : (y + 1) * rows, :], "x")
                for y in range(2)
            ]
        else:
            self.waits = [links.send(self.total.at[part(1 - self.y, 2 * rows), :], self.halves_in, "y")]

    def add(self, place, arrived_part):
        place[...] = (place[...].astype(f32) + arrived_part.astype(f32)).astype(bf16)

    def middle(self):
        arrived(self.waits)
        rows, x, y = self.rows, self.x, self.y
        if self.order == "xy":
            give, keep, device, index = self.chunk(1 - y, x), self.chunk(y, x), "y", y
        else:
            give, keep, device, index = self.chunk(y, 1 - x), self.chunk(y, x), "x", x
        self.add(give, self.halves_in[part(1 - index, rows), :])
        self.waits = [self.links.send(give, self.quarter_in, device)]
        self.add(keep, self.halves_in[part(index, rows), :])

    def result(self):
        arrived(self.waits)
        keep = self.chunk(self.y, self.x)
        return keep[...].astype(f32) + self.quarter_in[...].astype(f32)


def layer_kernel(names, *refs):
    r = types.SimpleNamespace(**dict(zip(names, refs)))
    place, own = lax.axis_index("dp"), lax.axis_index("head")
    pair, member, core = own // 2, own % 2, place % 2
    length = r.lengths[0]
    group_rows, width = r.layer_input.shape
    row_count = r.cotangent.shape[0]
    head_width = r.w_query.shape[1]
    block_heads = head_width // HDIM
    hidden_size = r.w_third.shape[0]
    share_size = width // 8
    chunk_rows = row_count // 2
    r.gated, r.x_rows = (r.x.at[i * row_count : (i + 1) * row_count, :] for i in (2, 3))
    r.branch, r.gate_grad, r.attention_grad, r.terms = (
        r.normed.at[i * row_count : (i + 1) * row_count, :] for i in range(4)
    )

    copies = []

    def load(source, target):
        copy = pltpu.make_async_copy(source, target, r.local_sems.at[len(copies)])
        copy.start()
        copies.append(copy)
        return copy

    load_x = load(r.layer_input, r.x)
    load_heads = [
        load(weight, r.heads.at[0, :, i * head_width : (i + 1) * head_width])
        for i, weight in enumerate((r.w_query, r.w_key, r.w_value))
    ]
    load_cotangent = load(r.cotangent, r.upstream)
    load_gate = load(r.w_gate, r.gate)
    load_out = load(r.w_out, r.out)
    load_first = load(r.w_first, r.first.at[:hidden_size, :])
    load_second = load(r.w_second, r.second.at[:hidden_size, :])
    load_third = load(r.w_third, r.third.at[:hidden_size, :])

    others = {
        "core": (flipped(place, 0), own),
        "x": (flipped(place, 1), own),
        "y": (flipped(place, 2), own),
        "mate": (place, flipped(own, 0)),
        "far": (place, flipped(own, 1)),
        "cross": (place, 3 - own),
    }
    barrier = pltpu.get_barrier_semaphore()
    for device in others.values():
        pl.semaphore_signal(barrier, inc=1, device_id=device, device_id_type=MESH)
    pl.semaphore_wait(barrier, len(others))
    links = Links(others, r.send_sems, r.recv_sems)

    head_share = lambda i: r.heads.at[1, part(i, share_size), :]
    ffn_share = lambda ref: lambda i: ref.at[hidden_size:, part(i, share_size)]
    row_halves = [lambda ref, j=j: ref.at[j * share_size // 2 : (j + 1) * share_size // 2, :] for j in range(2)]
    unit_halves = [lambda ref, j=j: ref.at[j * hidden_size // 2 : (j + 1) * hidden_size // 2, :] for j in range(2)]
    gather_heads = Gather(links, place, head_share, row_halves)
    gather_first = Gather(links, place, ffn_share(r.first), unit_halves)
    gather_second = Gather(links, place, ffn_share(r.second), unit_halves)
    gather_third = Gather(links, place, ffn_share(r.third), unit_halves)

    def fetch(gather, source):
        gather.fetch([(source.at[:, part(place, share_size)], gather.share(place))])

    gather_heads.fetch([
        (weight.at[part(place, share_size), :], head_share(place).at[:, i * head_width : (i + 1) * head_width])
        for i, weight in enumerate((r.w_query, r.w_key, r.w_value))
    ])
    rates_copy = links.send(r.rates, r.rates_far, "far")

    load_x.wait()

    def norm_step(i, carry):
        where = part(i, 128)
        r.normed[where, :] = normalize(r.x[where, :].astype(f32)).astype(bf16)
        return carry

    lax.fori_loop(0, group_rows // 128, norm_step, 0)
    r.x_rows[...] = r.x[part(own, row_count), :]
    block_rows = part(pair, SPAN)
    mask = (pair * SPAN + column(SPAN) < length).astype(f32)
    early_mask = (column(SPAN) < length).astype(f32) * pair.astype(f32)
    row_mask = (own * row_count + column(row_count) < length).astype(f32)
    places = column(SPAN).astype(f32)

    def project(index):
        wide = slice(index * head_width, (index + 1) * head_width)
        weights = [r.heads.at[index, :, i * head_width : (i + 1) * head_width] for i in range(3)]
        block = r.normed[block_rows, :]
        early = r.normed[0:SPAN, :]
        pre_query = dot_plain(block, weights[0][...])
        sigmoid = jax.nn.sigmoid(pre_query)
        r.queries[:, wide] = (pre_query * sigmoid).astype(bf16)
        r.query_slope[:, wide] = (sigmoid * (1.0 + pre_query * (1.0 - sigmoid))).astype(bf16)
        pre_key = dot_plain(block, weights[1][...])
        sigmoid = jax.nn.sigmoid(pre_key)
        r.keys[:, wide] = (mask * (pre_key * sigmoid)).astype(bf16)
        r.key_slope[:, wide] = (mask * (sigmoid * (1.0 + pre_key * (1.0 - sigmoid)))).astype(bf16)
        r.values[:, wide] = (mask * dot_plain(block, weights[2][...])).astype(bf16)
        early_key = dot_plain(early, weights[1][...])
        early_key = early_mask * (early_key * jax.nn.sigmoid(early_key)).astype(bf16).astype(f32)
        early_value = (early_mask * dot_plain(early, weights[2][...])).astype(bf16)
        return early_key, early_value

    def rate_of(index):
        ref = r.rates if index < block_heads else r.rates_far
        return ref[index % block_heads : index % block_heads + 1, 0:1]

    def attend(index, early_key, early_value):
        for head in range(block_heads):
            at = index * block_heads + head
            rate = rate_of(at)
            cols = slice(at * HDIM, (at + 1) * HDIM)
            early = slice(head * HDIM, (head + 1) * HDIM)
            q, k, v = r.queries[:, cols], r.keys[:, cols], r.values[:, cols]
            weights = (dot_right_t(q, k) * inner_decay(rate)).astype(bf16)
            keyed = (early_key[:, early] * jnp.exp(-rate * (SPAN - 1.0 - places))).astype(bf16)
            state = dot_left_t(keyed, early_value[:, early])
            r.states[at] = state.astype(bf16)
            decayed = (q.astype(f32) * jnp.exp(-rate * (places + 1.0))).astype(bf16)
            out = dot_plain(weights, v) + dot_plain(decayed, state.astype(bf16))
            r.attention[:, cols] = out.astype(bf16)
        wide = slice(index * head_width, (index + 1) * head_width)
        block = own if index == 0 else flipped(own, 1)
        target = r.attention_rows.at[:, part(block, head_width)]
        copy = links.send(r.attention.at[part(1 - member, row_count), wide], target, "mate")
        target[...] = r.attention[part(member, row_count), wide]
        return copy

    def split_transpose(source, keep, give, columns):
        for e in range(4):
            rows = slice(e * share_size, (e + 1) * share_size)
            keep[rows, columns] = transposed(source[:, part(2 * e + core, share_size)])
            give[rows, columns] = transposed(source[:, part(2 * e + 1 - core, share_size)])

    for copy in load_heads:
        copy.wait()
    early = project(0)
    attention_own = attend(0, *early)
    gather_heads.spread()
    fetch(gather_first, r.w_first)
    load_cotangent.wait()
    r.last[:row_count, :] = (row_mask * r.upstream[...].astype(f32)).astype(bf16)
    load_gate.wait()
    r.gate_pre[...] = dot_plain(r.normed[part(own, row_count), :], r.gate[...])
    fetch(gather_second, r.w_second)
    gather_heads.cross()
    split_transpose(r.normed.at[block_rows, :], r.normed_t, r.normed_give, slice(0, SPAN))
    normed_core = links.send(r.normed_give, r.normed_in, "core")
    gather_heads.last()
    gather_first.spread()
    fetch(gather_third, r.w_third)
    last_copy = links.send(r.last.at[:row_count, :], r.last.at[row_count:, :], "mate")
    gather_heads.done()
    rates_copy.wait_recv()
    early = project(1)
    gather_first.cross()
    attention_far = attend(1, *early)
    gather_second.spread()
    gather_first.last()
    load_out.wait()
    arrived([attention_own, attention_far])

    hidden_copies = []
    for j in range(2):
        rows = slice(j * chunk_rows, (j + 1) * chunk_rows)
        gated = (normalize(r.attention_rows[rows, :].astype(f32)) * r.gate_pre[rows, :]).astype(bf16)
        r.gated[rows, :] = gated
        hidden = r.x_rows[rows, :].astype(f32) + row_mask[rows] * dot_plain(gated, r.out[...])
        r.hidden[rows, :] = hidden
        r.hidden_low[rows, :] = normalize(hidden).astype(bf16)
        target = slice(row_count + j * chunk_rows, row_count + (j + 1) * chunk_rows)
        hidden_copies.append(links.send(r.hidden_low.at[rows, :], r.hidden_low.at[target, :], "mate"))
        if j == 0:
            gather_second.cross()

    own_tiles = [(0, 256), (256, 256), (512, 128)]
    far_tiles = [(640, 256), (896, 256), (1152, 256)]

    def forward(rows, tiles):
        for start, size in tiles:
            units = slice(start, start + size)
            first = dot_right_t(r.hidden_low[rows, :], r.first[units, :])
            second = dot_right_t(r.hidden_low[rows, :], r.second[units, :])
            r.first_act[rows, units] = first.astype(bf16)
            r.second_act[rows, units] = second.astype(bf16)
            r.product[rows, units] = (first * second).astype(bf16)

    def backward(rows, tiles):
        for start, size in tiles:
            units = slice(start, start + size)
            product_grad = dot_right_t(r.last[rows, :], r.third[units, :])
            first_grad = product_grad * r.second_act[rows, units].astype(f32)
            second_grad = product_grad * r.first_act[rows, units].astype(f32)
            r.first_act[rows, units] = first_grad.astype(bf16)
            r.second_act[rows, units] = second_grad.astype(bf16)

    units_all = slice(0, 2 * hidden_size)
    col_tiles = [slice(i, i + 256) for i in range(0, width, 256)]

    def norm_grad(rows, cols):
        return dot_plain(r.first_act[rows, units_all], r.first[:, cols]) + dot_plain(
            r.second_act[rows, units_all], r.second[:, cols]
        )

    def mix(rows, cols):
        return dot_plain(r.product[rows, units_all], r.third[:, cols])

    own_rows = slice(0, row_count)
    for copy in (load_first, load_second, load_third):
        copy.wait()
    forward(own_rows, own_tiles)
    gather_third.spread()
    backward(own_rows, own_tiles)
    gather_first.done()
    gather_second.last()
    split_transpose(r.last.at[:row_count, :], r.last_t, r.last_give, slice(0, row_count))
    gather_second.done()
    forward(own_rows, far_tiles)
    product_core = [links.send(r.product.at[own_rows, units_all], r.product_in.at[own_rows, :], "core")]
    gather_third.cross()
    last_copy.wait_recv()
    split_transpose(r.last.at[row_count:, :], r.last_t, r.last_give, slice(row_count, 2 * row_count))
    last_core = links.send(r.last_give, r.last_in, "core")
    split_transpose(r.hidden_low.at[:row_count, :], r.hidden_t, r.hidden_give, slice(0, row_count))
    gather_third.last()
    gather_third.done()
    backward(own_rows, far_tiles)
    grad_core = [
        [links.send(ref.at[own_rows, units_all], target.at[own_rows, :], "core")]
        for ref, target in ((r.first_act, r.first_in), (r.second_act, r.second_in))
    ]
    for cols in col_tiles:
        r.hidden_grad[:, cols] = norm_grad(own_rows, cols)
    mate_chunks = [slice(row_count + j * chunk_rows, row_count + (j + 1) * chunk_rows) for j in range(2)]
    norm_copies = []
    for j, rows in enumerate(mate_chunks):
        arrived([hidden_copies[j]])
        forward(rows, own_tiles + far_tiles)
        backward(rows, own_tiles + far_tiles)
        out_rows = slice(j * chunk_rows, (j + 1) * chunk_rows)
        for cols in col_tiles:
            r.x[out_rows, cols] = norm_grad(rows, cols).astype(bf16)
        norm_copies.append(links.send(r.x.at[out_rows, :], r.norm_in.at[out_rows, :], "mate"))
        product_core.append(links.send(r.product.at[rows, units_all], r.product_in.at[rows, :], "core"))
        for i, (ref, target) in enumerate(((r.first_act, r.first_in), (r.second_act, r.second_in))):
            grad_core[i].append(links.send(ref.at[rows, units_all], target.at[rows, :], "core"))
    split_transpose(
        r.hidden_low.at[row_count:, :], r.hidden_t, r.hidden_give, slice(row_count, 2 * row_count)
    )
    hidden_core = links.send(r.hidden_give, r.hidden_in, "core")

    def weight_grad(target, left, left_in, right, right_in):
        size = right.shape[1]
        for start in range(0, size, 256):
            cols = slice(start, min(start + 256, size))
            total = dot_plain(left[...], right[:, cols]) + dot_plain(left_in[...], right_in[:, cols])
            target[:, cols] = total.astype(bf16)

    arrived([last_core] + product_core)
    weight_grad(r.third_sum, r.last_t, r.last_in, r.product.at[:, units_all], r.product_in)
    chain_third = Chain(links, place, r.third_sum, r.third_half, r.third_quarter, "xy")
    chain_third.start()
    mate_rows = slice(row_count, 2 * row_count)
    for cols in col_tiles:
        r.x[mate_rows, cols] = mix(mate_rows, cols).astype(bf16)
    mix_copy = links.send(r.x.at[mate_rows, :], r.mix_in, "mate")
    for cols in col_tiles:
        r.mix[:, cols] = mix(own_rows, cols)
    arrived([hidden_core] + grad_core[0])
    links.left(product_core)
    first_sum = r.product.at[:, units_all]
    weight_grad(first_sum, r.hidden_t, r.hidden_in, r.first_act.at[:, units_all], r.first_in)
    chain_first = Chain(links, place, first_sum, r.first_half, r.first_quarter, "yx")
    chain_first.start()

    attention_copies = []
    mate_block, mate_far = flipped(own, 0), 3 - own
    for j in range(2):
        rows = slice(j * chunk_rows, (j + 1) * chunk_rows)
        arrived([norm_copies[j]])
        incoming = r.hidden_grad[rows, :] + r.norm_in[rows, :].astype(f32)
        hidden_grad = r.upstream[rows, :].astype(f32) + norm_back(r.hidden[rows, :], incoming)
        r.hidden_grad[rows, :] = hidden_grad
        branch = (row_mask[rows] * hidden_grad).astype(bf16)
        r.branch[rows, :] = branch
        gated_grad = dot_right_t(branch, r.out[...])
        attention = r.attention_rows[rows, :].astype(f32)
        r.gate_grad[rows, :] = (gated_grad * normalize(attention)).astype(bf16)
        grad = norm_back(attention, gated_grad * r.gate_pre[rows, :]).astype(bf16)
        r.attention_grad[rows, :] = grad
        target_rows = part(member * 2 + j, chunk_rows)
        for i, (mine, theirs) in enumerate(((own, mate_block), (flipped(own, 1), mate_far))):
            target = r.grad_block.at[target_rows, i * head_width : (i + 1) * head_width]
            source = r.attention_grad.at[rows, part(theirs, head_width)]
            attention_copies.append(links.send(source, target, "mate"))
            target[...] = r.attention_grad[rows, part(mine, head_width)]
    branch_core = links.send(r.branch, r.branch_in, "core")
    gate_core = links.send(r.gate_grad, r.gate_grad_in, "core")
    split_transpose(r.gated, r.gated_t, r.gated_give, slice(0, row_count))
    gated_core = links.send(r.gated_give, r.gated_in, "core")
    arrived(grad_core[1])
    links.left(grad_core[0])
    second_sum = r.first_act.at[:, units_all]
    weight_grad(second_sum, r.hidden_t, r.hidden_in, r.second_act.at[:, units_all], r.second_in)
    chain_second = Chain(links, place, second_sum, r.second_half, r.second_quarter, "yx")
    chain_second.start()

    arrived(attention_copies)
    heads_all = 2 * block_heads
    for at in range(heads_all):
        cols = slice(at * HDIM, (at + 1) * HDIM)
        decayed = (r.queries[:, cols].astype(f32) * jnp.exp(-rate_of(at) * (places + 1.0))).astype(bf16)
        r.state_grad[at] = dot_left_t(decayed, r.grad_block[:, cols])
    near_heads, far_heads = pl.ds(0, block_heads), pl.ds(block_heads, block_heads)
    state_copies = [
        links.send(r.state_grad.at[near_heads], r.state_in.at[far_heads], "far"),
        links.send(r.state_grad.at[far_heads], r.state_in.at[near_heads], "far"),
    ]

    def grad_cols(kind, at):
        start = (at // block_heads) * 3 * head_width + kind * head_width + (at % block_heads) * HDIM
        return slice(start, start + HDIM)

    for at in range(heads_all):
        rate = rate_of(at)
        cols = slice(at * HDIM, (at + 1) * HDIM)
        q, k, v, g = r.queries[:, cols], r.keys[:, cols], r.values[:, cols], r.grad_block[:, cols]
        decay = inner_decay(rate)
        weights = (dot_right_t(q, k) * decay).astype(bf16)
        score_grad = (dot_right_t(g, v) * decay).astype(bf16)
        dq = dot_plain(score_grad, k) + jnp.exp(-rate * (places + 1.0)) * dot_right_t(g, r.states[at])
        r.pre_grads[:, grad_cols(0, at)] = (dq * r.query_slope[:, cols].astype(f32)).astype(bf16)
        r.pre_grads[:, grad_cols(1, at)] = dot_left_t(score_grad, q).astype(bf16)
        r.pre_grads[:, grad_cols(2, at)] = dot_left_t(weights, g).astype(bf16)
    arrived(state_copies)
    leaving = 1.0 - pair.astype(f32)
    for at in range(heads_all):
        rate = rate_of(at)
        cols = slice(at * HDIM, (at + 1) * HDIM)
        key_decay = leaving * jnp.exp(-rate * (SPAN - 1.0 - places))
        carried = r.state_in[at].astype(bf16)
        dk = r.pre_grads[:, grad_cols(1, at)].astype(f32) + key_decay * dot_right_t(r.values[:, cols], carried)
        dv = r.pre_grads[:, grad_cols(2, at)].astype(f32) + key_decay * dot_plain(r.keys[:, cols], carried)
        r.pre_grads[:, grad_cols(1, at)] = (dk * r.key_slope[:, cols].astype(f32)).astype(bf16)
        r.pre_grads[:, grad_cols(2, at)] = (dv * mask).astype(bf16)
    pre_core = links.send(r.pre_grads, r.pre_in, "core")

    triple = 3 * head_width

    def head_terms(rows, cols):
        return dot_right_t(r.pre_grads[rows, :triple], r.heads[0, cols, :]) + dot_right_t(
            r.pre_grads[rows, triple:], r.heads[1, cols, :]
        )

    term_copies = []
    for start in range(0, width, 512):
        for cols in (slice(start, start + 256), slice(start + 256, start + 512)):
            r.terms[:, cols] = head_terms(part(1 - member, row_count), cols).astype(bf16)
        wide = slice(start, start + 512)
        term_copies.append(links.send(r.terms.at[:, wide], r.terms_in.at[:, wide], "mate"))
    chain_third.middle()
    arrived([pre_core, normed_core])
    links.left(grad_core[1])
    weight_grad(r.second_act, r.normed_t, r.normed_in, r.pre_grads, r.pre_in)
    chain_heads = Chain(links, place, r.second_act, r.heads_half, r.heads_quarter, "xy")
    chain_heads.start()
    chain_first.middle()

    arrived([branch_core, gated_core])
    out_sum = r.out.at[:SPAN, :]
    weight_grad(out_sum, r.gated_t, r.gated_in, r.branch, r.branch_in)
    chain_out = Chain(links, place, out_sum, r.out_half, r.out_quarter, "yx")
    chain_out.start()
    arrived([gate_core])
    gate_sum = r.out.at[SPAN:, :]
    lanes = part(member, row_count)
    weight_grad(gate_sum, r.normed_t.at[:, lanes], r.normed_in.at[:, lanes], r.gate_grad, r.gate_grad_in)
    chain_gate = Chain(links, place, gate_sum, r.gate_half, r.gate_quarter, "xy")
    chain_gate.start()
    chain_second.middle()

    for cols in col_tiles:
        r.terms_own[:, cols] = head_terms(part(member, row_count), cols) + dot_right_t(r.gate_grad[...], r.gate[cols, :])
    arrived([mix_copy])
    r.output[...] = (r.hidden[...] + row_mask * (r.mix[...] + r.mix_in[...].astype(f32))).astype(bf16)
    arrived(term_copies)
    for j in range(2):
        rows = slice(j * chunk_rows, (j + 1) * chunk_rows)
        incoming = r.terms_own[rows, :] + r.terms_in[rows, :].astype(f32)
        grad = r.hidden_grad[rows, :] + norm_back(r.x_rows[rows, :].astype(f32), incoming)
        r.input_grad[rows, :] = grad.astype(bf16)

    def to_far(chain, keep, give, target):
        total = chain.result().astype(bf16)
        size = keep.shape[1]
        keep[...] = total[:, :size]
        give[...] = total[:, size:]
        return links.send(give, target, "far")

    ends = [to_far(chain_third, r.third_keep, r.third_give, r.third_far)]
    ends.append(to_far(chain_first, r.first_keep, r.first_give, r.first_far))
    chain_heads.middle()
    chain_out.middle()
    ends.append(to_far(chain_second, r.second_keep, r.second_give, r.second_far))
    chain_gate.middle()

    def to_heads(chain, keep, target):
        total = chain.result().astype(bf16)
        slot = chain.chunk(chain.y, chain.x)
        slot[...] = total
        size = total.shape[0] // 4
        keep[...] = slot[part(own, size), :]
        return [
            links.send(slot.at[part(index, size), :], target.at[i], device)
            for i, (index, device) in enumerate(((mate_block, "mate"), (flipped(own, 1), "far"), (mate_far, "cross")))
        ]

    ends.append(to_far(chain_heads, r.heads_keep, r.heads_give, r.heads_far))
    ends += to_heads(chain_out, r.out_keep, r.out_far)
    ends += to_heads(chain_gate, r.gate_keep, r.gate_far)
    arrived(ends)
    links.finish()


def finish_kernel(
    output, input_grad, third_keep, third_far, first_keep, first_far, second_keep, second_far,
    heads_keep, heads_far, gate_keep, gate_far, out_keep, out_far,
    output_out, input_grad_out, grad_query, grad_key, grad_value, grad_gate, grad_out, grad_first, grad_second, grad_third,
):
    output_out[...] = output[...]
    input_grad_out[...] = input_grad[...]
    for keep, far, target in (
        (first_keep, first_far, grad_first), (second_keep, second_far, grad_second), (third_keep, third_far, grad_third)
    ):
        target[...] = (keep[...].astype(f32) + far[...].astype(f32)).T
    size = grad_query.shape[1]
    for i, target in enumerate((grad_query, grad_key, grad_value)):
        cols = slice(i * size, (i + 1) * size)
        target[...] = heads_keep[:, cols].astype(f32) + heads_far[:, cols].astype(f32)
    for keep, far, target in ((gate_keep, gate_far, grad_gate), (out_keep, out_far, grad_out)):
        total = keep[...].astype(f32)
        for i in range(3):
            total = total + far[i].astype(f32)
        target[...] = total


def fused_shards(
    layer_input, w_query, w_key, w_value, w_gate, w_out, w_first, w_second, w_third,
    decay_rates, seq_lengths, cotangent,
):
    group_rows, width = layer_input.shape
    row_count = cotangent.shape[0]
    heads = decay_rates.shape[0]
    head_width = w_query.shape[1]
    units = w_third.shape[0]
    rates = jnp.broadcast_to(jnp.pad(decay_rates, (0, 8 - heads))[:, None], (8, 128))
    shape = jax.ShapeDtypeStruct
    share = width // 8
    both = 2 * head_width
    triple = 3 * head_width
    inputs = dict(
        lengths=seq_lengths, rates=rates, layer_input=layer_input, w_query=w_query, w_key=w_key, w_value=w_value,
        w_gate=w_gate, w_out=w_out, w_first=w_first.T, w_second=w_second.T, w_third=w_third, cotangent=cotangent,
    )
    rows_shape = shape((row_count, width), bf16)
    ffn_shape = shape((share, units), bf16)
    head_shape = shape((share, triple), bf16)
    dense_shape = shape((share // 4, width), bf16)
    dense_far = shape((3, share // 4, width), bf16)
    outputs = dict(
        output=rows_shape, input_grad=rows_shape,
        third_keep=ffn_shape, third_far=ffn_shape, first_keep=ffn_shape, first_far=ffn_shape,
        second_keep=ffn_shape, second_far=ffn_shape, heads_keep=head_shape, heads_far=head_shape,
        gate_keep=dense_shape, gate_far=dense_far, out_keep=dense_shape, out_far=dense_far,
    )
    low = lambda *dims: pltpu.VMEM(dims, bf16)
    wide = lambda *dims: pltpu.VMEM(dims, f32)
    half = width // 2
    scratch = dict(
        x=low(group_rows, width), normed=low(group_rows, width),
        heads=low(2, width, triple), gate=low(width, width), out=low(width, width),
        first=low(2 * units, width), second=low(2 * units, width), third=low(2 * units, width),
        upstream=low(row_count, width), rates_far=wide(8, 128),
        queries=low(SPAN, both), keys=low(SPAN, both), values=low(SPAN, both),
        query_slope=low(SPAN, both), key_slope=low(SPAN, both), states=low(2 * heads, HDIM, HDIM),
        attention=low(SPAN, both), attention_rows=low(row_count, width), gate_pre=wide(row_count, width),
        hidden=wide(row_count, width),
        hidden_low=low(SPAN, width), last=low(SPAN, width),
        first_act=low(SPAN, 2 * units), second_act=low(SPAN, 2 * triple), product=low(SPAN, 2 * units),
        hidden_grad=wide(row_count, width), mix=wide(row_count, width), norm_in=low(row_count, width),
        mix_in=low(row_count, width), grad_block=low(SPAN, both),
        state_grad=wide(2 * heads, HDIM, HDIM), state_in=wide(2 * heads, HDIM, HDIM),
        pre_grads=low(SPAN, 2 * triple), terms_in=low(row_count, width),
        terms_own=wide(row_count, width),
        normed_t=low(half, SPAN), normed_give=low(half, SPAN), normed_in=low(half, SPAN),
        last_t=low(half, SPAN), last_give=low(half, SPAN), last_in=low(half, SPAN),
        hidden_t=low(half, SPAN), hidden_give=low(half, SPAN), hidden_in=low(half, SPAN),
        gated_t=low(half, row_count), gated_give=low(half, row_count), gated_in=low(half, row_count),
        product_in=low(SPAN, 2 * units), first_in=low(SPAN, 2 * units), second_in=low(SPAN, 2 * units),
        pre_in=low(SPAN, 2 * triple), branch_in=low(row_count, width), gate_grad_in=low(row_count, width),
        third_sum=low(half, 2 * units),
        third_half=low(2 * share, 2 * units), first_half=low(2 * share, 2 * units),
        second_half=low(2 * share, 2 * units), heads_half=low(2 * share, 2 * triple),
        gate_half=low(2 * share, width), out_half=low(2 * share, width),
        third_quarter=low(share, 2 * units), first_quarter=low(share, 2 * units),
        second_quarter=low(share, 2 * units), heads_quarter=low(share, 2 * triple),
        gate_quarter=low(share, width), out_quarter=low(share, width),
        third_give=low(share, units), first_give=low(share, units), second_give=low(share, units),
        heads_give=low(share, triple),
        local_sems=pltpu.SemaphoreType.DMA((16,)),
        send_sems=pltpu.SemaphoreType.DMA((128,)), recv_sems=pltpu.SemaphoreType.DMA((128,)),
    )
    results = pl.pallas_call(
        functools.partial(layer_kernel, list(inputs) + list(outputs) + list(scratch)),
        out_shape=list(outputs.values()),
        in_specs=[smem(), vmem()] + [pl.BlockSpec(memory_space=pl.ANY)] * (len(inputs) - 2),
        out_specs=[vmem()] * len(outputs),
        scratch_shapes=list(scratch.values()),
        compiler_params=pltpu.CompilerParams(
            collective_id=0, has_side_effects=True, vmem_limit_bytes=VMEM_ALL
        ),
        name="layer",
    )(*inputs.values())
    transposed_shape = shape((units, share), f32)
    finals = [rows_shape] * 2 + [shape((share, head_width), f32)] * 3 + [shape((share // 4, width), f32)] * 2
    finals += [transposed_shape] * 3
    results = local_call(finish_kernel, "finish", finals, list(results), 0, 10**6)
    return (*results[:7], results[7].T, results[8].T, results[9])


def solution(mesh):
    placed = (
        P("dp", None),
        P(None, "head"),
        P(None, "head"),
        P(None, "head"),
        P(),
        P(),
        P(None, "head"),
        P(None, "head"),
        P("head", None),
        P("head"),
        P("dp"),
        P(("dp", "head"), None),
    )
    n_dp, n_head = mesh.shape["dp"], mesh.shape["head"]
    body = fused_shards if (n_dp, n_head) == (8, 4) else functools.partial(shards, n_dp, n_head)
    return jax.shard_map(
        body,
        mesh=mesh,
        in_specs=placed,
        out_specs=(
            P(("dp", "head"), None),
            P(("dp", "head"), None),
            P("dp", "head"),
            P("dp", "head"),
            P("dp", "head"),
            P(("dp", "head"), None),
            P(("dp", "head"), None),
            P("dp", "head"),
            P("dp", "head"),
            P("head", "dp"),
        ),
        check_vma=False,
    )
```

```python
import functools
import types

import jax
import jax.numpy as jnp
from jax import lax
from jax.experimental import pallas as pl
from jax.experimental.pallas import tpu as pltpu
from jax.sharding import PartitionSpec as P

SPAN = 512
HDIM = 128

epsilon = 1e-06
bf16 = jnp.bfloat16
f32 = jnp.float32
VMEM_LIMIT = 48 * 2**20
VMEM_ALL = 63 * 2**20


def inverse_rms(values):
    return lax.rsqrt(jnp.mean(values * values, axis=-1, keepdims=True) + epsilon)


def normalize(values):
    return values * inverse_rms(values)


def norm_back(values, incoming):
    inverse = inverse_rms(values)
    unit_rows = values * inverse
    return inverse * (incoming - unit_rows * jnp.mean(incoming * unit_rows, axis=-1, keepdims=True))


def dot_plain(left, right):
    return jnp.dot(left, right, preferred_element_type=f32)


def dot_right_t(left, right):
    return lax.dot_general(left, right, (((1,), (1,)), ((), ())), preferred_element_type=f32)


def dot_left_t(left, right):
    return lax.dot_general(left, right, (((0,), (0,)), ((), ())), preferred_element_type=f32)


def transposed(values):
    return values.T


def column(length):
    return lax.broadcasted_iota(jnp.int32, (length, 1), 0)


def inner_decay(rate):
    rows = lax.broadcasted_iota(jnp.int32, (SPAN, SPAN), 0)
    cols = lax.broadcasted_iota(jnp.int32, (SPAN, SPAN), 1)
    offset = rows - cols
    return jnp.where(offset >= 0, jnp.exp(-rate * jnp.maximum(offset, 0).astype(f32)), 0.0)


def attend_kernel(
    meta, rates, x, w_own_q, w_own_k, w_own_v, w_other,
    normed, attention, queries, keys, values, query_slope, key_slope, states,
):
    pair, length = meta[0], meta[1]
    start = pl.multiple_of(pair * SPAN, SPAN)
    rows = x.shape[0]
    head_width = w_own_q.shape[1]

    def norm_step(i, carry):
        place = pl.ds(pl.multiple_of(i * 128, 128), 128)
        normed[place, :] = normalize(x[place, :].astype(f32)).astype(bf16)
        return carry

    lax.fori_loop(0, rows // 128, norm_step, 0)
    block = normed[pl.ds(start, SPAN), :]
    mask = (start + column(SPAN) < length).astype(f32)
    early_mask = (column(SPAN) < length).astype(f32) * pair.astype(f32)
    early = normed[0:SPAN, :]
    places = column(SPAN).astype(f32)
    for part in range(2):
        if part == 0:
            wq, wk, wv = w_own_q[...], w_own_k[...], w_own_v[...]
        else:
            wq, wk, wv = (w_other[:, i * head_width : (i + 1) * head_width] for i in range(3))
        pre_query = dot_plain(block, wq)
        pre_key = dot_plain(block, wk)
        pre_value = dot_plain(block, wv)
        sigmoid_query = jax.nn.sigmoid(pre_query)
        sigmoid_key = jax.nn.sigmoid(pre_key)
        query = (pre_query * sigmoid_query).astype(bf16)
        key = (mask * (pre_key * sigmoid_key)).astype(bf16)
        value = (mask * pre_value).astype(bf16)
        wide = slice(part * head_width, (part + 1) * head_width)
        query_slope[:, wide] = (sigmoid_query * (1.0 + pre_query * (1.0 - sigmoid_query))).astype(bf16)
        key_slope[:, wide] = (mask * (sigmoid_key * (1.0 + pre_key * (1.0 - sigmoid_key)))).astype(bf16)
        queries[:, wide] = query
        keys[:, wide] = key
        values[:, wide] = value
        early_key = dot_plain(early, wk)
        early_key = early_mask * (early_key * jax.nn.sigmoid(early_key)).astype(bf16).astype(f32)
        early_value = (early_mask * dot_plain(early, wv)).astype(bf16)
        for head in range(head_width // HDIM):
            index = part * (head_width // HDIM) + head
            rate = rates[index]
            cols = slice(head * HDIM, (head + 1) * HDIM)
            q, k, v = query[:, cols], key[:, cols], value[:, cols]
            scores = dot_right_t(q, k)
            weights = (scores * inner_decay(rate)).astype(bf16)
            keyed = (early_key[:, cols] * jnp.exp(-rate * (SPAN - 1.0 - places))).astype(bf16)
            state = dot_left_t(keyed, early_value[:, cols])
            states[index] = state
            decayed = (q.astype(f32) * jnp.exp(-rate * (places + 1.0))).astype(bf16)
            out = dot_plain(weights, v) + dot_plain(decayed, state.astype(bf16))
            attention[:, index * HDIM : (index + 1) * HDIM] = out.astype(bf16)


def state_kernel(rates, queries, upstream, state_grad):
    places = column(SPAN).astype(f32)
    for index in range(state_grad.shape[0]):
        cols = slice(index * HDIM, (index + 1) * HDIM)
        decayed = (queries[:, cols].astype(f32) * jnp.exp(-rates[index] * (places + 1.0))).astype(bf16)
        state_grad[index] = dot_left_t(decayed, upstream[:, cols])


def attend_back_kernel(
    meta, rates, queries, keys, values, upstream, query_slope, key_slope, states, state_grad, pre_grads
):
    pair, length = meta[0], meta[1]
    mask = (pair * SPAN + column(SPAN) < length).astype(f32)
    places = column(SPAN).astype(f32)
    heads = states.shape[0]
    half = heads // 2
    for index in range(heads):
        rate = rates[index]
        cols = slice(index * HDIM, (index + 1) * HDIM)
        q, k, v, g = queries[:, cols], keys[:, cols], values[:, cols], upstream[:, cols]
        decay = inner_decay(rate)
        query_decay = jnp.exp(-rate * (places + 1.0))
        key_decay = jnp.exp(-rate * (SPAN - 1.0 - places))
        state = states[index].astype(bf16)
        carried = state_grad[index].astype(bf16)
        weights = (dot_right_t(q, k) * decay).astype(bf16)
        score_grad = (dot_right_t(g, v) * decay).astype(bf16)
        dq = dot_plain(score_grad, k) + query_decay * dot_right_t(g, state)
        dk = dot_left_t(score_grad, q) + key_decay * dot_right_t(v, carried)
        dv = dot_left_t(weights, g) + key_decay * dot_plain(k, carried)
        base = (index // half) * (3 * half * HDIM) + (index % half) * HDIM
        pre_grads[:, base : base + HDIM] = (dq * query_slope[:, cols].astype(f32)).astype(bf16)
        base += half * HDIM
        pre_grads[:, base : base + HDIM] = (dk * key_slope[:, cols].astype(f32)).astype(bf16)
        base += half * HDIM
        pre_grads[:, base : base + HDIM] = (dv * mask).astype(bf16)


def vmem():
    return pl.BlockSpec(memory_space=pltpu.VMEM)


def smem():
    return pl.BlockSpec(memory_space=pltpu.SMEM)


def local_call(body, name, out_shapes, args, scalars, flops):
    size = sum(int(a.size) * a.dtype.itemsize for a in list(args) + list(out_shapes))
    return pl.pallas_call(
        body,
        out_shape=out_shapes,
        in_specs=[smem()] * scalars + [vmem()] * (len(args) - scalars),
        out_specs=[vmem()] * len(out_shapes),
        compiler_params=pltpu.CompilerParams(vmem_limit_bytes=VMEM_LIMIT),
        cost_estimate=pl.CostEstimate(flops=flops, bytes_accessed=size, transcendentals=0),
        name=name,
    )(*args)


def shards(
    n_dp, n_head,
    layer_input, w_query, w_key, w_value, w_gate, w_out, w_first, w_second, w_third,
    decay_rates, seq_lengths, cotangent,
):
    group_rows, width = layer_input.shape
    row_count = cotangent.shape[0]
    heads = decay_rates.shape[0]
    head_width = w_query.shape[1]
    place = lax.axis_index("dp")
    own = lax.axis_index("head")
    member, pair = own % 2, own // 2
    bits = n_dp.bit_length() - 1
    length = seq_lengths[0]

    def to_mate(array, bit):
        return lax.ppermute(array, "head", [(i, i ^ bit) for i in range(n_head)])

    def across(array, bit):
        return lax.ppermute(array, "dp", [(i, i ^ (1 << bit)) for i in range(n_dp)])

    def gathered(weight, axis):
        size = weight.shape[axis] // n_dp
        share = lax.dynamic_slice_in_dim(weight, place * size, size, axis)
        return lax.all_gather(to_mate(share, 2), "dp", axis=axis, tiled=True)

    w_heads = jnp.concatenate([w_query, w_key, w_value], axis=1)
    w_heads_other = gathered(w_heads, 0)
    w_first_other = gathered(w_first, 0)
    w_second_other = gathered(w_second, 0)
    w_third_other = gathered(w_third, 1)
    rates = jnp.concatenate([decay_rates, to_mate(decay_rates, 2)])

    block_start = pair * SPAN
    row_start = own * row_count
    positions = jnp.arange(row_count, dtype=jnp.int32)[:, None]
    row_mask = (row_start + positions < length).astype(f32)
    upstream = cotangent.astype(f32)
    last_own = (row_mask * upstream).astype(bf16)
    last_mate = to_mate(last_own, 1)

    meta = jnp.stack([pair, length]).astype(jnp.int32)
    both = 2 * head_width
    shape = jax.ShapeDtypeStruct
    block_shape = shape((SPAN, both), bf16)
    normed, attention_block, queries, keys, values, query_slope, key_slope, states = local_call(
        attend_kernel, "attend",
        [shape(layer_input.shape, bf16)] + [block_shape] * 6 + [shape((2 * heads, HDIM, HDIM), f32)],
        [meta, rates, layer_input, w_query, w_key, w_value, w_heads_other], 2, 6 * 10**9,
    )

    def rows_of(array, index):
        return lax.dynamic_slice_in_dim(array, index * row_count, row_count, 0)

    def ordered(mine, other):
        even, odd = jnp.where(member == 0, mine, other), jnp.where(member == 0, other, mine)
        flip = lambda a: jnp.where(pair == 0, a, jnp.concatenate([a[:, head_width:], a[:, :head_width]], axis=1))
        even, odd = flip(even), flip(odd)
        return jnp.concatenate(
            [even[:, :head_width], odd[:, :head_width], even[:, head_width:], odd[:, head_width:]], axis=1
        )

    def pieces(array):
        cut = [array[:, i * head_width : (i + 1) * head_width] for i in range(4)]
        even, odd = jnp.concatenate([cut[0], cut[2]], axis=1), jnp.concatenate([cut[1], cut[3]], axis=1)
        flip = lambda a: jnp.where(pair == 0, a, jnp.concatenate([a[:, head_width:], a[:, :head_width]], axis=1))
        even, odd = flip(even), flip(odd)
        return jnp.where(member == 0, even, odd), jnp.where(member == 0, odd, even)

    received = to_mate(rows_of(attention_block, 1 - member), 1)
    attention = ordered(rows_of(attention_block, member), received).astype(f32)
    attention_norm = normalize(attention)
    rows_low = rows_of(normed, own)
    input_rows = rows_of(layer_input, own).astype(f32)
    gate_pre = dot_plain(rows_low, w_gate)
    gated = (attention_norm * gate_pre).astype(bf16)
    hidden = input_rows + row_mask * dot_plain(gated, w_out)
    hidden_low = normalize(hidden).astype(bf16)
    hidden_mate = to_mate(hidden_low, 1)

    w_first_all = jnp.concatenate([w_first, w_first_other], axis=1)
    w_second_all = jnp.concatenate([w_second, w_second_other], axis=1)
    w_third_all = jnp.concatenate([w_third, w_third_other], axis=0)

    def forward_rows(rows_in):
        first, second = dot_plain(rows_in, w_first_all), dot_plain(rows_in, w_second_all)
        return first.astype(bf16), second.astype(bf16), (first * second).astype(bf16)

    def backward_rows(last, first, second):
        product_grad = dot_right_t(last, w_third_all)
        first_grad = (product_grad * second.astype(f32)).astype(bf16)
        second_grad = (product_grad * first.astype(f32)).astype(bf16)
        return first_grad, second_grad, dot_right_t(first_grad, w_first_all) + dot_right_t(second_grad, w_second_all)

    first_mate, second_mate, product_mate = forward_rows(hidden_mate)
    first_grad_mate, second_grad_mate, norm_grad_mate = backward_rows(last_mate, first_mate, second_mate)
    norm_grad_in = to_mate(norm_grad_mate.astype(bf16), 1)
    mix_in = to_mate(dot_plain(product_mate, w_third_all).astype(bf16), 1)
    first_own, second_own, product_own = forward_rows(hidden_low)
    first_grad_own, second_grad_own, norm_grad_own = backward_rows(last_own, first_own, second_own)
    hidden_grad = upstream + norm_back(hidden, norm_grad_own + norm_grad_in.astype(f32))
    mixed = dot_plain(product_own, w_third_all) + mix_in.astype(f32)
    output = (hidden + row_mask * mixed).astype(bf16)

    branch_grad = (row_mask * hidden_grad).astype(bf16)
    gated_grad = dot_right_t(branch_grad, w_out)
    gate_grad = (gated_grad * attention_norm).astype(bf16)
    attention_grad = norm_back(attention, gated_grad * gate_pre).astype(bf16)
    mine, for_mate = pieces(attention_grad)
    from_mate = to_mate(for_mate, 1)
    grad_block = jnp.concatenate(
        [jnp.where(member == 0, mine, from_mate), jnp.where(member == 0, from_mate, mine)], axis=0
    )
    state_shape = shape((2 * heads, HDIM, HDIM), f32)
    (state_grad,) = local_call(
        state_kernel, "state_grad", [state_shape], [rates, queries, grad_block], 1, 10**8
    )
    swapped = jnp.concatenate([state_grad[heads:], state_grad[:heads]], axis=0)
    carried = lax.ppermute(swapped, "head", [(i, i - 2) for i in range(2, n_head)])
    (pre_grads,) = local_call(
        attend_back_kernel, "attend_back", [shape((SPAN, 3 * both), bf16)],
        [meta, rates, queries, keys, values, grad_block, query_slope, key_slope, states, carried], 2, 2 * 10**9,
    )
    head_terms = dot_right_t(pre_grads[:, : 3 * head_width], w_heads) + dot_right_t(
        pre_grads[:, 3 * head_width :], w_heads_other
    )
    head_terms = head_terms.astype(bf16)
    terms_in = to_mate(rows_of(head_terms, 1 - member), 1)
    input_norm_grad = (
        rows_of(head_terms, member).astype(f32) + terms_in.astype(f32) + dot_right_t(gate_grad, w_gate)
    )
    input_grad = (hidden_grad + norm_back(input_rows, input_norm_grad)).astype(bf16)

    def summed(left, right, order):
        left = left.reshape((left.shape[0],) + (2,) * bits + (width // n_dp,))

        def pick(array, axis, bit, which):
            side = (place // (1 << bit)) % 2
            return lax.dynamic_index_in_dim(array, side if which else 1 - side, axis, keepdims=False)

        left_axis = lambda bit, done: 1 + (bits - 1 - bit) - sum(1 for b in done if b > bit)
        first_bit = order[0]
        make = lambda which: dot_left_t(
            pick(left, left_axis(first_bit, []), first_bit, which).reshape(left.shape[0], width // 2), right
        ).astype(bf16)
        arrived = across(make(False), first_bit)
        total = (make(True).astype(f32) + arrived.astype(f32)).astype(bf16)
        total = total.reshape((2,) * (bits - 1) + (width // n_dp, right.shape[1]))
        done = [first_bit]
        for bit in order[1:]:
            axis = left_axis(bit, done) - 1
            arrived = across(pick(total, axis, bit, False), bit)
            total = (pick(total, axis, bit, True).astype(f32) + arrived.astype(f32)).astype(bf16)
            done.append(bit)
        return total

    def with_mate(total):
        size = total.shape[1] // 2
        return total[:, :size].astype(f32) + to_mate(total[:, size:], 2).astype(f32)

    def over_heads(total):
        for bit in (1, 2):
            cut = total.reshape((2, -1) + total.shape[1:]) if bit == 2 else total.reshape((2, 2, -1) + total.shape[1:])
            side = (own // bit) % 2
            axis = 0 if bit == 2 else 1
            arrived = to_mate(lax.dynamic_index_in_dim(cut, 1 - side, axis, keepdims=False), bit)
            total = lax.dynamic_index_in_dim(cut, side, axis, keepdims=False).astype(f32) + arrived.astype(f32)
            if bit == 1:
                total = total.astype(bf16).reshape((-1,) + total.shape[2:])
        return total

    up = list(range(bits))
    down = [0] + up[:0:-1]
    stack = lambda a, b: jnp.concatenate([a, b], axis=0)
    hidden_all = stack(hidden_low, hidden_mate)
    last_all = stack(last_own, last_mate)
    grad_third_t = with_mate(summed(last_all, stack(product_own, product_mate), up))
    grad_first = with_mate(summed(hidden_all, stack(first_grad_own, first_grad_mate), up))
    grad_second = with_mate(summed(hidden_all, stack(second_grad_own, second_grad_mate), down))
    grad_out = over_heads(summed(gated, branch_grad, down))
    grad_gate = over_heads(summed(rows_low, gate_grad, up))
    normed_block = lax.dynamic_slice_in_dim(normed, block_start, SPAN, 0)
    grad_heads = with_mate(summed(normed_block, pre_grads, down))
    return (
        output,
        input_grad,
        grad_heads[:, :head_width],
        grad_heads[:, head_width : 2 * head_width],
        grad_heads[:, 2 * head_width :],
        grad_gate,
        grad_out,
        grad_first,
        grad_second,
        grad_third_t.T,
    )


MESH = pl.DeviceIdType.MESH


def flipped(index, bit):
    return index + (1 << bit) * (1 - 2 * ((index // (1 << bit)) % 2))


def part(index, size):
    return pl.ds(pl.multiple_of(index * size, size), size)


class Links:
    def __init__(self, others, send_sems, recv_sems):
        self.others, self.send_sems, self.recv_sems, self.started = others, send_sems, recv_sems, []

    def send(self, source, target, device):
        index = len(self.started)
        copy = pltpu.make_async_remote_copy(
            src_ref=source,
            dst_ref=target,
            send_sem=self.send_sems.at[index],
            recv_sem=self.recv_sems.at[index],
            device_id=self.others[device],
            device_id_type=MESH,
        )
        copy.start()
        self.started.append(copy)
        copy.sent = False
        return copy

    def left(self, copies):
        for copy in copies:
            if not copy.sent:
                copy.wait_send()
                copy.sent = True

    def finish(self):
        self.left(self.started)


def arrived(copies):
    for copy in copies:
        copy.wait_recv()


class Gather:
    def __init__(self, links, place, pieces, halves):
        self.links, self.pieces, self.halves = links, pieces, halves
        self.places = [place, flipped(place, 1), flipped(place, 2), flipped(flipped(place, 1), 2)]
        self.to_core, self.near, self.crossing, self.fetched = [], {}, {}, {}

    def pass_on(self, piece, which, device):
        ref = self.pieces[piece](self.places[which])
        return self.links.send(ref, ref, device)

    def fetch(self, sources):
        for i, source in enumerate(sources):
            self.fetched[i] = self.links.send(source, self.pieces[i](self.places[0]), "far")

    def spread(self, piece=0):
        arrived([self.fetched[piece]])
        self.near[piece] = (self.pass_on(piece, 0, "x"), self.pass_on(piece, 0, "y"))
        self.to_core.append(self.pass_on(piece, 0, "core"))

    def cross(self, piece=0):
        crossing = []
        for i, (half, device) in enumerate(zip(self.halves, ("y", "x"))):
            arrived([self.near[piece][i]])
            ref = half(self.pieces[piece](self.places[1 + i]))
            crossing.append(self.links.send(ref, ref, device))
            self.to_core.append(self.pass_on(piece, 1 + i, "core"))
        self.crossing[piece] = crossing

    def last(self, piece=0):
        arrived(self.crossing[piece])
        self.to_core.append(self.pass_on(piece, 3, "core"))

    def done(self):
        arrived(self.to_core)


class Chain:
    def __init__(self, links, place, total, halves_in, quarter_in, cut, orders=("xy", "yx")):
        self.links, self.total, self.halves_in, self.quarter_in = links, total, halves_in, quarter_in
        size = total.shape[1]
        self.parts = [(slice(0, cut), orders[0]), (slice(cut, size), orders[1])]
        self.x, self.y = (place // 2) % 2, (place // 4) % 2
        self.rows = quarter_in.shape[0]
        self.waits = []

    def chunk(self, y, x, cols=slice(None)):
        return self.total.at[part(2 * y + x, self.rows), cols]

    def start(self):
        links, rows = self.links, self.rows
        for cols, order in self.parts:
            if order == "xy":
                self.waits.append([
                    links.send(self.chunk(y, 1 - self.x, cols), self.halves_in.at[y * rows : (y + 1) * rows, cols], "x")
                    for y in range(2)
                ])
            else:
                give = self.total.at[part(1 - self.y, 2 * rows), cols]
                self.waits.append([links.send(give, self.halves_in.at[:, cols], "y")])

    def add(self, place, arrived_part):
        place[...] = (place[...].astype(f32) + arrived_part.astype(f32)).astype(bf16)

    def middle(self):
        rows, x, y = self.rows, self.x, self.y
        keep, waits = [], []
        for (cols, order), before in zip(self.parts, self.waits):
            arrived(before)
            give, device, index = (
                (self.chunk(1 - y, x, cols), "y", y) if order == "xy" else (self.chunk(y, 1 - x, cols), "x", x)
            )
            self.add(give, self.halves_in[part(1 - index, rows), cols])
            waits.append([self.links.send(give, self.quarter_in.at[:, cols], device)])
            keep.append((cols, index))
        for cols, index in keep:
            self.add(self.chunk(y, x, cols), self.halves_in[part(index, rows), cols])
        self.waits = waits

    def result(self):
        for before in self.waits:
            arrived(before)
        return self.chunk(self.y, self.x)[...].astype(f32) + self.quarter_in[...].astype(f32)


def layer_kernel(names, *refs):
    r = types.SimpleNamespace(**dict(zip(names, refs)))
    place, own = lax.axis_index("dp"), lax.axis_index("head")
    pair, member, core = own // 2, own % 2, place % 2
    length = r.lengths[0]
    group_rows, width = r.layer_input.shape
    row_count = r.cotangent.shape[0]
    head_width = r.w_query.shape[1]
    block_heads = head_width // HDIM
    hidden_size = r.w_third.shape[0]
    share_size = width // 8
    chunk_rows = row_count // 2
    r.gated, r.x_rows = (r.x.at[i * row_count : (i + 1) * row_count, :] for i in (2, 3))
    r.branch, r.gate_grad, r.attention_grad, r.terms = (
        r.normed.at[i * row_count : (i + 1) * row_count, :] for i in range(4)
    )

    copies = []

    def load(source, target):
        copy = pltpu.make_async_copy(source, target, r.local_sems.at[len(copies)])
        copy.start()
        copies.append(copy)
        return copy

    load_cotangent = load(r.cotangent, r.upstream)
    load_x = load(r.layer_input, r.x)
    load_heads = [
        load(weight, r.heads.at[0, :, i * head_width : (i + 1) * head_width])
        for i, weight in enumerate((r.w_query, r.w_key, r.w_value))
    ]
    load_gate = load(r.w_gate, r.gate)
    load_out = load(r.w_out, r.out)
    load_first = load(r.w_first, r.first.at[:hidden_size, :])
    load_second = load(r.w_second, r.second.at[:hidden_size, :])
    load_third = load(r.w_third, r.third.at[:hidden_size, :])

    others = {
        "core": (flipped(place, 0), own),
        "x": (flipped(place, 1), own),
        "y": (flipped(place, 2), own),
        "mate": (place, flipped(own, 0)),
        "far": (place, flipped(own, 1)),
        "cross": (place, 3 - own),
    }
    barrier = pltpu.get_barrier_semaphore()
    for device in others.values():
        pl.semaphore_signal(barrier, inc=1, device_id=device, device_id_type=MESH)
    pl.semaphore_wait(barrier, len(others))
    links = Links(others, r.send_sems, r.recv_sems)

    head_piece = lambda j: lambda i: r.heads.at[1, part(i, share_size), j * head_width : (j + 1) * head_width]
    ffn_piece = lambda ref: lambda i: ref.at[hidden_size:, part(i, share_size)]
    row_halves = [lambda ref, j=j: ref.at[j * share_size // 2 : (j + 1) * share_size // 2, :] for j in range(2)]
    unit_halves = [lambda ref, j=j: ref.at[j * hidden_size // 2 : (j + 1) * hidden_size // 2, :] for j in range(2)]
    gather_heads = Gather(links, place, [head_piece(j) for j in (1, 2, 0)], row_halves)
    gather_first = Gather(links, place, [ffn_piece(r.first)], unit_halves)
    gather_second = Gather(links, place, [ffn_piece(r.second)], unit_halves)
    gather_third = Gather(links, place, [ffn_piece(r.third)], unit_halves)

    def fetch(gather, source):
        gather.fetch([source.at[:, part(place, share_size)]])

    gather_heads.fetch([weight.at[part(place, share_size), :] for weight in (r.w_key, r.w_value, r.w_query)])
    for i in range(block_heads):
        r.rates[i : i + 1, :] = jnp.full((1, 128), r.decay_rates[i], f32)
    rates_copy = links.send(r.rates, r.rates_far, "far")
    row_mask = (own * row_count + column(row_count) < length).astype(f32)
    load_cotangent.wait()
    r.last[:row_count, :] = (row_mask * r.upstream[...].astype(f32)).astype(bf16)
    last_copy = links.send(r.last.at[:row_count, :], r.last.at[row_count:, :], "mate")
    fetch(gather_first, r.w_first)

    load_x.wait()

    def norm_step(i, carry):
        where = part(i, 128)
        r.normed[where, :] = normalize(r.x[where, :].astype(f32)).astype(bf16)
        return carry

    lax.fori_loop(0, group_rows // 128, norm_step, 0)
    r.x_rows[...] = r.x[part(own, row_count), :]
    block_rows = part(pair, SPAN)
    mask = (pair * SPAN + column(SPAN) < length).astype(f32)
    early_mask = (column(SPAN) < length).astype(f32) * pair.astype(f32)
    places = column(SPAN).astype(f32)

    def project(index):
        wide = slice(index * head_width, (index + 1) * head_width)
        weights = [r.heads.at[index, :, i * head_width : (i + 1) * head_width] for i in range(3)]
        block = r.normed[block_rows, :]
        early = r.normed[0:SPAN, :]
        pre_query = dot_plain(block, weights[0][...])
        sigmoid = jax.nn.sigmoid(pre_query)
        r.queries[:, wide] = (pre_query * sigmoid).astype(bf16)
        r.query_slope[:, wide] = (sigmoid * (1.0 + pre_query * (1.0 - sigmoid))).astype(bf16)
        pre_key = dot_plain(block, weights[1][...])
        sigmoid = jax.nn.sigmoid(pre_key)
        r.keys[:, wide] = (mask * (pre_key * sigmoid)).astype(bf16)
        r.key_slope[:, wide] = (mask * (sigmoid * (1.0 + pre_key * (1.0 - sigmoid)))).astype(bf16)
        r.values[:, wide] = (mask * dot_plain(block, weights[2][...])).astype(bf16)
        early_key = dot_plain(early, weights[1][...])
        early_key = early_mask * (early_key * jax.nn.sigmoid(early_key)).astype(bf16).astype(f32)
        early_value = (early_mask * dot_plain(early, weights[2][...])).astype(bf16)
        return early_key, early_value

    def rate_of(index):
        ref = r.rates if index < block_heads else r.rates_far
        return ref[index % block_heads : index % block_heads + 1, 0:1]

    def attend(index, early_key, early_value):
        for head in range(block_heads):
            at = index * block_heads + head
            rate = rate_of(at)
            cols = slice(at * HDIM, (at + 1) * HDIM)
            early = slice(head * HDIM, (head + 1) * HDIM)
            q, k, v = r.queries[:, cols], r.keys[:, cols], r.values[:, cols]
            weights = (dot_right_t(q, k) * inner_decay(rate)).astype(bf16)
            keyed = (early_key[:, early] * jnp.exp(-rate * (SPAN - 1.0 - places))).astype(bf16)
            state = dot_left_t(keyed, early_value[:, early])
            r.states[at] = state.astype(bf16)
            decayed = (q.astype(f32) * jnp.exp(-rate * (places + 1.0))).astype(bf16)
            out = dot_plain(weights, v) + dot_plain(decayed, state.astype(bf16))
            r.attention[:, cols] = out.astype(bf16)
        wide = slice(index * head_width, (index + 1) * head_width)
        block = own if index == 0 else flipped(own, 1)
        target = r.attention_rows.at[:, part(block, head_width)]
        copy = links.send(r.attention.at[part(1 - member, row_count), wide], target, "mate")
        target[...] = r.attention[part(member, row_count), wide]
        return copy

    def split_transpose(source, keep, give, columns):
        for e in range(4):
            rows = slice(e * share_size, (e + 1) * share_size)
            keep[rows, columns] = transposed(source[:, part(2 * e + core, share_size)])
            give[rows, columns] = transposed(source[:, part(2 * e + 1 - core, share_size)])

    for copy in load_heads:
        copy.wait()
    gather_heads.spread(0)
    early = project(0)
    gather_heads.spread(1)
    gather_heads.spread(2)
    gather_heads.cross(0)
    attention_own = attend(0, *early)
    fetch(gather_second, r.w_second)
    gather_heads.cross(1)
    gather_heads.cross(2)
    gather_heads.last(0)
    split_transpose(r.normed.at[block_rows, :], r.normed_t, r.normed_give, slice(0, SPAN))
    normed_core = links.send(r.normed_give, r.normed_in, "core")
    gather_heads.last(1)
    gather_heads.last(2)
    load_gate.wait()
    r.gate_pre[...] = dot_plain(r.normed[part(own, row_count), :], r.gate[...])
    gather_heads.done()
    rates_copy.wait_recv()
    early = project(1)
    gather_first.spread()
    attention_far = attend(1, *early)
    fetch(gather_third, r.w_third)
    split_transpose(r.last.at[:row_count, :], r.last_t, r.last_give, slice(0, row_count))
    gather_first.cross()
    gather_second.spread()
    load_out.wait()
    gather_first.last()
    arrived([attention_own, attention_far])

    hidden_copies = []
    for j in range(2):
        rows = slice(j * chunk_rows, (j + 1) * chunk_rows)
        gated = (normalize(r.attention_rows[rows, :].astype(f32)) * r.gate_pre[rows, :]).astype(bf16)
        r.gated[rows, :] = gated
        hidden = r.x_rows[rows, :].astype(f32) + row_mask[rows] * dot_plain(gated, r.out[...])
        r.hidden[rows, :] = hidden
        r.hidden_low[rows, :] = normalize(hidden).astype(bf16)
        target = slice(row_count + j * chunk_rows, row_count + (j + 1) * chunk_rows)
        hidden_copies.append(links.send(r.hidden_low.at[rows, :], r.hidden_low.at[target, :], "mate"))
        if j == 0:
            gather_second.cross()

    own_tiles = [(0, 256), (256, 256), (512, 128)]
    far_tiles = [(640, 256), (896, 256), (1152, 256)]

    def forward(rows, tiles):
        for start, size in tiles:
            units = slice(start, start + size)
            first = dot_right_t(r.hidden_low[rows, :], r.first[units, :])
            second = dot_right_t(r.hidden_low[rows, :], r.second[units, :])
            r.first_act[rows, units] = first.astype(bf16)
            r.second_act[rows, units] = second.astype(bf16)
            r.product[rows, units] = (first * second).astype(bf16)

    def backward(rows, tiles):
        for start, size in tiles:
            units = slice(start, start + size)
            product_grad = dot_right_t(r.last[rows, :], r.third[units, :])
            first_grad = product_grad * r.second_act[rows, units].astype(f32)
            second_grad = product_grad * r.first_act[rows, units].astype(f32)
            r.first_act[rows, units] = first_grad.astype(bf16)
            r.second_act[rows, units] = second_grad.astype(bf16)

    units_all = slice(0, 2 * hidden_size)
    col_tiles = [slice(i, i + 256) for i in range(0, width, 256)]

    def norm_grad(rows, cols):
        return dot_plain(r.first_act[rows, units_all], r.first[:, cols]) + dot_plain(
            r.second_act[rows, units_all], r.second[:, cols]
        )

    def mix(rows, cols):
        return dot_plain(r.product[rows, units_all], r.third[:, cols])

    own_rows = slice(0, row_count)
    for copy in (load_first, load_second, load_third):
        copy.wait()
    forward(own_rows, own_tiles)
    backward(own_rows, own_tiles)
    gather_second.last()
    split_transpose(r.hidden_low.at[:row_count, :], r.hidden_t, r.hidden_give, slice(0, row_count))
    gather_third.spread()
    last_copy.wait_recv()
    split_transpose(r.last.at[row_count:, :], r.last_t, r.last_give, slice(row_count, 2 * row_count))
    last_core = links.send(r.last_give, r.last_in, "core")
    gather_first.done()
    gather_second.done()
    forward(own_rows, far_tiles)
    product_core = [links.send(r.product.at[own_rows, units_all], r.product_in.at[own_rows, :], "core")]
    gather_third.cross()
    gather_third.last()
    gather_third.done()
    backward(own_rows, far_tiles)
    grad_core = [
        [links.send(ref.at[own_rows, units_all], target.at[own_rows, :], "core")]
        for ref, target in ((r.first_act, r.first_in), (r.second_act, r.second_in))
    ]
    for cols in col_tiles:
        r.hidden_grad[:, cols] = norm_grad(own_rows, cols)
    mate_chunks = [slice(row_count + j * chunk_rows, row_count + (j + 1) * chunk_rows) for j in range(2)]
    norm_copies = []
    for j, rows in enumerate(mate_chunks):
        arrived([hidden_copies[j]])
        forward(rows, own_tiles + far_tiles)
        backward(rows, own_tiles + far_tiles)
        out_rows = slice(j * chunk_rows, (j + 1) * chunk_rows)
        for cols in col_tiles:
            r.x[out_rows, cols] = norm_grad(rows, cols).astype(bf16)
        norm_copies.append(links.send(r.x.at[out_rows, :], r.norm_in.at[out_rows, :], "mate"))
        product_core.append(links.send(r.product.at[rows, units_all], r.product_in.at[rows, :], "core"))
        for i, (ref, target) in enumerate(((r.first_act, r.first_in), (r.second_act, r.second_in))):
            grad_core[i].append(links.send(ref.at[rows, units_all], target.at[rows, :], "core"))
    split_transpose(
        r.hidden_low.at[row_count:, :], r.hidden_t, r.hidden_give, slice(row_count, 2 * row_count)
    )
    hidden_core = links.send(r.hidden_give, r.hidden_in, "core")

    def weight_grad(target, left, left_in, right, right_in):
        size = right.shape[1]
        for start in range(0, size, 256):
            cols = slice(start, min(start + 256, size))
            total = dot_plain(left[...], right[:, cols]) + dot_plain(left_in[...], right_in[:, cols])
            target[:, cols] = total.astype(bf16)

    arrived([last_core] + product_core)
    weight_grad(r.third_sum, r.last_t, r.last_in, r.product.at[:, units_all], r.product_in)
    chain_third = Chain(links, place, r.third_sum, r.third_half, r.third_quarter, 768)
    chain_third.start()
    mate_rows = slice(row_count, 2 * row_count)
    for cols in col_tiles:
        r.x[mate_rows, cols] = mix(mate_rows, cols).astype(bf16)
    for cols in col_tiles:
        r.mix[:, cols] = mix(own_rows, cols)
    arrived([hidden_core] + grad_core[0])
    links.left(product_core)
    first_sum = r.product.at[:, units_all]
    weight_grad(first_sum, r.hidden_t, r.hidden_in, r.first_act.at[:, units_all], r.first_in)
    chain_first = Chain(links, place, first_sum, r.first_half, r.first_quarter, 640)
    chain_first.start()

    attention_copies = []
    mate_block, mate_far = flipped(own, 0), 3 - own
    for j in range(2):
        rows = slice(j * chunk_rows, (j + 1) * chunk_rows)
        arrived([norm_copies[j]])
        incoming = r.hidden_grad[rows, :] + r.norm_in[rows, :].astype(f32)
        hidden_grad = r.upstream[rows, :].astype(f32) + norm_back(r.hidden[rows, :], incoming)
        r.hidden_grad[rows, :] = hidden_grad
        branch = (row_mask[rows] * hidden_grad).astype(bf16)
        r.branch[rows, :] = branch
        gated_grad = dot_right_t(branch, r.out[...])
        attention = r.attention_rows[rows, :].astype(f32)
        r.gate_grad[rows, :] = (gated_grad * normalize(attention)).astype(bf16)
        grad = norm_back(attention, gated_grad * r.gate_pre[rows, :]).astype(bf16)
        r.attention_grad[rows, :] = grad
        target_rows = part(member * 2 + j, chunk_rows)
        for i, (mine, theirs) in enumerate(((own, mate_block), (flipped(own, 1), mate_far))):
            target = r.grad_block.at[target_rows, i * head_width : (i + 1) * head_width]
            source = r.attention_grad.at[rows, part(theirs, head_width)]
            attention_copies.append(links.send(source, target, "mate"))
            target[...] = r.attention_grad[rows, part(mine, head_width)]
    branch_core = links.send(r.branch, r.branch_in, "core")
    gate_core = links.send(r.gate_grad, r.gate_grad_in, "core")
    split_transpose(r.gated, r.gated_t, r.gated_give, slice(0, row_count))
    gated_core = links.send(r.gated_give, r.gated_in, "core")
    chain_third.middle()
    arrived(grad_core[1])
    links.left(grad_core[0])
    second_sum = r.first_act.at[:, units_all]
    weight_grad(second_sum, r.hidden_t, r.hidden_in, r.second_act.at[:, units_all], r.second_in)
    chain_second = Chain(links, place, second_sum, r.second_half, r.second_quarter, 768)
    chain_second.start()

    arrived([branch_core, gated_core])
    out_sum = r.out.at[:SPAN, :]
    weight_grad(out_sum, r.gated_t, r.gated_in, r.branch, r.branch_in)
    chain_out = Chain(links, place, out_sum, r.out_half, r.out_quarter, 512)
    chain_out.start()
    arrived([gate_core, normed_core])
    gate_sum = r.out.at[SPAN:, :]
    lanes = part(member, row_count)
    weight_grad(gate_sum, r.normed_t.at[:, lanes], r.normed_in.at[:, lanes], r.gate_grad, r.gate_grad_in)
    chain_gate = Chain(links, place, gate_sum, r.gate_half, r.gate_quarter, 512)
    chain_gate.start()

    arrived(attention_copies)
    heads_all = 2 * block_heads
    for at in range(heads_all):
        cols = slice(at * HDIM, (at + 1) * HDIM)
        decayed = (r.queries[:, cols].astype(f32) * jnp.exp(-rate_of(at) * (places + 1.0))).astype(bf16)
        r.state_grad[at] = dot_left_t(decayed, r.grad_block[:, cols]).astype(bf16)
    near_heads, far_heads = pl.ds(0, block_heads), pl.ds(block_heads, block_heads)
    state_copies = [
        links.send(r.state_grad.at[near_heads], r.state_in.at[far_heads], "far"),
        links.send(r.state_grad.at[far_heads], r.state_in.at[near_heads], "far"),
    ]
    mix_copy = links.send(r.x.at[mate_rows, :], r.mix_in, "mate")
    chain_first.middle()

    def grad_cols(kind, at):
        start = (at // block_heads) * 3 * head_width + kind * head_width + (at % block_heads) * HDIM
        return slice(start, start + HDIM)

    for at in range(heads_all):
        rate = rate_of(at)
        cols = slice(at * HDIM, (at + 1) * HDIM)
        q, k, v, g = r.queries[:, cols], r.keys[:, cols], r.values[:, cols], r.grad_block[:, cols]
        decay = inner_decay(rate)
        weights = (dot_right_t(q, k) * decay).astype(bf16)
        score_grad = (dot_right_t(g, v) * decay).astype(bf16)
        dq = dot_plain(score_grad, k) + jnp.exp(-rate * (places + 1.0)) * dot_right_t(g, r.states[at])
        r.pre_grads[:, grad_cols(0, at)] = (dq * r.query_slope[:, cols].astype(f32)).astype(bf16)
        r.pre_grads[:, grad_cols(1, at)] = dot_left_t(score_grad, q).astype(bf16)
        r.pre_grads[:, grad_cols(2, at)] = dot_left_t(weights, g).astype(bf16)

    def to_far(chain, keep, give, target):
        total = chain.result().astype(bf16)
        size = keep.shape[1]
        keep[...] = total[:, :size]
        give[...] = total[:, size:]
        return links.send(give, target, "far")

    ends = [to_far(chain_third, r.third_keep, r.third_give, r.third_far)]
    arrived(state_copies)
    leaving = 1.0 - pair.astype(f32)
    for at in range(heads_all):
        rate = rate_of(at)
        cols = slice(at * HDIM, (at + 1) * HDIM)
        key_decay = leaving * jnp.exp(-rate * (SPAN - 1.0 - places))
        carried = r.state_in[at]
        dk = r.pre_grads[:, grad_cols(1, at)].astype(f32) + key_decay * dot_right_t(r.values[:, cols], carried)
        dv = r.pre_grads[:, grad_cols(2, at)].astype(f32) + key_decay * dot_plain(r.keys[:, cols], carried)
        r.pre_grads[:, grad_cols(1, at)] = (dk * r.key_slope[:, cols].astype(f32)).astype(bf16)
        r.pre_grads[:, grad_cols(2, at)] = (dv * mask).astype(bf16)
    pre_core = links.send(r.pre_grads, r.pre_in, "core")

    triple = 3 * head_width

    def head_terms(rows, cols):
        return dot_right_t(r.pre_grads[rows, :triple], r.heads[0, cols, :]) + dot_right_t(
            r.pre_grads[rows, triple:], r.heads[1, cols, :]
        )

    term_copies = []
    for start in range(0, width, 512):
        for cols in (slice(start, start + 256), slice(start + 256, start + 512)):
            r.terms[:, cols] = head_terms(part(1 - member, row_count), cols).astype(bf16)
        wide = slice(start, start + 512)
        term_copies.append(links.send(r.terms.at[:, wide], r.terms_in.at[:, wide], "mate"))
    chain_second.middle()
    arrived([pre_core])
    links.left(grad_core[1])
    weight_grad(r.second_act, r.normed_t, r.normed_in, r.pre_grads, r.pre_in)
    chain_heads = Chain(links, place, r.second_act, r.heads_half, r.heads_quarter, 768)
    chain_heads.start()
    ends.append(to_far(chain_first, r.first_keep, r.first_give, r.first_far))
    chain_out.middle()
    for cols in col_tiles:
        r.terms_own[:, cols] = head_terms(part(member, row_count), cols) + dot_right_t(r.gate_grad[...], r.gate[cols, :])
    chain_gate.middle()
    arrived([mix_copy])
    r.output[...] = (r.hidden[...] + row_mask * (r.mix[...] + r.mix_in[...].astype(f32))).astype(bf16)
    ends.append(to_far(chain_second, r.second_keep, r.second_give, r.second_far))
    arrived(term_copies)
    for j in range(2):
        rows = slice(j * chunk_rows, (j + 1) * chunk_rows)
        incoming = r.terms_own[rows, :] + r.terms_in[rows, :].astype(f32)
        grad = r.hidden_grad[rows, :] + norm_back(r.x_rows[rows, :].astype(f32), incoming)
        r.input_grad[rows, :] = grad.astype(bf16)

    def to_heads(chain, keep, target):
        total = chain.result().astype(bf16)
        slot = chain.chunk(chain.y, chain.x)
        slot[...] = total
        size = total.shape[0] // 4
        keep[...] = slot[part(own, size), :]
        return [
            links.send(slot.at[part(index, size), :], target.at[i], device)
            for i, (index, device) in enumerate(((mate_block, "mate"), (flipped(own, 1), "far"), (mate_far, "cross")))
        ]

    chain_heads.middle()
    ends += to_heads(chain_out, r.out_keep, r.out_far)
    ends += to_heads(chain_gate, r.gate_keep, r.gate_far)
    ends.append(to_far(chain_heads, r.heads_keep, r.heads_give, r.heads_far))
    arrived(ends)
    links.finish()


def finish_kernel(count, *refs):
    sources, refs = refs[:count], refs[count:]
    (
        output, input_grad, grad_query, grad_key, grad_value, grad_gate, grad_out, grad_first, grad_second, grad_third
    ) = refs[:10]
    held, sems = refs[10:-1], refs[-1]
    targets = [output, input_grad] + list(held)
    copies = [pltpu.make_async_copy(a, b, sems.at[i]) for i, (a, b) in enumerate(zip(sources, targets))]
    for copy in copies:
        copy.start()
    for copy in copies:
        copy.wait()
    pairs = [(held[i], held[i + 1]) for i in range(0, len(held), 2)]
    for (keep, far), target in zip(pairs[:3], (grad_third, grad_first, grad_second)):
        target[...] = (keep[...].astype(f32) + far[...].astype(f32)).T
    size = grad_query.shape[1]
    keep, far = pairs[3]
    for i, target in enumerate((grad_query, grad_key, grad_value)):
        cols = slice(i * size, (i + 1) * size)
        target[...] = keep[:, cols].astype(f32) + far[:, cols].astype(f32)
    for (keep, far), target in zip(pairs[4:], (grad_gate, grad_out)):
        total = keep[...].astype(f32)
        for i in range(3):
            total = total + far[i].astype(f32)
        target[...] = total


def fused_shards(
    layer_input, w_query, w_key, w_value, w_gate, w_out, w_first, w_second, w_third,
    decay_rates, seq_lengths, cotangent,
):
    group_rows, width = layer_input.shape
    row_count = cotangent.shape[0]
    heads = decay_rates.shape[0]
    head_width = w_query.shape[1]
    units = w_third.shape[0]
    shape = jax.ShapeDtypeStruct
    share = width // 8
    both = 2 * head_width
    triple = 3 * head_width
    inputs = dict(
        lengths=seq_lengths, decay_rates=decay_rates, layer_input=layer_input, w_query=w_query, w_key=w_key, w_value=w_value,
        w_gate=w_gate, w_out=w_out, w_first=w_first.T, w_second=w_second.T, w_third=w_third, cotangent=cotangent,
    )
    rows_shape = shape((row_count, width), bf16)
    ffn_shape = shape((share, units), bf16)
    head_shape = shape((share, triple), bf16)
    dense_shape = shape((share // 4, width), bf16)
    dense_far = shape((3, share // 4, width), bf16)
    outputs = dict(
        output=rows_shape, input_grad=rows_shape,
        third_keep=ffn_shape, third_far=ffn_shape, first_keep=ffn_shape, first_far=ffn_shape,
        second_keep=ffn_shape, second_far=ffn_shape, heads_keep=head_shape, heads_far=head_shape,
        gate_keep=dense_shape, gate_far=dense_far, out_keep=dense_shape, out_far=dense_far,
    )
    low = lambda *dims: pltpu.VMEM(dims, bf16)
    wide = lambda *dims: pltpu.VMEM(dims, f32)
    half = width // 2
    scratch = dict(
        x=low(group_rows, width), normed=low(group_rows, width),
        heads=low(2, width, triple), gate=low(width, width), out=low(width, width),
        first=low(2 * units, width), second=low(2 * units, width), third=low(2 * units, width),
        upstream=low(row_count, width), rates=wide(8, 128), rates_far=wide(8, 128),
        queries=low(SPAN, both), keys=low(SPAN, both), values=low(SPAN, both),
        query_slope=low(SPAN, both), key_slope=low(SPAN, both), states=low(2 * heads, HDIM, HDIM),
        attention=low(SPAN, both), attention_rows=low(row_count, width), gate_pre=wide(row_count, width),
        hidden=wide(row_count, width),
        hidden_low=low(SPAN, width), last=low(SPAN, width),
        first_act=low(SPAN, 2 * units), second_act=low(SPAN, 2 * triple), product=low(SPAN, 2 * units),
        hidden_grad=wide(row_count, width), mix=wide(row_count, width), norm_in=low(row_count, width),
        mix_in=low(row_count, width), grad_block=low(SPAN, both),
        state_grad=low(2 * heads, HDIM, HDIM), state_in=low(2 * heads, HDIM, HDIM),
        pre_grads=low(SPAN, 2 * triple), terms_in=low(row_count, width),
        terms_own=wide(row_count, width),
        normed_t=low(half, SPAN), normed_give=low(half, SPAN), normed_in=low(half, SPAN),
        last_t=low(half, SPAN), last_give=low(half, SPAN), last_in=low(half, SPAN),
        hidden_t=low(half, SPAN), hidden_give=low(half, SPAN), hidden_in=low(half, SPAN),
        gated_t=low(half, row_count), gated_give=low(half, row_count), gated_in=low(half, row_count),
        product_in=low(SPAN, 2 * units), first_in=low(SPAN, 2 * units), second_in=low(SPAN, 2 * units),
        pre_in=low(SPAN, 2 * triple), branch_in=low(row_count, width), gate_grad_in=low(row_count, width),
        third_sum=low(half, 2 * units),
        third_half=low(2 * share, 2 * units), first_half=low(2 * share, 2 * units),
        second_half=low(2 * share, 2 * units), heads_half=low(2 * share, 2 * triple),
        gate_half=low(2 * share, width), out_half=low(2 * share, width),
        third_quarter=low(share, 2 * units), first_quarter=low(share, 2 * units),
        second_quarter=low(share, 2 * units), heads_quarter=low(share, 2 * triple),
        gate_quarter=low(share, width), out_quarter=low(share, width),
        third_give=low(share, units), first_give=low(share, units), second_give=low(share, units),
        heads_give=low(share, triple),
        local_sems=pltpu.SemaphoreType.DMA((16,)),
        send_sems=pltpu.SemaphoreType.DMA((144,)), recv_sems=pltpu.SemaphoreType.DMA((144,)),
    )
    results = pl.pallas_call(
        functools.partial(layer_kernel, list(inputs) + list(outputs) + list(scratch)),
        out_shape=list(outputs.values()),
        in_specs=[smem(), smem()] + [pl.BlockSpec(memory_space=pl.ANY)] * (len(inputs) - 2),
        out_specs=[vmem()] * len(outputs),
        scratch_shapes=list(scratch.values()),
        compiler_params=pltpu.CompilerParams(
            collective_id=0, has_side_effects=True, vmem_limit_bytes=VMEM_ALL
        ),
        name="layer",
    )(*inputs.values())
    transposed_shape = shape((units, share), f32)
    finals = [rows_shape] * 2 + [shape((share, head_width), f32)] * 3 + [shape((share // 4, width), f32)] * 2
    finals += [transposed_shape] * 3
    place_any = pl.BlockSpec(memory_space=pl.ANY)
    results = pl.pallas_call(
        functools.partial(finish_kernel, len(results)),
        out_shape=finals,
        in_specs=[place_any] * len(results),
        out_specs=[place_any] * 2 + [vmem()] * 8,
        scratch_shapes=[pltpu.VMEM(a.shape, a.dtype) for a in results[2:]] + [pltpu.SemaphoreType.DMA((len(results),))],
        compiler_params=pltpu.CompilerParams(vmem_limit_bytes=VMEM_LIMIT),
        name="finish",
    )(*results)
    return (*results[:7], results[7].T, results[8].T, results[9])


def solution(mesh):
    placed = (
        P("dp", None),
        P(None, "head"),
        P(None, "head"),
        P(None, "head"),
        P(),
        P(),
        P(None, "head"),
        P(None, "head"),
        P("head", None),
        P("head"),
        P("dp"),
        P(("dp", "head"), None),
    )
    n_dp, n_head = mesh.shape["dp"], mesh.shape["head"]
    body = fused_shards if (n_dp, n_head) == (8, 4) else functools.partial(shards, n_dp, n_head)
    return jax.shard_map(
        body,
        mesh=mesh,
        in_specs=placed,
        out_specs=(
            P(("dp", "head"), None),
            P(("dp", "head"), None),
            P("dp", "head"),
            P("dp", "head"),
            P("dp", "head"),
            P(("dp", "head"), None),
            P(("dp", "head"), None),
            P("dp", "head"),
            P("dp", "head"),
            P("head", "dp"),
        ),
        check_vma=False,
    )
```

```python
import functools
import types

import jax
import jax.numpy as jnp
from jax import lax
from jax.experimental import pallas as pl
from jax.experimental.pallas import tpu as pltpu
from jax.sharding import PartitionSpec as P

SPAN = 512
HDIM = 128

epsilon = 1e-06
bf16 = jnp.bfloat16
f32 = jnp.float32
VMEM_LIMIT = 48 * 2**20
VMEM_ALL = 63 * 2**20


def inverse_rms(values):
    return lax.rsqrt(jnp.mean(values * values, axis=-1, keepdims=True) + epsilon)


def normalize(values):
    return values * inverse_rms(values)


def norm_back(values, incoming):
    inverse = inverse_rms(values)
    unit_rows = values * inverse
    return inverse * (incoming - unit_rows * jnp.mean(incoming * unit_rows, axis=-1, keepdims=True))


def dot_plain(left, right):
    return jnp.dot(left, right, preferred_element_type=f32)


def dot_right_t(left, right):
    return lax.dot_general(left, right, (((1,), (1,)), ((), ())), preferred_element_type=f32)


def dot_left_t(left, right):
    return lax.dot_general(left, right, (((0,), (0,)), ((), ())), preferred_element_type=f32)


def transposed(values):
    return values.T


def column(length):
    return lax.broadcasted_iota(jnp.int32, (length, 1), 0)


def inner_decay(rate):
    rows = lax.broadcasted_iota(jnp.int32, (SPAN, SPAN), 0)
    cols = lax.broadcasted_iota(jnp.int32, (SPAN, SPAN), 1)
    offset = rows - cols
    return jnp.where(offset >= 0, jnp.exp(-rate * jnp.maximum(offset, 0).astype(f32)), 0.0)


def attend_kernel(
    meta, rates, x, w_own_q, w_own_k, w_own_v, w_other,
    normed, attention, queries, keys, values, query_slope, key_slope, states,
):
    pair, length = meta[0], meta[1]
    start = pl.multiple_of(pair * SPAN, SPAN)
    rows = x.shape[0]
    head_width = w_own_q.shape[1]

    def norm_step(i, carry):
        place = pl.ds(pl.multiple_of(i * 128, 128), 128)
        normed[place, :] = normalize(x[place, :].astype(f32)).astype(bf16)
        return carry

    lax.fori_loop(0, rows // 128, norm_step, 0)
    block = normed[pl.ds(start, SPAN), :]
    mask = (start + column(SPAN) < length).astype(f32)
    early_mask = (column(SPAN) < length).astype(f32) * pair.astype(f32)
    early = normed[0:SPAN, :]
    places = column(SPAN).astype(f32)
    for part in range(2):
        if part == 0:
            wq, wk, wv = w_own_q[...], w_own_k[...], w_own_v[...]
        else:
            wq, wk, wv = (w_other[:, i * head_width : (i + 1) * head_width] for i in range(3))
        pre_query = dot_plain(block, wq)
        pre_key = dot_plain(block, wk)
        pre_value = dot_plain(block, wv)
        sigmoid_query = jax.nn.sigmoid(pre_query)
        sigmoid_key = jax.nn.sigmoid(pre_key)
        query = (pre_query * sigmoid_query).astype(bf16)
        key = (mask * (pre_key * sigmoid_key)).astype(bf16)
        value = (mask * pre_value).astype(bf16)
        wide = slice(part * head_width, (part + 1) * head_width)
        query_slope[:, wide] = (sigmoid_query * (1.0 + pre_query * (1.0 - sigmoid_query))).astype(bf16)
        key_slope[:, wide] = (mask * (sigmoid_key * (1.0 + pre_key * (1.0 - sigmoid_key)))).astype(bf16)
        queries[:, wide] = query
        keys[:, wide] = key
        values[:, wide] = value
        early_key = dot_plain(early, wk)
        early_key = early_mask * (early_key * jax.nn.sigmoid(early_key)).astype(bf16).astype(f32)
        early_value = (early_mask * dot_plain(early, wv)).astype(bf16)
        for head in range(head_width // HDIM):
            index = part * (head_width // HDIM) + head
            rate = rates[index]
            cols = slice(head * HDIM, (head + 1) * HDIM)
            q, k, v = query[:, cols], key[:, cols], value[:, cols]
            scores = dot_right_t(q, k)
            weights = (scores * inner_decay(rate)).astype(bf16)
            keyed = (early_key[:, cols] * jnp.exp(-rate * (SPAN - 1.0 - places))).astype(bf16)
            state = dot_left_t(keyed, early_value[:, cols])
            states[index] = state
            decayed = (q.astype(f32) * jnp.exp(-rate * (places + 1.0))).astype(bf16)
            out = dot_plain(weights, v) + dot_plain(decayed, state.astype(bf16))
            attention[:, index * HDIM : (index + 1) * HDIM] = out.astype(bf16)


def state_kernel(rates, queries, upstream, state_grad):
    places = column(SPAN).astype(f32)
    for index in range(state_grad.shape[0]):
        cols = slice(index * HDIM, (index + 1) * HDIM)
        decayed = (queries[:, cols].astype(f32) * jnp.exp(-rates[index] * (places + 1.0))).astype(bf16)
        state_grad[index] = dot_left_t(decayed, upstream[:, cols])


def attend_back_kernel(
    meta, rates, queries, keys, values, upstream, query_slope, key_slope, states, state_grad, pre_grads
):
    pair, length = meta[0], meta[1]
    mask = (pair * SPAN + column(SPAN) < length).astype(f32)
    places = column(SPAN).astype(f32)
    heads = states.shape[0]
    half = heads // 2
    for index in range(heads):
        rate = rates[index]
        cols = slice(index * HDIM, (index + 1) * HDIM)
        q, k, v, g = queries[:, cols], keys[:, cols], values[:, cols], upstream[:, cols]
        decay = inner_decay(rate)
        query_decay = jnp.exp(-rate * (places + 1.0))
        key_decay = jnp.exp(-rate * (SPAN - 1.0 - places))
        state = states[index].astype(bf16)
        carried = state_grad[index].astype(bf16)
        weights = (dot_right_t(q, k) * decay).astype(bf16)
        score_grad = (dot_right_t(g, v) * decay).astype(bf16)
        dq = dot_plain(score_grad, k) + query_decay * dot_right_t(g, state)
        dk = dot_left_t(score_grad, q) + key_decay * dot_right_t(v, carried)
        dv = dot_left_t(weights, g) + key_decay * dot_plain(k, carried)
        base = (index // half) * (3 * half * HDIM) + (index % half) * HDIM
        pre_grads[:, base : base + HDIM] = (dq * query_slope[:, cols].astype(f32)).astype(bf16)
        base += half * HDIM
        pre_grads[:, base : base + HDIM] = (dk * key_slope[:, cols].astype(f32)).astype(bf16)
        base += half * HDIM
        pre_grads[:, base : base + HDIM] = (dv * mask).astype(bf16)


def vmem():
    return pl.BlockSpec(memory_space=pltpu.VMEM)


def smem():
    return pl.BlockSpec(memory_space=pltpu.SMEM)


def local_call(body, name, out_shapes, args, scalars, flops):
    size = sum(int(a.size) * a.dtype.itemsize for a in list(args) + list(out_shapes))
    return pl.pallas_call(
        body,
        out_shape=out_shapes,
        in_specs=[smem()] * scalars + [vmem()] * (len(args) - scalars),
        out_specs=[vmem()] * len(out_shapes),
        compiler_params=pltpu.CompilerParams(vmem_limit_bytes=VMEM_LIMIT),
        cost_estimate=pl.CostEstimate(flops=flops, bytes_accessed=size, transcendentals=0),
        name=name,
    )(*args)


def shards(
    n_dp, n_head,
    layer_input, w_query, w_key, w_value, w_gate, w_out, w_first, w_second, w_third,
    decay_rates, seq_lengths, cotangent,
):
    group_rows, width = layer_input.shape
    row_count = cotangent.shape[0]
    heads = decay_rates.shape[0]
    head_width = w_query.shape[1]
    place = lax.axis_index("dp")
    own = lax.axis_index("head")
    member, pair = own % 2, own // 2
    bits = n_dp.bit_length() - 1
    length = seq_lengths[0]

    def to_mate(array, bit):
        return lax.ppermute(array, "head", [(i, i ^ bit) for i in range(n_head)])

    def across(array, bit):
        return lax.ppermute(array, "dp", [(i, i ^ (1 << bit)) for i in range(n_dp)])

    def gathered(weight, axis):
        size = weight.shape[axis] // n_dp
        share = lax.dynamic_slice_in_dim(weight, place * size, size, axis)
        return lax.all_gather(to_mate(share, 2), "dp", axis=axis, tiled=True)

    w_heads = jnp.concatenate([w_query, w_key, w_value], axis=1)
    w_heads_other = gathered(w_heads, 0)
    w_first_other = gathered(w_first, 0)
    w_second_other = gathered(w_second, 0)
    w_third_other = gathered(w_third, 1)
    rates = jnp.concatenate([decay_rates, to_mate(decay_rates, 2)])

    block_start = pair * SPAN
    row_start = own * row_count
    positions = jnp.arange(row_count, dtype=jnp.int32)[:, None]
    row_mask = (row_start + positions < length).astype(f32)
    upstream = cotangent.astype(f32)
    last_own = (row_mask * upstream).astype(bf16)
    last_mate = to_mate(last_own, 1)

    meta = jnp.stack([pair, length]).astype(jnp.int32)
    both = 2 * head_width
    shape = jax.ShapeDtypeStruct
    block_shape = shape((SPAN, both), bf16)
    normed, attention_block, queries, keys, values, query_slope, key_slope, states = local_call(
        attend_kernel, "attend",
        [shape(layer_input.shape, bf16)] + [block_shape] * 6 + [shape((2 * heads, HDIM, HDIM), f32)],
        [meta, rates, layer_input, w_query, w_key, w_value, w_heads_other], 2, 6 * 10**9,
    )

    def rows_of(array, index):
        return lax.dynamic_slice_in_dim(array, index * row_count, row_count, 0)

    def ordered(mine, other):
        even, odd = jnp.where(member == 0, mine, other), jnp.where(member == 0, other, mine)
        flip = lambda a: jnp.where(pair == 0, a, jnp.concatenate([a[:, head_width:], a[:, :head_width]], axis=1))
        even, odd = flip(even), flip(odd)
        return jnp.concatenate(
            [even[:, :head_width], odd[:, :head_width], even[:, head_width:], odd[:, head_width:]], axis=1
        )

    def pieces(array):
        cut = [array[:, i * head_width : (i + 1) * head_width] for i in range(4)]
        even, odd = jnp.concatenate([cut[0], cut[2]], axis=1), jnp.concatenate([cut[1], cut[3]], axis=1)
        flip = lambda a: jnp.where(pair == 0, a, jnp.concatenate([a[:, head_width:], a[:, :head_width]], axis=1))
        even, odd = flip(even), flip(odd)
        return jnp.where(member == 0, even, odd), jnp.where(member == 0, odd, even)

    received = to_mate(rows_of(attention_block, 1 - member), 1)
    attention = ordered(rows_of(attention_block, member), received).astype(f32)
    attention_norm = normalize(attention)
    rows_low = rows_of(normed, own)
    input_rows = rows_of(layer_input, own).astype(f32)
    gate_pre = dot_plain(rows_low, w_gate)
    gated = (attention_norm * gate_pre).astype(bf16)
    hidden = input_rows + row_mask * dot_plain(gated, w_out)
    hidden_low = normalize(hidden).astype(bf16)
    hidden_mate = to_mate(hidden_low, 1)

    w_first_all = jnp.concatenate([w_first, w_first_other], axis=1)
    w_second_all = jnp.concatenate([w_second, w_second_other], axis=1)
    w_third_all = jnp.concatenate([w_third, w_third_other], axis=0)

    def forward_rows(rows_in):
        first, second = dot_plain(rows_in, w_first_all), dot_plain(rows_in, w_second_all)
        return first.astype(bf16), second.astype(bf16), (first * second).astype(bf16)

    def backward_rows(last, first, second):
        product_grad = dot_right_t(last, w_third_all)
        first_grad = (product_grad * second.astype(f32)).astype(bf16)
        second_grad = (product_grad * first.astype(f32)).astype(bf16)
        return first_grad, second_grad, dot_right_t(first_grad, w_first_all) + dot_right_t(second_grad, w_second_all)

    first_mate, second_mate, product_mate = forward_rows(hidden_mate)
    first_grad_mate, second_grad_mate, norm_grad_mate = backward_rows(last_mate, first_mate, second_mate)
    norm_grad_in = to_mate(norm_grad_mate.astype(bf16), 1)
    mix_in = to_mate(dot_plain(product_mate, w_third_all).astype(bf16), 1)
    first_own, second_own, product_own = forward_rows(hidden_low)
    first_grad_own, second_grad_own, norm_grad_own = backward_rows(last_own, first_own, second_own)
    hidden_grad = upstream + norm_back(hidden, norm_grad_own + norm_grad_in.astype(f32))
    mixed = dot_plain(product_own, w_third_all) + mix_in.astype(f32)
    output = (hidden + row_mask * mixed).astype(bf16)

    branch_grad = (row_mask * hidden_grad).astype(bf16)
    gated_grad = dot_right_t(branch_grad, w_out)
    gate_grad = (gated_grad * attention_norm).astype(bf16)
    attention_grad = norm_back(attention, gated_grad * gate_pre).astype(bf16)
    mine, for_mate = pieces(attention_grad)
    from_mate = to_mate(for_mate, 1)
    grad_block = jnp.concatenate(
        [jnp.where(member == 0, mine, from_mate), jnp.where(member == 0, from_mate, mine)], axis=0
    )
    state_shape = shape((2 * heads, HDIM, HDIM), f32)
    (state_grad,) = local_call(
        state_kernel, "state_grad", [state_shape], [rates, queries, grad_block], 1, 10**8
    )
    swapped = jnp.concatenate([state_grad[heads:], state_grad[:heads]], axis=0)
    carried = lax.ppermute(swapped, "head", [(i, i - 2) for i in range(2, n_head)])
    (pre_grads,) = local_call(
        attend_back_kernel, "attend_back", [shape((SPAN, 3 * both), bf16)],
        [meta, rates, queries, keys, values, grad_block, query_slope, key_slope, states, carried], 2, 2 * 10**9,
    )
    head_terms = dot_right_t(pre_grads[:, : 3 * head_width], w_heads) + dot_right_t(
        pre_grads[:, 3 * head_width :], w_heads_other
    )
    head_terms = head_terms.astype(bf16)
    terms_in = to_mate(rows_of(head_terms, 1 - member), 1)
    input_norm_grad = (
        rows_of(head_terms, member).astype(f32) + terms_in.astype(f32) + dot_right_t(gate_grad, w_gate)
    )
    input_grad = (hidden_grad + norm_back(input_rows, input_norm_grad)).astype(bf16)

    def summed(left, right, order):
        left = left.reshape((left.shape[0],) + (2,) * bits + (width // n_dp,))

        def pick(array, axis, bit, which):
            side = (place // (1 << bit)) % 2
            return lax.dynamic_index_in_dim(array, side if which else 1 - side, axis, keepdims=False)

        left_axis = lambda bit, done: 1 + (bits - 1 - bit) - sum(1 for b in done if b > bit)
        first_bit = order[0]
        make = lambda which: dot_left_t(
            pick(left, left_axis(first_bit, []), first_bit, which).reshape(left.shape[0], width // 2), right
        ).astype(bf16)
        arrived = across(make(False), first_bit)
        total = (make(True).astype(f32) + arrived.astype(f32)).astype(bf16)
        total = total.reshape((2,) * (bits - 1) + (width // n_dp, right.shape[1]))
        done = [first_bit]
        for bit in order[1:]:
            axis = left_axis(bit, done) - 1
            arrived = across(pick(total, axis, bit, False), bit)
            total = (pick(total, axis, bit, True).astype(f32) + arrived.astype(f32)).astype(bf16)
            done.append(bit)
        return total

    def with_mate(total):
        size = total.shape[1] // 2
        return total[:, :size].astype(f32) + to_mate(total[:, size:], 2).astype(f32)

    def over_heads(total):
        for bit in (1, 2):
            cut = total.reshape((2, -1) + total.shape[1:]) if bit == 2 else total.reshape((2, 2, -1) + total.shape[1:])
            side = (own // bit) % 2
            axis = 0 if bit == 2 else 1
            arrived = to_mate(lax.dynamic_index_in_dim(cut, 1 - side, axis, keepdims=False), bit)
            total = lax.dynamic_index_in_dim(cut, side, axis, keepdims=False).astype(f32) + arrived.astype(f32)
            if bit == 1:
                total = total.astype(bf16).reshape((-1,) + total.shape[2:])
        return total

    up = list(range(bits))
    down = [0] + up[:0:-1]
    stack = lambda a, b: jnp.concatenate([a, b], axis=0)
    hidden_all = stack(hidden_low, hidden_mate)
    last_all = stack(last_own, last_mate)
    grad_third_t = with_mate(summed(last_all, stack(product_own, product_mate), up))
    grad_first = with_mate(summed(hidden_all, stack(first_grad_own, first_grad_mate), up))
    grad_second = with_mate(summed(hidden_all, stack(second_grad_own, second_grad_mate), down))
    grad_out = over_heads(summed(gated, branch_grad, down))
    grad_gate = over_heads(summed(rows_low, gate_grad, up))
    normed_block = lax.dynamic_slice_in_dim(normed, block_start, SPAN, 0)
    grad_heads = with_mate(summed(normed_block, pre_grads, down))
    return (
        output,
        input_grad,
        grad_heads[:, :head_width],
        grad_heads[:, head_width : 2 * head_width],
        grad_heads[:, 2 * head_width :],
        grad_gate,
        grad_out,
        grad_first,
        grad_second,
        grad_third_t.T,
    )


MESH = pl.DeviceIdType.MESH


def flipped(index, bit):
    return index + (1 << bit) * (1 - 2 * ((index // (1 << bit)) % 2))


def part(index, size):
    return pl.ds(pl.multiple_of(index * size, size), size)


class Links:
    def __init__(self, others, send_sems, recv_sems):
        self.others, self.send_sems, self.recv_sems, self.started = others, send_sems, recv_sems, []

    def send(self, source, target, device):
        index = len(self.started)
        copy = pltpu.make_async_remote_copy(
            src_ref=source,
            dst_ref=target,
            send_sem=self.send_sems.at[index],
            recv_sem=self.recv_sems.at[index],
            device_id=self.others[device],
            device_id_type=MESH,
        )
        copy.start()
        self.started.append(copy)
        copy.sent = False
        return copy

    def left(self, copies):
        for copy in copies:
            if not copy.sent:
                copy.wait_send()
                copy.sent = True

    def finish(self):
        self.left(self.started)


def arrived(copies):
    for copy in copies:
        copy.wait_recv()


class Gather:
    def __init__(self, links, place, pieces, halves):
        self.links, self.pieces, self.halves = links, pieces, halves
        self.places = [place, flipped(place, 1), flipped(place, 2), flipped(flipped(place, 1), 2)]
        self.to_core, self.near, self.crossing, self.fetched = [], {}, {}, {}

    def pass_on(self, piece, which, device):
        ref = self.pieces[piece](self.places[which])
        return self.links.send(ref, ref, device)

    def fetch(self, sources):
        for i, source in enumerate(sources):
            self.fetched[i] = self.links.send(source, self.pieces[i](self.places[0]), "far")

    def spread(self, piece=0):
        arrived([self.fetched[piece]])
        self.near[piece] = (self.pass_on(piece, 0, "x"), self.pass_on(piece, 0, "y"))
        self.to_core.append(self.pass_on(piece, 0, "core"))

    def cross(self, piece=0):
        crossing = []
        for i, (half, device) in enumerate(zip(self.halves, ("y", "x"))):
            arrived([self.near[piece][i]])
            ref = half(self.pieces[piece](self.places[1 + i]))
            crossing.append(self.links.send(ref, ref, device))
            self.to_core.append(self.pass_on(piece, 1 + i, "core"))
        self.crossing[piece] = crossing

    def last(self, piece=0):
        arrived(self.crossing[piece])
        self.to_core.append(self.pass_on(piece, 3, "core"))

    def done(self):
        arrived(self.to_core)


class Chain:
    def __init__(self, links, place, total, halves_in, quarter_in, cut, orders=("xy", "yx")):
        self.links, self.total, self.halves_in, self.quarter_in = links, total, halves_in, quarter_in
        size = total.shape[1]
        self.parts = [(slice(0, cut), orders[0]), (slice(cut, size), orders[1])]
        self.x, self.y = (place // 2) % 2, (place // 4) % 2
        self.rows = quarter_in.shape[0]
        self.waits = []

    def chunk(self, y, x, cols=slice(None)):
        return self.total.at[part(2 * y + x, self.rows), cols]

    def start(self):
        links, rows = self.links, self.rows
        for cols, order in self.parts:
            if order == "xy":
                self.waits.append([
                    links.send(self.chunk(y, 1 - self.x, cols), self.halves_in.at[y * rows : (y + 1) * rows, cols], "x")
                    for y in range(2)
                ])
            else:
                give = self.total.at[part(1 - self.y, 2 * rows), cols]
                self.waits.append([links.send(give, self.halves_in.at[:, cols], "y")])

    def add(self, place, arrived_part):
        place[...] = (place[...].astype(f32) + arrived_part.astype(f32)).astype(bf16)

    def middle(self):
        rows, x, y = self.rows, self.x, self.y
        keep, waits = [], []
        for (cols, order), before in zip(self.parts, self.waits):
            arrived(before)
            give, device, index = (
                (self.chunk(1 - y, x, cols), "y", y) if order == "xy" else (self.chunk(y, 1 - x, cols), "x", x)
            )
            self.add(give, self.halves_in[part(1 - index, rows), cols])
            waits.append([self.links.send(give, self.quarter_in.at[:, cols], device)])
            keep.append((cols, index))
        for cols, index in keep:
            self.add(self.chunk(y, x, cols), self.halves_in[part(index, rows), cols])
        self.waits = waits

    def result(self):
        for before in self.waits:
            arrived(before)
        return self.chunk(self.y, self.x)[...].astype(f32) + self.quarter_in[...].astype(f32)


def layer_kernel(names, *refs):
    r = types.SimpleNamespace(**dict(zip(names, refs)))
    place, own = lax.axis_index("dp"), lax.axis_index("head")
    pair, member, core = own // 2, own % 2, place % 2
    length = r.lengths[0]
    group_rows, width = r.layer_input.shape
    row_count = r.cotangent.shape[0]
    head_width = r.w_query.shape[1]
    block_heads = head_width // HDIM
    hidden_size = r.w_third.shape[0]
    share_size = width // 8
    chunk_rows = row_count // 2
    r.gated, r.x_rows = (r.x.at[i * row_count : (i + 1) * row_count, :] for i in (2, 3))
    r.branch, r.gate_grad, r.attention_grad, r.terms = (
        r.normed.at[i * row_count : (i + 1) * row_count, :] for i in range(4)
    )

    copies = []

    def load(source, target):
        copy = pltpu.make_async_copy(source, target, r.local_sems.at[len(copies)])
        copy.start()
        copies.append(copy)
        return copy

    load_cotangent = load(r.cotangent, r.upstream)
    load_x = load(r.layer_input, r.x)
    load_heads = [
        load(weight, r.heads.at[0, :, i * head_width : (i + 1) * head_width])
        for i, weight in enumerate((r.w_query, r.w_key, r.w_value))
    ]
    load_gate = load(r.w_gate, r.gate)
    load_out = load(r.w_out, r.out)
    load_first = load(r.w_first, r.first.at[:hidden_size, :])
    load_second = load(r.w_second, r.second.at[:hidden_size, :])
    load_third = load(r.w_third, r.third.at[:hidden_size, :])

    others = {
        "core": (flipped(place, 0), own),
        "x": (flipped(place, 1), own),
        "y": (flipped(place, 2), own),
        "mate": (place, flipped(own, 0)),
        "far": (place, flipped(own, 1)),
        "cross": (place, 3 - own),
    }
    barrier = pltpu.get_barrier_semaphore()
    for device in others.values():
        pl.semaphore_signal(barrier, inc=1, device_id=device, device_id_type=MESH)
    pl.semaphore_wait(barrier, len(others))
    links = Links(others, r.send_sems, r.recv_sems)

    head_piece = lambda j: lambda i: r.heads.at[1, part(i, share_size), j * head_width : (j + 1) * head_width]
    ffn_piece = lambda ref: lambda i: ref.at[hidden_size:, part(i, share_size)]
    row_halves = [lambda ref, j=j: ref.at[j * share_size // 2 : (j + 1) * share_size // 2, :] for j in range(2)]
    unit_halves = [lambda ref, j=j: ref.at[j * hidden_size // 2 : (j + 1) * hidden_size // 2, :] for j in range(2)]
    gather_heads = Gather(links, place, [head_piece(j) for j in (1, 2, 0)], row_halves)
    gather_first = Gather(links, place, [ffn_piece(r.first)], unit_halves)
    gather_second = Gather(links, place, [ffn_piece(r.second)], unit_halves)
    gather_third = Gather(links, place, [ffn_piece(r.third)], unit_halves)

    def fetch(gather, source):
        gather.fetch([source.at[:, part(place, share_size)]])

    gather_heads.fetch([weight.at[part(place, share_size), :] for weight in (r.w_key, r.w_value, r.w_query)])
    for i in range(block_heads):
        r.rates[i : i + 1, :] = jnp.full((1, 128), r.decay_rates[i], f32)
    rates_copy = links.send(r.rates, r.rates_far, "far")
    row_mask = (own * row_count + column(row_count) < length).astype(f32)
    load_cotangent.wait()
    r.last[:row_count, :] = (row_mask * r.upstream[...].astype(f32)).astype(bf16)
    last_copy = links.send(r.last.at[:row_count, :], r.last.at[row_count:, :], "mate")
    fetch(gather_first, r.w_first)

    load_x.wait()

    def norm_step(i, carry):
        where = part(i, 128)
        r.normed[where, :] = normalize(r.x[where, :].astype(f32)).astype(bf16)
        return carry

    lax.fori_loop(0, group_rows // 128, norm_step, 0)
    r.x_rows[...] = r.x[part(own, row_count), :]
    block_rows = part(pair, SPAN)
    mask = (pair * SPAN + column(SPAN) < length).astype(f32)
    early_mask = (column(SPAN) < length).astype(f32) * pair.astype(f32)
    places = column(SPAN).astype(f32)

    def project(index):
        wide = slice(index * head_width, (index + 1) * head_width)
        weights = [r.heads.at[index, :, i * head_width : (i + 1) * head_width] for i in range(3)]
        block = r.normed[block_rows, :]
        early = r.normed[0:SPAN, :]
        pre_query = dot_plain(block, weights[0][...])
        sigmoid = jax.nn.sigmoid(pre_query)
        r.queries[:, wide] = (pre_query * sigmoid).astype(bf16)
        r.query_slope[:, wide] = (sigmoid * (1.0 + pre_query * (1.0 - sigmoid))).astype(bf16)
        pre_key = dot_plain(block, weights[1][...])
        sigmoid = jax.nn.sigmoid(pre_key)
        r.keys[:, wide] = (mask * (pre_key * sigmoid)).astype(bf16)
        r.key_slope[:, wide] = (mask * (sigmoid * (1.0 + pre_key * (1.0 - sigmoid)))).astype(bf16)
        r.values[:, wide] = (mask * dot_plain(block, weights[2][...])).astype(bf16)
        early_key = dot_plain(early, weights[1][...])
        early_key = early_mask * (early_key * jax.nn.sigmoid(early_key)).astype(bf16).astype(f32)
        early_value = (early_mask * dot_plain(early, weights[2][...])).astype(bf16)
        return early_key, early_value

    def rate_of(index):
        ref = r.rates if index < block_heads else r.rates_far
        return ref[index % block_heads : index % block_heads + 1, 0:1]

    def attend(index, early_key, early_value):
        for head in range(block_heads):
            at = index * block_heads + head
            rate = rate_of(at)
            cols = slice(at * HDIM, (at + 1) * HDIM)
            early = slice(head * HDIM, (head + 1) * HDIM)
            q, k, v = r.queries[:, cols], r.keys[:, cols], r.values[:, cols]
            weights = (dot_right_t(q, k) * inner_decay(rate)).astype(bf16)
            keyed = (early_key[:, early] * jnp.exp(-rate * (SPAN - 1.0 - places))).astype(bf16)
            state = dot_left_t(keyed, early_value[:, early])
            r.states[at] = state.astype(bf16)
            decayed = (q.astype(f32) * jnp.exp(-rate * (places + 1.0))).astype(bf16)
            out = dot_plain(weights, v) + dot_plain(decayed, state.astype(bf16))
            r.attention[:, cols] = out.astype(bf16)
        wide = slice(index * head_width, (index + 1) * head_width)
        block = own if index == 0 else flipped(own, 1)
        target = r.attention_rows.at[:, part(block, head_width)]
        copy = links.send(r.attention.at[part(1 - member, row_count), wide], target, "mate")
        target[...] = r.attention[part(member, row_count), wide]
        return copy

    def split_transpose(source, keep, give, columns):
        for e in range(4):
            rows = slice(e * share_size, (e + 1) * share_size)
            keep[rows, columns] = transposed(source[:, part(2 * e + core, share_size)])
            give[rows, columns] = transposed(source[:, part(2 * e + 1 - core, share_size)])

    for copy in load_heads:
        copy.wait()
    gather_heads.spread(0)
    early = project(0)
    gather_heads.spread(1)
    gather_heads.spread(2)
    gather_heads.cross(0)
    attention_own = attend(0, *early)
    fetch(gather_second, r.w_second)
    gather_heads.cross(1)
    gather_heads.cross(2)
    gather_heads.last(0)
    split_transpose(r.normed.at[block_rows, :], r.normed_t, r.normed_give, slice(0, SPAN))
    normed_core = links.send(r.normed_give, r.normed_in, "core")
    gather_heads.last(1)
    gather_heads.last(2)
    load_gate.wait()
    r.gate_pre[...] = dot_plain(r.normed[part(own, row_count), :], r.gate[...])
    gather_heads.done()
    rates_copy.wait_recv()
    early = project(1)
    gather_first.spread()
    attention_far = attend(1, *early)
    fetch(gather_third, r.w_third)
    split_transpose(r.last.at[:row_count, :], r.last_t, r.last_give, slice(0, row_count))
    gather_first.cross()
    gather_second.spread()
    load_out.wait()
    gather_first.last()
    arrived([attention_own, attention_far])

    hidden_copies = []
    for j in range(2):
        rows = slice(j * chunk_rows, (j + 1) * chunk_rows)
        gated = (normalize(r.attention_rows[rows, :].astype(f32)) * r.gate_pre[rows, :]).astype(bf16)
        r.gated[rows, :] = gated
        hidden = r.x_rows[rows, :].astype(f32) + row_mask[rows] * dot_plain(gated, r.out[...])
        r.hidden[rows, :] = hidden
        r.hidden_low[rows, :] = normalize(hidden).astype(bf16)
        target = slice(row_count + j * chunk_rows, row_count + (j + 1) * chunk_rows)
        hidden_copies.append(links.send(r.hidden_low.at[rows, :], r.hidden_low.at[target, :], "mate"))
        if j == 0:
            gather_second.cross()

    own_tiles = [(0, 256), (256, 256), (512, 128)]
    far_tiles = [(640, 256), (896, 256), (1152, 256)]

    def forward(rows, tiles):
        for start, size in tiles:
            units = slice(start, start + size)
            first = dot_right_t(r.hidden_low[rows, :], r.first[units, :])
            second = dot_right_t(r.hidden_low[rows, :], r.second[units, :])
            r.first_act[rows, units] = first.astype(bf16)
            r.second_act[rows, units] = second.astype(bf16)
            r.product[rows, units] = (first * second).astype(bf16)

    def backward(rows, tiles):
        for start, size in tiles:
            units = slice(start, start + size)
            product_grad = dot_right_t(r.last[rows, :], r.third[units, :])
            first_grad = product_grad * r.second_act[rows, units].astype(f32)
            second_grad = product_grad * r.first_act[rows, units].astype(f32)
            r.first_act[rows, units] = first_grad.astype(bf16)
            r.second_act[rows, units] = second_grad.astype(bf16)

    units_all = slice(0, 2 * hidden_size)
    col_tiles = [slice(i, i + 256) for i in range(0, width, 256)]

    def norm_grad(rows, cols):
        return dot_plain(r.first_act[rows, units_all], r.first[:, cols]) + dot_plain(
            r.second_act[rows, units_all], r.second[:, cols]
        )

    def mix(rows, cols):
        return dot_plain(r.product[rows, units_all], r.third[:, cols])

    own_rows = slice(0, row_count)
    for copy in (load_first, load_second, load_third):
        copy.wait()
    forward(own_rows, own_tiles)
    backward(own_rows, own_tiles)
    gather_second.last()
    split_transpose(r.hidden_low.at[:row_count, :], r.hidden_t, r.hidden_give, slice(0, row_count))
    gather_third.spread()
    last_copy.wait_recv()
    split_transpose(r.last.at[row_count:, :], r.last_t, r.last_give, slice(row_count, 2 * row_count))
    last_core = links.send(r.last_give, r.last_in, "core")
    gather_first.done()
    gather_second.done()
    forward(own_rows, far_tiles)
    product_core = [links.send(r.product.at[own_rows, units_all], r.product_in.at[own_rows, :], "core")]
    gather_third.cross()
    gather_third.last()
    gather_third.done()
    backward(own_rows, far_tiles)
    grad_core = [
        [links.send(ref.at[own_rows, units_all], target.at[own_rows, :], "core")]
        for ref, target in ((r.first_act, r.first_in), (r.second_act, r.second_in))
    ]
    for cols in col_tiles:
        r.hidden_grad[:, cols] = norm_grad(own_rows, cols)
    mate_chunks = [slice(row_count + j * chunk_rows, row_count + (j + 1) * chunk_rows) for j in range(2)]
    norm_copies = []
    for j, rows in enumerate(mate_chunks):
        arrived([hidden_copies[j]])
        forward(rows, own_tiles + far_tiles)
        backward(rows, own_tiles + far_tiles)
        out_rows = slice(j * chunk_rows, (j + 1) * chunk_rows)
        for cols in col_tiles:
            r.x[out_rows, cols] = norm_grad(rows, cols).astype(bf16)
        norm_copies.append(links.send(r.x.at[out_rows, :], r.norm_in.at[out_rows, :], "mate"))
        product_core.append(links.send(r.product.at[rows, units_all], r.product_in.at[rows, :], "core"))
        for i, (ref, target) in enumerate(((r.first_act, r.first_in), (r.second_act, r.second_in))):
            grad_core[i].append(links.send(ref.at[rows, units_all], target.at[rows, :], "core"))
    split_transpose(
        r.hidden_low.at[row_count:, :], r.hidden_t, r.hidden_give, slice(row_count, 2 * row_count)
    )
    hidden_core = links.send(r.hidden_give, r.hidden_in, "core")

    def weight_grad(target, left, left_in, right, right_in):
        size = right.shape[1]
        for start in range(0, size, 256):
            cols = slice(start, min(start + 256, size))
            total = dot_plain(left[...], right[:, cols]) + dot_plain(left_in[...], right_in[:, cols])
            target[:, cols] = total.astype(bf16)

    arrived([last_core] + product_core)
    weight_grad(r.third_sum, r.last_t, r.last_in, r.product.at[:, units_all], r.product_in)
    chain_third = Chain(links, place, r.third_sum, r.third_half, r.third_quarter, 768)
    chain_third.start()
    mate_rows = slice(row_count, 2 * row_count)
    for cols in col_tiles:
        r.x[mate_rows, cols] = mix(mate_rows, cols).astype(bf16)
    for cols in col_tiles:
        r.mix[:, cols] = mix(own_rows, cols)
    arrived([hidden_core] + grad_core[0])
    links.left(product_core)
    first_sum = r.product.at[:, units_all]
    weight_grad(first_sum, r.hidden_t, r.hidden_in, r.first_act.at[:, units_all], r.first_in)
    chain_first = Chain(links, place, first_sum, r.first_half, r.first_quarter, 640)
    chain_first.start()

    attention_copies = []
    mate_block, mate_far = flipped(own, 0), 3 - own
    for j in range(2):
        rows = slice(j * chunk_rows, (j + 1) * chunk_rows)
        arrived([norm_copies[j]])
        incoming = r.hidden_grad[rows, :] + r.norm_in[rows, :].astype(f32)
        hidden_grad = r.upstream[rows, :].astype(f32) + norm_back(r.hidden[rows, :], incoming)
        r.hidden_grad[rows, :] = hidden_grad
        branch = (row_mask[rows] * hidden_grad).astype(bf16)
        r.branch[rows, :] = branch
        gated_grad = dot_right_t(branch, r.out[...])
        attention = r.attention_rows[rows, :].astype(f32)
        r.gate_grad[rows, :] = (gated_grad * normalize(attention)).astype(bf16)
        grad = norm_back(attention, gated_grad * r.gate_pre[rows, :]).astype(bf16)
        r.attention_grad[rows, :] = grad
        target_rows = part(member * 2 + j, chunk_rows)
        for i, (mine, theirs) in enumerate(((own, mate_block), (flipped(own, 1), mate_far))):
            target = r.grad_block.at[target_rows, i * head_width : (i + 1) * head_width]
            source = r.attention_grad.at[rows, part(theirs, head_width)]
            attention_copies.append(links.send(source, target, "mate"))
            target[...] = r.attention_grad[rows, part(mine, head_width)]
    branch_core = links.send(r.branch, r.branch_in, "core")
    gate_core = links.send(r.gate_grad, r.gate_grad_in, "core")
    split_transpose(r.gated, r.gated_t, r.gated_give, slice(0, row_count))
    gated_core = links.send(r.gated_give, r.gated_in, "core")
    chain_third.middle()
    arrived(grad_core[1])
    links.left(grad_core[0])
    second_sum = r.first_act.at[:, units_all]
    weight_grad(second_sum, r.hidden_t, r.hidden_in, r.second_act.at[:, units_all], r.second_in)
    chain_second = Chain(links, place, second_sum, r.second_half, r.second_quarter, 768)
    chain_second.start()

    arrived(attention_copies)
    heads_all = 2 * block_heads
    for at in range(heads_all):
        cols = slice(at * HDIM, (at + 1) * HDIM)
        decayed = (r.queries[:, cols].astype(f32) * jnp.exp(-rate_of(at) * (places + 1.0))).astype(bf16)
        r.state_grad[at] = dot_left_t(decayed, r.grad_block[:, cols]).astype(bf16)
    near_heads, far_heads = pl.ds(0, block_heads), pl.ds(block_heads, block_heads)
    state_copies = [
        links.send(r.state_grad.at[near_heads], r.state_in.at[far_heads], "far"),
        links.send(r.state_grad.at[far_heads], r.state_in.at[near_heads], "far"),
    ]
    mix_copy = links.send(r.x.at[mate_rows, :], r.mix_in, "mate")
    chain_first.middle()

    def grad_cols(kind, at):
        start = (at // block_heads) * 3 * head_width + kind * head_width + (at % block_heads) * HDIM
        return slice(start, start + HDIM)

    for at in range(heads_all):
        rate = rate_of(at)
        cols = slice(at * HDIM, (at + 1) * HDIM)
        q, k, v, g = r.queries[:, cols], r.keys[:, cols], r.values[:, cols], r.grad_block[:, cols]
        decay = inner_decay(rate)
        weights = (dot_right_t(q, k) * decay).astype(bf16)
        score_grad = (dot_right_t(g, v) * decay).astype(bf16)
        dq = dot_plain(score_grad, k) + jnp.exp(-rate * (places + 1.0)) * dot_right_t(g, r.states[at])
        r.pre_grads[:, grad_cols(0, at)] = (dq * r.query_slope[:, cols].astype(f32)).astype(bf16)
        r.pre_grads[:, grad_cols(1, at)] = dot_left_t(score_grad, q).astype(bf16)
        r.pre_grads[:, grad_cols(2, at)] = dot_left_t(weights, g).astype(bf16)

    def to_far(chain, keep, give, target):
        total = chain.result().astype(bf16)
        size = keep.shape[1]
        keep[...] = total[:, :size]
        give[...] = total[:, size:]
        return links.send(give, target, "far")

    ends = [to_far(chain_third, r.third_keep, r.third_give, r.third_far)]
    arrived(state_copies)
    leaving = 1.0 - pair.astype(f32)
    for at in range(heads_all):
        rate = rate_of(at)
        cols = slice(at * HDIM, (at + 1) * HDIM)
        key_decay = leaving * jnp.exp(-rate * (SPAN - 1.0 - places))
        carried = r.state_in[at]
        dk = r.pre_grads[:, grad_cols(1, at)].astype(f32) + key_decay * dot_right_t(r.values[:, cols], carried)
        dv = r.pre_grads[:, grad_cols(2, at)].astype(f32) + key_decay * dot_plain(r.keys[:, cols], carried)
        r.pre_grads[:, grad_cols(1, at)] = (dk * r.key_slope[:, cols].astype(f32)).astype(bf16)
        r.pre_grads[:, grad_cols(2, at)] = (dv * mask).astype(bf16)
    pre_core = links.send(r.pre_grads, r.pre_in, "core")

    triple = 3 * head_width

    def head_terms(rows, cols):
        return dot_right_t(r.pre_grads[rows, :triple], r.heads[0, cols, :]) + dot_right_t(
            r.pre_grads[rows, triple:], r.heads[1, cols, :]
        )

    term_copies = []
    for start in range(0, width, 512):
        for cols in (slice(start, start + 256), slice(start + 256, start + 512)):
            r.terms[:, cols] = head_terms(part(1 - member, row_count), cols).astype(bf16)
        wide = slice(start, start + 512)
        term_copies.append(links.send(r.terms.at[:, wide], r.terms_in.at[:, wide], "mate"))
    arrived([pre_core, normed_core])
    links.left(grad_core[1])
    weight_grad(r.second_act, r.normed_t, r.normed_in, r.pre_grads, r.pre_in)
    chain_heads = Chain(links, place, r.second_act, r.heads_half, r.heads_quarter, 768)
    chain_heads.start()
    chain_second.middle()
    for cols in col_tiles:
        r.terms_own[:, cols] = head_terms(part(member, row_count), cols) + dot_right_t(r.gate_grad[...], r.gate[cols, :])
    ends.append(to_far(chain_first, r.first_keep, r.first_give, r.first_far))

    arrived([branch_core, gated_core])
    out_sum = r.out.at[:SPAN, :]
    weight_grad(out_sum, r.gated_t, r.gated_in, r.branch, r.branch_in)
    chain_out = Chain(links, place, out_sum, r.out_half, r.out_quarter, 512)
    chain_out.start()
    arrived([mix_copy])
    r.output[...] = (r.hidden[...] + row_mask * (r.mix[...] + r.mix_in[...].astype(f32))).astype(bf16)
    chain_heads.middle()
    arrived([gate_core])
    gate_sum = r.out.at[SPAN:, :]
    lanes = part(member, row_count)
    weight_grad(gate_sum, r.normed_t.at[:, lanes], r.normed_in.at[:, lanes], r.gate_grad, r.gate_grad_in)
    chain_gate = Chain(links, place, gate_sum, r.gate_half, r.gate_quarter, 512)
    chain_gate.start()
    arrived(term_copies)
    for j in range(2):
        rows = slice(j * chunk_rows, (j + 1) * chunk_rows)
        incoming = r.terms_own[rows, :] + r.terms_in[rows, :].astype(f32)
        grad = r.hidden_grad[rows, :] + norm_back(r.x_rows[rows, :].astype(f32), incoming)
        r.input_grad[rows, :] = grad.astype(bf16)
    ends.append(to_far(chain_second, r.second_keep, r.second_give, r.second_far))

    def to_heads(chain, keep, target):
        total = chain.result().astype(bf16)
        slot = chain.chunk(chain.y, chain.x)
        slot[...] = total
        size = total.shape[0] // 4
        keep[...] = slot[part(own, size), :]
        return [
            links.send(slot.at[part(index, size), :], target.at[i], device)
            for i, (index, device) in enumerate(((mate_block, "mate"), (flipped(own, 1), "far"), (mate_far, "cross")))
        ]

    chain_out.middle()
    ends.append(to_far(chain_heads, r.heads_keep, r.heads_give, r.heads_far))
    chain_gate.middle()
    ends += to_heads(chain_out, r.out_keep, r.out_far)
    ends += to_heads(chain_gate, r.gate_keep, r.gate_far)
    arrived(ends)
    links.finish()


def finish_kernel(count, *refs):
    sources, refs = refs[:count], refs[count:]
    (
        output, input_grad, grad_query, grad_key, grad_value, grad_gate, grad_out, grad_first, grad_second, grad_third
    ) = refs[:10]
    held, sems = refs[10:-1], refs[-1]
    targets = [output, input_grad] + list(held)
    copies = [pltpu.make_async_copy(a, b, sems.at[i]) for i, (a, b) in enumerate(zip(sources, targets))]
    for copy in copies:
        copy.start()
    for copy in copies:
        copy.wait()
    pairs = [(held[i], held[i + 1]) for i in range(0, len(held), 2)]
    for (keep, far), target in zip(pairs[:3], (grad_third, grad_first, grad_second)):
        target[...] = (keep[...].astype(f32) + far[...].astype(f32)).T
    size = grad_query.shape[1]
    keep, far = pairs[3]
    for i, target in enumerate((grad_query, grad_key, grad_value)):
        cols = slice(i * size, (i + 1) * size)
        target[...] = keep[:, cols].astype(f32) + far[:, cols].astype(f32)
    for (keep, far), target in zip(pairs[4:], (grad_gate, grad_out)):
        total = keep[...].astype(f32)
        for i in range(3):
            total = total + far[i].astype(f32)
        target[...] = total


def fused_shards(
    layer_input, w_query, w_key, w_value, w_gate, w_out, w_first, w_second, w_third,
    decay_rates, seq_lengths, cotangent,
):
    group_rows, width = layer_input.shape
    row_count = cotangent.shape[0]
    heads = decay_rates.shape[0]
    head_width = w_query.shape[1]
    units = w_third.shape[0]
    shape = jax.ShapeDtypeStruct
    share = width // 8
    both = 2 * head_width
    triple = 3 * head_width
    inputs = dict(
        lengths=seq_lengths, decay_rates=decay_rates, layer_input=layer_input, w_query=w_query, w_key=w_key, w_value=w_value,
        w_gate=w_gate, w_out=w_out, w_first=w_first.T, w_second=w_second.T, w_third=w_third, cotangent=cotangent,
    )
    rows_shape = shape((row_count, width), bf16)
    ffn_shape = shape((share, units), bf16)
    head_shape = shape((share, triple), bf16)
    dense_shape = shape((share // 4, width), bf16)
    dense_far = shape((3, share // 4, width), bf16)
    outputs = dict(
        output=rows_shape, input_grad=rows_shape,
        third_keep=ffn_shape, third_far=ffn_shape, first_keep=ffn_shape, first_far=ffn_shape,
        second_keep=ffn_shape, second_far=ffn_shape, heads_keep=head_shape, heads_far=head_shape,
        gate_keep=dense_shape, gate_far=dense_far, out_keep=dense_shape, out_far=dense_far,
    )
    low = lambda *dims: pltpu.VMEM(dims, bf16)
    wide = lambda *dims: pltpu.VMEM(dims, f32)
    half = width // 2
    scratch = dict(
        x=low(group_rows, width), normed=low(group_rows, width),
        heads=low(2, width, triple), gate=low(width, width), out=low(width, width),
        first=low(2 * units, width), second=low(2 * units, width), third=low(2 * units, width),
        upstream=low(row_count, width), rates=wide(8, 128), rates_far=wide(8, 128),
        queries=low(SPAN, both), keys=low(SPAN, both), values=low(SPAN, both),
        query_slope=low(SPAN, both), key_slope=low(SPAN, both), states=low(2 * heads, HDIM, HDIM),
        attention=low(SPAN, both), attention_rows=low(row_count, width), gate_pre=wide(row_count, width),
        hidden=wide(row_count, width),
        hidden_low=low(SPAN, width), last=low(SPAN, width),
        first_act=low(SPAN, 2 * units), second_act=low(SPAN, 2 * triple), product=low(SPAN, 2 * units),
        hidden_grad=wide(row_count, width), mix=wide(row_count, width), norm_in=low(row_count, width),
        mix_in=low(row_count, width), grad_block=low(SPAN, both),
        state_grad=low(2 * heads, HDIM, HDIM), state_in=low(2 * heads, HDIM, HDIM),
        pre_grads=low(SPAN, 2 * triple), terms_in=low(row_count, width),
        terms_own=wide(row_count, width),
        normed_t=low(half, SPAN), normed_give=low(half, SPAN), normed_in=low(half, SPAN),
        last_t=low(half, SPAN), last_give=low(half, SPAN), last_in=low(half, SPAN),
        hidden_t=low(half, SPAN), hidden_give=low(half, SPAN), hidden_in=low(half, SPAN),
        gated_t=low(half, row_count), gated_give=low(half, row_count), gated_in=low(half, row_count),
        product_in=low(SPAN, 2 * units), first_in=low(SPAN, 2 * units), second_in=low(SPAN, 2 * units),
        pre_in=low(SPAN, 2 * triple), branch_in=low(row_count, width), gate_grad_in=low(row_count, width),
        third_sum=low(half, 2 * units),
        third_half=low(2 * share, 2 * units), first_half=low(2 * share, 2 * units),
        second_half=low(2 * share, 2 * units), heads_half=low(2 * share, 2 * triple),
        gate_half=low(2 * share, width), out_half=low(2 * share, width),
        third_quarter=low(share, 2 * units), first_quarter=low(share, 2 * units),
        second_quarter=low(share, 2 * units), heads_quarter=low(share, 2 * triple),
        gate_quarter=low(share, width), out_quarter=low(share, width),
        third_give=low(share, units), first_give=low(share, units), second_give=low(share, units),
        heads_give=low(share, triple),
        local_sems=pltpu.SemaphoreType.DMA((16,)),
        send_sems=pltpu.SemaphoreType.DMA((144,)), recv_sems=pltpu.SemaphoreType.DMA((144,)),
    )
    results = pl.pallas_call(
        functools.partial(layer_kernel, list(inputs) + list(outputs) + list(scratch)),
        out_shape=list(outputs.values()),
        in_specs=[smem(), smem()] + [pl.BlockSpec(memory_space=pl.ANY)] * (len(inputs) - 2),
        out_specs=[vmem()] * len(outputs),
        scratch_shapes=list(scratch.values()),
        compiler_params=pltpu.CompilerParams(
            collective_id=0, has_side_effects=True, vmem_limit_bytes=VMEM_ALL
        ),
        name="layer",
    )(*inputs.values())
    transposed_shape = shape((units, share), f32)
    finals = [rows_shape] * 2 + [shape((share, head_width), f32)] * 3 + [shape((share // 4, width), f32)] * 2
    finals += [transposed_shape] * 3
    place_any = pl.BlockSpec(memory_space=pltpu.HBM)
    results = pl.pallas_call(
        functools.partial(finish_kernel, len(results)),
        out_shape=finals,
        in_specs=[place_any] * len(results),
        out_specs=[vmem()] * 10,
        scratch_shapes=[pltpu.VMEM(a.shape, a.dtype) for a in results[2:]] + [pltpu.SemaphoreType.DMA((len(results),))],
        compiler_params=pltpu.CompilerParams(vmem_limit_bytes=VMEM_ALL),
        name="finish",
    )(*results)
    return (*results[:7], results[7].T, results[8].T, results[9])


def solution(mesh):
    placed = (
        P("dp", None),
        P(None, "head"),
        P(None, "head"),
        P(None, "head"),
        P(),
        P(),
        P(None, "head"),
        P(None, "head"),
        P("head", None),
        P("head"),
        P("dp"),
        P(("dp", "head"), None),
    )
    n_dp, n_head = mesh.shape["dp"], mesh.shape["head"]
    body = fused_shards if (n_dp, n_head) == (8, 4) else functools.partial(shards, n_dp, n_head)
    return jax.shard_map(
        body,
        mesh=mesh,
        in_specs=placed,
        out_specs=(
            P(("dp", "head"), None),
            P(("dp", "head"), None),
            P("dp", "head"),
            P("dp", "head"),
            P("dp", "head"),
            P(("dp", "head"), None),
            P(("dp", "head"), None),
            P("dp", "head"),
            P("dp", "head"),
            P("head", "dp"),
        ),
        check_vma=False,
    )
```

```python
import functools
import types

import jax
import jax.numpy as jnp
from jax import lax
from jax.experimental import pallas as pl
from jax.experimental.pallas import tpu as pltpu
from jax.sharding import PartitionSpec as P

SPAN = 512
HDIM = 128

epsilon = 1e-06
bf16 = jnp.bfloat16
f32 = jnp.float32
VMEM_LIMIT = 48 * 2**20
VMEM_ALL = 63 * 2**20


def inverse_rms(values):
    return lax.rsqrt(jnp.mean(values * values, axis=-1, keepdims=True) + epsilon)


def normalize(values):
    return values * inverse_rms(values)


def norm_back(values, incoming):
    inverse = inverse_rms(values)
    unit_rows = values * inverse
    return inverse * (incoming - unit_rows * jnp.mean(incoming * unit_rows, axis=-1, keepdims=True))


def dot_plain(left, right):
    return jnp.dot(left, right, preferred_element_type=f32)


def dot_right_t(left, right):
    return lax.dot_general(left, right, (((1,), (1,)), ((), ())), preferred_element_type=f32)


def dot_left_t(left, right):
    return lax.dot_general(left, right, (((0,), (0,)), ((), ())), preferred_element_type=f32)


def transposed(values):
    return values.T


def column(length):
    return lax.broadcasted_iota(jnp.int32, (length, 1), 0)


def inner_decay(rate):
    rows = lax.broadcasted_iota(jnp.int32, (SPAN, SPAN), 0)
    cols = lax.broadcasted_iota(jnp.int32, (SPAN, SPAN), 1)
    offset = rows - cols
    return jnp.where(offset >= 0, jnp.exp(-rate * jnp.maximum(offset, 0).astype(f32)), 0.0)


def attend_kernel(
    meta, rates, x, w_own_q, w_own_k, w_own_v, w_other,
    normed, attention, queries, keys, values, query_slope, key_slope, states,
):
    pair, length = meta[0], meta[1]
    start = pl.multiple_of(pair * SPAN, SPAN)
    rows = x.shape[0]
    head_width = w_own_q.shape[1]

    def norm_step(i, carry):
        place = pl.ds(pl.multiple_of(i * 128, 128), 128)
        normed[place, :] = normalize(x[place, :].astype(f32)).astype(bf16)
        return carry

    lax.fori_loop(0, rows // 128, norm_step, 0)
    block = normed[pl.ds(start, SPAN), :]
    mask = (start + column(SPAN) < length).astype(f32)
    early_mask = (column(SPAN) < length).astype(f32) * pair.astype(f32)
    early = normed[0:SPAN, :]
    places = column(SPAN).astype(f32)
    for part in range(2):
        if part == 0:
            wq, wk, wv = w_own_q[...], w_own_k[...], w_own_v[...]
        else:
            wq, wk, wv = (w_other[:, i * head_width : (i + 1) * head_width] for i in range(3))
        pre_query = dot_plain(block, wq)
        pre_key = dot_plain(block, wk)
        pre_value = dot_plain(block, wv)
        sigmoid_query = jax.nn.sigmoid(pre_query)
        sigmoid_key = jax.nn.sigmoid(pre_key)
        query = (pre_query * sigmoid_query).astype(bf16)
        key = (mask * (pre_key * sigmoid_key)).astype(bf16)
        value = (mask * pre_value).astype(bf16)
        wide = slice(part * head_width, (part + 1) * head_width)
        query_slope[:, wide] = (sigmoid_query * (1.0 + pre_query * (1.0 - sigmoid_query))).astype(bf16)
        key_slope[:, wide] = (mask * (sigmoid_key * (1.0 + pre_key * (1.0 - sigmoid_key)))).astype(bf16)
        queries[:, wide] = query
        keys[:, wide] = key
        values[:, wide] = value
        early_key = dot_plain(early, wk)
        early_key = early_mask * (early_key * jax.nn.sigmoid(early_key)).astype(bf16).astype(f32)
        early_value = (early_mask * dot_plain(early, wv)).astype(bf16)
        for head in range(head_width // HDIM):
            index = part * (head_width // HDIM) + head
            rate = rates[index]
            cols = slice(head * HDIM, (head + 1) * HDIM)
            q, k, v = query[:, cols], key[:, cols], value[:, cols]
            scores = dot_right_t(q, k)
            weights = (scores * inner_decay(rate)).astype(bf16)
            keyed = (early_key[:, cols] * jnp.exp(-rate * (SPAN - 1.0 - places))).astype(bf16)
            state = dot_left_t(keyed, early_value[:, cols])
            states[index] = state
            decayed = (q.astype(f32) * jnp.exp(-rate * (places + 1.0))).astype(bf16)
            out = dot_plain(weights, v) + dot_plain(decayed, state.astype(bf16))
            attention[:, index * HDIM : (index + 1) * HDIM] = out.astype(bf16)


def state_kernel(rates, queries, upstream, state_grad):
    places = column(SPAN).astype(f32)
    for index in range(state_grad.shape[0]):
        cols = slice(index * HDIM, (index + 1) * HDIM)
        decayed = (queries[:, cols].astype(f32) * jnp.exp(-rates[index] * (places + 1.0))).astype(bf16)
        state_grad[index] = dot_left_t(decayed, upstream[:, cols])


def attend_back_kernel(
    meta, rates, queries, keys, values, upstream, query_slope, key_slope, states, state_grad, pre_grads
):
    pair, length = meta[0], meta[1]
    mask = (pair * SPAN + column(SPAN) < length).astype(f32)
    places = column(SPAN).astype(f32)
    heads = states.shape[0]
    half = heads // 2
    for index in range(heads):
        rate = rates[index]
        cols = slice(index * HDIM, (index + 1) * HDIM)
        q, k, v, g = queries[:, cols], keys[:, cols], values[:, cols], upstream[:, cols]
        decay = inner_decay(rate)
        query_decay = jnp.exp(-rate * (places + 1.0))
        key_decay = jnp.exp(-rate * (SPAN - 1.0 - places))
        state = states[index].astype(bf16)
        carried = state_grad[index].astype(bf16)
        weights = (dot_right_t(q, k) * decay).astype(bf16)
        score_grad = (dot_right_t(g, v) * decay).astype(bf16)
        dq = dot_plain(score_grad, k) + query_decay * dot_right_t(g, state)
        dk = dot_left_t(score_grad, q) + key_decay * dot_right_t(v, carried)
        dv = dot_left_t(weights, g) + key_decay * dot_plain(k, carried)
        base = (index // half) * (3 * half * HDIM) + (index % half) * HDIM
        pre_grads[:, base : base + HDIM] = (dq * query_slope[:, cols].astype(f32)).astype(bf16)
        base += half * HDIM
        pre_grads[:, base : base + HDIM] = (dk * key_slope[:, cols].astype(f32)).astype(bf16)
        base += half * HDIM
        pre_grads[:, base : base + HDIM] = (dv * mask).astype(bf16)


def vmem():
    return pl.BlockSpec(memory_space=pltpu.VMEM)


def smem():
    return pl.BlockSpec(memory_space=pltpu.SMEM)


def local_call(body, name, out_shapes, args, scalars, flops):
    size = sum(int(a.size) * a.dtype.itemsize for a in list(args) + list(out_shapes))
    return pl.pallas_call(
        body,
        out_shape=out_shapes,
        in_specs=[smem()] * scalars + [vmem()] * (len(args) - scalars),
        out_specs=[vmem()] * len(out_shapes),
        compiler_params=pltpu.CompilerParams(vmem_limit_bytes=VMEM_LIMIT),
        cost_estimate=pl.CostEstimate(flops=flops, bytes_accessed=size, transcendentals=0),
        name=name,
    )(*args)


def shards(
    n_dp, n_head,
    layer_input, w_query, w_key, w_value, w_gate, w_out, w_first, w_second, w_third,
    decay_rates, seq_lengths, cotangent,
):
    group_rows, width = layer_input.shape
    row_count = cotangent.shape[0]
    heads = decay_rates.shape[0]
    head_width = w_query.shape[1]
    place = lax.axis_index("dp")
    own = lax.axis_index("head")
    member, pair = own % 2, own // 2
    bits = n_dp.bit_length() - 1
    length = seq_lengths[0]

    def to_mate(array, bit):
        return lax.ppermute(array, "head", [(i, i ^ bit) for i in range(n_head)])

    def across(array, bit):
        return lax.ppermute(array, "dp", [(i, i ^ (1 << bit)) for i in range(n_dp)])

    def gathered(weight, axis):
        size = weight.shape[axis] // n_dp
        share = lax.dynamic_slice_in_dim(weight, place * size, size, axis)
        return lax.all_gather(to_mate(share, 2), "dp", axis=axis, tiled=True)

    w_heads = jnp.concatenate([w_query, w_key, w_value], axis=1)
    w_heads_other = gathered(w_heads, 0)
    w_first_other = gathered(w_first, 0)
    w_second_other = gathered(w_second, 0)
    w_third_other = gathered(w_third, 1)
    rates = jnp.concatenate([decay_rates, to_mate(decay_rates, 2)])

    block_start = pair * SPAN
    row_start = own * row_count
    positions = jnp.arange(row_count, dtype=jnp.int32)[:, None]
    row_mask = (row_start + positions < length).astype(f32)
    upstream = cotangent.astype(f32)
    last_own = (row_mask * upstream).astype(bf16)
    last_mate = to_mate(last_own, 1)

    meta = jnp.stack([pair, length]).astype(jnp.int32)
    both = 2 * head_width
    shape = jax.ShapeDtypeStruct
    block_shape = shape((SPAN, both), bf16)
    normed, attention_block, queries, keys, values, query_slope, key_slope, states = local_call(
        attend_kernel, "attend",
        [shape(layer_input.shape, bf16)] + [block_shape] * 6 + [shape((2 * heads, HDIM, HDIM), f32)],
        [meta, rates, layer_input, w_query, w_key, w_value, w_heads_other], 2, 6 * 10**9,
    )

    def rows_of(array, index):
        return lax.dynamic_slice_in_dim(array, index * row_count, row_count, 0)

    def ordered(mine, other):
        even, odd = jnp.where(member == 0, mine, other), jnp.where(member == 0, other, mine)
        flip = lambda a: jnp.where(pair == 0, a, jnp.concatenate([a[:, head_width:], a[:, :head_width]], axis=1))
        even, odd = flip(even), flip(odd)
        return jnp.concatenate(
            [even[:, :head_width], odd[:, :head_width], even[:, head_width:], odd[:, head_width:]], axis=1
        )

    def pieces(array):
        cut = [array[:, i * head_width : (i + 1) * head_width] for i in range(4)]
        even, odd = jnp.concatenate([cut[0], cut[2]], axis=1), jnp.concatenate([cut[1], cut[3]], axis=1)
        flip = lambda a: jnp.where(pair == 0, a, jnp.concatenate([a[:, head_width:], a[:, :head_width]], axis=1))
        even, odd = flip(even), flip(odd)
        return jnp.where(member == 0, even, odd), jnp.where(member == 0, odd, even)

    received = to_mate(rows_of(attention_block, 1 - member), 1)
    attention = ordered(rows_of(attention_block, member), received).astype(f32)
    attention_norm = normalize(attention)
    rows_low = rows_of(normed, own)
    input_rows = rows_of(layer_input, own).astype(f32)
    gate_pre = dot_plain(rows_low, w_gate)
    gated = (attention_norm * gate_pre).astype(bf16)
    hidden = input_rows + row_mask * dot_plain(gated, w_out)
    hidden_low = normalize(hidden).astype(bf16)
    hidden_mate = to_mate(hidden_low, 1)

    w_first_all = jnp.concatenate([w_first, w_first_other], axis=1)
    w_second_all = jnp.concatenate([w_second, w_second_other], axis=1)
    w_third_all = jnp.concatenate([w_third, w_third_other], axis=0)

    def forward_rows(rows_in):
        first, second = dot_plain(rows_in, w_first_all), dot_plain(rows_in, w_second_all)
        return first.astype(bf16), second.astype(bf16), (first * second).astype(bf16)

    def backward_rows(last, first, second):
        product_grad = dot_right_t(last, w_third_all)
        first_grad = (product_grad * second.astype(f32)).astype(bf16)
        second_grad = (product_grad * first.astype(f32)).astype(bf16)
        return first_grad, second_grad, dot_right_t(first_grad, w_first_all) + dot_right_t(second_grad, w_second_all)

    first_mate, second_mate, product_mate = forward_rows(hidden_mate)
    first_grad_mate, second_grad_mate, norm_grad_mate = backward_rows(last_mate, first_mate, second_mate)
    norm_grad_in = to_mate(norm_grad_mate.astype(bf16), 1)
    mix_in = to_mate(dot_plain(product_mate, w_third_all).astype(bf16), 1)
    first_own, second_own, product_own = forward_rows(hidden_low)
    first_grad_own, second_grad_own, norm_grad_own = backward_rows(last_own, first_own, second_own)
    hidden_grad = upstream + norm_back(hidden, norm_grad_own + norm_grad_in.astype(f32))
    mixed = dot_plain(product_own, w_third_all) + mix_in.astype(f32)
    output = (hidden + row_mask * mixed).astype(bf16)

    branch_grad = (row_mask * hidden_grad).astype(bf16)
    gated_grad = dot_right_t(branch_grad, w_out)
    gate_grad = (gated_grad * attention_norm).astype(bf16)
    attention_grad = norm_back(attention, gated_grad * gate_pre).astype(bf16)
    mine, for_mate = pieces(attention_grad)
    from_mate = to_mate(for_mate, 1)
    grad_block = jnp.concatenate(
        [jnp.where(member == 0, mine, from_mate), jnp.where(member == 0, from_mate, mine)], axis=0
    )
    state_shape = shape((2 * heads, HDIM, HDIM), f32)
    (state_grad,) = local_call(
        state_kernel, "state_grad", [state_shape], [rates, queries, grad_block], 1, 10**8
    )
    swapped = jnp.concatenate([state_grad[heads:], state_grad[:heads]], axis=0)
    carried = lax.ppermute(swapped, "head", [(i, i - 2) for i in range(2, n_head)])
    (pre_grads,) = local_call(
        attend_back_kernel, "attend_back", [shape((SPAN, 3 * both), bf16)],
        [meta, rates, queries, keys, values, grad_block, query_slope, key_slope, states, carried], 2, 2 * 10**9,
    )
    head_terms = dot_right_t(pre_grads[:, : 3 * head_width], w_heads) + dot_right_t(
        pre_grads[:, 3 * head_width :], w_heads_other
    )
    head_terms = head_terms.astype(bf16)
    terms_in = to_mate(rows_of(head_terms, 1 - member), 1)
    input_norm_grad = (
        rows_of(head_terms, member).astype(f32) + terms_in.astype(f32) + dot_right_t(gate_grad, w_gate)
    )
    input_grad = (hidden_grad + norm_back(input_rows, input_norm_grad)).astype(bf16)

    def summed(left, right, order):
        left = left.reshape((left.shape[0],) + (2,) * bits + (width // n_dp,))

        def pick(array, axis, bit, which):
            side = (place // (1 << bit)) % 2
            return lax.dynamic_index_in_dim(array, side if which else 1 - side, axis, keepdims=False)

        left_axis = lambda bit, done: 1 + (bits - 1 - bit) - sum(1 for b in done if b > bit)
        first_bit = order[0]
        make = lambda which: dot_left_t(
            pick(left, left_axis(first_bit, []), first_bit, which).reshape(left.shape[0], width // 2), right
        ).astype(bf16)
        arrived = across(make(False), first_bit)
        total = (make(True).astype(f32) + arrived.astype(f32)).astype(bf16)
        total = total.reshape((2,) * (bits - 1) + (width // n_dp, right.shape[1]))
        done = [first_bit]
        for bit in order[1:]:
            axis = left_axis(bit, done) - 1
            arrived = across(pick(total, axis, bit, False), bit)
            total = (pick(total, axis, bit, True).astype(f32) + arrived.astype(f32)).astype(bf16)
            done.append(bit)
        return total

    def with_mate(total):
        size = total.shape[1] // 2
        return total[:, :size].astype(f32) + to_mate(total[:, size:], 2).astype(f32)

    def over_heads(total):
        for bit in (1, 2):
            cut = total.reshape((2, -1) + total.shape[1:]) if bit == 2 else total.reshape((2, 2, -1) + total.shape[1:])
            side = (own // bit) % 2
            axis = 0 if bit == 2 else 1
            arrived = to_mate(lax.dynamic_index_in_dim(cut, 1 - side, axis, keepdims=False), bit)
            total = lax.dynamic_index_in_dim(cut, side, axis, keepdims=False).astype(f32) + arrived.astype(f32)
            if bit == 1:
                total = total.astype(bf16).reshape((-1,) + total.shape[2:])
        return total

    up = list(range(bits))
    down = [0] + up[:0:-1]
    stack = lambda a, b: jnp.concatenate([a, b], axis=0)
    hidden_all = stack(hidden_low, hidden_mate)
    last_all = stack(last_own, last_mate)
    grad_third_t = with_mate(summed(last_all, stack(product_own, product_mate), up))
    grad_first = with_mate(summed(hidden_all, stack(first_grad_own, first_grad_mate), up))
    grad_second = with_mate(summed(hidden_all, stack(second_grad_own, second_grad_mate), down))
    grad_out = over_heads(summed(gated, branch_grad, down))
    grad_gate = over_heads(summed(rows_low, gate_grad, up))
    normed_block = lax.dynamic_slice_in_dim(normed, block_start, SPAN, 0)
    grad_heads = with_mate(summed(normed_block, pre_grads, down))
    return (
        output,
        input_grad,
        grad_heads[:, :head_width],
        grad_heads[:, head_width : 2 * head_width],
        grad_heads[:, 2 * head_width :],
        grad_gate,
        grad_out,
        grad_first,
        grad_second,
        grad_third_t.T,
    )


MESH = pl.DeviceIdType.MESH


def flipped(index, bit):
    return index + (1 << bit) * (1 - 2 * ((index // (1 << bit)) % 2))


def part(index, size):
    return pl.ds(pl.multiple_of(index * size, size), size)


class Links:
    def __init__(self, others, send_sems, recv_sems):
        self.others, self.send_sems, self.recv_sems, self.started = others, send_sems, recv_sems, []

    def send(self, source, target, device):
        index = len(self.started)
        copy = pltpu.make_async_remote_copy(
            src_ref=source,
            dst_ref=target,
            send_sem=self.send_sems.at[index],
            recv_sem=self.recv_sems.at[index],
            device_id=self.others[device],
            device_id_type=MESH,
        )
        copy.start()
        self.started.append(copy)
        copy.sent = False
        return copy

    def left(self, copies):
        for copy in copies:
            if not copy.sent:
                copy.wait_send()
                copy.sent = True

    def finish(self):
        self.left(self.started)


def arrived(copies):
    for copy in copies:
        copy.wait_recv()


class Gather:
    def __init__(self, links, place, pieces, halves):
        self.links, self.pieces, self.halves = links, pieces, halves
        self.places = [place, flipped(place, 1), flipped(place, 2), flipped(flipped(place, 1), 2)]
        self.to_core, self.near, self.crossing, self.fetched = [], {}, {}, {}

    def pass_on(self, piece, which, device):
        ref = self.pieces[piece](self.places[which])
        return self.links.send(ref, ref, device)

    def fetch(self, sources):
        for i, source in enumerate(sources):
            self.fetched[i] = self.links.send(source, self.pieces[i](self.places[0]), "far")

    def spread(self, piece=0):
        arrived([self.fetched[piece]])
        self.near[piece] = (self.pass_on(piece, 0, "x"), self.pass_on(piece, 0, "y"))
        self.to_core.append(self.pass_on(piece, 0, "core"))

    def cross(self, piece=0):
        crossing = []
        for i, (half, device) in enumerate(zip(self.halves, ("y", "x"))):
            arrived([self.near[piece][i]])
            ref = half(self.pieces[piece](self.places[1 + i]))
            crossing.append(self.links.send(ref, ref, device))
            self.to_core.append(self.pass_on(piece, 1 + i, "core"))
        self.crossing[piece] = crossing

    def last(self, piece=0):
        arrived(self.crossing[piece])
        self.to_core.append(self.pass_on(piece, 3, "core"))

    def done(self):
        arrived(self.to_core)


class Chain:
    def __init__(self, links, place, total, halves_in, quarter_in, cut, orders=("xy", "yx")):
        self.links, self.total, self.halves_in, self.quarter_in = links, total, halves_in, quarter_in
        size = total.shape[1]
        self.parts = [(slice(0, cut), orders[0]), (slice(cut, size), orders[1])]
        self.x, self.y = (place // 2) % 2, (place // 4) % 2
        self.rows = quarter_in.shape[0]
        self.waits = []

    def chunk(self, y, x, cols=slice(None)):
        return self.total.at[part(2 * y + x, self.rows), cols]

    def start(self):
        links, rows = self.links, self.rows
        for cols, order in self.parts:
            if order == "xy":
                self.waits.append([
                    links.send(self.chunk(y, 1 - self.x, cols), self.halves_in.at[y * rows : (y + 1) * rows, cols], "x")
                    for y in range(2)
                ])
            else:
                give = self.total.at[part(1 - self.y, 2 * rows), cols]
                self.waits.append([links.send(give, self.halves_in.at[:, cols], "y")])

    def add(self, place, arrived_part):
        place[...] = (place[...].astype(f32) + arrived_part.astype(f32)).astype(bf16)

    def middle(self):
        rows, x, y = self.rows, self.x, self.y
        keep, waits = [], []
        for (cols, order), before in zip(self.parts, self.waits):
            arrived(before)
            give, device, index = (
                (self.chunk(1 - y, x, cols), "y", y) if order == "xy" else (self.chunk(y, 1 - x, cols), "x", x)
            )
            self.add(give, self.halves_in[part(1 - index, rows), cols])
            waits.append([self.links.send(give, self.quarter_in.at[:, cols], device)])
            keep.append((cols, index))
        for cols, index in keep:
            self.add(self.chunk(y, x, cols), self.halves_in[part(index, rows), cols])
        self.waits = waits

    def result(self):
        for before in self.waits:
            arrived(before)
        return self.chunk(self.y, self.x)[...].astype(f32) + self.quarter_in[...].astype(f32)


def layer_kernel(names, *refs):
    r = types.SimpleNamespace(**dict(zip(names, refs)))
    place, own = lax.axis_index("dp"), lax.axis_index("head")
    pair, member, core = own // 2, own % 2, place % 2
    length = r.lengths[0]
    group_rows, width = r.layer_input.shape
    row_count = r.cotangent.shape[0]
    head_width = r.w_query.shape[1]
    block_heads = head_width // HDIM
    hidden_size = r.w_third.shape[0]
    share_size = width // 8
    chunk_rows = row_count // 2
    r.gated, r.x_rows = (r.x.at[i * row_count : (i + 1) * row_count, :] for i in (2, 3))
    r.branch, r.gate_grad, r.attention_grad, r.terms = (
        r.normed.at[i * row_count : (i + 1) * row_count, :] for i in range(4)
    )

    copies = []

    def load(source, target):
        copy = pltpu.make_async_copy(source, target, r.local_sems.at[len(copies)])
        copy.start()
        copies.append(copy)
        return copy

    load_cotangent = load(r.cotangent, r.upstream)
    load_x = load(r.layer_input, r.x)
    load_heads = [
        load(weight, r.heads.at[0, :, i * head_width : (i + 1) * head_width])
        for i, weight in enumerate((r.w_query, r.w_key, r.w_value))
    ]
    load_gate = load(r.w_gate, r.gate)
    load_out = load(r.w_out, r.out)
    load_first = load(r.w_first, r.first.at[:hidden_size, :])
    load_second = load(r.w_second, r.second.at[:hidden_size, :])
    load_third = load(r.w_third, r.third.at[:hidden_size, :])

    others = {
        "core": (flipped(place, 0), own),
        "x": (flipped(place, 1), own),
        "y": (flipped(place, 2), own),
        "mate": (place, flipped(own, 0)),
        "far": (place, flipped(own, 1)),
        "cross": (place, 3 - own),
    }
    barrier = pltpu.get_barrier_semaphore()
    for device in others.values():
        pl.semaphore_signal(barrier, inc=1, device_id=device, device_id_type=MESH)
    pl.semaphore_wait(barrier, len(others))
    links = Links(others, r.send_sems, r.recv_sems)

    head_piece = lambda j: lambda i: r.heads.at[1, part(i, share_size), j * head_width : (j + 1) * head_width]
    ffn_piece = lambda ref: lambda i: ref.at[hidden_size:, part(i, share_size)]
    row_halves = [lambda ref, j=j: ref.at[j * share_size // 2 : (j + 1) * share_size // 2, :] for j in range(2)]
    unit_halves = [lambda ref, j=j: ref.at[j * hidden_size // 2 : (j + 1) * hidden_size // 2, :] for j in range(2)]
    gather_heads = Gather(links, place, [head_piece(j) for j in (1, 2, 0)], row_halves)
    gather_first = Gather(links, place, [ffn_piece(r.first)], unit_halves)
    gather_second = Gather(links, place, [ffn_piece(r.second)], unit_halves)
    gather_third = Gather(links, place, [ffn_piece(r.third)], unit_halves)

    def fetch(gather, source):
        gather.fetch([source.at[:, part(place, share_size)]])

    row_mask = (own * row_count + column(row_count) < length).astype(f32)
    load_cotangent.wait()
    r.last[:row_count, :] = (row_mask * r.upstream[...].astype(f32)).astype(bf16)

    def send_last(j):
        source = slice(j * chunk_rows, (j + 1) * chunk_rows)
        target = slice(row_count + j * chunk_rows, row_count + (j + 1) * chunk_rows)
        return links.send(r.last.at[source, :], r.last.at[target, :], "mate")

    last_copies = [send_last(0)]
    gather_heads.fetch([weight.at[part(place, share_size), :] for weight in (r.w_key, r.w_value, r.w_query)])
    for i in range(block_heads):
        r.rates[i : i + 1, :] = jnp.full((1, 128), r.decay_rates[i], f32)
    rates_copy = links.send(r.rates, r.rates_far, "far")
    fetch(gather_first, r.w_first)
    last_copies.append(send_last(1))

    load_x.wait()

    def norm_step(i, carry):
        where = part(i, 128)
        r.normed[where, :] = normalize(r.x[where, :].astype(f32)).astype(bf16)
        return carry

    lax.fori_loop(0, group_rows // 128, norm_step, 0)
    r.x_rows[...] = r.x[part(own, row_count), :]
    block_rows = part(pair, SPAN)
    mask = (pair * SPAN + column(SPAN) < length).astype(f32)
    early_mask = (column(SPAN) < length).astype(f32) * pair.astype(f32)
    places = column(SPAN).astype(f32)

    def project(index):
        wide = slice(index * head_width, (index + 1) * head_width)
        weights = [r.heads.at[index, :, i * head_width : (i + 1) * head_width] for i in range(3)]
        block = r.normed[block_rows, :]
        early = r.normed[0:SPAN, :]
        pre_query = dot_plain(block, weights[0][...])
        sigmoid = jax.nn.sigmoid(pre_query)
        r.queries[:, wide] = (pre_query * sigmoid).astype(bf16)
        r.query_slope[:, wide] = (sigmoid * (1.0 + pre_query * (1.0 - sigmoid))).astype(bf16)
        pre_key = dot_plain(block, weights[1][...])
        sigmoid = jax.nn.sigmoid(pre_key)
        r.keys[:, wide] = (mask * (pre_key * sigmoid)).astype(bf16)
        r.key_slope[:, wide] = (mask * (sigmoid * (1.0 + pre_key * (1.0 - sigmoid)))).astype(bf16)
        r.values[:, wide] = (mask * dot_plain(block, weights[2][...])).astype(bf16)
        early_key = dot_plain(early, weights[1][...])
        early_key = early_mask * (early_key * jax.nn.sigmoid(early_key)).astype(bf16).astype(f32)
        early_value = (early_mask * dot_plain(early, weights[2][...])).astype(bf16)
        return early_key, early_value

    def rate_of(index):
        ref = r.rates if index < block_heads else r.rates_far
        return ref[index % block_heads : index % block_heads + 1, 0:1]

    def attend(index, early_key, early_value):
        for head in range(block_heads):
            at = index * block_heads + head
            rate = rate_of(at)
            cols = slice(at * HDIM, (at + 1) * HDIM)
            early = slice(head * HDIM, (head + 1) * HDIM)
            q, k, v = r.queries[:, cols], r.keys[:, cols], r.values[:, cols]
            weights = (dot_right_t(q, k) * inner_decay(rate)).astype(bf16)
            keyed = (early_key[:, early] * jnp.exp(-rate * (SPAN - 1.0 - places))).astype(bf16)
            state = dot_left_t(keyed, early_value[:, early])
            r.states[at] = state.astype(bf16)
            decayed = (q.astype(f32) * jnp.exp(-rate * (places + 1.0))).astype(bf16)
            out = dot_plain(weights, v) + dot_plain(decayed, state.astype(bf16))
            r.attention[:, cols] = out.astype(bf16)
        wide = slice(index * head_width, (index + 1) * head_width)
        block = own if index == 0 else flipped(own, 1)
        target = r.attention_rows.at[:, part(block, head_width)]
        copy = links.send(r.attention.at[part(1 - member, row_count), wide], target, "mate")
        target[...] = r.attention[part(member, row_count), wide]
        return copy

    def split_transpose(source, keep, give, columns):
        for e in range(4):
            rows = slice(e * share_size, (e + 1) * share_size)
            keep[rows, columns] = transposed(source[:, part(2 * e + core, share_size)])
            give[rows, columns] = transposed(source[:, part(2 * e + 1 - core, share_size)])

    for copy in load_heads:
        copy.wait()
    gather_heads.spread(0)
    early = project(0)
    gather_heads.spread(1)
    gather_heads.spread(2)
    gather_heads.cross(0)
    attention_own = attend(0, *early)
    fetch(gather_second, r.w_second)
    gather_heads.cross(1)
    gather_heads.cross(2)
    gather_heads.last(0)
    split_transpose(r.normed.at[block_rows, :], r.normed_t, r.normed_give, slice(0, SPAN))
    normed_core = links.send(r.normed_give, r.normed_in, "core")
    gather_heads.last(1)
    gather_heads.last(2)
    gather_first.spread()
    load_gate.wait()
    r.gate_pre[...] = dot_plain(r.normed[part(own, row_count), :], r.gate[...])
    gather_heads.done()
    rates_copy.wait_recv()
    early = project(1)
    gather_first.cross()
    attention_far = attend(1, *early)
    fetch(gather_third, r.w_third)
    split_transpose(r.last.at[:row_count, :], r.last_t, r.last_give, slice(0, row_count))
    gather_first.last()
    arrived(last_copies)
    split_transpose(r.last.at[row_count:, :], r.last_t, r.last_give, slice(row_count, 2 * row_count))
    last_core = links.send(r.last_give, r.last_in, "core")
    gather_second.spread()
    load_out.wait()
    arrived([attention_own, attention_far])

    hidden_copies = []
    for j in range(2):
        rows = slice(j * chunk_rows, (j + 1) * chunk_rows)
        gated = (normalize(r.attention_rows[rows, :].astype(f32)) * r.gate_pre[rows, :]).astype(bf16)
        r.gated[rows, :] = gated
        hidden = r.x_rows[rows, :].astype(f32) + row_mask[rows] * dot_plain(gated, r.out[...])
        r.hidden[rows, :] = hidden
        r.hidden_low[rows, :] = normalize(hidden).astype(bf16)
        target = slice(row_count + j * chunk_rows, row_count + (j + 1) * chunk_rows)
        hidden_copies.append(links.send(r.hidden_low.at[rows, :], r.hidden_low.at[target, :], "mate"))
        if j == 0:
            gather_second.cross()

    own_tiles = [(0, 256), (256, 256), (512, 128)]
    far_tiles = [(640, 256), (896, 256), (1152, 256)]

    def forward(rows, tiles):
        for start, size in tiles:
            units = slice(start, start + size)
            first = dot_right_t(r.hidden_low[rows, :], r.first[units, :])
            second = dot_right_t(r.hidden_low[rows, :], r.second[units, :])
            r.first_act[rows, units] = first.astype(bf16)
            r.second_act[rows, units] = second.astype(bf16)
            r.product[rows, units] = (first * second).astype(bf16)

    def backward(rows, tiles):
        for start, size in tiles:
            units = slice(start, start + size)
            product_grad = dot_right_t(r.last[rows, :], r.third[units, :])
            first_grad = product_grad * r.second_act[rows, units].astype(f32)
            second_grad = product_grad * r.first_act[rows, units].astype(f32)
            r.first_act[rows, units] = first_grad.astype(bf16)
            r.second_act[rows, units] = second_grad.astype(bf16)

    units_all = slice(0, 2 * hidden_size)
    col_tiles = [slice(i, i + 256) for i in range(0, width, 256)]

    def norm_grad(rows, cols):
        return dot_plain(r.first_act[rows, units_all], r.first[:, cols]) + dot_plain(
            r.second_act[rows, units_all], r.second[:, cols]
        )

    def mix(rows, cols):
        return dot_plain(r.product[rows, units_all], r.third[:, cols])

    own_rows = slice(0, row_count)
    for copy in (load_first, load_second, load_third):
        copy.wait()
    mate_chunks = [slice(row_count + j * chunk_rows, row_count + (j + 1) * chunk_rows) for j in range(2)]
    mate_rows = slice(row_count, 2 * row_count)

    def give_core(source, target, rows):
        return links.send(source.at[rows, units_all], target.at[rows, :], "core")

    def weight_grad(target, left, left_in, right, right_in):
        size = right.shape[1]
        for start in range(0, size, 256):
            cols = slice(start, min(start + 256, size))
            total = dot_plain(left[...], right[:, cols]) + dot_plain(left_in[...], right_in[:, cols])
            target[:, cols] = total.astype(bf16)

    forward(own_rows, own_tiles)
    gather_second.last()
    split_transpose(r.hidden_low.at[own_rows, :], r.hidden_t, r.hidden_give, own_rows)
    gather_third.spread()
    gather_first.done()
    gather_second.done()
    forward(own_rows, far_tiles)
    product_core = [give_core(r.product, r.product_in, own_rows)]
    gather_third.cross()
    arrived(hidden_copies[:1])
    forward(mate_chunks[0], own_tiles + far_tiles)
    gather_third.last()
    backward(own_rows, own_tiles)
    arrived(hidden_copies[1:])
    forward(mate_chunks[1], own_tiles + far_tiles)
    product_core.append(give_core(r.product, r.product_in, mate_rows))
    gather_third.done()
    norm_copies = []

    def back_mate(j):
        rows, out_rows = mate_chunks[j], slice(j * chunk_rows, (j + 1) * chunk_rows)
        backward(rows, own_tiles + far_tiles)
        for cols in col_tiles:
            r.x[out_rows, cols] = norm_grad(rows, cols).astype(bf16)
        norm_copies.append(links.send(r.x.at[out_rows, :], r.norm_in.at[out_rows, :], "mate"))

    back_mate(0)
    backward(own_rows, far_tiles)
    grad_core = [
        [give_core(ref, target, own_rows)] for ref, target in ((r.first_act, r.first_in), (r.second_act, r.second_in))
    ]
    arrived([last_core] + product_core)
    weight_grad(r.third_sum, r.last_t, r.last_in, r.product.at[:, units_all], r.product_in)
    chain_third = Chain(links, place, r.third_sum, r.third_half, r.third_quarter, 768)
    chain_third.start()
    back_mate(1)
    for copies_of, ref, target in zip(grad_core, (r.first_act, r.second_act), (r.first_in, r.second_in)):
        copies_of.append(give_core(ref, target, mate_rows))
    split_transpose(r.hidden_low.at[mate_rows, :], r.hidden_t, r.hidden_give, mate_rows)
    hidden_core = links.send(r.hidden_give, r.hidden_in, "core")
    for cols in col_tiles:
        r.hidden_grad[:, cols] = norm_grad(own_rows, cols)
    for cols in col_tiles:
        r.x[mate_rows, cols] = mix(mate_rows, cols).astype(bf16)
    for cols in col_tiles:
        r.mix[:, cols] = mix(own_rows, cols)
    arrived([hidden_core] + grad_core[0])
    links.left(product_core)
    first_sum = r.product.at[:, units_all]
    weight_grad(first_sum, r.hidden_t, r.hidden_in, r.first_act.at[:, units_all], r.first_in)
    chain_first = Chain(links, place, first_sum, r.first_half, r.first_quarter, 640)
    chain_first.start()
    chain_third.middle()

    attention_copies = []
    mate_block, mate_far = flipped(own, 0), 3 - own
    for j in range(2):
        rows = slice(j * chunk_rows, (j + 1) * chunk_rows)
        arrived([norm_copies[j]])
        incoming = r.hidden_grad[rows, :] + r.norm_in[rows, :].astype(f32)
        hidden_grad = r.upstream[rows, :].astype(f32) + norm_back(r.hidden[rows, :], incoming)
        r.hidden_grad[rows, :] = hidden_grad
        branch = (row_mask[rows] * hidden_grad).astype(bf16)
        r.branch[rows, :] = branch
        gated_grad = dot_right_t(branch, r.out[...])
        attention = r.attention_rows[rows, :].astype(f32)
        r.gate_grad[rows, :] = (gated_grad * normalize(attention)).astype(bf16)
        grad = norm_back(attention, gated_grad * r.gate_pre[rows, :]).astype(bf16)
        r.attention_grad[rows, :] = grad
        target_rows = part(member * 2 + j, chunk_rows)
        for i, (mine, theirs) in enumerate(((own, mate_block), (flipped(own, 1), mate_far))):
            target = r.grad_block.at[target_rows, i * head_width : (i + 1) * head_width]
            source = r.attention_grad.at[rows, part(theirs, head_width)]
            attention_copies.append(links.send(source, target, "mate"))
            target[...] = r.attention_grad[rows, part(mine, head_width)]
    branch_core = links.send(r.branch, r.branch_in, "core")
    gate_core = links.send(r.gate_grad, r.gate_grad_in, "core")
    split_transpose(r.gated, r.gated_t, r.gated_give, slice(0, row_count))
    gated_core = links.send(r.gated_give, r.gated_in, "core")
    arrived(grad_core[1])
    links.left(grad_core[0])
    second_sum = r.first_act.at[:, units_all]
    weight_grad(second_sum, r.hidden_t, r.hidden_in, r.second_act.at[:, units_all], r.second_in)
    chain_second = Chain(links, place, second_sum, r.second_half, r.second_quarter, 768)
    chain_first.middle()
    chain_second.start()

    arrived(attention_copies)
    heads_all = 2 * block_heads
    for at in range(heads_all):
        cols = slice(at * HDIM, (at + 1) * HDIM)
        decayed = (r.queries[:, cols].astype(f32) * jnp.exp(-rate_of(at) * (places + 1.0))).astype(bf16)
        r.state_grad[at] = dot_left_t(decayed, r.grad_block[:, cols]).astype(bf16)
    near_heads, far_heads = pl.ds(0, block_heads), pl.ds(block_heads, block_heads)
    state_copies = [
        links.send(r.state_grad.at[near_heads], r.state_in.at[far_heads], "far"),
        links.send(r.state_grad.at[far_heads], r.state_in.at[near_heads], "far"),
    ]
    mix_copy = links.send(r.x.at[mate_rows, :], r.mix_in, "mate")

    def grad_cols(kind, at):
        start = (at // block_heads) * 3 * head_width + kind * head_width + (at % block_heads) * HDIM
        return slice(start, start + HDIM)

    for at in range(heads_all):
        rate = rate_of(at)
        cols = slice(at * HDIM, (at + 1) * HDIM)
        q, k, v, g = r.queries[:, cols], r.keys[:, cols], r.values[:, cols], r.grad_block[:, cols]
        decay = inner_decay(rate)
        weights = (dot_right_t(q, k) * decay).astype(bf16)
        score_grad = (dot_right_t(g, v) * decay).astype(bf16)
        dq = dot_plain(score_grad, k) + jnp.exp(-rate * (places + 1.0)) * dot_right_t(g, r.states[at])
        r.pre_grads[:, grad_cols(0, at)] = (dq * r.query_slope[:, cols].astype(f32)).astype(bf16)
        r.pre_grads[:, grad_cols(1, at)] = dot_left_t(score_grad, q).astype(bf16)
        r.pre_grads[:, grad_cols(2, at)] = dot_left_t(weights, g).astype(bf16)

    def to_far(chain, keep, give, target):
        total = chain.result().astype(bf16)
        size = keep.shape[1]
        keep[...] = total[:, :size]
        give[...] = total[:, size:]
        return links.send(give, target, "far")

    ends = [to_far(chain_third, r.third_keep, r.third_give, r.third_far)]
    arrived(state_copies)
    leaving = 1.0 - pair.astype(f32)
    for at in range(heads_all):
        rate = rate_of(at)
        cols = slice(at * HDIM, (at + 1) * HDIM)
        key_decay = leaving * jnp.exp(-rate * (SPAN - 1.0 - places))
        carried = r.state_in[at]
        dk = r.pre_grads[:, grad_cols(1, at)].astype(f32) + key_decay * dot_right_t(r.values[:, cols], carried)
        dv = r.pre_grads[:, grad_cols(2, at)].astype(f32) + key_decay * dot_plain(r.keys[:, cols], carried)
        r.pre_grads[:, grad_cols(1, at)] = (dk * r.key_slope[:, cols].astype(f32)).astype(bf16)
        r.pre_grads[:, grad_cols(2, at)] = (dv * mask).astype(bf16)
    pre_core = links.send(r.pre_grads, r.pre_in, "core")

    triple = 3 * head_width

    def head_terms(rows, cols):
        return dot_right_t(r.pre_grads[rows, :triple], r.heads[0, cols, :]) + dot_right_t(
            r.pre_grads[rows, triple:], r.heads[1, cols, :]
        )

    term_copies = []
    for start in range(0, width, 512):
        for cols in (slice(start, start + 256), slice(start + 256, start + 512)):
            r.terms[:, cols] = head_terms(part(1 - member, row_count), cols).astype(bf16)
        wide = slice(start, start + 512)
        term_copies.append(links.send(r.terms.at[:, wide], r.terms_in.at[:, wide], "mate"))
    ends.append(to_far(chain_first, r.first_keep, r.first_give, r.first_far))
    arrived([pre_core, normed_core])
    links.left(grad_core[1])
    weight_grad(r.second_act, r.normed_t, r.normed_in, r.pre_grads, r.pre_in)
    chain_heads = Chain(links, place, r.second_act, r.heads_half, r.heads_quarter, 768)
    chain_heads.start()
    chain_second.middle()
    for cols in col_tiles:
        r.terms_own[:, cols] = head_terms(part(member, row_count), cols) + dot_right_t(r.gate_grad[...], r.gate[cols, :])

    def to_heads(chain, keep, target):
        total = chain.result().astype(bf16)
        slot = chain.chunk(chain.y, chain.x)
        slot[...] = total
        size = total.shape[0] // 4
        keep[...] = slot[part(own, size), :]
        return [
            links.send(slot.at[part(index, size), :], target.at[i], device)
            for i, (index, device) in enumerate(((mate_block, "mate"), (flipped(own, 1), "far"), (mate_far, "cross")))
        ]

    arrived([branch_core, gated_core])
    out_sum = r.out.at[:SPAN, :]
    weight_grad(out_sum, r.gated_t, r.gated_in, r.branch, r.branch_in)
    chain_out = Chain(links, place, out_sum, r.out_half, r.out_quarter, 512)
    chain_heads.middle()
    chain_out.start()
    ends.append(to_far(chain_second, r.second_keep, r.second_give, r.second_far))
    arrived([gate_core])
    gate_sum = r.out.at[SPAN:, :]
    lanes = part(member, row_count)
    weight_grad(gate_sum, r.normed_t.at[:, lanes], r.normed_in.at[:, lanes], r.gate_grad, r.gate_grad_in)
    chain_gate = Chain(links, place, gate_sum, r.gate_half, r.gate_quarter, 512)
    chain_gate.start()
    ends.append(to_far(chain_heads, r.heads_keep, r.heads_give, r.heads_far))
    chain_out.middle()
    arrived([mix_copy])
    r.output[...] = (r.hidden[...] + row_mask * (r.mix[...] + r.mix_in[...].astype(f32))).astype(bf16)
    chain_gate.middle()
    ends += to_heads(chain_out, r.out_keep, r.out_far)
    arrived(term_copies)
    for j in range(2):
        rows = slice(j * chunk_rows, (j + 1) * chunk_rows)
        incoming = r.terms_own[rows, :] + r.terms_in[rows, :].astype(f32)
        grad = r.hidden_grad[rows, :] + norm_back(r.x_rows[rows, :].astype(f32), incoming)
        r.input_grad[rows, :] = grad.astype(bf16)
    ends += to_heads(chain_gate, r.gate_keep, r.gate_far)
    arrived(ends)
    links.finish()


def finish_kernel(count, *refs):
    sources, refs = refs[:count], refs[count:]
    (
        output, input_grad, grad_query, grad_key, grad_value, grad_gate, grad_out, grad_first, grad_second, grad_third
    ) = refs[:10]
    held, sems = refs[10:-1], refs[-1]
    targets = [output, input_grad] + list(held)
    copies = [pltpu.make_async_copy(a, b, sems.at[i]) for i, (a, b) in enumerate(zip(sources, targets))]
    for copy in copies:
        copy.start()
    for copy in copies:
        copy.wait()
    pairs = [(held[i], held[i + 1]) for i in range(0, len(held), 2)]
    for (keep, far), target in zip(pairs[:3], (grad_third, grad_first, grad_second)):
        target[...] = (keep[...].astype(f32) + far[...].astype(f32)).T
    size = grad_query.shape[1]
    keep, far = pairs[3]
    for i, target in enumerate((grad_query, grad_key, grad_value)):
        cols = slice(i * size, (i + 1) * size)
        target[...] = keep[:, cols].astype(f32) + far[:, cols].astype(f32)
    for (keep, far), target in zip(pairs[4:], (grad_gate, grad_out)):
        total = keep[...].astype(f32)
        for i in range(3):
            total = total + far[i].astype(f32)
        target[...] = total


def fused_shards(
    layer_input, w_query, w_key, w_value, w_gate, w_out, w_first, w_second, w_third,
    decay_rates, seq_lengths, cotangent,
):
    group_rows, width = layer_input.shape
    row_count = cotangent.shape[0]
    heads = decay_rates.shape[0]
    head_width = w_query.shape[1]
    units = w_third.shape[0]
    shape = jax.ShapeDtypeStruct
    share = width // 8
    both = 2 * head_width
    triple = 3 * head_width
    inputs = dict(
        lengths=seq_lengths, decay_rates=decay_rates, layer_input=layer_input, w_query=w_query, w_key=w_key, w_value=w_value,
        w_gate=w_gate, w_out=w_out, w_first=w_first.T, w_second=w_second.T, w_third=w_third, cotangent=cotangent,
    )
    rows_shape = shape((row_count, width), bf16)
    ffn_shape = shape((share, units), bf16)
    head_shape = shape((share, triple), bf16)
    dense_shape = shape((share // 4, width), bf16)
    dense_far = shape((3, share // 4, width), bf16)
    outputs = dict(
        output=rows_shape, input_grad=rows_shape,
        third_keep=ffn_shape, third_far=ffn_shape, first_keep=ffn_shape, first_far=ffn_shape,
        second_keep=ffn_shape, second_far=ffn_shape, heads_keep=head_shape, heads_far=head_shape,
        gate_keep=dense_shape, gate_far=dense_far, out_keep=dense_shape, out_far=dense_far,
    )
    low = lambda *dims: pltpu.VMEM(dims, bf16)
    wide = lambda *dims: pltpu.VMEM(dims, f32)
    half = width // 2
    scratch = dict(
        x=low(group_rows, width), normed=low(group_rows, width),
        heads=low(2, width, triple), gate=low(width, width), out=low(width, width),
        first=low(2 * units, width), second=low(2 * units, width), third=low(2 * units, width),
        upstream=low(row_count, width), rates=wide(8, 128), rates_far=wide(8, 128),
        queries=low(SPAN, both), keys=low(SPAN, both), values=low(SPAN, both),
        query_slope=low(SPAN, both), key_slope=low(SPAN, both), states=low(2 * heads, HDIM, HDIM),
        attention=low(SPAN, both), attention_rows=low(row_count, width), gate_pre=wide(row_count, width),
        hidden=wide(row_count, width),
        hidden_low=low(SPAN, width), last=low(SPAN, width),
        first_act=low(SPAN, 2 * units), second_act=low(SPAN, 2 * triple), product=low(SPAN, 2 * units),
        hidden_grad=wide(row_count, width), mix=wide(row_count, width), norm_in=low(row_count, width),
        mix_in=low(row_count, width), grad_block=low(SPAN, both),
        state_grad=low(2 * heads, HDIM, HDIM), state_in=low(2 * heads, HDIM, HDIM),
        pre_grads=low(SPAN, 2 * triple), terms_in=low(row_count, width),
        terms_own=wide(row_count, width),
        normed_t=low(half, SPAN), normed_give=low(half, SPAN), normed_in=low(half, SPAN),
        last_t=low(half, SPAN), last_give=low(half, SPAN), last_in=low(half, SPAN),
        hidden_t=low(half, SPAN), hidden_give=low(half, SPAN), hidden_in=low(half, SPAN),
        gated_t=low(half, row_count), gated_give=low(half, row_count), gated_in=low(half, row_count),
        product_in=low(SPAN, 2 * units), first_in=low(SPAN, 2 * units), second_in=low(SPAN, 2 * units),
        pre_in=low(SPAN, 2 * triple), branch_in=low(row_count, width), gate_grad_in=low(row_count, width),
        third_sum=low(half, 2 * units),
        third_half=low(2 * share, 2 * units), first_half=low(2 * share, 2 * units),
        second_half=low(2 * share, 2 * units), heads_half=low(2 * share, 2 * triple),
        gate_half=low(2 * share, width), out_half=low(2 * share, width),
        third_quarter=low(share, 2 * units), first_quarter=low(share, 2 * units),
        second_quarter=low(share, 2 * units), heads_quarter=low(share, 2 * triple),
        gate_quarter=low(share, width), out_quarter=low(share, width),
        third_give=low(share, units), first_give=low(share, units), second_give=low(share, units),
        heads_give=low(share, triple),
        local_sems=pltpu.SemaphoreType.DMA((16,)),
        send_sems=pltpu.SemaphoreType.DMA((144,)), recv_sems=pltpu.SemaphoreType.DMA((144,)),
    )
    results = pl.pallas_call(
        functools.partial(layer_kernel, list(inputs) + list(outputs) + list(scratch)),
        out_shape=list(outputs.values()),
        in_specs=[smem(), smem()] + [pl.BlockSpec(memory_space=pl.ANY)] * (len(inputs) - 2),
        out_specs=[vmem()] * len(outputs),
        scratch_shapes=list(scratch.values()),
        compiler_params=pltpu.CompilerParams(
            collective_id=0, has_side_effects=True, vmem_limit_bytes=VMEM_ALL
        ),
        name="layer",
    )(*inputs.values())
    transposed_shape = shape((units, share), f32)
    finals = [rows_shape] * 2 + [shape((share, head_width), f32)] * 3 + [shape((share // 4, width), f32)] * 2
    finals += [transposed_shape] * 3
    place_any = pl.BlockSpec(memory_space=pltpu.HBM)
    results = pl.pallas_call(
        functools.partial(finish_kernel, len(results)),
        out_shape=finals,
        in_specs=[place_any] * len(results),
        out_specs=[vmem()] * 10,
        scratch_shapes=[pltpu.VMEM(a.shape, a.dtype) for a in results[2:]] + [pltpu.SemaphoreType.DMA((len(results),))],
        compiler_params=pltpu.CompilerParams(vmem_limit_bytes=VMEM_ALL),
        name="finish",
    )(*results)
    return (*results[:7], results[7].T, results[8].T, results[9])


def solution(mesh):
    placed = (
        P("dp", None),
        P(None, "head"),
        P(None, "head"),
        P(None, "head"),
        P(),
        P(),
        P(None, "head"),
        P(None, "head"),
        P("head", None),
        P("head"),
        P("dp"),
        P(("dp", "head"), None),
    )
    n_dp, n_head = mesh.shape["dp"], mesh.shape["head"]
    body = fused_shards if (n_dp, n_head) == (8, 4) else functools.partial(shards, n_dp, n_head)
    return jax.shard_map(
        body,
        mesh=mesh,
        in_specs=placed,
        out_specs=(
            P(("dp", "head"), None),
            P(("dp", "head"), None),
            P("dp", "head"),
            P("dp", "head"),
            P("dp", "head"),
            P(("dp", "head"), None),
            P(("dp", "head"), None),
            P("dp", "head"),
            P("dp", "head"),
            P("head", "dp"),
        ),
        check_vma=False,
    )
```

```python
import functools
import types

import jax
import jax.numpy as jnp
from jax import lax
from jax.experimental import pallas as pl
from jax.experimental.pallas import tpu as pltpu
from jax.sharding import PartitionSpec as P

SPAN = 512
HDIM = 128

epsilon = 1e-06
bf16 = jnp.bfloat16
f32 = jnp.float32
VMEM_LIMIT = 48 * 2**20
VMEM_ALL = 63 * 2**20


def inverse_rms(values):
    return lax.rsqrt(jnp.mean(values * values, axis=-1, keepdims=True) + epsilon)


def normalize(values):
    return values * inverse_rms(values)


def norm_back(values, incoming):
    inverse = inverse_rms(values)
    unit_rows = values * inverse
    return inverse * (incoming - unit_rows * jnp.mean(incoming * unit_rows, axis=-1, keepdims=True))


def dot_plain(left, right):
    return jnp.dot(left, right, preferred_element_type=f32)


def dot_right_t(left, right):
    return lax.dot_general(left, right, (((1,), (1,)), ((), ())), preferred_element_type=f32)


def dot_left_t(left, right):
    return lax.dot_general(left, right, (((0,), (0,)), ((), ())), preferred_element_type=f32)


def transposed(values):
    return values.T


def column(length):
    return lax.broadcasted_iota(jnp.int32, (length, 1), 0)


def inner_decay(rate):
    rows = lax.broadcasted_iota(jnp.int32, (SPAN, SPAN), 0)
    cols = lax.broadcasted_iota(jnp.int32, (SPAN, SPAN), 1)
    offset = rows - cols
    return jnp.where(offset >= 0, jnp.exp(-rate * jnp.maximum(offset, 0).astype(f32)), 0.0)


def attend_kernel(
    meta, rates, x, w_own_q, w_own_k, w_own_v, w_other,
    normed, attention, queries, keys, values, query_slope, key_slope, states,
):
    pair, length = meta[0], meta[1]
    start = pl.multiple_of(pair * SPAN, SPAN)
    rows = x.shape[0]
    head_width = w_own_q.shape[1]

    def norm_step(i, carry):
        place = pl.ds(pl.multiple_of(i * 128, 128), 128)
        normed[place, :] = normalize(x[place, :].astype(f32)).astype(bf16)
        return carry

    lax.fori_loop(0, rows // 128, norm_step, 0)
    block = normed[pl.ds(start, SPAN), :]
    mask = (start + column(SPAN) < length).astype(f32)
    early_mask = (column(SPAN) < length).astype(f32) * pair.astype(f32)
    early = normed[0:SPAN, :]
    places = column(SPAN).astype(f32)
    for part in range(2):
        if part == 0:
            wq, wk, wv = w_own_q[...], w_own_k[...], w_own_v[...]
        else:
            wq, wk, wv = (w_other[:, i * head_width : (i + 1) * head_width] for i in range(3))
        pre_query = dot_plain(block, wq)
        pre_key = dot_plain(block, wk)
        pre_value = dot_plain(block, wv)
        sigmoid_query = jax.nn.sigmoid(pre_query)
        sigmoid_key = jax.nn.sigmoid(pre_key)
        query = (pre_query * sigmoid_query).astype(bf16)
        key = (mask * (pre_key * sigmoid_key)).astype(bf16)
        value = (mask * pre_value).astype(bf16)
        wide = slice(part * head_width, (part + 1) * head_width)
        query_slope[:, wide] = (sigmoid_query * (1.0 + pre_query * (1.0 - sigmoid_query))).astype(bf16)
        key_slope[:, wide] = (mask * (sigmoid_key * (1.0 + pre_key * (1.0 - sigmoid_key)))).astype(bf16)
        queries[:, wide] = query
        keys[:, wide] = key
        values[:, wide] = value
        early_key = dot_plain(early, wk)
        early_key = early_mask * (early_key * jax.nn.sigmoid(early_key)).astype(bf16).astype(f32)
        early_value = (early_mask * dot_plain(early, wv)).astype(bf16)
        for head in range(head_width // HDIM):
            index = part * (head_width // HDIM) + head
            rate = rates[index]
            cols = slice(head * HDIM, (head + 1) * HDIM)
            q, k, v = query[:, cols], key[:, cols], value[:, cols]
            scores = dot_right_t(q, k)
            weights = (scores * inner_decay(rate)).astype(bf16)
            keyed = (early_key[:, cols] * jnp.exp(-rate * (SPAN - 1.0 - places))).astype(bf16)
            state = dot_left_t(keyed, early_value[:, cols])
            states[index] = state
            decayed = (q.astype(f32) * jnp.exp(-rate * (places + 1.0))).astype(bf16)
            out = dot_plain(weights, v) + dot_plain(decayed, state.astype(bf16))
            attention[:, index * HDIM : (index + 1) * HDIM] = out.astype(bf16)


def state_kernel(rates, queries, upstream, state_grad):
    places = column(SPAN).astype(f32)
    for index in range(state_grad.shape[0]):
        cols = slice(index * HDIM, (index + 1) * HDIM)
        decayed = (queries[:, cols].astype(f32) * jnp.exp(-rates[index] * (places + 1.0))).astype(bf16)
        state_grad[index] = dot_left_t(decayed, upstream[:, cols])


def attend_back_kernel(
    meta, rates, queries, keys, values, upstream, query_slope, key_slope, states, state_grad, pre_grads
):
    pair, length = meta[0], meta[1]
    mask = (pair * SPAN + column(SPAN) < length).astype(f32)
    places = column(SPAN).astype(f32)
    heads = states.shape[0]
    half = heads // 2
    for index in range(heads):
        rate = rates[index]
        cols = slice(index * HDIM, (index + 1) * HDIM)
        q, k, v, g = queries[:, cols], keys[:, cols], values[:, cols], upstream[:, cols]
        decay = inner_decay(rate)
        query_decay = jnp.exp(-rate * (places + 1.0))
        key_decay = jnp.exp(-rate * (SPAN - 1.0 - places))
        state = states[index].astype(bf16)
        carried = state_grad[index].astype(bf16)
        weights = (dot_right_t(q, k) * decay).astype(bf16)
        score_grad = (dot_right_t(g, v) * decay).astype(bf16)
        dq = dot_plain(score_grad, k) + query_decay * dot_right_t(g, state)
        dk = dot_left_t(score_grad, q) + key_decay * dot_right_t(v, carried)
        dv = dot_left_t(weights, g) + key_decay * dot_plain(k, carried)
        base = (index // half) * (3 * half * HDIM) + (index % half) * HDIM
        pre_grads[:, base : base + HDIM] = (dq * query_slope[:, cols].astype(f32)).astype(bf16)
        base += half * HDIM
        pre_grads[:, base : base + HDIM] = (dk * key_slope[:, cols].astype(f32)).astype(bf16)
        base += half * HDIM
        pre_grads[:, base : base + HDIM] = (dv * mask).astype(bf16)


def vmem():
    return pl.BlockSpec(memory_space=pltpu.VMEM)


def smem():
    return pl.BlockSpec(memory_space=pltpu.SMEM)


def local_call(body, name, out_shapes, args, scalars, flops):
    size = sum(int(a.size) * a.dtype.itemsize for a in list(args) + list(out_shapes))
    return pl.pallas_call(
        body,
        out_shape=out_shapes,
        in_specs=[smem()] * scalars + [vmem()] * (len(args) - scalars),
        out_specs=[vmem()] * len(out_shapes),
        compiler_params=pltpu.CompilerParams(vmem_limit_bytes=VMEM_LIMIT),
        cost_estimate=pl.CostEstimate(flops=flops, bytes_accessed=size, transcendentals=0),
        name=name,
    )(*args)


def shards(
    n_dp, n_head,
    layer_input, w_query, w_key, w_value, w_gate, w_out, w_first, w_second, w_third,
    decay_rates, seq_lengths, cotangent,
):
    group_rows, width = layer_input.shape
    row_count = cotangent.shape[0]
    heads = decay_rates.shape[0]
    head_width = w_query.shape[1]
    place = lax.axis_index("dp")
    own = lax.axis_index("head")
    member, pair = own % 2, own // 2
    bits = n_dp.bit_length() - 1
    length = seq_lengths[0]

    def to_mate(array, bit):
        return lax.ppermute(array, "head", [(i, i ^ bit) for i in range(n_head)])

    def across(array, bit):
        return lax.ppermute(array, "dp", [(i, i ^ (1 << bit)) for i in range(n_dp)])

    def gathered(weight, axis):
        size = weight.shape[axis] // n_dp
        share = lax.dynamic_slice_in_dim(weight, place * size, size, axis)
        return lax.all_gather(to_mate(share, 2), "dp", axis=axis, tiled=True)

    w_heads = jnp.concatenate([w_query, w_key, w_value], axis=1)
    w_heads_other = gathered(w_heads, 0)
    w_first_other = gathered(w_first, 0)
    w_second_other = gathered(w_second, 0)
    w_third_other = gathered(w_third, 1)
    rates = jnp.concatenate([decay_rates, to_mate(decay_rates, 2)])

    block_start = pair * SPAN
    row_start = own * row_count
    positions = jnp.arange(row_count, dtype=jnp.int32)[:, None]
    row_mask = (row_start + positions < length).astype(f32)
    upstream = cotangent.astype(f32)
    last_own = (row_mask * upstream).astype(bf16)
    last_mate = to_mate(last_own, 1)

    meta = jnp.stack([pair, length]).astype(jnp.int32)
    both = 2 * head_width
    shape = jax.ShapeDtypeStruct
    block_shape = shape((SPAN, both), bf16)
    normed, attention_block, queries, keys, values, query_slope, key_slope, states = local_call(
        attend_kernel, "attend",
        [shape(layer_input.shape, bf16)] + [block_shape] * 6 + [shape((2 * heads, HDIM, HDIM), f32)],
        [meta, rates, layer_input, w_query, w_key, w_value, w_heads_other], 2, 6 * 10**9,
    )

    def rows_of(array, index):
        return lax.dynamic_slice_in_dim(array, index * row_count, row_count, 0)

    def ordered(mine, other):
        even, odd = jnp.where(member == 0, mine, other), jnp.where(member == 0, other, mine)
        flip = lambda a: jnp.where(pair == 0, a, jnp.concatenate([a[:, head_width:], a[:, :head_width]], axis=1))
        even, odd = flip(even), flip(odd)
        return jnp.concatenate(
            [even[:, :head_width], odd[:, :head_width], even[:, head_width:], odd[:, head_width:]], axis=1
        )

    def pieces(array):
        cut = [array[:, i * head_width : (i + 1) * head_width] for i in range(4)]
        even, odd = jnp.concatenate([cut[0], cut[2]], axis=1), jnp.concatenate([cut[1], cut[3]], axis=1)
        flip = lambda a: jnp.where(pair == 0, a, jnp.concatenate([a[:, head_width:], a[:, :head_width]], axis=1))
        even, odd = flip(even), flip(odd)
        return jnp.where(member == 0, even, odd), jnp.where(member == 0, odd, even)

    received = to_mate(rows_of(attention_block, 1 - member), 1)
    attention = ordered(rows_of(attention_block, member), received).astype(f32)
    attention_norm = normalize(attention)
    rows_low = rows_of(normed, own)
    input_rows = rows_of(layer_input, own).astype(f32)
    gate_pre = dot_plain(rows_low, w_gate)
    gated = (attention_norm * gate_pre).astype(bf16)
    hidden = input_rows + row_mask * dot_plain(gated, w_out)
    hidden_low = normalize(hidden).astype(bf16)
    hidden_mate = to_mate(hidden_low, 1)

    w_first_all = jnp.concatenate([w_first, w_first_other], axis=1)
    w_second_all = jnp.concatenate([w_second, w_second_other], axis=1)
    w_third_all = jnp.concatenate([w_third, w_third_other], axis=0)

    def forward_rows(rows_in):
        first, second = dot_plain(rows_in, w_first_all), dot_plain(rows_in, w_second_all)
        return first.astype(bf16), second.astype(bf16), (first * second).astype(bf16)

    def backward_rows(last, first, second):
        product_grad = dot_right_t(last, w_third_all)
        first_grad = (product_grad * second.astype(f32)).astype(bf16)
        second_grad = (product_grad * first.astype(f32)).astype(bf16)
        return first_grad, second_grad, dot_right_t(first_grad, w_first_all) + dot_right_t(second_grad, w_second_all)

    first_mate, second_mate, product_mate = forward_rows(hidden_mate)
    first_grad_mate, second_grad_mate, norm_grad_mate = backward_rows(last_mate, first_mate, second_mate)
    norm_grad_in = to_mate(norm_grad_mate.astype(bf16), 1)
    mix_in = to_mate(dot_plain(product_mate, w_third_all).astype(bf16), 1)
    first_own, second_own, product_own = forward_rows(hidden_low)
    first_grad_own, second_grad_own, norm_grad_own = backward_rows(last_own, first_own, second_own)
    hidden_grad = upstream + norm_back(hidden, norm_grad_own + norm_grad_in.astype(f32))
    mixed = dot_plain(product_own, w_third_all) + mix_in.astype(f32)
    output = (hidden + row_mask * mixed).astype(bf16)

    branch_grad = (row_mask * hidden_grad).astype(bf16)
    gated_grad = dot_right_t(branch_grad, w_out)
    gate_grad = (gated_grad * attention_norm).astype(bf16)
    attention_grad = norm_back(attention, gated_grad * gate_pre).astype(bf16)
    mine, for_mate = pieces(attention_grad)
    from_mate = to_mate(for_mate, 1)
    grad_block = jnp.concatenate(
        [jnp.where(member == 0, mine, from_mate), jnp.where(member == 0, from_mate, mine)], axis=0
    )
    state_shape = shape((2 * heads, HDIM, HDIM), f32)
    (state_grad,) = local_call(
        state_kernel, "state_grad", [state_shape], [rates, queries, grad_block], 1, 10**8
    )
    swapped = jnp.concatenate([state_grad[heads:], state_grad[:heads]], axis=0)
    carried = lax.ppermute(swapped, "head", [(i, i - 2) for i in range(2, n_head)])
    (pre_grads,) = local_call(
        attend_back_kernel, "attend_back", [shape((SPAN, 3 * both), bf16)],
        [meta, rates, queries, keys, values, grad_block, query_slope, key_slope, states, carried], 2, 2 * 10**9,
    )
    head_terms = dot_right_t(pre_grads[:, : 3 * head_width], w_heads) + dot_right_t(
        pre_grads[:, 3 * head_width :], w_heads_other
    )
    head_terms = head_terms.astype(bf16)
    terms_in = to_mate(rows_of(head_terms, 1 - member), 1)
    input_norm_grad = (
        rows_of(head_terms, member).astype(f32) + terms_in.astype(f32) + dot_right_t(gate_grad, w_gate)
    )
    input_grad = (hidden_grad + norm_back(input_rows, input_norm_grad)).astype(bf16)

    def summed(left, right, order):
        left = left.reshape((left.shape[0],) + (2,) * bits + (width // n_dp,))

        def pick(array, axis, bit, which):
            side = (place // (1 << bit)) % 2
            return lax.dynamic_index_in_dim(array, side if which else 1 - side, axis, keepdims=False)

        left_axis = lambda bit, done: 1 + (bits - 1 - bit) - sum(1 for b in done if b > bit)
        first_bit = order[0]
        make = lambda which: dot_left_t(
            pick(left, left_axis(first_bit, []), first_bit, which).reshape(left.shape[0], width // 2), right
        ).astype(bf16)
        arrived = across(make(False), first_bit)
        total = (make(True).astype(f32) + arrived.astype(f32)).astype(bf16)
        total = total.reshape((2,) * (bits - 1) + (width // n_dp, right.shape[1]))
        done = [first_bit]
        for bit in order[1:]:
            axis = left_axis(bit, done) - 1
            arrived = across(pick(total, axis, bit, False), bit)
            total = (pick(total, axis, bit, True).astype(f32) + arrived.astype(f32)).astype(bf16)
            done.append(bit)
        return total

    def with_mate(total):
        size = total.shape[1] // 2
        return total[:, :size].astype(f32) + to_mate(total[:, size:], 2).astype(f32)

    def over_heads(total):
        for bit in (1, 2):
            cut = total.reshape((2, -1) + total.shape[1:]) if bit == 2 else total.reshape((2, 2, -1) + total.shape[1:])
            side = (own // bit) % 2
            axis = 0 if bit == 2 else 1
            arrived = to_mate(lax.dynamic_index_in_dim(cut, 1 - side, axis, keepdims=False), bit)
            total = lax.dynamic_index_in_dim(cut, side, axis, keepdims=False).astype(f32) + arrived.astype(f32)
            if bit == 1:
                total = total.astype(bf16).reshape((-1,) + total.shape[2:])
        return total

    up = list(range(bits))
    down = [0] + up[:0:-1]
    stack = lambda a, b: jnp.concatenate([a, b], axis=0)
    hidden_all = stack(hidden_low, hidden_mate)
    last_all = stack(last_own, last_mate)
    grad_third_t = with_mate(summed(last_all, stack(product_own, product_mate), up))
    grad_first = with_mate(summed(hidden_all, stack(first_grad_own, first_grad_mate), up))
    grad_second = with_mate(summed(hidden_all, stack(second_grad_own, second_grad_mate), down))
    grad_out = over_heads(summed(gated, branch_grad, down))
    grad_gate = over_heads(summed(rows_low, gate_grad, up))
    normed_block = lax.dynamic_slice_in_dim(normed, block_start, SPAN, 0)
    grad_heads = with_mate(summed(normed_block, pre_grads, down))
    return (
        output,
        input_grad,
        grad_heads[:, :head_width],
        grad_heads[:, head_width : 2 * head_width],
        grad_heads[:, 2 * head_width :],
        grad_gate,
        grad_out,
        grad_first,
        grad_second,
        grad_third_t.T,
    )


MESH = pl.DeviceIdType.MESH


def flipped(index, bit):
    return index + (1 << bit) * (1 - 2 * ((index // (1 << bit)) % 2))


def part(index, size):
    return pl.ds(pl.multiple_of(index * size, size), size)


class Links:
    def __init__(self, others, send_sems, recv_sems):
        self.others, self.send_sems, self.recv_sems, self.started = others, send_sems, recv_sems, []

    def send(self, source, target, device):
        index = len(self.started)
        copy = pltpu.make_async_remote_copy(
            src_ref=source,
            dst_ref=target,
            send_sem=self.send_sems.at[index],
            recv_sem=self.recv_sems.at[index],
            device_id=self.others[device],
            device_id_type=MESH,
        )
        copy.start()
        self.started.append(copy)
        copy.sent = False
        return copy

    def left(self, copies):
        for copy in copies:
            if not copy.sent:
                copy.wait_send()
                copy.sent = True

    def finish(self):
        self.left(self.started)


def arrived(copies):
    for copy in copies:
        copy.wait_recv()


class Gather:
    def __init__(self, links, place, pieces, halves):
        self.links, self.pieces, self.halves = links, pieces, halves
        self.places = [place, flipped(place, 1), flipped(place, 2), flipped(flipped(place, 1), 2)]
        self.to_core, self.near, self.crossing, self.fetched = [], {}, {}, {}

    def pass_on(self, piece, which, device):
        ref = self.pieces[piece](self.places[which])
        return self.links.send(ref, ref, device)

    def fetch(self, sources):
        for i, source in enumerate(sources):
            self.fetched[i] = self.links.send(source, self.pieces[i](self.places[0]), "far")

    def spread(self, piece=0):
        arrived([self.fetched[piece]])
        self.near[piece] = (self.pass_on(piece, 0, "x"), self.pass_on(piece, 0, "y"))
        self.to_core.append(self.pass_on(piece, 0, "core"))

    def cross(self, piece=0):
        crossing = []
        for i, (half, device) in enumerate(zip(self.halves, ("y", "x"))):
            arrived([self.near[piece][i]])
            ref = half(self.pieces[piece](self.places[1 + i]))
            crossing.append(self.links.send(ref, ref, device))
            self.to_core.append(self.pass_on(piece, 1 + i, "core"))
        self.crossing[piece] = crossing

    def last(self, piece=0):
        arrived(self.crossing[piece])
        self.to_core.append(self.pass_on(piece, 3, "core"))

    def done(self):
        arrived(self.to_core)


class Chain:
    def __init__(self, links, place, total, halves_in, quarter_in, cut, orders=("xy", "yx")):
        self.links, self.total, self.halves_in, self.quarter_in = links, total, halves_in, quarter_in
        size = total.shape[1]
        self.parts = [(slice(0, cut), orders[0]), (slice(cut, size), orders[1])]
        self.x, self.y = (place // 2) % 2, (place // 4) % 2
        self.rows = quarter_in.shape[0]
        self.waits = []

    def chunk(self, y, x, cols=slice(None)):
        return self.total.at[part(2 * y + x, self.rows), cols]

    def start(self):
        links, rows = self.links, self.rows
        for cols, order in self.parts:
            if order == "xy":
                self.waits.append([
                    links.send(self.chunk(y, 1 - self.x, cols), self.halves_in.at[y * rows : (y + 1) * rows, cols], "x")
                    for y in range(2)
                ])
            else:
                give = self.total.at[part(1 - self.y, 2 * rows), cols]
                self.waits.append([links.send(give, self.halves_in.at[:, cols], "y")])

    def add(self, place, arrived_part):
        place[...] = (place[...].astype(f32) + arrived_part.astype(f32)).astype(bf16)

    def middle(self):
        rows, x, y = self.rows, self.x, self.y
        keep, waits = [], []
        for (cols, order), before in zip(self.parts, self.waits):
            arrived(before)
            give, device, index = (
                (self.chunk(1 - y, x, cols), "y", y) if order == "xy" else (self.chunk(y, 1 - x, cols), "x", x)
            )
            self.add(give, self.halves_in[part(1 - index, rows), cols])
            waits.append([self.links.send(give, self.quarter_in.at[:, cols], device)])
            keep.append((cols, index))
        for cols, index in keep:
            self.add(self.chunk(y, x, cols), self.halves_in[part(index, rows), cols])
        self.waits = waits

    def result(self):
        for before in self.waits:
            arrived(before)
        return self.chunk(self.y, self.x)[...].astype(f32) + self.quarter_in[...].astype(f32)


def layer_kernel(names, *refs):
    r = types.SimpleNamespace(**dict(zip(names, refs)))
    place, own = lax.axis_index("dp"), lax.axis_index("head")
    pair, member, core = own // 2, own % 2, place % 2
    length = r.lengths[0]
    group_rows, width = r.layer_input.shape
    row_count = r.cotangent.shape[0]
    head_width = r.w_query.shape[1]
    block_heads = head_width // HDIM
    hidden_size = r.w_third.shape[0]
    share_size = width // 8
    chunk_rows = row_count // 2
    r.gated, r.x_rows = (r.x.at[i * row_count : (i + 1) * row_count, :] for i in (2, 3))
    r.branch, r.gate_grad, r.attention_grad, r.terms = (
        r.normed.at[i * row_count : (i + 1) * row_count, :] for i in range(4)
    )

    copies = []

    def load(source, target):
        copy = pltpu.make_async_copy(source, target, r.local_sems.at[len(copies)])
        copy.start()
        copies.append(copy)
        return copy

    load_cotangent = load(r.cotangent, r.upstream)
    load_x = load(r.layer_input, r.x)
    load_heads = [
        load(weight, r.heads.at[0, :, i * head_width : (i + 1) * head_width])
        for i, weight in enumerate((r.w_query, r.w_key, r.w_value))
    ]
    load_gate = load(r.w_gate, r.gate)
    load_out = load(r.w_out, r.out)
    load_first = load(r.w_first, r.first.at[:hidden_size, :])
    load_second = load(r.w_second, r.second.at[:hidden_size, :])
    load_third = load(r.w_third, r.third.at[:hidden_size, :])

    others = {
        "core": (flipped(place, 0), own),
        "x": (flipped(place, 1), own),
        "y": (flipped(place, 2), own),
        "mate": (place, flipped(own, 0)),
        "far": (place, flipped(own, 1)),
        "cross": (place, 3 - own),
    }
    barrier = pltpu.get_barrier_semaphore()
    for device in others.values():
        pl.semaphore_signal(barrier, inc=1, device_id=device, device_id_type=MESH)
    pl.semaphore_wait(barrier, len(others))
    links = Links(others, r.send_sems, r.recv_sems)

    head_piece = lambda j: lambda i: r.heads.at[1, part(i, share_size), j * head_width : (j + 1) * head_width]
    ffn_piece = lambda ref: lambda i: ref.at[hidden_size:, part(i, share_size)]
    row_halves = [lambda ref, j=j: ref.at[j * share_size // 2 : (j + 1) * share_size // 2, :] for j in range(2)]
    unit_halves = [lambda ref, j=j: ref.at[j * hidden_size // 2 : (j + 1) * hidden_size // 2, :] for j in range(2)]
    gather_heads = Gather(links, place, [head_piece(j) for j in (1, 2, 0)], row_halves)
    gather_first = Gather(links, place, [ffn_piece(r.first)], unit_halves)
    gather_second = Gather(links, place, [ffn_piece(r.second)], unit_halves)
    gather_third = Gather(links, place, [ffn_piece(r.third)], unit_halves)

    def fetch(gather, source):
        gather.fetch([source.at[:, part(place, share_size)]])

    row_mask = (own * row_count + column(row_count) < length).astype(f32)
    load_cotangent.wait()
    r.last[:row_count, :] = (row_mask * r.upstream[...].astype(f32)).astype(bf16)

    def send_last(j):
        source = slice(j * chunk_rows, (j + 1) * chunk_rows)
        target = slice(row_count + j * chunk_rows, row_count + (j + 1) * chunk_rows)
        return links.send(r.last.at[source, :], r.last.at[target, :], "mate")

    last_copies = [send_last(0)]
    gather_heads.fetch([weight.at[part(place, share_size), :] for weight in (r.w_key, r.w_value, r.w_query)])
    for i in range(block_heads):
        r.rates[i : i + 1, :] = jnp.full((1, 128), r.decay_rates[i], f32)
    rates_copy = links.send(r.rates, r.rates_far, "far")
    fetch(gather_first, r.w_first)
    last_copies.append(send_last(1))

    load_x.wait()

    def norm_step(i, carry):
        where = part(i, 128)
        r.normed[where, :] = normalize(r.x[where, :].astype(f32)).astype(bf16)
        return carry

    lax.fori_loop(0, group_rows // 128, norm_step, 0)
    r.x_rows[...] = r.x[part(own, row_count), :]
    block_rows = part(pair, SPAN)
    mask = (pair * SPAN + column(SPAN) < length).astype(f32)
    early_mask = (column(SPAN) < length).astype(f32) * pair.astype(f32)
    places = column(SPAN).astype(f32)

    def project(index):
        wide = slice(index * head_width, (index + 1) * head_width)
        weights = [r.heads.at[index, :, i * head_width : (i + 1) * head_width] for i in range(3)]
        block = r.normed[block_rows, :]
        early = r.normed[0:SPAN, :]
        pre_query = dot_plain(block, weights[0][...])
        sigmoid = jax.nn.sigmoid(pre_query)
        r.queries[:, wide] = (pre_query * sigmoid).astype(bf16)
        r.query_slope[:, wide] = (sigmoid * (1.0 + pre_query * (1.0 - sigmoid))).astype(bf16)
        pre_key = dot_plain(block, weights[1][...])
        sigmoid = jax.nn.sigmoid(pre_key)
        r.keys[:, wide] = (mask * (pre_key * sigmoid)).astype(bf16)
        r.key_slope[:, wide] = (mask * (sigmoid * (1.0 + pre_key * (1.0 - sigmoid)))).astype(bf16)
        r.values[:, wide] = (mask * dot_plain(block, weights[2][...])).astype(bf16)
        early_key = dot_plain(early, weights[1][...])
        early_key = early_mask * (early_key * jax.nn.sigmoid(early_key)).astype(bf16).astype(f32)
        early_value = (early_mask * dot_plain(early, weights[2][...])).astype(bf16)
        return early_key, early_value

    def rate_of(index):
        ref = r.rates if index < block_heads else r.rates_far
        return ref[index % block_heads : index % block_heads + 1, 0:1]

    def attend(index, early_key, early_value):
        for head in range(block_heads):
            at = index * block_heads + head
            rate = rate_of(at)
            cols = slice(at * HDIM, (at + 1) * HDIM)
            early = slice(head * HDIM, (head + 1) * HDIM)
            q, k, v = r.queries[:, cols], r.keys[:, cols], r.values[:, cols]
            weights = (dot_right_t(q, k) * inner_decay(rate)).astype(bf16)
            keyed = (early_key[:, early] * jnp.exp(-rate * (SPAN - 1.0 - places))).astype(bf16)
            state = dot_left_t(keyed, early_value[:, early])
            r.states[at] = state.astype(bf16)
            decayed = (q.astype(f32) * jnp.exp(-rate * (places + 1.0))).astype(bf16)
            out = dot_plain(weights, v) + dot_plain(decayed, state.astype(bf16))
            r.attention[:, cols] = out.astype(bf16)
        wide = slice(index * head_width, (index + 1) * head_width)
        block = own if index == 0 else flipped(own, 1)
        target = r.attention_rows.at[:, part(block, head_width)]
        copy = links.send(r.attention.at[part(1 - member, row_count), wide], target, "mate")
        target[...] = r.attention[part(member, row_count), wide]
        return copy

    def split_transpose(source, keep, give, columns):
        for e in range(4):
            rows = slice(e * share_size, (e + 1) * share_size)
            keep[rows, columns] = transposed(source[:, part(2 * e + core, share_size)])
            give[rows, columns] = transposed(source[:, part(2 * e + 1 - core, share_size)])

    for copy in load_heads:
        copy.wait()
    gather_heads.spread(0)
    early = project(0)
    gather_heads.spread(1)
    gather_heads.spread(2)
    gather_heads.cross(0)
    attention_own = attend(0, *early)
    fetch(gather_second, r.w_second)
    gather_heads.cross(1)
    gather_heads.cross(2)
    gather_heads.last(0)
    split_transpose(r.normed.at[block_rows, :], r.normed_t, r.normed_give, slice(0, SPAN))
    normed_core = links.send(r.normed_give, r.normed_in, "core")
    gather_heads.last(1)
    gather_heads.last(2)
    gather_first.spread()
    load_gate.wait()
    r.gate_pre[...] = dot_plain(r.normed[part(own, row_count), :], r.gate[...])
    gather_heads.done()
    rates_copy.wait_recv()
    early = project(1)
    gather_first.cross()
    attention_far = attend(1, *early)
    fetch(gather_third, r.w_third)
    split_transpose(r.last.at[:row_count, :], r.last_t, r.last_give, slice(0, row_count))
    gather_first.last()
    arrived(last_copies)
    split_transpose(r.last.at[row_count:, :], r.last_t, r.last_give, slice(row_count, 2 * row_count))
    last_core = links.send(r.last_give, r.last_in, "core")
    gather_second.spread()
    load_out.wait()
    arrived([attention_own, attention_far])

    hidden_copies = []
    for j in range(2):
        rows = slice(j * chunk_rows, (j + 1) * chunk_rows)
        gated = (normalize(r.attention_rows[rows, :].astype(f32)) * r.gate_pre[rows, :]).astype(bf16)
        r.gated[rows, :] = gated
        hidden = r.x_rows[rows, :].astype(f32) + row_mask[rows] * dot_plain(gated, r.out[...])
        r.hidden[rows, :] = hidden
        r.hidden_low[rows, :] = normalize(hidden).astype(bf16)
        target = slice(row_count + j * chunk_rows, row_count + (j + 1) * chunk_rows)
        hidden_copies.append(links.send(r.hidden_low.at[rows, :], r.hidden_low.at[target, :], "mate"))
        if j == 0:
            gather_second.cross()

    own_tiles = [(0, 256), (256, 256), (512, 128)]
    far_tiles = [(640, 256), (896, 256), (1152, 256)]

    def forward(rows, tiles):
        for start, size in tiles:
            units = slice(start, start + size)
            first = dot_right_t(r.hidden_low[rows, :], r.first[units, :])
            second = dot_right_t(r.hidden_low[rows, :], r.second[units, :])
            r.first_act[rows, units] = first.astype(bf16)
            r.second_act[rows, units] = second.astype(bf16)
            r.product[rows, units] = (first * second).astype(bf16)

    def backward(rows, tiles):
        for start, size in tiles:
            units = slice(start, start + size)
            product_grad = dot_right_t(r.last[rows, :], r.third[units, :])
            first_grad = product_grad * r.second_act[rows, units].astype(f32)
            second_grad = product_grad * r.first_act[rows, units].astype(f32)
            r.first_act[rows, units] = first_grad.astype(bf16)
            r.second_act[rows, units] = second_grad.astype(bf16)

    units_all = slice(0, 2 * hidden_size)
    col_tiles = [slice(i, i + 256) for i in range(0, width, 256)]

    def norm_grad(rows, cols):
        return dot_plain(r.first_act[rows, units_all], r.first[:, cols]) + dot_plain(
            r.second_act[rows, units_all], r.second[:, cols]
        )

    def mix(rows, cols):
        return dot_plain(r.product[rows, units_all], r.third[:, cols])

    own_rows = slice(0, row_count)
    for copy in (load_first, load_second, load_third):
        copy.wait()
    mate_chunks = [slice(row_count + j * chunk_rows, row_count + (j + 1) * chunk_rows) for j in range(2)]
    mate_rows = slice(row_count, 2 * row_count)

    def give_core(source, target, rows):
        return links.send(source.at[rows, units_all], target.at[rows, :], "core")

    def weight_grad(target, left, left_in, right, right_in):
        size = right.shape[1]
        for start in range(0, size, 256):
            cols = slice(start, min(start + 256, size))
            total = dot_plain(left[...], right[:, cols]) + dot_plain(left_in[...], right_in[:, cols])
            target[:, cols] = total.astype(bf16)

    forward(own_rows, own_tiles)
    gather_second.last()
    split_transpose(r.hidden_low.at[own_rows, :], r.hidden_t, r.hidden_give, own_rows)
    gather_third.spread()
    gather_first.done()
    gather_second.done()
    forward(own_rows, far_tiles)
    product_core = [give_core(r.product, r.product_in, own_rows)]
    gather_third.cross()
    arrived(hidden_copies[:1])
    forward(mate_chunks[0], own_tiles + far_tiles)
    gather_third.last()
    backward(own_rows, own_tiles)
    arrived(hidden_copies[1:])
    forward(mate_chunks[1], own_tiles + far_tiles)
    product_core.append(give_core(r.product, r.product_in, mate_rows))
    gather_third.done()
    norm_copies = []

    def back_mate(j):
        rows, out_rows = mate_chunks[j], slice(j * chunk_rows, (j + 1) * chunk_rows)
        backward(rows, own_tiles + far_tiles)
        for cols in col_tiles:
            r.x[out_rows, cols] = norm_grad(rows, cols).astype(bf16)
        norm_copies.append(links.send(r.x.at[out_rows, :], r.norm_in.at[out_rows, :], "mate"))

    back_mate(0)
    backward(own_rows, far_tiles)
    grad_core = [
        [give_core(ref, target, own_rows)] for ref, target in ((r.first_act, r.first_in), (r.second_act, r.second_in))
    ]
    arrived([last_core] + product_core)
    weight_grad(r.third_sum, r.last_t, r.last_in, r.product.at[:, units_all], r.product_in)
    chain_third = Chain(links, place, r.third_sum, r.third_half, r.third_quarter, 768)
    chain_third.start()
    back_mate(1)
    for copies_of, ref, target in zip(grad_core, (r.first_act, r.second_act), (r.first_in, r.second_in)):
        copies_of.append(give_core(ref, target, mate_rows))
    split_transpose(r.hidden_low.at[mate_rows, :], r.hidden_t, r.hidden_give, mate_rows)
    hidden_core = links.send(r.hidden_give, r.hidden_in, "core")
    for cols in col_tiles:
        r.hidden_grad[:, cols] = norm_grad(own_rows, cols)
    for cols in col_tiles:
        r.x[mate_rows, cols] = mix(mate_rows, cols).astype(bf16)

    def send_mix(j):
        rows = slice(j * chunk_rows, (j + 1) * chunk_rows)
        return links.send(r.x.at[mate_chunks[j], :], r.mix_in.at[rows, :], "mate")

    mix_copies = [send_mix(0)]
    for cols in col_tiles:
        r.mix[:, cols] = mix(own_rows, cols)
    arrived([hidden_core] + grad_core[0])
    links.left(product_core)
    first_sum = r.product.at[:, units_all]
    weight_grad(first_sum, r.hidden_t, r.hidden_in, r.first_act.at[:, units_all], r.first_in)
    chain_first = Chain(links, place, first_sum, r.first_half, r.first_quarter, 640)
    chain_first.start()
    chain_third.middle()

    attention_copies = []
    mate_block, mate_far = flipped(own, 0), 3 - own
    for j in range(2):
        rows = slice(j * chunk_rows, (j + 1) * chunk_rows)
        arrived([norm_copies[j]])
        incoming = r.hidden_grad[rows, :] + r.norm_in[rows, :].astype(f32)
        hidden_grad = r.upstream[rows, :].astype(f32) + norm_back(r.hidden[rows, :], incoming)
        r.hidden_grad[rows, :] = hidden_grad
        branch = (row_mask[rows] * hidden_grad).astype(bf16)
        r.branch[rows, :] = branch
        gated_grad = dot_right_t(branch, r.out[...])
        attention = r.attention_rows[rows, :].astype(f32)
        r.gate_grad[rows, :] = (gated_grad * normalize(attention)).astype(bf16)
        grad = norm_back(attention, gated_grad * r.gate_pre[rows, :]).astype(bf16)
        r.attention_grad[rows, :] = grad
        target_rows = part(member * 2 + j, chunk_rows)
        for i, (mine, theirs) in enumerate(((own, mate_block), (flipped(own, 1), mate_far))):
            target = r.grad_block.at[target_rows, i * head_width : (i + 1) * head_width]
            source = r.attention_grad.at[rows, part(theirs, head_width)]
            attention_copies.append(links.send(source, target, "mate"))
            target[...] = r.attention_grad[rows, part(mine, head_width)]
    branch_core = links.send(r.branch, r.branch_in, "core")
    gate_core = links.send(r.gate_grad, r.gate_grad_in, "core")
    split_transpose(r.gated, r.gated_t, r.gated_give, slice(0, row_count))
    gated_core = links.send(r.gated_give, r.gated_in, "core")
    arrived(grad_core[1])
    links.left(grad_core[0])
    second_sum = r.first_act.at[:, units_all]
    weight_grad(second_sum, r.hidden_t, r.hidden_in, r.second_act.at[:, units_all], r.second_in)
    chain_second = Chain(links, place, second_sum, r.second_half, r.second_quarter, 768)
    chain_first.middle()
    chain_second.start()

    arrived([branch_core, gated_core])
    out_sum = r.out.at[:SPAN, :]
    weight_grad(out_sum, r.gated_t, r.gated_in, r.branch, r.branch_in)
    chain_out = Chain(links, place, out_sum, r.out_half, r.out_quarter, 512)
    chain_out.start()

    arrived(attention_copies)
    heads_all = 2 * block_heads
    for at in range(heads_all):
        cols = slice(at * HDIM, (at + 1) * HDIM)
        decayed = (r.queries[:, cols].astype(f32) * jnp.exp(-rate_of(at) * (places + 1.0))).astype(bf16)
        r.state_grad[at] = dot_left_t(decayed, r.grad_block[:, cols]).astype(bf16)
    near_heads, far_heads = pl.ds(0, block_heads), pl.ds(block_heads, block_heads)
    state_copies = [
        links.send(r.state_grad.at[near_heads], r.state_in.at[far_heads], "far"),
        links.send(r.state_grad.at[far_heads], r.state_in.at[near_heads], "far"),
    ]
    mix_copies.append(send_mix(1))

    def grad_cols(kind, at):
        start = (at // block_heads) * 3 * head_width + kind * head_width + (at % block_heads) * HDIM
        return slice(start, start + HDIM)

    for at in range(heads_all):
        rate = rate_of(at)
        cols = slice(at * HDIM, (at + 1) * HDIM)
        q, k, v, g = r.queries[:, cols], r.keys[:, cols], r.values[:, cols], r.grad_block[:, cols]
        decay = inner_decay(rate)
        weights = (dot_right_t(q, k) * decay).astype(bf16)
        score_grad = (dot_right_t(g, v) * decay).astype(bf16)
        dq = dot_plain(score_grad, k) + jnp.exp(-rate * (places + 1.0)) * dot_right_t(g, r.states[at])
        r.pre_grads[:, grad_cols(0, at)] = (dq * r.query_slope[:, cols].astype(f32)).astype(bf16)
        r.pre_grads[:, grad_cols(1, at)] = dot_left_t(score_grad, q).astype(bf16)
        r.pre_grads[:, grad_cols(2, at)] = dot_left_t(weights, g).astype(bf16)

    def to_far(chain, keep, give, target):
        total = chain.result().astype(bf16)
        size = keep.shape[1]
        keep[...] = total[:, :size]
        give[...] = total[:, size:]
        return links.send(give, target, "far")

    ends = [to_far(chain_third, r.third_keep, r.third_give, r.third_far)]
    arrived(state_copies)
    leaving = 1.0 - pair.astype(f32)
    for at in range(heads_all):
        rate = rate_of(at)
        cols = slice(at * HDIM, (at + 1) * HDIM)
        key_decay = leaving * jnp.exp(-rate * (SPAN - 1.0 - places))
        carried = r.state_in[at]
        dk = r.pre_grads[:, grad_cols(1, at)].astype(f32) + key_decay * dot_right_t(r.values[:, cols], carried)
        dv = r.pre_grads[:, grad_cols(2, at)].astype(f32) + key_decay * dot_plain(r.keys[:, cols], carried)
        r.pre_grads[:, grad_cols(1, at)] = (dk * r.key_slope[:, cols].astype(f32)).astype(bf16)
        r.pre_grads[:, grad_cols(2, at)] = (dv * mask).astype(bf16)
    pre_core = links.send(r.pre_grads, r.pre_in, "core")

    triple = 3 * head_width

    def head_terms(rows, cols):
        return dot_right_t(r.pre_grads[rows, :triple], r.heads[0, cols, :]) + dot_right_t(
            r.pre_grads[rows, triple:], r.heads[1, cols, :]
        )

    term_copies = []
    for start in range(0, width, 512):
        for cols in (slice(start, start + 256), slice(start + 256, start + 512)):
            r.terms[:, cols] = head_terms(part(1 - member, row_count), cols).astype(bf16)
        wide = slice(start, start + 512)
        term_copies.append(links.send(r.terms.at[:, wide], r.terms_in.at[:, wide], "mate"))
    ends.append(to_far(chain_first, r.first_keep, r.first_give, r.first_far))
    arrived([pre_core, normed_core])
    links.left(grad_core[1])
    weight_grad(r.second_act, r.normed_t, r.normed_in, r.pre_grads, r.pre_in)
    chain_heads = Chain(links, place, r.second_act, r.heads_half, r.heads_quarter, 768)
    chain_second.middle()
    chain_heads.start()
    for cols in col_tiles:
        r.terms_own[:, cols] = head_terms(part(member, row_count), cols) + dot_right_t(r.gate_grad[...], r.gate[cols, :])

    def to_heads(chain, keep, target):
        total = chain.result().astype(bf16)
        slot = chain.chunk(chain.y, chain.x)
        slot[...] = total
        size = total.shape[0] // 4
        keep[...] = slot[part(own, size), :]
        return [
            links.send(slot.at[part(index, size), :], target.at[i], device)
            for i, (index, device) in enumerate(((mate_block, "mate"), (flipped(own, 1), "far"), (mate_far, "cross")))
        ]

    chain_out.middle()
    arrived([gate_core])
    gate_sum = r.out.at[SPAN:, :]
    lanes = part(member, row_count)
    weight_grad(gate_sum, r.normed_t.at[:, lanes], r.normed_in.at[:, lanes], r.gate_grad, r.gate_grad_in)
    chain_gate = Chain(links, place, gate_sum, r.gate_half, r.gate_quarter, 512)
    ends.append(to_far(chain_second, r.second_keep, r.second_give, r.second_far))
    chain_heads.middle()
    chain_gate.start()
    ends += to_heads(chain_out, r.out_keep, r.out_far)
    arrived(mix_copies)
    r.output[...] = (r.hidden[...] + row_mask * (r.mix[...] + r.mix_in[...].astype(f32))).astype(bf16)
    ends.append(to_far(chain_heads, r.heads_keep, r.heads_give, r.heads_far))
    arrived(term_copies)
    for j in range(2):
        rows = slice(j * chunk_rows, (j + 1) * chunk_rows)
        incoming = r.terms_own[rows, :] + r.terms_in[rows, :].astype(f32)
        grad = r.hidden_grad[rows, :] + norm_back(r.x_rows[rows, :].astype(f32), incoming)
        r.input_grad[rows, :] = grad.astype(bf16)
    chain_gate.middle()
    ends += to_heads(chain_gate, r.gate_keep, r.gate_far)
    arrived(ends)
    links.finish()


def finish_kernel(count, *refs):
    sources, targets, refs = refs[:count], refs[count : count + 10], refs[count + 10 :]
    held, results, in_sems, out_sems = refs[:count], refs[count : count + 8], refs[-2], refs[-1]
    loads = [pltpu.make_async_copy(a, b, in_sems.at[i]) for i, (a, b) in enumerate(zip(sources, held))]
    for load in loads:
        load.start()
    stores = []

    def ready(index):
        for load in loads[2 * index : 2 * index + 2]:
            load.wait()
        return held[2 * index], held[2 * index + 1]

    def store(source, index):
        copy = pltpu.make_async_copy(source, targets[index], out_sems.at[index])
        copy.start()
        stores.append(copy)

    for i, rows in enumerate(ready(0)):
        store(rows, i)
    for i, index in ((1, 9), (2, 7), (3, 8)):
        keep, far = ready(i)
        results[index - 2][...] = (keep[...].astype(f32) + far[...].astype(f32)).T
        store(results[index - 2], index)
    keep, far = ready(4)
    size = targets[2].shape[1]
    for i in range(3):
        cols = slice(i * size, (i + 1) * size)
        results[i][...] = keep[:, cols].astype(f32) + far[:, cols].astype(f32)
        store(results[i], 2 + i)
    for i in (5, 6):
        keep, others = ready(i)
        total = keep[...].astype(f32)
        for j in range(3):
            total = total + others[j].astype(f32)
        results[i - 2][...] = total
        store(results[i - 2], i)
    for copy in stores:
        copy.wait()


def fused_shards(
    layer_input, w_query, w_key, w_value, w_gate, w_out, w_first, w_second, w_third,
    decay_rates, seq_lengths, cotangent,
):
    group_rows, width = layer_input.shape
    row_count = cotangent.shape[0]
    heads = decay_rates.shape[0]
    head_width = w_query.shape[1]
    units = w_third.shape[0]
    shape = jax.ShapeDtypeStruct
    share = width // 8
    both = 2 * head_width
    triple = 3 * head_width
    inputs = dict(
        lengths=seq_lengths, decay_rates=decay_rates, layer_input=layer_input, w_query=w_query, w_key=w_key, w_value=w_value,
        w_gate=w_gate, w_out=w_out, w_first=w_first.T, w_second=w_second.T, w_third=w_third, cotangent=cotangent,
    )
    rows_shape = shape((row_count, width), bf16)
    ffn_shape = shape((share, units), bf16)
    head_shape = shape((share, triple), bf16)
    dense_shape = shape((share // 4, width), bf16)
    dense_far = shape((3, share // 4, width), bf16)
    outputs = dict(
        output=rows_shape, input_grad=rows_shape,
        third_keep=ffn_shape, third_far=ffn_shape, first_keep=ffn_shape, first_far=ffn_shape,
        second_keep=ffn_shape, second_far=ffn_shape, heads_keep=head_shape, heads_far=head_shape,
        gate_keep=dense_shape, gate_far=dense_far, out_keep=dense_shape, out_far=dense_far,
    )
    low = lambda *dims: pltpu.VMEM(dims, bf16)
    wide = lambda *dims: pltpu.VMEM(dims, f32)
    half = width // 2
    scratch = dict(
        x=low(group_rows, width), normed=low(group_rows, width),
        heads=low(2, width, triple), gate=low(width, width), out=low(width, width),
        first=low(2 * units, width), second=low(2 * units, width), third=low(2 * units, width),
        upstream=low(row_count, width), rates=wide(8, 128), rates_far=wide(8, 128),
        queries=low(SPAN, both), keys=low(SPAN, both), values=low(SPAN, both),
        query_slope=low(SPAN, both), key_slope=low(SPAN, both), states=low(2 * heads, HDIM, HDIM),
        attention=low(SPAN, both), attention_rows=low(row_count, width), gate_pre=wide(row_count, width),
        hidden=wide(row_count, width),
        hidden_low=low(SPAN, width), last=low(SPAN, width),
        first_act=low(SPAN, 2 * units), second_act=low(SPAN, 2 * triple), product=low(SPAN, 2 * units),
        hidden_grad=wide(row_count, width), mix=wide(row_count, width), norm_in=low(row_count, width),
        mix_in=low(row_count, width), grad_block=low(SPAN, both),
        state_grad=low(2 * heads, HDIM, HDIM), state_in=low(2 * heads, HDIM, HDIM),
        pre_grads=low(SPAN, 2 * triple), terms_in=low(row_count, width),
        terms_own=wide(row_count, width),
        normed_t=low(half, SPAN), normed_give=low(half, SPAN), normed_in=low(half, SPAN),
        last_t=low(half, SPAN), last_give=low(half, SPAN), last_in=low(half, SPAN),
        hidden_t=low(half, SPAN), hidden_give=low(half, SPAN), hidden_in=low(half, SPAN),
        gated_t=low(half, row_count), gated_give=low(half, row_count), gated_in=low(half, row_count),
        product_in=low(SPAN, 2 * units), first_in=low(SPAN, 2 * units), second_in=low(SPAN, 2 * units),
        pre_in=low(SPAN, 2 * triple), branch_in=low(row_count, width), gate_grad_in=low(row_count, width),
        third_sum=low(half, 2 * units),
        third_half=low(2 * share, 2 * units), first_half=low(2 * share, 2 * units),
        second_half=low(2 * share, 2 * units), heads_half=low(2 * share, 2 * triple),
        gate_half=low(2 * share, width), out_half=low(2 * share, width),
        third_quarter=low(share, 2 * units), first_quarter=low(share, 2 * units),
        second_quarter=low(share, 2 * units), heads_quarter=low(share, 2 * triple),
        gate_quarter=low(share, width), out_quarter=low(share, width),
        third_give=low(share, units), first_give=low(share, units), second_give=low(share, units),
        heads_give=low(share, triple),
        local_sems=pltpu.SemaphoreType.DMA((16,)),
        send_sems=pltpu.SemaphoreType.DMA((144,)), recv_sems=pltpu.SemaphoreType.DMA((144,)),
    )
    results = pl.pallas_call(
        functools.partial(layer_kernel, list(inputs) + list(outputs) + list(scratch)),
        out_shape=list(outputs.values()),
        in_specs=[smem(), smem()] + [pl.BlockSpec(memory_space=pl.ANY)] * (len(inputs) - 2),
        out_specs=[vmem()] * len(outputs),
        scratch_shapes=list(scratch.values()),
        compiler_params=pltpu.CompilerParams(
            collective_id=0, has_side_effects=True, vmem_limit_bytes=VMEM_ALL
        ),
        name="layer",
    )(*inputs.values())
    transposed_shape = shape((units, share), f32)
    finals = [rows_shape] * 2 + [shape((share, head_width), f32)] * 3 + [shape((share // 4, width), f32)] * 2
    finals += [transposed_shape] * 3
    place_any = pl.BlockSpec(memory_space=pltpu.HBM)
    results = pl.pallas_call(
        functools.partial(finish_kernel, len(results)),
        out_shape=finals,
        in_specs=[place_any] * len(results),
        out_specs=[place_any] * 10,
        scratch_shapes=[pltpu.VMEM(a.shape, a.dtype) for a in list(results) + finals[2:]]
        + [pltpu.SemaphoreType.DMA((len(results),)), pltpu.SemaphoreType.DMA((10,))],
        compiler_params=pltpu.CompilerParams(vmem_limit_bytes=VMEM_ALL),
        name="finish",
    )(*results)
    return (*results[:7], results[7].T, results[8].T, results[9])


def solution(mesh):
    placed = (
        P("dp", None),
        P(None, "head"),
        P(None, "head"),
        P(None, "head"),
        P(),
        P(),
        P(None, "head"),
        P(None, "head"),
        P("head", None),
        P("head"),
        P("dp"),
        P(("dp", "head"), None),
    )
    n_dp, n_head = mesh.shape["dp"], mesh.shape["head"]
    body = fused_shards if (n_dp, n_head) == (8, 4) else functools.partial(shards, n_dp, n_head)
    return jax.shard_map(
        body,
        mesh=mesh,
        in_specs=placed,
        out_specs=(
            P(("dp", "head"), None),
            P(("dp", "head"), None),
            P("dp", "head"),
            P("dp", "head"),
            P("dp", "head"),
            P(("dp", "head"), None),
            P(("dp", "head"), None),
            P("dp", "head"),
            P("dp", "head"),
            P("head", "dp"),
        ),
        check_vma=False,
    )
```

```python
import functools
import types

import jax
import jax.numpy as jnp
from jax import lax
from jax.experimental import pallas as pl
from jax.experimental.pallas import tpu as pltpu
from jax.sharding import PartitionSpec as P

SPAN = 512
HDIM = 128

epsilon = 1e-06
bf16 = jnp.bfloat16
f32 = jnp.float32
VMEM_LIMIT = 48 * 2**20
VMEM_ALL = 63 * 2**20


def inverse_rms(values):
    return lax.rsqrt(jnp.mean(values * values, axis=-1, keepdims=True) + epsilon)


def normalize(values):
    return values * inverse_rms(values)


def norm_back(values, incoming):
    inverse = inverse_rms(values)
    unit_rows = values * inverse
    return inverse * (incoming - unit_rows * jnp.mean(incoming * unit_rows, axis=-1, keepdims=True))


def dot_plain(left, right):
    return jnp.dot(left, right, preferred_element_type=f32)


def dot_right_t(left, right):
    return lax.dot_general(left, right, (((1,), (1,)), ((), ())), preferred_element_type=f32)


def dot_left_t(left, right):
    return lax.dot_general(left, right, (((0,), (0,)), ((), ())), preferred_element_type=f32)


def transposed(values):
    return values.T


def column(length):
    return lax.broadcasted_iota(jnp.int32, (length, 1), 0)


def inner_decay(rate):
    rows = lax.broadcasted_iota(jnp.int32, (SPAN, SPAN), 0)
    cols = lax.broadcasted_iota(jnp.int32, (SPAN, SPAN), 1)
    offset = rows - cols
    return jnp.where(offset >= 0, jnp.exp(-rate * jnp.maximum(offset, 0).astype(f32)), 0.0)


def attend_kernel(
    meta, rates, x, w_own_q, w_own_k, w_own_v, w_other,
    normed, attention, queries, keys, values, query_slope, key_slope, states,
):
    pair, length = meta[0], meta[1]
    start = pl.multiple_of(pair * SPAN, SPAN)
    rows = x.shape[0]
    head_width = w_own_q.shape[1]

    def norm_step(i, carry):
        place = pl.ds(pl.multiple_of(i * 128, 128), 128)
        normed[place, :] = normalize(x[place, :].astype(f32)).astype(bf16)
        return carry

    lax.fori_loop(0, rows // 128, norm_step, 0)
    block = normed[pl.ds(start, SPAN), :]
    mask = (start + column(SPAN) < length).astype(f32)
    early_mask = (column(SPAN) < length).astype(f32) * pair.astype(f32)
    early = normed[0:SPAN, :]
    places = column(SPAN).astype(f32)
    for part in range(2):
        if part == 0:
            wq, wk, wv = w_own_q[...], w_own_k[...], w_own_v[...]
        else:
            wq, wk, wv = (w_other[:, i * head_width : (i + 1) * head_width] for i in range(3))
        pre_query = dot_plain(block, wq)
        pre_key = dot_plain(block, wk)
        pre_value = dot_plain(block, wv)
        sigmoid_query = jax.nn.sigmoid(pre_query)
        sigmoid_key = jax.nn.sigmoid(pre_key)
        query = (pre_query * sigmoid_query).astype(bf16)
        key = (mask * (pre_key * sigmoid_key)).astype(bf16)
        value = (mask * pre_value).astype(bf16)
        wide = slice(part * head_width, (part + 1) * head_width)
        query_slope[:, wide] = (sigmoid_query * (1.0 + pre_query * (1.0 - sigmoid_query))).astype(bf16)
        key_slope[:, wide] = (mask * (sigmoid_key * (1.0 + pre_key * (1.0 - sigmoid_key)))).astype(bf16)
        queries[:, wide] = query
        keys[:, wide] = key
        values[:, wide] = value
        early_key = dot_plain(early, wk)
        early_key = early_mask * (early_key * jax.nn.sigmoid(early_key)).astype(bf16).astype(f32)
        early_value = (early_mask * dot_plain(early, wv)).astype(bf16)
        for head in range(head_width // HDIM):
            index = part * (head_width // HDIM) + head
            rate = rates[index]
            cols = slice(head * HDIM, (head + 1) * HDIM)
            q, k, v = query[:, cols], key[:, cols], value[:, cols]
            scores = dot_right_t(q, k)
            weights = (scores * inner_decay(rate)).astype(bf16)
            keyed = (early_key[:, cols] * jnp.exp(-rate * (SPAN - 1.0 - places))).astype(bf16)
            state = dot_left_t(keyed, early_value[:, cols])
            states[index] = state
            decayed = (q.astype(f32) * jnp.exp(-rate * (places + 1.0))).astype(bf16)
            out = dot_plain(weights, v) + dot_plain(decayed, state.astype(bf16))
            attention[:, index * HDIM : (index + 1) * HDIM] = out.astype(bf16)


def state_kernel(rates, queries, upstream, state_grad):
    places = column(SPAN).astype(f32)
    for index in range(state_grad.shape[0]):
        cols = slice(index * HDIM, (index + 1) * HDIM)
        decayed = (queries[:, cols].astype(f32) * jnp.exp(-rates[index] * (places + 1.0))).astype(bf16)
        state_grad[index] = dot_left_t(decayed, upstream[:, cols])


def attend_back_kernel(
    meta, rates, queries, keys, values, upstream, query_slope, key_slope, states, state_grad, pre_grads
):
    pair, length = meta[0], meta[1]
    mask = (pair * SPAN + column(SPAN) < length).astype(f32)
    places = column(SPAN).astype(f32)
    heads = states.shape[0]
    half = heads // 2
    for index in range(heads):
        rate = rates[index]
        cols = slice(index * HDIM, (index + 1) * HDIM)
        q, k, v, g = queries[:, cols], keys[:, cols], values[:, cols], upstream[:, cols]
        decay = inner_decay(rate)
        query_decay = jnp.exp(-rate * (places + 1.0))
        key_decay = jnp.exp(-rate * (SPAN - 1.0 - places))
        state = states[index].astype(bf16)
        carried = state_grad[index].astype(bf16)
        weights = (dot_right_t(q, k) * decay).astype(bf16)
        score_grad = (dot_right_t(g, v) * decay).astype(bf16)
        dq = dot_plain(score_grad, k) + query_decay * dot_right_t(g, state)
        dk = dot_left_t(score_grad, q) + key_decay * dot_right_t(v, carried)
        dv = dot_left_t(weights, g) + key_decay * dot_plain(k, carried)
        base = (index // half) * (3 * half * HDIM) + (index % half) * HDIM
        pre_grads[:, base : base + HDIM] = (dq * query_slope[:, cols].astype(f32)).astype(bf16)
        base += half * HDIM
        pre_grads[:, base : base + HDIM] = (dk * key_slope[:, cols].astype(f32)).astype(bf16)
        base += half * HDIM
        pre_grads[:, base : base + HDIM] = (dv * mask).astype(bf16)


def vmem():
    return pl.BlockSpec(memory_space=pltpu.VMEM)


def smem():
    return pl.BlockSpec(memory_space=pltpu.SMEM)


def local_call(body, name, out_shapes, args, scalars, flops):
    size = sum(int(a.size) * a.dtype.itemsize for a in list(args) + list(out_shapes))
    return pl.pallas_call(
        body,
        out_shape=out_shapes,
        in_specs=[smem()] * scalars + [vmem()] * (len(args) - scalars),
        out_specs=[vmem()] * len(out_shapes),
        compiler_params=pltpu.CompilerParams(vmem_limit_bytes=VMEM_LIMIT),
        cost_estimate=pl.CostEstimate(flops=flops, bytes_accessed=size, transcendentals=0),
        name=name,
    )(*args)


def shards(
    n_dp, n_head,
    layer_input, w_query, w_key, w_value, w_gate, w_out, w_first, w_second, w_third,
    decay_rates, seq_lengths, cotangent,
):
    group_rows, width = layer_input.shape
    row_count = cotangent.shape[0]
    heads = decay_rates.shape[0]
    head_width = w_query.shape[1]
    place = lax.axis_index("dp")
    own = lax.axis_index("head")
    member, pair = own % 2, own // 2
    bits = n_dp.bit_length() - 1
    length = seq_lengths[0]

    def to_mate(array, bit):
        return lax.ppermute(array, "head", [(i, i ^ bit) for i in range(n_head)])

    def across(array, bit):
        return lax.ppermute(array, "dp", [(i, i ^ (1 << bit)) for i in range(n_dp)])

    def gathered(weight, axis):
        size = weight.shape[axis] // n_dp
        share = lax.dynamic_slice_in_dim(weight, place * size, size, axis)
        return lax.all_gather(to_mate(share, 2), "dp", axis=axis, tiled=True)

    w_heads = jnp.concatenate([w_query, w_key, w_value], axis=1)
    w_heads_other = gathered(w_heads, 0)
    w_first_other = gathered(w_first, 0)
    w_second_other = gathered(w_second, 0)
    w_third_other = gathered(w_third, 1)
    rates = jnp.concatenate([decay_rates, to_mate(decay_rates, 2)])

    block_start = pair * SPAN
    row_start = own * row_count
    positions = jnp.arange(row_count, dtype=jnp.int32)[:, None]
    row_mask = (row_start + positions < length).astype(f32)
    upstream = cotangent.astype(f32)
    last_own = (row_mask * upstream).astype(bf16)
    last_mate = to_mate(last_own, 1)

    meta = jnp.stack([pair, length]).astype(jnp.int32)
    both = 2 * head_width
    shape = jax.ShapeDtypeStruct
    block_shape = shape((SPAN, both), bf16)
    normed, attention_block, queries, keys, values, query_slope, key_slope, states = local_call(
        attend_kernel, "attend",
        [shape(layer_input.shape, bf16)] + [block_shape] * 6 + [shape((2 * heads, HDIM, HDIM), f32)],
        [meta, rates, layer_input, w_query, w_key, w_value, w_heads_other], 2, 6 * 10**9,
    )

    def rows_of(array, index):
        return lax.dynamic_slice_in_dim(array, index * row_count, row_count, 0)

    def ordered(mine, other):
        even, odd = jnp.where(member == 0, mine, other), jnp.where(member == 0, other, mine)
        flip = lambda a: jnp.where(pair == 0, a, jnp.concatenate([a[:, head_width:], a[:, :head_width]], axis=1))
        even, odd = flip(even), flip(odd)
        return jnp.concatenate(
            [even[:, :head_width], odd[:, :head_width], even[:, head_width:], odd[:, head_width:]], axis=1
        )

    def pieces(array):
        cut = [array[:, i * head_width : (i + 1) * head_width] for i in range(4)]
        even, odd = jnp.concatenate([cut[0], cut[2]], axis=1), jnp.concatenate([cut[1], cut[3]], axis=1)
        flip = lambda a: jnp.where(pair == 0, a, jnp.concatenate([a[:, head_width:], a[:, :head_width]], axis=1))
        even, odd = flip(even), flip(odd)
        return jnp.where(member == 0, even, odd), jnp.where(member == 0, odd, even)

    received = to_mate(rows_of(attention_block, 1 - member), 1)
    attention = ordered(rows_of(attention_block, member), received).astype(f32)
    attention_norm = normalize(attention)
    rows_low = rows_of(normed, own)
    input_rows = rows_of(layer_input, own).astype(f32)
    gate_pre = dot_plain(rows_low, w_gate)
    gated = (attention_norm * gate_pre).astype(bf16)
    hidden = input_rows + row_mask * dot_plain(gated, w_out)
    hidden_low = normalize(hidden).astype(bf16)
    hidden_mate = to_mate(hidden_low, 1)

    w_first_all = jnp.concatenate([w_first, w_first_other], axis=1)
    w_second_all = jnp.concatenate([w_second, w_second_other], axis=1)
    w_third_all = jnp.concatenate([w_third, w_third_other], axis=0)

    def forward_rows(rows_in):
        first, second = dot_plain(rows_in, w_first_all), dot_plain(rows_in, w_second_all)
        return first.astype(bf16), second.astype(bf16), (first * second).astype(bf16)

    def backward_rows(last, first, second):
        product_grad = dot_right_t(last, w_third_all)
        first_grad = (product_grad * second.astype(f32)).astype(bf16)
        second_grad = (product_grad * first.astype(f32)).astype(bf16)
        return first_grad, second_grad, dot_right_t(first_grad, w_first_all) + dot_right_t(second_grad, w_second_all)

    first_mate, second_mate, product_mate = forward_rows(hidden_mate)
    first_grad_mate, second_grad_mate, norm_grad_mate = backward_rows(last_mate, first_mate, second_mate)
    norm_grad_in = to_mate(norm_grad_mate.astype(bf16), 1)
    mix_in = to_mate(dot_plain(product_mate, w_third_all).astype(bf16), 1)
    first_own, second_own, product_own = forward_rows(hidden_low)
    first_grad_own, second_grad_own, norm_grad_own = backward_rows(last_own, first_own, second_own)
    hidden_grad = upstream + norm_back(hidden, norm_grad_own + norm_grad_in.astype(f32))
    mixed = dot_plain(product_own, w_third_all) + mix_in.astype(f32)
    output = (hidden + row_mask * mixed).astype(bf16)

    branch_grad = (row_mask * hidden_grad).astype(bf16)
    gated_grad = dot_right_t(branch_grad, w_out)
    gate_grad = (gated_grad * attention_norm).astype(bf16)
    attention_grad = norm_back(attention, gated_grad * gate_pre).astype(bf16)
    mine, for_mate = pieces(attention_grad)
    from_mate = to_mate(for_mate, 1)
    grad_block = jnp.concatenate(
        [jnp.where(member == 0, mine, from_mate), jnp.where(member == 0, from_mate, mine)], axis=0
    )
    state_shape = shape((2 * heads, HDIM, HDIM), f32)
    (state_grad,) = local_call(
        state_kernel, "state_grad", [state_shape], [rates, queries, grad_block], 1, 10**8
    )
    swapped = jnp.concatenate([state_grad[heads:], state_grad[:heads]], axis=0)
    carried = lax.ppermute(swapped, "head", [(i, i - 2) for i in range(2, n_head)])
    (pre_grads,) = local_call(
        attend_back_kernel, "attend_back", [shape((SPAN, 3 * both), bf16)],
        [meta, rates, queries, keys, values, grad_block, query_slope, key_slope, states, carried], 2, 2 * 10**9,
    )
    head_terms = dot_right_t(pre_grads[:, : 3 * head_width], w_heads) + dot_right_t(
        pre_grads[:, 3 * head_width :], w_heads_other
    )
    head_terms = head_terms.astype(bf16)
    terms_in = to_mate(rows_of(head_terms, 1 - member), 1)
    input_norm_grad = (
        rows_of(head_terms, member).astype(f32) + terms_in.astype(f32) + dot_right_t(gate_grad, w_gate)
    )
    input_grad = (hidden_grad + norm_back(input_rows, input_norm_grad)).astype(bf16)

    def summed(left, right, order):
        left = left.reshape((left.shape[0],) + (2,) * bits + (width // n_dp,))

        def pick(array, axis, bit, which):
            side = (place // (1 << bit)) % 2
            return lax.dynamic_index_in_dim(array, side if which else 1 - side, axis, keepdims=False)

        left_axis = lambda bit, done: 1 + (bits - 1 - bit) - sum(1 for b in done if b > bit)
        first_bit = order[0]
        make = lambda which: dot_left_t(
            pick(left, left_axis(first_bit, []), first_bit, which).reshape(left.shape[0], width // 2), right
        ).astype(bf16)
        arrived = across(make(False), first_bit)
        total = (make(True).astype(f32) + arrived.astype(f32)).astype(bf16)
        total = total.reshape((2,) * (bits - 1) + (width // n_dp, right.shape[1]))
        done = [first_bit]
        for bit in order[1:]:
            axis = left_axis(bit, done) - 1
            arrived = across(pick(total, axis, bit, False), bit)
            total = (pick(total, axis, bit, True).astype(f32) + arrived.astype(f32)).astype(bf16)
            done.append(bit)
        return total

    def with_mate(total):
        size = total.shape[1] // 2
        return total[:, :size].astype(f32) + to_mate(total[:, size:], 2).astype(f32)

    def over_heads(total):
        for bit in (1, 2):
            cut = total.reshape((2, -1) + total.shape[1:]) if bit == 2 else total.reshape((2, 2, -1) + total.shape[1:])
            side = (own // bit) % 2
            axis = 0 if bit == 2 else 1
            arrived = to_mate(lax.dynamic_index_in_dim(cut, 1 - side, axis, keepdims=False), bit)
            total = lax.dynamic_index_in_dim(cut, side, axis, keepdims=False).astype(f32) + arrived.astype(f32)
            if bit == 1:
                total = total.astype(bf16).reshape((-1,) + total.shape[2:])
        return total

    up = list(range(bits))
    down = [0] + up[:0:-1]
    stack = lambda a, b: jnp.concatenate([a, b], axis=0)
    hidden_all = stack(hidden_low, hidden_mate)
    last_all = stack(last_own, last_mate)
    grad_third_t = with_mate(summed(last_all, stack(product_own, product_mate), up))
    grad_first = with_mate(summed(hidden_all, stack(first_grad_own, first_grad_mate), up))
    grad_second = with_mate(summed(hidden_all, stack(second_grad_own, second_grad_mate), down))
    grad_out = over_heads(summed(gated, branch_grad, down))
    grad_gate = over_heads(summed(rows_low, gate_grad, up))
    normed_block = lax.dynamic_slice_in_dim(normed, block_start, SPAN, 0)
    grad_heads = with_mate(summed(normed_block, pre_grads, down))
    return (
        output,
        input_grad,
        grad_heads[:, :head_width],
        grad_heads[:, head_width : 2 * head_width],
        grad_heads[:, 2 * head_width :],
        grad_gate,
        grad_out,
        grad_first,
        grad_second,
        grad_third_t.T,
    )


MESH = pl.DeviceIdType.MESH


def flipped(index, bit):
    return index + (1 << bit) * (1 - 2 * ((index // (1 << bit)) % 2))


def part(index, size):
    return pl.ds(pl.multiple_of(index * size, size), size)


class Links:
    def __init__(self, others, send_sems, recv_sems):
        self.others, self.send_sems, self.recv_sems, self.started = others, send_sems, recv_sems, []

    def send(self, source, target, device):
        index = len(self.started)
        copy = pltpu.make_async_remote_copy(
            src_ref=source,
            dst_ref=target,
            send_sem=self.send_sems.at[index],
            recv_sem=self.recv_sems.at[index],
            device_id=self.others[device],
            device_id_type=MESH,
        )
        copy.start()
        self.started.append(copy)
        copy.sent = False
        return copy

    def left(self, copies):
        for copy in copies:
            if not copy.sent:
                copy.wait_send()
                copy.sent = True

    def finish(self):
        self.left(self.started)


def arrived(copies):
    for copy in copies:
        copy.wait_recv()


class Gather:
    def __init__(self, links, place, pieces, halves):
        self.links, self.pieces, self.halves = links, pieces, halves
        self.places = [place, flipped(place, 1), flipped(place, 2), flipped(flipped(place, 1), 2)]
        self.to_core, self.near, self.crossing, self.fetched = [], {}, {}, {}

    def pass_on(self, piece, which, device):
        ref = self.pieces[piece](self.places[which])
        return self.links.send(ref, ref, device)

    def fetch(self, sources):
        for i, source in enumerate(sources):
            self.fetched[i] = self.links.send(source, self.pieces[i](self.places[0]), "far")

    def spread(self, piece=0):
        arrived([self.fetched[piece]])
        self.near[piece] = (self.pass_on(piece, 0, "x"), self.pass_on(piece, 0, "y"))
        self.to_core.append(self.pass_on(piece, 0, "core"))

    def cross(self, piece=0):
        crossing = []
        for i, (half, device) in enumerate(zip(self.halves, ("y", "x"))):
            arrived([self.near[piece][i]])
            ref = half(self.pieces[piece](self.places[1 + i]))
            crossing.append(self.links.send(ref, ref, device))
            self.to_core.append(self.pass_on(piece, 1 + i, "core"))
        self.crossing[piece] = crossing

    def last(self, piece=0):
        arrived(self.crossing[piece])
        self.to_core.append(self.pass_on(piece, 3, "core"))

    def done(self):
        arrived(self.to_core)


class Chain:
    def __init__(self, links, place, total, halves_in, quarter_in, cut, orders=("xy", "yx")):
        self.links, self.total, self.halves_in, self.quarter_in = links, total, halves_in, quarter_in
        size = total.shape[1]
        self.parts = [(slice(0, cut), orders[0]), (slice(cut, size), orders[1])]
        self.x, self.y = (place // 2) % 2, (place // 4) % 2
        self.rows = quarter_in.shape[0]
        self.waits = []

    def chunk(self, y, x, cols=slice(None)):
        return self.total.at[part(2 * y + x, self.rows), cols]

    def start(self):
        links, rows = self.links, self.rows
        for cols, order in self.parts:
            if order == "xy":
                self.waits.append([
                    links.send(self.chunk(y, 1 - self.x, cols), self.halves_in.at[y * rows : (y + 1) * rows, cols], "x")
                    for y in range(2)
                ])
            else:
                give = self.total.at[part(1 - self.y, 2 * rows), cols]
                self.waits.append([links.send(give, self.halves_in.at[:, cols], "y")])

    def add(self, place, arrived_part):
        place[...] = (place[...].astype(f32) + arrived_part.astype(f32)).astype(bf16)

    def middle(self):
        rows, x, y = self.rows, self.x, self.y
        keep, waits = [], []
        for (cols, order), before in zip(self.parts, self.waits):
            arrived(before)
            give, device, index = (
                (self.chunk(1 - y, x, cols), "y", y) if order == "xy" else (self.chunk(y, 1 - x, cols), "x", x)
            )
            self.add(give, self.halves_in[part(1 - index, rows), cols])
            waits.append([self.links.send(give, self.quarter_in.at[:, cols], device)])
            keep.append((cols, index))
        for cols, index in keep:
            self.add(self.chunk(y, x, cols), self.halves_in[part(index, rows), cols])
        self.waits = waits

    def result(self):
        for before in self.waits:
            arrived(before)
        return self.chunk(self.y, self.x)[...].astype(f32) + self.quarter_in[...].astype(f32)


def layer_kernel(names, *refs):
    r = types.SimpleNamespace(**dict(zip(names, refs)))
    place, own = lax.axis_index("dp"), lax.axis_index("head")
    pair, member, core = own // 2, own % 2, place % 2
    length = r.lengths[0]
    group_rows, width = r.layer_input.shape
    row_count = r.cotangent.shape[0]
    head_width = r.w_query.shape[1]
    block_heads = head_width // HDIM
    hidden_size = r.w_third.shape[0]
    share_size = width // 8
    chunk_rows = row_count // 2
    r.gated, r.x_rows = (r.x.at[i * row_count : (i + 1) * row_count, :] for i in (2, 3))
    r.branch, r.gate_grad, r.attention_grad, r.terms = (
        r.normed.at[i * row_count : (i + 1) * row_count, :] for i in range(4)
    )

    copies = []

    def load(source, target):
        copy = pltpu.make_async_copy(source, target, r.local_sems.at[len(copies)])
        copy.start()
        copies.append(copy)
        return copy

    load_cotangent = load(r.cotangent, r.upstream)
    load_x = load(r.layer_input, r.x)
    load_heads = [
        load(weight, r.heads.at[0, :, i * head_width : (i + 1) * head_width])
        for i, weight in enumerate((r.w_query, r.w_key, r.w_value))
    ]
    load_gate = load(r.w_gate, r.gate)
    load_out = load(r.w_out, r.out)
    load_first = load(r.w_first, r.first.at[:hidden_size, :])
    load_second = load(r.w_second, r.second.at[:hidden_size, :])
    load_third = load(r.w_third, r.third.at[:hidden_size, :])

    others = {
        "core": (flipped(place, 0), own),
        "x": (flipped(place, 1), own),
        "y": (flipped(place, 2), own),
        "mate": (place, flipped(own, 0)),
        "far": (place, flipped(own, 1)),
        "cross": (place, 3 - own),
    }
    barrier = pltpu.get_barrier_semaphore()
    for device in others.values():
        pl.semaphore_signal(barrier, inc=1, device_id=device, device_id_type=MESH)
    pl.semaphore_wait(barrier, len(others))
    links = Links(others, r.send_sems, r.recv_sems)

    head_piece = lambda j: lambda i: r.heads.at[1, part(i, share_size), j * head_width : (j + 1) * head_width]
    ffn_piece = lambda ref: lambda i: ref.at[hidden_size:, part(i, share_size)]
    row_halves = [lambda ref, j=j: ref.at[j * share_size // 2 : (j + 1) * share_size // 2, :] for j in range(2)]
    unit_halves = [lambda ref, j=j: ref.at[j * hidden_size // 2 : (j + 1) * hidden_size // 2, :] for j in range(2)]
    gather_heads = Gather(links, place, [head_piece(j) for j in (1, 2, 0)], row_halves)
    gather_first = Gather(links, place, [ffn_piece(r.first)], unit_halves)
    gather_second = Gather(links, place, [ffn_piece(r.second)], unit_halves)
    gather_third = Gather(links, place, [ffn_piece(r.third)], unit_halves)

    def fetch(gather, source):
        gather.fetch([source.at[:, part(place, share_size)]])

    row_mask = (own * row_count + column(row_count) < length).astype(f32)
    load_cotangent.wait()
    r.last[:row_count, :] = (row_mask * r.upstream[...].astype(f32)).astype(bf16)

    def send_last(j):
        source = slice(j * chunk_rows, (j + 1) * chunk_rows)
        target = slice(row_count + j * chunk_rows, row_count + (j + 1) * chunk_rows)
        return links.send(r.last.at[source, :], r.last.at[target, :], "mate")

    last_copies = [send_last(0)]
    gather_heads.fetch([weight.at[part(place, share_size), :] for weight in (r.w_key, r.w_value, r.w_query)])
    for i in range(block_heads):
        r.rates[i : i + 1, :] = jnp.full((1, 128), r.decay_rates[i], f32)
    rates_copy = links.send(r.rates, r.rates_far, "far")
    fetch(gather_first, r.w_first)
    last_copies.append(send_last(1))

    load_x.wait()

    def norm_step(i, carry):
        where = part(i, 128)
        r.normed[where, :] = normalize(r.x[where, :].astype(f32)).astype(bf16)
        return carry

    lax.fori_loop(0, group_rows // 128, norm_step, 0)
    r.x_rows[...] = r.x[part(own, row_count), :]
    block_rows = part(pair, SPAN)
    mask = (pair * SPAN + column(SPAN) < length).astype(f32)
    early_mask = (column(SPAN) < length).astype(f32) * pair.astype(f32)
    places = column(SPAN).astype(f32)

    def project(index):
        wide = slice(index * head_width, (index + 1) * head_width)
        weights = [r.heads.at[index, :, i * head_width : (i + 1) * head_width] for i in range(3)]
        block = r.normed[block_rows, :]
        early = r.normed[0:SPAN, :]
        pre_query = dot_plain(block, weights[0][...])
        sigmoid = jax.nn.sigmoid(pre_query)
        r.queries[:, wide] = (pre_query * sigmoid).astype(bf16)
        r.query_slope[:, wide] = (sigmoid * (1.0 + pre_query * (1.0 - sigmoid))).astype(bf16)
        pre_key = dot_plain(block, weights[1][...])
        sigmoid = jax.nn.sigmoid(pre_key)
        r.keys[:, wide] = (mask * (pre_key * sigmoid)).astype(bf16)
        r.key_slope[:, wide] = (mask * (sigmoid * (1.0 + pre_key * (1.0 - sigmoid)))).astype(bf16)
        r.values[:, wide] = (mask * dot_plain(block, weights[2][...])).astype(bf16)
        early_key = dot_plain(early, weights[1][...])
        early_key = early_mask * (early_key * jax.nn.sigmoid(early_key)).astype(bf16).astype(f32)
        early_value = (early_mask * dot_plain(early, weights[2][...])).astype(bf16)
        return early_key, early_value

    def rate_of(index):
        ref = r.rates if index < block_heads else r.rates_far
        return ref[index % block_heads : index % block_heads + 1, 0:1]

    def attend(index, early_key, early_value):
        for head in range(block_heads):
            at = index * block_heads + head
            rate = rate_of(at)
            cols = slice(at * HDIM, (at + 1) * HDIM)
            early = slice(head * HDIM, (head + 1) * HDIM)
            q, k, v = r.queries[:, cols], r.keys[:, cols], r.values[:, cols]
            weights = (dot_right_t(q, k) * inner_decay(rate)).astype(bf16)
            keyed = (early_key[:, early] * jnp.exp(-rate * (SPAN - 1.0 - places))).astype(bf16)
            state = dot_left_t(keyed, early_value[:, early])
            r.states[at] = state.astype(bf16)
            decayed = (q.astype(f32) * jnp.exp(-rate * (places + 1.0))).astype(bf16)
            out = dot_plain(weights, v) + dot_plain(decayed, state.astype(bf16))
            r.attention[:, cols] = out.astype(bf16)
        wide = slice(index * head_width, (index + 1) * head_width)
        block = own if index == 0 else flipped(own, 1)
        target = r.attention_rows.at[:, part(block, head_width)]
        copy = links.send(r.attention.at[part(1 - member, row_count), wide], target, "mate")
        target[...] = r.attention[part(member, row_count), wide]
        return copy

    def split_transpose(source, keep, give, columns):
        for e in range(4):
            rows = slice(e * share_size, (e + 1) * share_size)
            keep[rows, columns] = transposed(source[:, part(2 * e + core, share_size)])
            give[rows, columns] = transposed(source[:, part(2 * e + 1 - core, share_size)])

    for copy in load_heads:
        copy.wait()
    gather_heads.spread(0)
    early = project(0)
    gather_heads.spread(1)
    gather_heads.spread(2)
    gather_heads.cross(0)
    attention_own = attend(0, *early)
    fetch(gather_second, r.w_second)
    gather_heads.cross(1)
    gather_heads.cross(2)
    gather_heads.last(0)
    split_transpose(r.normed.at[block_rows, :], r.normed_t, r.normed_give, slice(0, SPAN))
    normed_core = links.send(r.normed_give, r.normed_in, "core")
    gather_heads.last(1)
    gather_heads.last(2)
    gather_first.spread()
    load_gate.wait()
    r.gate_pre[...] = dot_plain(r.normed[part(own, row_count), :], r.gate[...])
    gather_heads.done()
    rates_copy.wait_recv()
    early = project(1)
    gather_first.cross()
    attention_far = attend(1, *early)
    fetch(gather_third, r.w_third)
    split_transpose(r.last.at[:row_count, :], r.last_t, r.last_give, slice(0, row_count))
    gather_first.last()
    arrived(last_copies)
    split_transpose(r.last.at[row_count:, :], r.last_t, r.last_give, slice(row_count, 2 * row_count))
    last_core = links.send(r.last_give, r.last_in, "core")
    gather_second.spread()
    load_out.wait()
    arrived([attention_own, attention_far])

    hidden_copies = []
    for j in range(2):
        rows = slice(j * chunk_rows, (j + 1) * chunk_rows)
        gated = (normalize(r.attention_rows[rows, :].astype(f32)) * r.gate_pre[rows, :]).astype(bf16)
        r.gated[rows, :] = gated
        hidden = r.x_rows[rows, :].astype(f32) + row_mask[rows] * dot_plain(gated, r.out[...])
        r.hidden[rows, :] = hidden
        r.hidden_low[rows, :] = normalize(hidden).astype(bf16)
        target = slice(row_count + j * chunk_rows, row_count + (j + 1) * chunk_rows)
        hidden_copies.append(links.send(r.hidden_low.at[rows, :], r.hidden_low.at[target, :], "mate"))
        if j == 0:
            gather_second.cross()

    own_tiles = [(0, 256), (256, 256), (512, 128)]
    far_tiles = [(640, 256), (896, 256), (1152, 256)]

    def forward(rows, tiles):
        for start, size in tiles:
            units = slice(start, start + size)
            first = dot_right_t(r.hidden_low[rows, :], r.first[units, :])
            second = dot_right_t(r.hidden_low[rows, :], r.second[units, :])
            r.first_act[rows, units] = first.astype(bf16)
            r.second_act[rows, units] = second.astype(bf16)
            r.product[rows, units] = (first * second).astype(bf16)

    def backward(rows, tiles):
        for start, size in tiles:
            units = slice(start, start + size)
            product_grad = dot_right_t(r.last[rows, :], r.third[units, :])
            first_grad = product_grad * r.second_act[rows, units].astype(f32)
            second_grad = product_grad * r.first_act[rows, units].astype(f32)
            r.first_act[rows, units] = first_grad.astype(bf16)
            r.second_act[rows, units] = second_grad.astype(bf16)

    units_all = slice(0, 2 * hidden_size)
    col_tiles = [slice(i, i + 256) for i in range(0, width, 256)]

    def norm_grad(rows, cols):
        return dot_plain(r.first_act[rows, units_all], r.first[:, cols]) + dot_plain(
            r.second_act[rows, units_all], r.second[:, cols]
        )

    def mix(rows, cols):
        return dot_plain(r.product[rows, units_all], r.third[:, cols])

    own_rows = slice(0, row_count)
    for copy in (load_first, load_second, load_third):
        copy.wait()
    mate_chunks = [slice(row_count + j * chunk_rows, row_count + (j + 1) * chunk_rows) for j in range(2)]
    mate_rows = slice(row_count, 2 * row_count)

    def give_core(source, target, rows):
        return links.send(source.at[rows, units_all], target.at[rows, :], "core")

    def weight_grad(target, left, left_in, right, right_in):
        size = right.shape[1]
        for start in range(0, size, 256):
            cols = slice(start, min(start + 256, size))
            total = dot_plain(left[...], right[:, cols]) + dot_plain(left_in[...], right_in[:, cols])
            target[:, cols] = total.astype(bf16)

    forward(own_rows, own_tiles)
    gather_second.last()
    split_transpose(r.hidden_low.at[own_rows, :], r.hidden_t, r.hidden_give, own_rows)
    gather_third.spread()
    gather_first.done()
    gather_second.done()
    forward(own_rows, far_tiles)
    product_core = [give_core(r.product, r.product_in, own_rows)]
    gather_third.cross()
    arrived(hidden_copies[:1])
    forward(mate_chunks[0], own_tiles + far_tiles)
    gather_third.last()
    backward(own_rows, own_tiles)
    arrived(hidden_copies[1:])
    forward(mate_chunks[1], own_tiles + far_tiles)
    product_core.append(give_core(r.product, r.product_in, mate_rows))
    gather_third.done()
    norm_copies = []

    def back_mate(j):
        rows, out_rows = mate_chunks[j], slice(j * chunk_rows, (j + 1) * chunk_rows)
        backward(rows, own_tiles + far_tiles)
        for cols in col_tiles:
            r.x[out_rows, cols] = norm_grad(rows, cols).astype(bf16)
        norm_copies.append(links.send(r.x.at[out_rows, :], r.norm_in.at[out_rows, :], "mate"))

    back_mate(0)
    backward(own_rows, far_tiles)
    grad_core = [
        [give_core(ref, target, own_rows)] for ref, target in ((r.first_act, r.first_in), (r.second_act, r.second_in))
    ]
    arrived([last_core] + product_core)
    weight_grad(r.third_sum, r.last_t, r.last_in, r.product.at[:, units_all], r.product_in)
    chain_third = Chain(links, place, r.third_sum, r.third_half, r.third_quarter, 768)
    chain_third.start()
    back_mate(1)
    for copies_of, ref, target in zip(grad_core, (r.first_act, r.second_act), (r.first_in, r.second_in)):
        copies_of.append(give_core(ref, target, mate_rows))
    split_transpose(r.hidden_low.at[mate_rows, :], r.hidden_t, r.hidden_give, mate_rows)
    hidden_core = links.send(r.hidden_give, r.hidden_in, "core")
    for cols in col_tiles:
        r.hidden_grad[:, cols] = norm_grad(own_rows, cols)
    for cols in col_tiles:
        r.x[mate_rows, cols] = mix(mate_rows, cols).astype(bf16)

    def send_mix(j):
        rows = slice(j * chunk_rows, (j + 1) * chunk_rows)
        return links.send(r.x.at[mate_chunks[j], :], r.mix_in.at[rows, :], "mate")

    mix_copies = [send_mix(0)]
    for cols in col_tiles:
        r.mix[:, cols] = mix(own_rows, cols)
    arrived([hidden_core] + grad_core[0])
    links.left(product_core)
    first_sum = r.product.at[:, units_all]
    weight_grad(first_sum, r.hidden_t, r.hidden_in, r.first_act.at[:, units_all], r.first_in)
    chain_first = Chain(links, place, first_sum, r.first_half, r.first_quarter, 640)
    chain_first.start()
    chain_third.middle()

    attention_copies = []
    mate_block, mate_far = flipped(own, 0), 3 - own
    for j in range(2):
        rows = slice(j * chunk_rows, (j + 1) * chunk_rows)
        arrived([norm_copies[j]])
        incoming = r.hidden_grad[rows, :] + r.norm_in[rows, :].astype(f32)
        hidden_grad = r.upstream[rows, :].astype(f32) + norm_back(r.hidden[rows, :], incoming)
        r.hidden_grad[rows, :] = hidden_grad
        branch = (row_mask[rows] * hidden_grad).astype(bf16)
        r.branch[rows, :] = branch
        gated_grad = dot_right_t(branch, r.out[...])
        attention = r.attention_rows[rows, :].astype(f32)
        r.gate_grad[rows, :] = (gated_grad * normalize(attention)).astype(bf16)
        grad = norm_back(attention, gated_grad * r.gate_pre[rows, :]).astype(bf16)
        r.attention_grad[rows, :] = grad
        target_rows = part(member * 2 + j, chunk_rows)
        for i, (mine, theirs) in enumerate(((own, mate_block), (flipped(own, 1), mate_far))):
            target = r.grad_block.at[target_rows, i * head_width : (i + 1) * head_width]
            source = r.attention_grad.at[rows, part(theirs, head_width)]
            attention_copies.append(links.send(source, target, "mate"))
            target[...] = r.attention_grad[rows, part(mine, head_width)]
    branch_core = links.send(r.branch, r.branch_in, "core")
    gate_core = links.send(r.gate_grad, r.gate_grad_in, "core")
    split_transpose(r.gated, r.gated_t, r.gated_give, slice(0, row_count))
    gated_core = links.send(r.gated_give, r.gated_in, "core")
    arrived(grad_core[1])
    links.left(grad_core[0])
    second_sum = r.first_act.at[:, units_all]
    weight_grad(second_sum, r.hidden_t, r.hidden_in, r.second_act.at[:, units_all], r.second_in)
    chain_second = Chain(links, place, second_sum, r.second_half, r.second_quarter, 768)
    chain_first.middle()
    chain_second.start()

    arrived([branch_core, gated_core])
    out_sum = r.out.at[:SPAN, :]
    weight_grad(out_sum, r.gated_t, r.gated_in, r.branch, r.branch_in)
    chain_out = Chain(links, place, out_sum, r.out_half, r.out_quarter, 512)
    chain_out.start()

    arrived(attention_copies)
    heads_all = 2 * block_heads
    for at in range(heads_all):
        cols = slice(at * HDIM, (at + 1) * HDIM)
        decayed = (r.queries[:, cols].astype(f32) * jnp.exp(-rate_of(at) * (places + 1.0))).astype(bf16)
        r.state_grad[at] = dot_left_t(decayed, r.grad_block[:, cols]).astype(bf16)
    near_heads, far_heads = pl.ds(0, block_heads), pl.ds(block_heads, block_heads)
    state_copies = [
        links.send(r.state_grad.at[near_heads], r.state_in.at[far_heads], "far"),
        links.send(r.state_grad.at[far_heads], r.state_in.at[near_heads], "far"),
    ]
    mix_copies.append(send_mix(1))

    def grad_cols(kind, at):
        start = (at // block_heads) * 3 * head_width + kind * head_width + (at % block_heads) * HDIM
        return slice(start, start + HDIM)

    for at in range(heads_all):
        rate = rate_of(at)
        cols = slice(at * HDIM, (at + 1) * HDIM)
        q, k, v, g = r.queries[:, cols], r.keys[:, cols], r.values[:, cols], r.grad_block[:, cols]
        decay = inner_decay(rate)
        weights = (dot_right_t(q, k) * decay).astype(bf16)
        score_grad = (dot_right_t(g, v) * decay).astype(bf16)
        dq = dot_plain(score_grad, k) + jnp.exp(-rate * (places + 1.0)) * dot_right_t(g, r.states[at])
        r.pre_grads[:, grad_cols(0, at)] = (dq * r.query_slope[:, cols].astype(f32)).astype(bf16)
        r.pre_grads[:, grad_cols(1, at)] = dot_left_t(score_grad, q).astype(bf16)
        r.pre_grads[:, grad_cols(2, at)] = dot_left_t(weights, g).astype(bf16)

    def to_far(chain, keep, give, target):
        total = chain.result().astype(bf16)
        size = keep.shape[1]
        keep[...] = total[:, :size]
        give[...] = total[:, size:]
        return links.send(give, target, "far")

    ends = [to_far(chain_third, r.third_keep, r.third_give, r.third_far)]
    arrived(state_copies)
    leaving = 1.0 - pair.astype(f32)
    for at in range(heads_all):
        rate = rate_of(at)
        cols = slice(at * HDIM, (at + 1) * HDIM)
        key_decay = leaving * jnp.exp(-rate * (SPAN - 1.0 - places))
        carried = r.state_in[at]
        dk = r.pre_grads[:, grad_cols(1, at)].astype(f32) + key_decay * dot_right_t(r.values[:, cols], carried)
        dv = r.pre_grads[:, grad_cols(2, at)].astype(f32) + key_decay * dot_plain(r.keys[:, cols], carried)
        r.pre_grads[:, grad_cols(1, at)] = (dk * r.key_slope[:, cols].astype(f32)).astype(bf16)
        r.pre_grads[:, grad_cols(2, at)] = (dv * mask).astype(bf16)
    pre_core = links.send(r.pre_grads, r.pre_in, "core")

    triple = 3 * head_width

    def head_terms(rows, cols):
        return dot_right_t(r.pre_grads[rows, :triple], r.heads[0, cols, :]) + dot_right_t(
            r.pre_grads[rows, triple:], r.heads[1, cols, :]
        )

    term_copies = []
    for start in range(0, width, 512):
        for cols in (slice(start, start + 256), slice(start + 256, start + 512)):
            r.terms[:, cols] = head_terms(part(1 - member, row_count), cols).astype(bf16)
        wide = slice(start, start + 512)
        term_copies.append(links.send(r.terms.at[:, wide], r.terms_in.at[:, wide], "mate"))
    chain_second.middle()
    ends.append(to_far(chain_first, r.first_keep, r.first_give, r.first_far))
    arrived([pre_core, normed_core])
    links.left(grad_core[1])
    weight_grad(r.second_act, r.normed_t, r.normed_in, r.pre_grads, r.pre_in)
    chain_heads = Chain(links, place, r.second_act, r.heads_half, r.heads_quarter, 768)
    chain_heads.start()
    for cols in col_tiles:
        r.terms_own[:, cols] = head_terms(part(member, row_count), cols) + dot_right_t(r.gate_grad[...], r.gate[cols, :])

    def to_heads(chain, keep, target):
        total = chain.result().astype(bf16)
        slot = chain.chunk(chain.y, chain.x)
        slot[...] = total
        size = total.shape[0] // 4
        keep[...] = slot[part(own, size), :]
        return [
            links.send(slot.at[part(index, size), :], target.at[i], device)
            for i, (index, device) in enumerate(((mate_block, "mate"), (flipped(own, 1), "far"), (mate_far, "cross")))
        ]

    chain_out.middle()
    arrived([gate_core])
    gate_sum = r.out.at[SPAN:, :]
    lanes = part(member, row_count)
    weight_grad(gate_sum, r.normed_t.at[:, lanes], r.normed_in.at[:, lanes], r.gate_grad, r.gate_grad_in)
    chain_gate = Chain(links, place, gate_sum, r.gate_half, r.gate_quarter, 512)
    ends.append(to_far(chain_second, r.second_keep, r.second_give, r.second_far))
    chain_heads.middle()
    chain_gate.start()
    ends += to_heads(chain_out, r.out_keep, r.out_far)
    arrived(mix_copies)
    r.output[...] = (r.hidden[...] + row_mask * (r.mix[...] + r.mix_in[...].astype(f32))).astype(bf16)
    ends.append(to_far(chain_heads, r.heads_keep, r.heads_give, r.heads_far))
    arrived(term_copies)
    for j in range(2):
        rows = slice(j * chunk_rows, (j + 1) * chunk_rows)
        incoming = r.terms_own[rows, :] + r.terms_in[rows, :].astype(f32)
        grad = r.hidden_grad[rows, :] + norm_back(r.x_rows[rows, :].astype(f32), incoming)
        r.input_grad[rows, :] = grad.astype(bf16)
    chain_gate.middle()
    ends += to_heads(chain_gate, r.gate_keep, r.gate_far)
    arrived(ends)
    links.finish()


def finish_kernel(count, *refs):
    sources, targets, refs = refs[:count], refs[count : count + 10], refs[count + 10 :]
    held, results, in_sems, out_sems = refs[:count], refs[count : count + 8], refs[-2], refs[-1]
    loads = [pltpu.make_async_copy(a, b, in_sems.at[i]) for i, (a, b) in enumerate(zip(sources, held))]
    for load in loads:
        load.start()
    stores = []

    def ready(index):
        for load in loads[2 * index : 2 * index + 2]:
            load.wait()
        return held[2 * index], held[2 * index + 1]

    def store(source, index):
        copy = pltpu.make_async_copy(source, targets[index], out_sems.at[index])
        copy.start()
        stores.append(copy)

    for i, rows in enumerate(ready(0)):
        store(rows, i)
    for i, index in ((1, 9), (2, 7), (3, 8)):
        keep, far = ready(i)
        results[index - 2][...] = (keep[...].astype(f32) + far[...].astype(f32)).T
        store(results[index - 2], index)
    keep, far = ready(4)
    size = targets[2].shape[1]
    for i in range(3):
        cols = slice(i * size, (i + 1) * size)
        results[i][...] = keep[:, cols].astype(f32) + far[:, cols].astype(f32)
        store(results[i], 2 + i)
    for i in (5, 6):
        keep, others = ready(i)
        total = keep[...].astype(f32)
        for j in range(3):
            total = total + others[j].astype(f32)
        results[i - 2][...] = total
        store(results[i - 2], i)
    for copy in stores:
        copy.wait()


def fused_shards(
    layer_input, w_query, w_key, w_value, w_gate, w_out, w_first, w_second, w_third,
    decay_rates, seq_lengths, cotangent,
):
    group_rows, width = layer_input.shape
    row_count = cotangent.shape[0]
    heads = decay_rates.shape[0]
    head_width = w_query.shape[1]
    units = w_third.shape[0]
    shape = jax.ShapeDtypeStruct
    share = width // 8
    both = 2 * head_width
    triple = 3 * head_width
    inputs = dict(
        lengths=seq_lengths, decay_rates=decay_rates, layer_input=layer_input, w_query=w_query, w_key=w_key, w_value=w_value,
        w_gate=w_gate, w_out=w_out, w_first=w_first.T, w_second=w_second.T, w_third=w_third, cotangent=cotangent,
    )
    rows_shape = shape((row_count, width), bf16)
    ffn_shape = shape((share, units), bf16)
    head_shape = shape((share, triple), bf16)
    dense_shape = shape((share // 4, width), bf16)
    dense_far = shape((3, share // 4, width), bf16)
    outputs = dict(
        output=rows_shape, input_grad=rows_shape,
        third_keep=ffn_shape, third_far=ffn_shape, first_keep=ffn_shape, first_far=ffn_shape,
        second_keep=ffn_shape, second_far=ffn_shape, heads_keep=head_shape, heads_far=head_shape,
        gate_keep=dense_shape, gate_far=dense_far, out_keep=dense_shape, out_far=dense_far,
    )
    low = lambda *dims: pltpu.VMEM(dims, bf16)
    wide = lambda *dims: pltpu.VMEM(dims, f32)
    half = width // 2
    scratch = dict(
        x=low(group_rows, width), normed=low(group_rows, width),
        heads=low(2, width, triple), gate=low(width, width), out=low(width, width),
        first=low(2 * units, width), second=low(2 * units, width), third=low(2 * units, width),
        upstream=low(row_count, width), rates=wide(8, 128), rates_far=wide(8, 128),
        queries=low(SPAN, both), keys=low(SPAN, both), values=low(SPAN, both),
        query_slope=low(SPAN, both), key_slope=low(SPAN, both), states=low(2 * heads, HDIM, HDIM),
        attention=low(SPAN, both), attention_rows=low(row_count, width), gate_pre=wide(row_count, width),
        hidden=wide(row_count, width),
        hidden_low=low(SPAN, width), last=low(SPAN, width),
        first_act=low(SPAN, 2 * units), second_act=low(SPAN, 2 * triple), product=low(SPAN, 2 * units),
        hidden_grad=wide(row_count, width), mix=wide(row_count, width), norm_in=low(row_count, width),
        mix_in=low(row_count, width), grad_block=low(SPAN, both),
        state_grad=low(2 * heads, HDIM, HDIM), state_in=low(2 * heads, HDIM, HDIM),
        pre_grads=low(SPAN, 2 * triple), terms_in=low(row_count, width),
        terms_own=wide(row_count, width),
        normed_t=low(half, SPAN), normed_give=low(half, SPAN), normed_in=low(half, SPAN),
        last_t=low(half, SPAN), last_give=low(half, SPAN), last_in=low(half, SPAN),
        hidden_t=low(half, SPAN), hidden_give=low(half, SPAN), hidden_in=low(half, SPAN),
        gated_t=low(half, row_count), gated_give=low(half, row_count), gated_in=low(half, row_count),
        product_in=low(SPAN, 2 * units), first_in=low(SPAN, 2 * units), second_in=low(SPAN, 2 * units),
        pre_in=low(SPAN, 2 * triple), branch_in=low(row_count, width), gate_grad_in=low(row_count, width),
        third_sum=low(half, 2 * units),
        third_half=low(2 * share, 2 * units), first_half=low(2 * share, 2 * units),
        second_half=low(2 * share, 2 * units), heads_half=low(2 * share, 2 * triple),
        gate_half=low(2 * share, width), out_half=low(2 * share, width),
        third_quarter=low(share, 2 * units), first_quarter=low(share, 2 * units),
        second_quarter=low(share, 2 * units), heads_quarter=low(share, 2 * triple),
        gate_quarter=low(share, width), out_quarter=low(share, width),
        third_give=low(share, units), first_give=low(share, units), second_give=low(share, units),
        heads_give=low(share, triple),
        local_sems=pltpu.SemaphoreType.DMA((16,)),
        send_sems=pltpu.SemaphoreType.DMA((144,)), recv_sems=pltpu.SemaphoreType.DMA((144,)),
    )
    results = pl.pallas_call(
        functools.partial(layer_kernel, list(inputs) + list(outputs) + list(scratch)),
        out_shape=list(outputs.values()),
        in_specs=[smem(), smem()] + [pl.BlockSpec(memory_space=pl.ANY)] * (len(inputs) - 2),
        out_specs=[vmem()] * len(outputs),
        scratch_shapes=list(scratch.values()),
        compiler_params=pltpu.CompilerParams(
            collective_id=0, has_side_effects=True, vmem_limit_bytes=VMEM_ALL
        ),
        name="layer",
    )(*inputs.values())
    transposed_shape = shape((units, share), f32)
    finals = [rows_shape] * 2 + [shape((share, head_width), f32)] * 3 + [shape((share // 4, width), f32)] * 2
    finals += [transposed_shape] * 3
    place_any = pl.BlockSpec(memory_space=pltpu.HBM)
    results = pl.pallas_call(
        functools.partial(finish_kernel, len(results)),
        out_shape=finals,
        in_specs=[place_any] * len(results),
        out_specs=[place_any] * 10,
        scratch_shapes=[pltpu.VMEM(a.shape, a.dtype) for a in list(results) + finals[2:]]
        + [pltpu.SemaphoreType.DMA((len(results),)), pltpu.SemaphoreType.DMA((10,))],
        compiler_params=pltpu.CompilerParams(vmem_limit_bytes=VMEM_ALL),
        name="finish",
    )(*results)
    return (*results[:7], results[7].T, results[8].T, results[9])


def solution(mesh):
    placed = (
        P("dp", None),
        P(None, "head"),
        P(None, "head"),
        P(None, "head"),
        P(),
        P(),
        P(None, "head"),
        P(None, "head"),
        P("head", None),
        P("head"),
        P("dp"),
        P(("dp", "head"), None),
    )
    n_dp, n_head = mesh.shape["dp"], mesh.shape["head"]
    body = fused_shards if (n_dp, n_head) == (8, 4) else functools.partial(shards, n_dp, n_head)
    return jax.shard_map(
        body,
        mesh=mesh,
        in_specs=placed,
        out_specs=(
            P(("dp", "head"), None),
            P(("dp", "head"), None),
            P("dp", "head"),
            P("dp", "head"),
            P("dp", "head"),
            P(("dp", "head"), None),
            P(("dp", "head"), None),
            P("dp", "head"),
            P("dp", "head"),
            P("head", "dp"),
        ),
        check_vma=False,
    )
```

```python
import functools
import types

import jax
import jax.numpy as jnp
from jax import lax
from jax.experimental import pallas as pl
from jax.experimental.pallas import tpu as pltpu
from jax.sharding import PartitionSpec as P

SPAN = 512
HDIM = 128

epsilon = 1e-06
bf16 = jnp.bfloat16
f32 = jnp.float32
VMEM_LIMIT = 48 * 2**20
VMEM_ALL = 63 * 2**20


def inverse_rms(values):
    return lax.rsqrt(jnp.mean(values * values, axis=-1, keepdims=True) + epsilon)


def normalize(values):
    return values * inverse_rms(values)


def norm_back(values, incoming):
    inverse = inverse_rms(values)
    unit_rows = values * inverse
    return inverse * (incoming - unit_rows * jnp.mean(incoming * unit_rows, axis=-1, keepdims=True))


def dot_plain(left, right):
    return jnp.dot(left, right, preferred_element_type=f32)


def dot_right_t(left, right):
    return lax.dot_general(left, right, (((1,), (1,)), ((), ())), preferred_element_type=f32)


def dot_left_t(left, right):
    return lax.dot_general(left, right, (((0,), (0,)), ((), ())), preferred_element_type=f32)


def transposed(values):
    return values.T


def column(length):
    return lax.broadcasted_iota(jnp.int32, (length, 1), 0)


def inner_decay(rate):
    rows = lax.broadcasted_iota(jnp.int32, (SPAN, SPAN), 0)
    cols = lax.broadcasted_iota(jnp.int32, (SPAN, SPAN), 1)
    offset = rows - cols
    return jnp.where(offset >= 0, jnp.exp(-rate * jnp.maximum(offset, 0).astype(f32)), 0.0)


def attend_kernel(
    meta, rates, x, w_own_q, w_own_k, w_own_v, w_other,
    normed, attention, queries, keys, values, query_slope, key_slope, states,
):
    pair, length = meta[0], meta[1]
    start = pl.multiple_of(pair * SPAN, SPAN)
    rows = x.shape[0]
    head_width = w_own_q.shape[1]

    def norm_step(i, carry):
        place = pl.ds(pl.multiple_of(i * 128, 128), 128)
        normed[place, :] = normalize(x[place, :].astype(f32)).astype(bf16)
        return carry

    lax.fori_loop(0, rows // 128, norm_step, 0)
    block = normed[pl.ds(start, SPAN), :]
    mask = (start + column(SPAN) < length).astype(f32)
    early_mask = (column(SPAN) < length).astype(f32) * pair.astype(f32)
    early = normed[0:SPAN, :]
    places = column(SPAN).astype(f32)
    for part in range(2):
        if part == 0:
            wq, wk, wv = w_own_q[...], w_own_k[...], w_own_v[...]
        else:
            wq, wk, wv = (w_other[:, i * head_width : (i + 1) * head_width] for i in range(3))
        pre_query = dot_plain(block, wq)
        pre_key = dot_plain(block, wk)
        pre_value = dot_plain(block, wv)
        sigmoid_query = jax.nn.sigmoid(pre_query)
        sigmoid_key = jax.nn.sigmoid(pre_key)
        query = (pre_query * sigmoid_query).astype(bf16)
        key = (mask * (pre_key * sigmoid_key)).astype(bf16)
        value = (mask * pre_value).astype(bf16)
        wide = slice(part * head_width, (part + 1) * head_width)
        query_slope[:, wide] = (sigmoid_query * (1.0 + pre_query * (1.0 - sigmoid_query))).astype(bf16)
        key_slope[:, wide] = (mask * (sigmoid_key * (1.0 + pre_key * (1.0 - sigmoid_key)))).astype(bf16)
        queries[:, wide] = query
        keys[:, wide] = key
        values[:, wide] = value
        early_key = dot_plain(early, wk)
        early_key = early_mask * (early_key * jax.nn.sigmoid(early_key)).astype(bf16).astype(f32)
        early_value = (early_mask * dot_plain(early, wv)).astype(bf16)
        for head in range(head_width // HDIM):
            index = part * (head_width // HDIM) + head
            rate = rates[index]
            cols = slice(head * HDIM, (head + 1) * HDIM)
            q, k, v = query[:, cols], key[:, cols], value[:, cols]
            scores = dot_right_t(q, k)
            weights = (scores * inner_decay(rate)).astype(bf16)
            keyed = (early_key[:, cols] * jnp.exp(-rate * (SPAN - 1.0 - places))).astype(bf16)
            state = dot_left_t(keyed, early_value[:, cols])
            states[index] = state
            decayed = (q.astype(f32) * jnp.exp(-rate * (places + 1.0))).astype(bf16)
            out = dot_plain(weights, v) + dot_plain(decayed, state.astype(bf16))
            attention[:, index * HDIM : (index + 1) * HDIM] = out.astype(bf16)


def state_kernel(rates, queries, upstream, state_grad):
    places = column(SPAN).astype(f32)
    for index in range(state_grad.shape[0]):
        cols = slice(index * HDIM, (index + 1) * HDIM)
        decayed = (queries[:, cols].astype(f32) * jnp.exp(-rates[index] * (places + 1.0))).astype(bf16)
        state_grad[index] = dot_left_t(decayed, upstream[:, cols])


def attend_back_kernel(
    meta, rates, queries, keys, values, upstream, query_slope, key_slope, states, state_grad, pre_grads
):
    pair, length = meta[0], meta[1]
    mask = (pair * SPAN + column(SPAN) < length).astype(f32)
    places = column(SPAN).astype(f32)
    heads = states.shape[0]
    half = heads // 2
    for index in range(heads):
        rate = rates[index]
        cols = slice(index * HDIM, (index + 1) * HDIM)
        q, k, v, g = queries[:, cols], keys[:, cols], values[:, cols], upstream[:, cols]
        decay = inner_decay(rate)
        query_decay = jnp.exp(-rate * (places + 1.0))
        key_decay = jnp.exp(-rate * (SPAN - 1.0 - places))
        state = states[index].astype(bf16)
        carried = state_grad[index].astype(bf16)
        weights = (dot_right_t(q, k) * decay).astype(bf16)
        score_grad = (dot_right_t(g, v) * decay).astype(bf16)
        dq = dot_plain(score_grad, k) + query_decay * dot_right_t(g, state)
        dk = dot_left_t(score_grad, q) + key_decay * dot_right_t(v, carried)
        dv = dot_left_t(weights, g) + key_decay * dot_plain(k, carried)
        base = (index // half) * (3 * half * HDIM) + (index % half) * HDIM
        pre_grads[:, base : base + HDIM] = (dq * query_slope[:, cols].astype(f32)).astype(bf16)
        base += half * HDIM
        pre_grads[:, base : base + HDIM] = (dk * key_slope[:, cols].astype(f32)).astype(bf16)
        base += half * HDIM
        pre_grads[:, base : base + HDIM] = (dv * mask).astype(bf16)


def vmem():
    return pl.BlockSpec(memory_space=pltpu.VMEM)


def smem():
    return pl.BlockSpec(memory_space=pltpu.SMEM)


def local_call(body, name, out_shapes, args, scalars, flops):
    size = sum(int(a.size) * a.dtype.itemsize for a in list(args) + list(out_shapes))
    return pl.pallas_call(
        body,
        out_shape=out_shapes,
        in_specs=[smem()] * scalars + [vmem()] * (len(args) - scalars),
        out_specs=[vmem()] * len(out_shapes),
        compiler_params=pltpu.CompilerParams(vmem_limit_bytes=VMEM_LIMIT),
        cost_estimate=pl.CostEstimate(flops=flops, bytes_accessed=size, transcendentals=0),
        name=name,
    )(*args)


def shards(
    n_dp, n_head,
    layer_input, w_query, w_key, w_value, w_gate, w_out, w_first, w_second, w_third,
    decay_rates, seq_lengths, cotangent,
):
    group_rows, width = layer_input.shape
    row_count = cotangent.shape[0]
    heads = decay_rates.shape[0]
    head_width = w_query.shape[1]
    place = lax.axis_index("dp")
    own = lax.axis_index("head")
    member, pair = own % 2, own // 2
    bits = n_dp.bit_length() - 1
    length = seq_lengths[0]

    def to_mate(array, bit):
        return lax.ppermute(array, "head", [(i, i ^ bit) for i in range(n_head)])

    def across(array, bit):
        return lax.ppermute(array, "dp", [(i, i ^ (1 << bit)) for i in range(n_dp)])

    def gathered(weight, axis):
        size = weight.shape[axis] // n_dp
        share = lax.dynamic_slice_in_dim(weight, place * size, size, axis)
        return lax.all_gather(to_mate(share, 2), "dp", axis=axis, tiled=True)

    w_heads = jnp.concatenate([w_query, w_key, w_value], axis=1)
    w_heads_other = gathered(w_heads, 0)
    w_first_other = gathered(w_first, 0)
    w_second_other = gathered(w_second, 0)
    w_third_other = gathered(w_third, 1)
    rates = jnp.concatenate([decay_rates, to_mate(decay_rates, 2)])

    block_start = pair * SPAN
    row_start = own * row_count
    positions = jnp.arange(row_count, dtype=jnp.int32)[:, None]
    row_mask = (row_start + positions < length).astype(f32)
    upstream = cotangent.astype(f32)
    last_own = (row_mask * upstream).astype(bf16)
    last_mate = to_mate(last_own, 1)

    meta = jnp.stack([pair, length]).astype(jnp.int32)
    both = 2 * head_width
    shape = jax.ShapeDtypeStruct
    block_shape = shape((SPAN, both), bf16)
    normed, attention_block, queries, keys, values, query_slope, key_slope, states = local_call(
        attend_kernel, "attend",
        [shape(layer_input.shape, bf16)] + [block_shape] * 6 + [shape((2 * heads, HDIM, HDIM), f32)],
        [meta, rates, layer_input, w_query, w_key, w_value, w_heads_other], 2, 6 * 10**9,
    )

    def rows_of(array, index):
        return lax.dynamic_slice_in_dim(array, index * row_count, row_count, 0)

    def ordered(mine, other):
        even, odd = jnp.where(member == 0, mine, other), jnp.where(member == 0, other, mine)
        flip = lambda a: jnp.where(pair == 0, a, jnp.concatenate([a[:, head_width:], a[:, :head_width]], axis=1))
        even, odd = flip(even), flip(odd)
        return jnp.concatenate(
            [even[:, :head_width], odd[:, :head_width], even[:, head_width:], odd[:, head_width:]], axis=1
        )

    def pieces(array):
        cut = [array[:, i * head_width : (i + 1) * head_width] for i in range(4)]
        even, odd = jnp.concatenate([cut[0], cut[2]], axis=1), jnp.concatenate([cut[1], cut[3]], axis=1)
        flip = lambda a: jnp.where(pair == 0, a, jnp.concatenate([a[:, head_width:], a[:, :head_width]], axis=1))
        even, odd = flip(even), flip(odd)
        return jnp.where(member == 0, even, odd), jnp.where(member == 0, odd, even)

    received = to_mate(rows_of(attention_block, 1 - member), 1)
    attention = ordered(rows_of(attention_block, member), received).astype(f32)
    attention_norm = normalize(attention)
    rows_low = rows_of(normed, own)
    input_rows = rows_of(layer_input, own).astype(f32)
    gate_pre = dot_plain(rows_low, w_gate)
    gated = (attention_norm * gate_pre).astype(bf16)
    hidden = input_rows + row_mask * dot_plain(gated, w_out)
    hidden_low = normalize(hidden).astype(bf16)
    hidden_mate = to_mate(hidden_low, 1)

    w_first_all = jnp.concatenate([w_first, w_first_other], axis=1)
    w_second_all = jnp.concatenate([w_second, w_second_other], axis=1)
    w_third_all = jnp.concatenate([w_third, w_third_other], axis=0)

    def forward_rows(rows_in):
        first, second = dot_plain(rows_in, w_first_all), dot_plain(rows_in, w_second_all)
        return first.astype(bf16), second.astype(bf16), (first * second).astype(bf16)

    def backward_rows(last, first, second):
        product_grad = dot_right_t(last, w_third_all)
        first_grad = (product_grad * second.astype(f32)).astype(bf16)
        second_grad = (product_grad * first.astype(f32)).astype(bf16)
        return first_grad, second_grad, dot_right_t(first_grad, w_first_all) + dot_right_t(second_grad, w_second_all)

    first_mate, second_mate, product_mate = forward_rows(hidden_mate)
    first_grad_mate, second_grad_mate, norm_grad_mate = backward_rows(last_mate, first_mate, second_mate)
    norm_grad_in = to_mate(norm_grad_mate.astype(bf16), 1)
    mix_in = to_mate(dot_plain(product_mate, w_third_all).astype(bf16), 1)
    first_own, second_own, product_own = forward_rows(hidden_low)
    first_grad_own, second_grad_own, norm_grad_own = backward_rows(last_own, first_own, second_own)
    hidden_grad = upstream + norm_back(hidden, norm_grad_own + norm_grad_in.astype(f32))
    mixed = dot_plain(product_own, w_third_all) + mix_in.astype(f32)
    output = (hidden + row_mask * mixed).astype(bf16)

    branch_grad = (row_mask * hidden_grad).astype(bf16)
    gated_grad = dot_right_t(branch_grad, w_out)
    gate_grad = (gated_grad * attention_norm).astype(bf16)
    attention_grad = norm_back(attention, gated_grad * gate_pre).astype(bf16)
    mine, for_mate = pieces(attention_grad)
    from_mate = to_mate(for_mate, 1)
    grad_block = jnp.concatenate(
        [jnp.where(member == 0, mine, from_mate), jnp.where(member == 0, from_mate, mine)], axis=0
    )
    state_shape = shape((2 * heads, HDIM, HDIM), f32)
    (state_grad,) = local_call(
        state_kernel, "state_grad", [state_shape], [rates, queries, grad_block], 1, 10**8
    )
    swapped = jnp.concatenate([state_grad[heads:], state_grad[:heads]], axis=0)
    carried = lax.ppermute(swapped, "head", [(i, i - 2) for i in range(2, n_head)])
    (pre_grads,) = local_call(
        attend_back_kernel, "attend_back", [shape((SPAN, 3 * both), bf16)],
        [meta, rates, queries, keys, values, grad_block, query_slope, key_slope, states, carried], 2, 2 * 10**9,
    )
    head_terms = dot_right_t(pre_grads[:, : 3 * head_width], w_heads) + dot_right_t(
        pre_grads[:, 3 * head_width :], w_heads_other
    )
    head_terms = head_terms.astype(bf16)
    terms_in = to_mate(rows_of(head_terms, 1 - member), 1)
    input_norm_grad = (
        rows_of(head_terms, member).astype(f32) + terms_in.astype(f32) + dot_right_t(gate_grad, w_gate)
    )
    input_grad = (hidden_grad + norm_back(input_rows, input_norm_grad)).astype(bf16)

    def summed(left, right, order):
        left = left.reshape((left.shape[0],) + (2,) * bits + (width // n_dp,))

        def pick(array, axis, bit, which):
            side = (place // (1 << bit)) % 2
            return lax.dynamic_index_in_dim(array, side if which else 1 - side, axis, keepdims=False)

        left_axis = lambda bit, done: 1 + (bits - 1 - bit) - sum(1 for b in done if b > bit)
        first_bit = order[0]
        make = lambda which: dot_left_t(
            pick(left, left_axis(first_bit, []), first_bit, which).reshape(left.shape[0], width // 2), right
        ).astype(bf16)
        arrived = across(make(False), first_bit)
        total = (make(True).astype(f32) + arrived.astype(f32)).astype(bf16)
        total = total.reshape((2,) * (bits - 1) + (width // n_dp, right.shape[1]))
        done = [first_bit]
        for bit in order[1:]:
            axis = left_axis(bit, done) - 1
            arrived = across(pick(total, axis, bit, False), bit)
            total = (pick(total, axis, bit, True).astype(f32) + arrived.astype(f32)).astype(bf16)
            done.append(bit)
        return total

    def with_mate(total):
        size = total.shape[1] // 2
        return total[:, :size].astype(f32) + to_mate(total[:, size:], 2).astype(f32)

    def over_heads(total):
        for bit in (1, 2):
            cut = total.reshape((2, -1) + total.shape[1:]) if bit == 2 else total.reshape((2, 2, -1) + total.shape[1:])
            side = (own // bit) % 2
            axis = 0 if bit == 2 else 1
            arrived = to_mate(lax.dynamic_index_in_dim(cut, 1 - side, axis, keepdims=False), bit)
            total = lax.dynamic_index_in_dim(cut, side, axis, keepdims=False).astype(f32) + arrived.astype(f32)
            if bit == 1:
                total = total.astype(bf16).reshape((-1,) + total.shape[2:])
        return total

    up = list(range(bits))
    down = [0] + up[:0:-1]
    stack = lambda a, b: jnp.concatenate([a, b], axis=0)
    hidden_all = stack(hidden_low, hidden_mate)
    last_all = stack(last_own, last_mate)
    grad_third_t = with_mate(summed(last_all, stack(product_own, product_mate), up))
    grad_first = with_mate(summed(hidden_all, stack(first_grad_own, first_grad_mate), up))
    grad_second = with_mate(summed(hidden_all, stack(second_grad_own, second_grad_mate), down))
    grad_out = over_heads(summed(gated, branch_grad, down))
    grad_gate = over_heads(summed(rows_low, gate_grad, up))
    normed_block = lax.dynamic_slice_in_dim(normed, block_start, SPAN, 0)
    grad_heads = with_mate(summed(normed_block, pre_grads, down))
    return (
        output,
        input_grad,
        grad_heads[:, :head_width],
        grad_heads[:, head_width : 2 * head_width],
        grad_heads[:, 2 * head_width :],
        grad_gate,
        grad_out,
        grad_first,
        grad_second,
        grad_third_t.T,
    )


MESH = pl.DeviceIdType.MESH


def flipped(index, bit):
    return index + (1 << bit) * (1 - 2 * ((index // (1 << bit)) % 2))


def part(index, size):
    return pl.ds(pl.multiple_of(index * size, size), size)


class Links:
    def __init__(self, others, send_sems, recv_sems):
        self.others, self.send_sems, self.recv_sems, self.started = others, send_sems, recv_sems, []

    def send(self, source, target, device):
        index = len(self.started)
        copy = pltpu.make_async_remote_copy(
            src_ref=source,
            dst_ref=target,
            send_sem=self.send_sems.at[index],
            recv_sem=self.recv_sems.at[index],
            device_id=self.others[device],
            device_id_type=MESH,
        )
        copy.start()
        self.started.append(copy)
        copy.sent = False
        return copy

    def left(self, copies):
        for copy in copies:
            if not copy.sent:
                copy.wait_send()
                copy.sent = True

    def finish(self):
        self.left(self.started)


def arrived(copies):
    for copy in copies:
        copy.wait_recv()


class Gather:
    def __init__(self, links, place, pieces, halves):
        self.links, self.pieces, self.halves = links, pieces, halves
        self.places = [place, flipped(place, 1), flipped(place, 2), flipped(flipped(place, 1), 2)]
        self.to_core, self.near, self.crossing, self.fetched = [], {}, {}, {}

    def pass_on(self, piece, which, device):
        ref = self.pieces[piece](self.places[which])
        return self.links.send(ref, ref, device)

    def fetch(self, sources):
        for i, source in enumerate(sources):
            self.fetched[i] = self.links.send(source, self.pieces[i](self.places[0]), "far")

    def spread(self, piece=0):
        arrived([self.fetched[piece]])
        self.near[piece] = (self.pass_on(piece, 0, "x"), self.pass_on(piece, 0, "y"))
        self.to_core.append(self.pass_on(piece, 0, "core"))

    def cross(self, piece=0):
        crossing = []
        for i, (half, device) in enumerate(zip(self.halves, ("y", "x"))):
            arrived([self.near[piece][i]])
            ref = half(self.pieces[piece](self.places[1 + i]))
            crossing.append(self.links.send(ref, ref, device))
            self.to_core.append(self.pass_on(piece, 1 + i, "core"))
        self.crossing[piece] = crossing

    def last(self, piece=0):
        arrived(self.crossing[piece])
        self.to_core.append(self.pass_on(piece, 3, "core"))

    def done(self):
        arrived(self.to_core)


class Chain:
    def __init__(self, links, place, total, halves_in, quarter_in, cut, orders=("xy", "yx")):
        self.links, self.total, self.halves_in, self.quarter_in = links, total, halves_in, quarter_in
        size = total.shape[1]
        self.parts = [(slice(0, cut), orders[0]), (slice(cut, size), orders[1])]
        self.x, self.y = (place // 2) % 2, (place // 4) % 2
        self.rows = quarter_in.shape[0]
        self.waits = []

    def chunk(self, y, x, cols=slice(None)):
        return self.total.at[part(2 * y + x, self.rows), cols]

    def start(self):
        links, rows = self.links, self.rows
        for cols, order in self.parts:
            if order == "xy":
                self.waits.append([
                    links.send(self.chunk(y, 1 - self.x, cols), self.halves_in.at[y * rows : (y + 1) * rows, cols], "x")
                    for y in range(2)
                ])
            else:
                give = self.total.at[part(1 - self.y, 2 * rows), cols]
                self.waits.append([links.send(give, self.halves_in.at[:, cols], "y")])

    def add(self, place, arrived_part):
        place[...] = (place[...].astype(f32) + arrived_part.astype(f32)).astype(bf16)

    def middle(self):
        rows, x, y = self.rows, self.x, self.y
        keep, waits = [], []
        for (cols, order), before in zip(self.parts, self.waits):
            arrived(before)
            give, device, index = (
                (self.chunk(1 - y, x, cols), "y", y) if order == "xy" else (self.chunk(y, 1 - x, cols), "x", x)
            )
            self.add(give, self.halves_in[part(1 - index, rows), cols])
            waits.append([self.links.send(give, self.quarter_in.at[:, cols], device)])
            keep.append((cols, index))
        for cols, index in keep:
            self.add(self.chunk(y, x, cols), self.halves_in[part(index, rows), cols])
        self.waits = waits

    def result(self):
        for before in self.waits:
            arrived(before)
        return self.chunk(self.y, self.x)[...].astype(f32) + self.quarter_in[...].astype(f32)


def layer_kernel(names, *refs):
    r = types.SimpleNamespace(**dict(zip(names, refs)))
    place, own = lax.axis_index("dp"), lax.axis_index("head")
    pair, member, core = own // 2, own % 2, place % 2
    length = r.lengths[0]
    group_rows, width = r.layer_input.shape
    row_count = r.cotangent.shape[0]
    head_width = r.w_query.shape[1]
    block_heads = head_width // HDIM
    hidden_size = r.w_third.shape[0]
    share_size = width // 8
    chunk_rows = row_count // 2
    r.gated, r.x_rows = (r.x.at[i * row_count : (i + 1) * row_count, :] for i in (2, 3))
    r.branch, r.gate_grad, r.attention_grad, r.terms = (
        r.normed.at[i * row_count : (i + 1) * row_count, :] for i in range(4)
    )

    copies = []

    def load(source, target):
        copy = pltpu.make_async_copy(source, target, r.local_sems.at[len(copies)])
        copy.start()
        copies.append(copy)
        return copy

    load_cotangent = load(r.cotangent, r.upstream)
    load_x = load(r.layer_input, r.x)
    load_heads = [
        load(weight, r.heads.at[0, :, i * head_width : (i + 1) * head_width])
        for i, weight in enumerate((r.w_query, r.w_key, r.w_value))
    ]
    load_gate = load(r.w_gate, r.gate)
    load_out = load(r.w_out, r.out)
    load_first = load(r.w_first, r.first.at[:hidden_size, :])
    load_second = load(r.w_second, r.second.at[:hidden_size, :])
    load_third = load(r.w_third, r.third.at[:hidden_size, :])

    others = {
        "core": (flipped(place, 0), own),
        "x": (flipped(place, 1), own),
        "y": (flipped(place, 2), own),
        "mate": (place, flipped(own, 0)),
        "far": (place, flipped(own, 1)),
        "cross": (place, 3 - own),
    }
    barrier = pltpu.get_barrier_semaphore()
    for device in others.values():
        pl.semaphore_signal(barrier, inc=1, device_id=device, device_id_type=MESH)
    row_mask = (own * row_count + column(row_count) < length).astype(f32)
    load_cotangent.wait()
    r.last[:row_count, :] = (row_mask * r.upstream[...].astype(f32)).astype(bf16)
    for i in range(block_heads):
        r.rates[i : i + 1, :] = jnp.full((1, 128), r.decay_rates[i], f32)
    pl.semaphore_wait(barrier, len(others))
    links = Links(others, r.send_sems, r.recv_sems)

    head_piece = lambda j: lambda i: r.heads.at[1, part(i, share_size), j * head_width : (j + 1) * head_width]
    ffn_piece = lambda ref: lambda i: ref.at[hidden_size:, part(i, share_size)]
    row_halves = [lambda ref, j=j: ref.at[j * share_size // 2 : (j + 1) * share_size // 2, :] for j in range(2)]
    unit_halves = [lambda ref, j=j: ref.at[j * hidden_size // 2 : (j + 1) * hidden_size // 2, :] for j in range(2)]
    gather_heads = Gather(links, place, [head_piece(j) for j in (1, 2, 0)], row_halves)
    gather_first = Gather(links, place, [ffn_piece(r.first)], unit_halves)
    gather_second = Gather(links, place, [ffn_piece(r.second)], unit_halves)
    gather_third = Gather(links, place, [ffn_piece(r.third)], unit_halves)

    def fetch(gather, source):
        gather.fetch([source.at[:, part(place, share_size)]])


    def send_last(j):
        source = slice(j * chunk_rows, (j + 1) * chunk_rows)
        target = slice(row_count + j * chunk_rows, row_count + (j + 1) * chunk_rows)
        return links.send(r.last.at[source, :], r.last.at[target, :], "mate")

    last_copies = [send_last(0)]
    gather_heads.fetch([weight.at[part(place, share_size), :] for weight in (r.w_key, r.w_value, r.w_query)])
    rates_copy = links.send(r.rates, r.rates_far, "far")
    fetch(gather_first, r.w_first)
    last_copies.append(send_last(1))

    load_x.wait()

    def norm_step(i, carry):
        where = part(i, 128)
        r.normed[where, :] = normalize(r.x[where, :].astype(f32)).astype(bf16)
        return carry

    lax.fori_loop(0, group_rows // 128, norm_step, 0)
    r.x_rows[...] = r.x[part(own, row_count), :]
    block_rows = part(pair, SPAN)
    mask = (pair * SPAN + column(SPAN) < length).astype(f32)
    early_mask = (column(SPAN) < length).astype(f32) * pair.astype(f32)
    places = column(SPAN).astype(f32)

    def project(index):
        wide = slice(index * head_width, (index + 1) * head_width)
        weights = [r.heads.at[index, :, i * head_width : (i + 1) * head_width] for i in range(3)]
        block = r.normed[block_rows, :]
        early = r.normed[0:SPAN, :]
        pre_query = dot_plain(block, weights[0][...])
        sigmoid = jax.nn.sigmoid(pre_query)
        r.queries[:, wide] = (pre_query * sigmoid).astype(bf16)
        r.query_slope[:, wide] = (sigmoid * (1.0 + pre_query * (1.0 - sigmoid))).astype(bf16)
        pre_key = dot_plain(block, weights[1][...])
        sigmoid = jax.nn.sigmoid(pre_key)
        r.keys[:, wide] = (mask * (pre_key * sigmoid)).astype(bf16)
        r.key_slope[:, wide] = (mask * (sigmoid * (1.0 + pre_key * (1.0 - sigmoid)))).astype(bf16)
        r.values[:, wide] = (mask * dot_plain(block, weights[2][...])).astype(bf16)
        early_key = dot_plain(early, weights[1][...])
        early_key = early_mask * (early_key * jax.nn.sigmoid(early_key)).astype(bf16).astype(f32)
        early_value = (early_mask * dot_plain(early, weights[2][...])).astype(bf16)
        return early_key, early_value

    def rate_of(index):
        ref = r.rates if index < block_heads else r.rates_far
        return ref[index % block_heads : index % block_heads + 1, 0:1]

    def attend(index, early_key, early_value):
        for head in range(block_heads):
            at = index * block_heads + head
            rate = rate_of(at)
            cols = slice(at * HDIM, (at + 1) * HDIM)
            early = slice(head * HDIM, (head + 1) * HDIM)
            q, k, v = r.queries[:, cols], r.keys[:, cols], r.values[:, cols]
            weights = (dot_right_t(q, k) * inner_decay(rate)).astype(bf16)
            keyed = (early_key[:, early] * jnp.exp(-rate * (SPAN - 1.0 - places))).astype(bf16)
            state = dot_left_t(keyed, early_value[:, early])
            r.states[at] = state.astype(bf16)
            decayed = (q.astype(f32) * jnp.exp(-rate * (places + 1.0))).astype(bf16)
            out = dot_plain(weights, v) + dot_plain(decayed, state.astype(bf16))
            r.attention[:, cols] = out.astype(bf16)
        wide = slice(index * head_width, (index + 1) * head_width)
        block = own if index == 0 else flipped(own, 1)
        target = r.attention_rows.at[:, part(block, head_width)]
        copy = links.send(r.attention.at[part(1 - member, row_count), wide], target, "mate")
        target[...] = r.attention[part(member, row_count), wide]
        return copy

    def split_transpose(source, keep, give, columns):
        for e in range(4):
            rows = slice(e * share_size, (e + 1) * share_size)
            keep[rows, columns] = transposed(source[:, part(2 * e + core, share_size)])
            give[rows, columns] = transposed(source[:, part(2 * e + 1 - core, share_size)])

    for copy in load_heads:
        copy.wait()
    gather_heads.spread(0)
    early = project(0)
    gather_heads.spread(1)
    gather_heads.spread(2)
    gather_heads.cross(0)
    attention_own = attend(0, *early)
    fetch(gather_second, r.w_second)
    gather_heads.cross(1)
    gather_heads.cross(2)
    gather_heads.last(0)
    split_transpose(r.normed.at[block_rows, :], r.normed_t, r.normed_give, slice(0, SPAN))
    normed_core = links.send(r.normed_give, r.normed_in, "core")
    gather_heads.last(1)
    gather_heads.last(2)
    gather_first.spread()
    load_gate.wait()
    r.gate_pre[...] = dot_plain(r.normed[part(own, row_count), :], r.gate[...])
    gather_heads.done()
    rates_copy.wait_recv()
    early = project(1)
    gather_first.cross()
    attention_far = attend(1, *early)
    fetch(gather_third, r.w_third)
    split_transpose(r.last.at[:row_count, :], r.last_t, r.last_give, slice(0, row_count))
    gather_first.last()
    arrived(last_copies)
    split_transpose(r.last.at[row_count:, :], r.last_t, r.last_give, slice(row_count, 2 * row_count))
    last_core = links.send(r.last_give, r.last_in, "core")
    gather_second.spread()
    load_out.wait()
    arrived([attention_own, attention_far])

    hidden_copies = []
    for j in range(2):
        rows = slice(j * chunk_rows, (j + 1) * chunk_rows)
        gated = (normalize(r.attention_rows[rows, :].astype(f32)) * r.gate_pre[rows, :]).astype(bf16)
        r.gated[rows, :] = gated
        hidden = r.x_rows[rows, :].astype(f32) + row_mask[rows] * dot_plain(gated, r.out[...])
        r.hidden[rows, :] = hidden
        r.hidden_low[rows, :] = normalize(hidden).astype(bf16)
        target = slice(row_count + j * chunk_rows, row_count + (j + 1) * chunk_rows)
        hidden_copies.append(links.send(r.hidden_low.at[rows, :], r.hidden_low.at[target, :], "mate"))
        if j == 0:
            gather_second.cross()

    own_tiles = [(0, 256), (256, 256), (512, 128)]
    far_tiles = [(640, 256), (896, 256), (1152, 256)]

    def forward(rows, tiles):
        for start, size in tiles:
            units = slice(start, start + size)
            first = dot_right_t(r.hidden_low[rows, :], r.first[units, :])
            second = dot_right_t(r.hidden_low[rows, :], r.second[units, :])
            r.first_act[rows, units] = first.astype(bf16)
            r.second_act[rows, units] = second.astype(bf16)
            r.product[rows, units] = (first * second).astype(bf16)

    def backward(rows, tiles):
        for start, size in tiles:
            units = slice(start, start + size)
            product_grad = dot_right_t(r.last[rows, :], r.third[units, :])
            first_grad = product_grad * r.second_act[rows, units].astype(f32)
            second_grad = product_grad * r.first_act[rows, units].astype(f32)
            r.first_act[rows, units] = first_grad.astype(bf16)
            r.second_act[rows, units] = second_grad.astype(bf16)

    units_all = slice(0, 2 * hidden_size)
    col_tiles = [slice(i, i + 256) for i in range(0, width, 256)]

    def norm_grad(rows, cols):
        return dot_plain(r.first_act[rows, units_all], r.first[:, cols]) + dot_plain(
            r.second_act[rows, units_all], r.second[:, cols]
        )

    def mix(rows, cols):
        return dot_plain(r.product[rows, units_all], r.third[:, cols])

    own_rows = slice(0, row_count)
    for copy in (load_first, load_second, load_third):
        copy.wait()
    mate_chunks = [slice(row_count + j * chunk_rows, row_count + (j + 1) * chunk_rows) for j in range(2)]
    mate_rows = slice(row_count, 2 * row_count)

    def give_core(source, target, rows):
        return links.send(source.at[rows, units_all], target.at[rows, :], "core")

    def weight_grad(target, left, left_in, right, right_in):
        size = right.shape[1]
        for start in range(0, size, 256):
            cols = slice(start, min(start + 256, size))
            total = dot_plain(left[...], right[:, cols]) + dot_plain(left_in[...], right_in[:, cols])
            target[:, cols] = total.astype(bf16)

    forward(own_rows, own_tiles)
    gather_second.last()
    split_transpose(r.hidden_low.at[own_rows, :], r.hidden_t, r.hidden_give, own_rows)
    gather_third.spread()
    gather_first.done()
    gather_second.done()
    forward(own_rows, far_tiles)
    product_core = [give_core(r.product, r.product_in, own_rows)]
    gather_third.cross()
    arrived(hidden_copies[:1])
    forward(mate_chunks[0], own_tiles + far_tiles)
    gather_third.last()
    backward(own_rows, own_tiles)
    arrived(hidden_copies[1:])
    forward(mate_chunks[1], own_tiles + far_tiles)
    product_core.append(give_core(r.product, r.product_in, mate_rows))
    gather_third.done()
    norm_copies = []

    def back_mate(j):
        rows, out_rows = mate_chunks[j], slice(j * chunk_rows, (j + 1) * chunk_rows)
        backward(rows, own_tiles + far_tiles)
        for cols in col_tiles:
            r.x[out_rows, cols] = norm_grad(rows, cols).astype(bf16)
        norm_copies.append(links.send(r.x.at[out_rows, :], r.norm_in.at[out_rows, :], "mate"))

    back_mate(0)
    arrived([last_core] + product_core)
    weight_grad(r.third_sum, r.last_t, r.last_in, r.product.at[:, units_all], r.product_in)
    chain_third = Chain(links, place, r.third_sum, r.third_half, r.third_quarter, 768)
    chain_third.start()
    backward(own_rows, far_tiles)
    grad_core = [
        [give_core(ref, target, own_rows)] for ref, target in ((r.first_act, r.first_in), (r.second_act, r.second_in))
    ]
    back_mate(1)
    for copies_of, ref, target in zip(grad_core, (r.first_act, r.second_act), (r.first_in, r.second_in)):
        copies_of.append(give_core(ref, target, mate_rows))
    split_transpose(r.hidden_low.at[mate_rows, :], r.hidden_t, r.hidden_give, mate_rows)
    hidden_core = links.send(r.hidden_give, r.hidden_in, "core")
    for cols in col_tiles:
        r.x[mate_rows, cols] = mix(mate_rows, cols).astype(bf16)

    def send_mix(j):
        rows = slice(j * chunk_rows, (j + 1) * chunk_rows)
        return links.send(r.x.at[mate_chunks[j], :], r.mix_in.at[rows, :], "mate")

    mix_copies = [send_mix(0)]
    for cols in col_tiles:
        r.mix[:, cols] = mix(own_rows, cols)
    arrived([hidden_core] + grad_core[0])
    links.left(product_core)
    first_sum = r.product.at[:, units_all]
    weight_grad(first_sum, r.hidden_t, r.hidden_in, r.first_act.at[:, units_all], r.first_in)
    chain_first = Chain(links, place, first_sum, r.first_half, r.first_quarter, 640)
    chain_first.start()
    for cols in col_tiles:
        r.hidden_grad[:, cols] = norm_grad(own_rows, cols)
    chain_third.middle()

    attention_copies = []
    mate_block, mate_far = flipped(own, 0), 3 - own
    for j in range(2):
        rows = slice(j * chunk_rows, (j + 1) * chunk_rows)
        arrived([norm_copies[j]])
        incoming = r.hidden_grad[rows, :] + r.norm_in[rows, :].astype(f32)
        hidden_grad = r.upstream[rows, :].astype(f32) + norm_back(r.hidden[rows, :], incoming)
        r.hidden_grad[rows, :] = hidden_grad
        branch = (row_mask[rows] * hidden_grad).astype(bf16)
        r.branch[rows, :] = branch
        gated_grad = dot_right_t(branch, r.out[...])
        attention = r.attention_rows[rows, :].astype(f32)
        r.gate_grad[rows, :] = (gated_grad * normalize(attention)).astype(bf16)
        grad = norm_back(attention, gated_grad * r.gate_pre[rows, :]).astype(bf16)
        r.attention_grad[rows, :] = grad
        target_rows = part(member * 2 + j, chunk_rows)
        for i, (mine, theirs) in enumerate(((own, mate_block), (flipped(own, 1), mate_far))):
            target = r.grad_block.at[target_rows, i * head_width : (i + 1) * head_width]
            source = r.attention_grad.at[rows, part(theirs, head_width)]
            attention_copies.append(links.send(source, target, "mate"))
            target[...] = r.attention_grad[rows, part(mine, head_width)]
    branch_core = links.send(r.branch, r.branch_in, "core")
    gate_core = links.send(r.gate_grad, r.gate_grad_in, "core")
    split_transpose(r.gated, r.gated_t, r.gated_give, slice(0, row_count))
    gated_core = links.send(r.gated_give, r.gated_in, "core")
    arrived(grad_core[1])
    links.left(grad_core[0])
    second_sum = r.first_act.at[:, units_all]
    weight_grad(second_sum, r.hidden_t, r.hidden_in, r.second_act.at[:, units_all], r.second_in)
    chain_second = Chain(links, place, second_sum, r.second_half, r.second_quarter, 768)
    chain_first.middle()
    chain_second.start()

    arrived([branch_core, gated_core])
    out_sum = r.out.at[:SPAN, :]
    weight_grad(out_sum, r.gated_t, r.gated_in, r.branch, r.branch_in)
    chain_out = Chain(links, place, out_sum, r.out_half, r.out_quarter, 512)
    chain_out.start()

    arrived(attention_copies)
    heads_all = 2 * block_heads
    for at in range(heads_all):
        cols = slice(at * HDIM, (at + 1) * HDIM)
        decayed = (r.queries[:, cols].astype(f32) * jnp.exp(-rate_of(at) * (places + 1.0))).astype(bf16)
        r.state_grad[at] = dot_left_t(decayed, r.grad_block[:, cols]).astype(bf16)
    near_heads, far_heads = pl.ds(0, block_heads), pl.ds(block_heads, block_heads)
    state_copies = [
        links.send(r.state_grad.at[near_heads], r.state_in.at[far_heads], "far"),
        links.send(r.state_grad.at[far_heads], r.state_in.at[near_heads], "far"),
    ]
    mix_copies.append(send_mix(1))

    def grad_cols(kind, at):
        start = (at // block_heads) * 3 * head_width + kind * head_width + (at % block_heads) * HDIM
        return slice(start, start + HDIM)

    for at in range(heads_all):
        rate = rate_of(at)
        cols = slice(at * HDIM, (at + 1) * HDIM)
        q, k, v, g = r.queries[:, cols], r.keys[:, cols], r.values[:, cols], r.grad_block[:, cols]
        decay = inner_decay(rate)
        weights = (dot_right_t(q, k) * decay).astype(bf16)
        score_grad = (dot_right_t(g, v) * decay).astype(bf16)
        dq = dot_plain(score_grad, k) + jnp.exp(-rate * (places + 1.0)) * dot_right_t(g, r.states[at])
        r.pre_grads[:, grad_cols(0, at)] = (dq * r.query_slope[:, cols].astype(f32)).astype(bf16)
        r.pre_grads[:, grad_cols(1, at)] = dot_left_t(score_grad, q).astype(bf16)
        r.pre_grads[:, grad_cols(2, at)] = dot_left_t(weights, g).astype(bf16)

    def to_far(chain, keep, give, target):
        total = chain.result().astype(bf16)
        size = keep.shape[1]
        keep[...] = total[:, :size]
        give[...] = total[:, size:]
        return links.send(give, target, "far")

    ends = [to_far(chain_third, r.third_keep, r.third_give, r.third_far)]
    arrived(state_copies)
    leaving = 1.0 - pair.astype(f32)
    for at in range(heads_all):
        rate = rate_of(at)
        cols = slice(at * HDIM, (at + 1) * HDIM)
        key_decay = leaving * jnp.exp(-rate * (SPAN - 1.0 - places))
        carried = r.state_in[at]
        dk = r.pre_grads[:, grad_cols(1, at)].astype(f32) + key_decay * dot_right_t(r.values[:, cols], carried)
        dv = r.pre_grads[:, grad_cols(2, at)].astype(f32) + key_decay * dot_plain(r.keys[:, cols], carried)
        r.pre_grads[:, grad_cols(1, at)] = (dk * r.key_slope[:, cols].astype(f32)).astype(bf16)
        r.pre_grads[:, grad_cols(2, at)] = (dv * mask).astype(bf16)
    pre_core = links.send(r.pre_grads, r.pre_in, "core")

    triple = 3 * head_width

    def head_terms(rows, cols):
        return dot_right_t(r.pre_grads[rows, :triple], r.heads[0, cols, :]) + dot_right_t(
            r.pre_grads[rows, triple:], r.heads[1, cols, :]
        )

    term_copies = []
    for start in range(0, width, 512):
        for cols in (slice(start, start + 256), slice(start + 256, start + 512)):
            r.terms[:, cols] = head_terms(part(1 - member, row_count), cols).astype(bf16)
        wide = slice(start, start + 512)
        term_copies.append(links.send(r.terms.at[:, wide], r.terms_in.at[:, wide], "mate"))
    chain_second.middle()
    ends.append(to_far(chain_first, r.first_keep, r.first_give, r.first_far))
    arrived([pre_core, normed_core])
    links.left(grad_core[1])
    weight_grad(r.second_act, r.normed_t, r.normed_in, r.pre_grads, r.pre_in)
    chain_heads = Chain(links, place, r.second_act, r.heads_half, r.heads_quarter, 768)
    chain_heads.start()
    for cols in col_tiles:
        r.terms_own[:, cols] = head_terms(part(member, row_count), cols) + dot_right_t(r.gate_grad[...], r.gate[cols, :])

    def to_heads(chain, keep, target):
        total = chain.result().astype(bf16)
        slot = chain.chunk(chain.y, chain.x)
        slot[...] = total
        size = total.shape[0] // 4
        keep[...] = slot[part(own, size), :]
        return [
            links.send(slot.at[part(index, size), :], target.at[i], device)
            for i, (index, device) in enumerate(((mate_block, "mate"), (flipped(own, 1), "far"), (mate_far, "cross")))
        ]

    chain_out.middle()
    arrived([gate_core])
    gate_sum = r.out.at[SPAN:, :]
    lanes = part(member, row_count)
    weight_grad(gate_sum, r.normed_t.at[:, lanes], r.normed_in.at[:, lanes], r.gate_grad, r.gate_grad_in)
    chain_gate = Chain(links, place, gate_sum, r.gate_half, r.gate_quarter, 512)
    ends.append(to_far(chain_second, r.second_keep, r.second_give, r.second_far))
    chain_heads.middle()
    chain_gate.start()
    ends += to_heads(chain_out, r.out_keep, r.out_far)
    arrived(mix_copies)
    r.output[...] = (r.hidden[...] + row_mask * (r.mix[...] + r.mix_in[...].astype(f32))).astype(bf16)
    ends.append(to_far(chain_heads, r.heads_keep, r.heads_give, r.heads_far))
    arrived(term_copies)
    for j in range(2):
        rows = slice(j * chunk_rows, (j + 1) * chunk_rows)
        incoming = r.terms_own[rows, :] + r.terms_in[rows, :].astype(f32)
        grad = r.hidden_grad[rows, :] + norm_back(r.x_rows[rows, :].astype(f32), incoming)
        r.input_grad[rows, :] = grad.astype(bf16)
    chain_gate.middle()
    ends += to_heads(chain_gate, r.gate_keep, r.gate_far)
    arrived(ends)
    links.finish()


def finish_kernel(count, *refs):
    sources, targets, refs = refs[:count], refs[count : count + 10], refs[count + 10 :]
    held, results, in_sems, out_sems = refs[:count], refs[count : count + 8], refs[-2], refs[-1]
    loads = [pltpu.make_async_copy(a, b, in_sems.at[i]) for i, (a, b) in enumerate(zip(sources, held))]
    for load in loads:
        load.start()
    stores = []

    def ready(index):
        for load in loads[2 * index : 2 * index + 2]:
            load.wait()
        return held[2 * index], held[2 * index + 1]

    def store(source, index):
        copy = pltpu.make_async_copy(source, targets[index], out_sems.at[index])
        copy.start()
        stores.append(copy)

    for i, rows in enumerate(ready(0)):
        store(rows, i)
    for i, index in ((1, 9), (2, 7), (3, 8)):
        keep, far = ready(i)
        results[index - 2][...] = (keep[...].astype(f32) + far[...].astype(f32)).T
        store(results[index - 2], index)
    keep, far = ready(4)
    size = targets[2].shape[1]
    for i in range(3):
        cols = slice(i * size, (i + 1) * size)
        results[i][...] = keep[:, cols].astype(f32) + far[:, cols].astype(f32)
        store(results[i], 2 + i)
    for i in (5, 6):
        keep, others = ready(i)
        total = keep[...].astype(f32)
        for j in range(3):
            total = total + others[j].astype(f32)
        results[i - 2][...] = total
        store(results[i - 2], i)
    for copy in stores:
        copy.wait()


def fused_shards(
    layer_input, w_query, w_key, w_value, w_gate, w_out, w_first, w_second, w_third,
    decay_rates, seq_lengths, cotangent,
):
    group_rows, width = layer_input.shape
    row_count = cotangent.shape[0]
    heads = decay_rates.shape[0]
    head_width = w_query.shape[1]
    units = w_third.shape[0]
    shape = jax.ShapeDtypeStruct
    share = width // 8
    both = 2 * head_width
    triple = 3 * head_width
    inputs = dict(
        lengths=seq_lengths, decay_rates=decay_rates, layer_input=layer_input, w_query=w_query, w_key=w_key, w_value=w_value,
        w_gate=w_gate, w_out=w_out, w_first=w_first.T, w_second=w_second.T, w_third=w_third, cotangent=cotangent,
    )
    rows_shape = shape((row_count, width), bf16)
    ffn_shape = shape((share, units), bf16)
    head_shape = shape((share, triple), bf16)
    dense_shape = shape((share // 4, width), bf16)
    dense_far = shape((3, share // 4, width), bf16)
    outputs = dict(
        output=rows_shape, input_grad=rows_shape,
        third_keep=ffn_shape, third_far=ffn_shape, first_keep=ffn_shape, first_far=ffn_shape,
        second_keep=ffn_shape, second_far=ffn_shape, heads_keep=head_shape, heads_far=head_shape,
        gate_keep=dense_shape, gate_far=dense_far, out_keep=dense_shape, out_far=dense_far,
    )
    low = lambda *dims: pltpu.VMEM(dims, bf16)
    wide = lambda *dims: pltpu.VMEM(dims, f32)
    half = width // 2
    scratch = dict(
        x=low(group_rows, width), normed=low(group_rows, width),
        heads=low(2, width, triple), gate=low(width, width), out=low(width, width),
        first=low(2 * units, width), second=low(2 * units, width), third=low(2 * units, width),
        upstream=low(row_count, width), rates=wide(8, 128), rates_far=wide(8, 128),
        queries=low(SPAN, both), keys=low(SPAN, both), values=low(SPAN, both),
        query_slope=low(SPAN, both), key_slope=low(SPAN, both), states=low(2 * heads, HDIM, HDIM),
        attention=low(SPAN, both), attention_rows=low(row_count, width), gate_pre=wide(row_count, width),
        hidden=wide(row_count, width),
        hidden_low=low(SPAN, width), last=low(SPAN, width),
        first_act=low(SPAN, 2 * units), second_act=low(SPAN, 2 * triple), product=low(SPAN, 2 * units),
        hidden_grad=wide(row_count, width), mix=wide(row_count, width), norm_in=low(row_count, width),
        mix_in=low(row_count, width), grad_block=low(SPAN, both),
        state_grad=low(2 * heads, HDIM, HDIM), state_in=low(2 * heads, HDIM, HDIM),
        pre_grads=low(SPAN, 2 * triple), terms_in=low(row_count, width),
        terms_own=wide(row_count, width),
        normed_t=low(half, SPAN), normed_give=low(half, SPAN), normed_in=low(half, SPAN),
        last_t=low(half, SPAN), last_give=low(half, SPAN), last_in=low(half, SPAN),
        hidden_t=low(half, SPAN), hidden_give=low(half, SPAN), hidden_in=low(half, SPAN),
        gated_t=low(half, row_count), gated_give=low(half, row_count), gated_in=low(half, row_count),
        product_in=low(SPAN, 2 * units), first_in=low(SPAN, 2 * units), second_in=low(SPAN, 2 * units),
        pre_in=low(SPAN, 2 * triple), branch_in=low(row_count, width), gate_grad_in=low(row_count, width),
        third_sum=low(half, 2 * units),
        third_half=low(2 * share, 2 * units), first_half=low(2 * share, 2 * units),
        second_half=low(2 * share, 2 * units), heads_half=low(2 * share, 2 * triple),
        gate_half=low(2 * share, width), out_half=low(2 * share, width),
        third_quarter=low(share, 2 * units), first_quarter=low(share, 2 * units),
        second_quarter=low(share, 2 * units), heads_quarter=low(share, 2 * triple),
        gate_quarter=low(share, width), out_quarter=low(share, width),
        third_give=low(share, units), first_give=low(share, units), second_give=low(share, units),
        heads_give=low(share, triple),
        local_sems=pltpu.SemaphoreType.DMA((16,)),
        send_sems=pltpu.SemaphoreType.DMA((144,)), recv_sems=pltpu.SemaphoreType.DMA((144,)),
    )
    results = pl.pallas_call(
        functools.partial(layer_kernel, list(inputs) + list(outputs) + list(scratch)),
        out_shape=list(outputs.values()),
        in_specs=[smem(), smem()] + [pl.BlockSpec(memory_space=pl.ANY)] * (len(inputs) - 2),
        out_specs=[vmem()] * len(outputs),
        scratch_shapes=list(scratch.values()),
        compiler_params=pltpu.CompilerParams(
            collective_id=0, has_side_effects=True, vmem_limit_bytes=VMEM_ALL
        ),
        name="layer",
    )(*inputs.values())
    transposed_shape = shape((units, share), f32)
    finals = [rows_shape] * 2 + [shape((share, head_width), f32)] * 3 + [shape((share // 4, width), f32)] * 2
    finals += [transposed_shape] * 3
    place_any = pl.BlockSpec(memory_space=pltpu.HBM)
    results = pl.pallas_call(
        functools.partial(finish_kernel, len(results)),
        out_shape=finals,
        in_specs=[place_any] * len(results),
        out_specs=[place_any] * 10,
        scratch_shapes=[pltpu.VMEM(a.shape, a.dtype) for a in list(results) + finals[2:]]
        + [pltpu.SemaphoreType.DMA((len(results),)), pltpu.SemaphoreType.DMA((10,))],
        compiler_params=pltpu.CompilerParams(vmem_limit_bytes=VMEM_ALL),
        name="finish",
    )(*results)
    return (*results[:7], results[7].T, results[8].T, results[9])


def solution(mesh):
    placed = (
        P("dp", None),
        P(None, "head"),
        P(None, "head"),
        P(None, "head"),
        P(),
        P(),
        P(None, "head"),
        P(None, "head"),
        P("head", None),
        P("head"),
        P("dp"),
        P(("dp", "head"), None),
    )
    n_dp, n_head = mesh.shape["dp"], mesh.shape["head"]
    body = fused_shards if (n_dp, n_head) == (8, 4) else functools.partial(shards, n_dp, n_head)
    return jax.shard_map(
        body,
        mesh=mesh,
        in_specs=placed,
        out_specs=(
            P(("dp", "head"), None),
            P(("dp", "head"), None),
            P("dp", "head"),
            P("dp", "head"),
            P("dp", "head"),
            P(("dp", "head"), None),
            P(("dp", "head"), None),
            P("dp", "head"),
            P("dp", "head"),
            P("head", "dp"),
        ),
        check_vma=False,
    )
```
